32 devices in a mesh: dp: 8 (over y, x, core), mp: 4 (over z).
Axes of the slice: x: 2, y: 2, z: 4, core: 2. Of those that a mesh axis runs over, the one named last changes fastest.
Arguments:
- x_long: bfloat16 [8, 1024, 768], P('dp', 'mp'), may hold values from -6 to 6
- x_short: bfloat16 [8, 512, 768], P('dp', 'mp'), may hold values from -6 to 6
- dy_long: bfloat16 [8, 1024, 768], P('dp', 'mp'), may hold values from -6 to 6
- dy_short: bfloat16 [8, 512, 768], P('dp', 'mp'), may hold values from -6 to 6
- ln_gain: bfloat16 [2, 2, 768], replicated, may hold values from 0.5 to 1.5
- ln_bias: bfloat16 [2, 2, 768], replicated, may hold values from -1 to 1
- w_qkv: bfloat16 [2, 768, 3, 768], P(None, None, None, 'mp'), may hold values from -0.21875 to 0.21875
- b_qv: bfloat16 [2, 2, 768], P(None, None, 'mp'), may hold values from -1.5 to 1.5
- w_out: bfloat16 [2, 768, 768], P(None, 'mp'), may hold values from -0.4375 to 0.4375
- b_out: bfloat16 [2, 768], replicated, may hold values from -1 to 1
- w_up: bfloat16 [2, 768, 3072], P(None, None, 'mp'), may hold values from -0.21875 to 0.21875
- b_up: bfloat16 [2, 3072], P(None, 'mp'), may hold values from -1.5 to 1.5
- w_down: bfloat16 [2, 3072, 768], P(None, 'mp'), may hold values from -0.109375 to 0.109375
- b_down: bfloat16 [2, 768], replicated, may hold values from -1 to 1
- threshold: int32 [2], replicated, may hold values from 16 to 79
Outputs:
- y_long: bfloat16 [8, 1024, 768], P('dp', 'mp')
- y_short: bfloat16 [8, 512, 768], P('dp', 'mp')
- dx_long: float32 [8, 1024, 768], P('dp', 'mp')
- dx_short: float32 [8, 512, 768], P('dp', 'mp')
- g_ln_gain: float32 [2, 2, 768], replicated
- g_ln_bias: float32 [2, 2, 768], replicated
- g_w_qkv: float32 [2, 768, 3, 768], P(None, 'dp', None, 'mp')
- g_b_qv: float32 [2, 2, 768], P(None, None, 'mp')
- g_w_out: float32 [2, 768, 768], P(None, 'mp', 'dp')
- g_b_out: float32 [2, 768], replicated
- g_w_up: float32 [2, 768, 3072], P(None, 'dp', 'mp')
- g_b_up: float32 [2, 3072], P(None, 'mp')
- g_w_down: float32 [2, 3072, 768], P(None, 'mp', 'dp')
- g_b_down: float32 [2, 768], replicated
- key_share: float32 [2], replicated
The draws below stay inside these ranges and needn't reach their ends.
All inputs are finite; a program needn't handle non-finite values.
Results may differ from the reference program's by a relative error of at most 0.03.
Values may be sent and summed in bfloat16 or wider, within the bound.
A program may use at most 192 MiB of HBM per device.

```python
import math
import jax
import jax.numpy as jnp
from jax import lax

D = 768
HEADS = 12
HEAD_DIM = 64
FF = 3072
LAYERS = 2
LONG = 1024
SHORT = 512
LSEQ = 8
SSEQ = 8


def shard_levels(stream_key, dims, cuts, least, top_value):
    factor_of, own = 1.0, jax.random.fold_in(stream_key, 6)
    for dim, parts in cuts:
        steps = jnp.exp(jax.random.uniform(jax.random.fold_in(own, dim), (parts,), jnp.float32, least / len(cuts), top_value / len(cuts)))
        factor_of = factor_of * jnp.repeat(steps, dims[dim] // parts).reshape([-1 if axis == dim else 1 for axis in range(len(dims))])
    return factor_of


def noise(rng, extent, deviation, limit, cuts=(), dtype=jnp.bfloat16):
    entries = jax.random.normal(rng, extent, jnp.float32) * deviation
    if len(cuts) > 0:
        entries = shard_levels(rng, extent, cuts, -0.22, 0.18) * entries
    return jnp.clip(entries, min=-limit, max=limit).astype(dtype)


def setup_inputs(seed: int = 0) -> dict:
    key_of = jax.random.split(jax.random.key(seed), 16)
    x_long = noise(key_of[0], (LSEQ, LONG, D), 1.0, 6.0, ((0, 8), (1, 4)))
    x_short = noise(key_of[1], (SSEQ, SHORT, D), 1.0, 6.0, ((0, 8), (1, 4)))
    dy_long = noise(key_of[2], (LSEQ, LONG, D), 1.0, 6.0, ((0, 8), (1, 4)))
    dy_short = noise(key_of[3], (SSEQ, SHORT, D), 1.0, 6.0, ((0, 8), (1, 4)))
    ln_gain = jnp.clip(1.0 + 0.1 * jax.random.normal(key_of[4], (LAYERS, 2, D), jnp.float32), 0.5, 1.5).astype(jnp.bfloat16)
    ln_bias = noise(key_of[5], (LAYERS, 2, D), 0.2, 1.0)
    w_qkv = noise(key_of[6], (LAYERS, D, 3, HEADS * HEAD_DIM), D ** -0.5, 0.21875, ((3, 4),))
    b_qv = noise(key_of[7], (LAYERS, 2, HEADS * HEAD_DIM), 0.3, 1.5, ((2, 4),))
    w_out = noise(key_of[8], (LAYERS, HEADS * HEAD_DIM, D), (HEADS * HEAD_DIM // 4) ** -0.5, 0.4375, ((1, 4),))
    b_out = noise(key_of[9], (LAYERS, D), 0.2, 1.0)
    w_up = noise(key_of[10], (LAYERS, D, FF), D ** -0.5, 0.21875, ((2, 4),))
    b_up = noise(key_of[11], (LAYERS, FF), 0.3, 1.5, ((1, 4),))
    w_down = noise(key_of[12], (LAYERS, FF, D), FF ** -0.5, 0.109375, ((1, 4),))
    b_down = noise(key_of[13], (LAYERS, D), 0.2, 1.0)
    threshold = jax.random.randint(key_of[14], (LAYERS,), 16, 80).astype(jnp.int32)
    return {"x_long": x_long, "x_short": x_short, "dy_long": dy_long, "dy_short": dy_short, "ln_gain": ln_gain, "ln_bias": ln_bias, "w_qkv": w_qkv, "b_qv": b_qv, "w_out": w_out, "b_out": b_out, "w_up": w_up, "b_up": b_up, "w_down": w_down, "b_down": b_down, "threshold": threshold}


HIGHEST_PRECISION = lax.Precision.HIGHEST
norm_eps = 1e-05

@jax.custom_vjp
def low(v):
    return lax.optimization_barrier(v.astype(jnp.bfloat16)).astype(jnp.float32)

@jax.custom_vjp
def low_back(v):
    return v

def low_keep(v):
    return (low(v), None)

def low_pass(kept, grad):
    return (grad,)

def back_keep(v):
    return (v, None)

def back_low(kept, grad):
    return (low(grad),)
low.defvjp(low_keep, low_pass)
low_back.defvjp(back_keep, back_low)

def layer_norm(resid, norm_gain, norm_shift):
    average = lax.optimization_barrier(jnp.mean(resid, axis=-1, keepdims=True))
    centred = resid - average
    variance = lax.optimization_barrier(jnp.mean(centred * centred, axis=-1, keepdims=True))
    return centred * lax.rsqrt(variance + norm_eps) * norm_gain + norm_shift

def attend_one(inputs):
    queries, keys_all, values = inputs
    seq_len = queries.shape[0]
    score_scale = 1.0 / math.sqrt(HEAD_DIM)
    scores = low_back(jnp.einsum('ihd,jhd->hij', queries, keys_all, precision=HIGHEST_PRECISION) * score_scale)
    sel_score = jnp.einsum('id,jd->ij', queries[:, 0], keys_all[:, 0], precision=HIGHEST_PRECISION) * score_scale
    row_ids = lax.broadcasted_iota(jnp.int32, (seq_len, seq_len), 0)
    col_ids = lax.broadcasted_iota(jnp.int32, (seq_len, seq_len), 1)
    chosen = jnp.logical_and(col_ids >= 1, row_ids > col_ids)
    select = jnp.where(chosen, jax.nn.softplus(sel_score), 0.0)
    penalty = jnp.cumsum(select, axis=0) - select
    logits = jnp.where(row_ids >= col_ids, scores - penalty[None], -jnp.inf)
    weights = low(jax.nn.softmax(logits, axis=-1))
    output = jnp.einsum('hij,jhd->ihd', weights, values, precision=HIGHEST_PRECISION)
    return (output, lax.optimization_barrier(jnp.sum(select, axis=0)))

def layer_forward(groups, layer_params, limit_value):
    norm_gain, norm_shift, w_qkv_l, b_qv_l, w_out_l, b_out_l, w_up_l, b_up_l, w_down_l, b_down_l = layer_params
    results = []
    share_sum = jnp.zeros((), jnp.float32)
    for resid in groups:
        seq_count, seq_len, model_width = resid.shape
        normed = low(layer_norm(resid, norm_gain[0], norm_shift[0]))
        projected = jnp.einsum('std,dce->stce', normed, w_qkv_l, precision=HIGHEST_PRECISION)
        head_shape = (seq_count, seq_len, HEADS, HEAD_DIM)
        queries = low(low_back(projected[:, :, 0] + b_qv_l[0])).reshape(head_shape)
        keys_all = low(low_back(projected[:, :, 1])).reshape(head_shape)
        values = low(low_back(projected[:, :, 2] + b_qv_l[1])).reshape(head_shape)
        attended, sel_sums = lax.map(jax.checkpoint(attend_one), (queries, keys_all, values))
        attended = low(low_back(attended.reshape(seq_count, seq_len, HEADS * HEAD_DIM)))
        branch = low_back(jnp.einsum('ste,ed->std', attended, w_out_l, precision=HIGHEST_PRECISION))
        middle = resid + branch + b_out_l
        normed2 = low(layer_norm(middle, norm_gain[1], norm_shift[1]))
        upper = low_back(jnp.einsum('std,df->stf', normed2, w_up_l, precision=HIGHEST_PRECISION) + b_up_l)
        active = low(jax.nn.gelu(upper, approximate=True))
        branch2 = low_back(jnp.einsum('stf,fd->std', active, w_down_l, precision=HIGHEST_PRECISION))
        results.append(middle + branch2 + b_down_l)
        later_rows = (seq_len - 1 - jnp.arange(seq_len)).astype(jnp.float32)
        share_sum = share_sum + jnp.sum(jax.nn.sigmoid(4.0 * (sel_sums / jnp.maximum(later_rows, 1.0) - limit_value)))
    return (tuple(results), share_sum)

def reference(x_long, x_short, dy_long, dy_short, ln_gain, ln_bias, w_qkv, b_qv, w_out, b_out, w_up, b_up, w_down, b_down, threshold):
    params = tuple((arr.astype(jnp.float32) for arr in (ln_gain, ln_bias, w_qkv, b_qv, w_out, b_out, w_up, b_up, w_down, b_down)))
    groups = (x_long.astype(jnp.float32), x_short.astype(jnp.float32))
    limits = threshold.astype(jnp.float32) / 64.0
    total_keys = LSEQ * LONG + SSEQ * SHORT

    def forward(params_in, groups_in):
        current = groups_in
        shares = []
        for layer in range(LAYERS):
            current, share_sum = layer_forward(current, tuple((arr[layer] for arr in params_in)), limits[layer])
            shares.append(share_sum)
        return (current, jnp.stack(shares) / total_keys)
    outputs, pullback, key_share = jax.vjp(forward, params, groups, has_aux=True)
    grad_params, grad_groups = pullback((dy_long.astype(jnp.float32), dy_short.astype(jnp.float32)))
    g_gain, g_shift, g_wqkv, g_bqv, g_wout, g_bout, g_wup, g_bup, g_wdown, g_bdown = grad_params
    return (outputs[0].astype(jnp.bfloat16), outputs[1].astype(jnp.bfloat16), grad_groups[0], grad_groups[1], g_gain, g_shift, g_wqkv, g_bqv, g_wout, g_bout, g_wup, g_bup, g_wdown, g_bdown, key_share)
```

```python
import functools

import jax, jax.numpy as jnp
from jax import lax
from jax.experimental import pallas as pl
from jax.experimental.pallas import tpu as pltpu
from jax.sharding import Mesh
from jax.sharding import PartitionSpec as P

HD = 64
BR = 256
BIG = 1e30
NT = (((1,), (1,)), ((), ()))
NN = (((1,), (0,)), ((), ()))


def mm(a, b, dims=NN):
    return lax.dot_general(a, b, dims, preferred_element_type=jnp.float32)


def halves(v):
    hi = v.astype(jnp.bfloat16)
    lo = (v - hi.astype(jnp.float32)).astype(jnp.bfloat16)
    return hi, lo


def softplus(v):
    return jnp.maximum(v, 0.0) + jnp.log(1.0 + jnp.exp(-jnp.abs(v)))


def fwd_one(x_ref, o_ref, lse_ref, carry_ref):
    size = x_ref.shape[0]
    nh = (x_ref.shape[1] - 2 * HD) // (3 * HD)
    w = nh * HD
    nb = size // BR
    first = lax.broadcasted_iota(jnp.int32, (BR, BR), 0)
    second = lax.broadcasted_iota(jnp.int32, (BR, BR), 1)
    tri = (first > second).astype(jnp.bfloat16)
    lanes = lax.broadcasted_iota(jnp.int32, (BR, 128), 1)
    lse_ref[...] = jnp.zeros_like(lse_ref)
    carry_ref[...] = jnp.zeros_like(carry_ref)
    for b in range(nb):
        rows = pl.ds(b * BR, BR)
        q0 = x_ref[rows, 3 * w : 3 * w + HD] * 0.125
        pens = []
        for c in range(b + 1):
            cols = pl.ds(c * BR, BR)
            sp = softplus(mm(q0, x_ref[cols, 3 * w + HD : 3 * w + 2 * HD], NT))
            if c == b:
                keep = first > second
                if c == 0:
                    keep = jnp.logical_and(keep, second >= 1)
                sp = jnp.where(keep, sp, 0.0)
            elif c == 0:
                sp = jnp.where(second >= 1, sp, 0.0)
            hi, lo = halves(sp)
            pen = mm(tri, hi) + mm(tri, lo) + carry_ref[b : b + 1, cols]
            carry_ref[b + 1 : b + 2, cols] = pen[BR - 1 :] + sp[BR - 1 :]
            if c == b:
                pen = jnp.where(first >= second, pen, BIG)
            pens.append(pen)
        stats = jnp.zeros((BR, 128), jnp.float32)
        for h in range(nh):
            qh = x_ref[rows, h * HD : (h + 1) * HD] * 0.125
            scores = [
                mm(qh, x_ref[c * BR : (c + 1) * BR, w + h * HD : w + (h + 1) * HD], NT) - pens[c]
                for c in range(b + 1)
            ]
            top = scores[0]
            for s in scores[1:]:
                top = jnp.maximum(top, s)
            top = jnp.max(top, axis=1, keepdims=True)
            total = None
            acc = None
            for c in range(b + 1):
                e = jnp.exp(scores[c] - top)
                total = e if total is None else total + e
                part = mm(
                    e.astype(jnp.bfloat16),
                    x_ref[c * BR : (c + 1) * BR, 2 * w + h * HD : 2 * w + (h + 1) * HD],
                )
                acc = part if acc is None else acc + part
            total = jnp.sum(total, axis=1, keepdims=True)
            o_ref[rows, h * HD : (h + 1) * HD] = (acc / total).astype(jnp.bfloat16)
            stats = jnp.where(lanes == h, top + jnp.log(total), stats)
        lse_ref[:, rows] = jnp.transpose(stats)[:8]


def bwd_one(x_ref, g_ref, o_ref, lse_ref, carry_ref, d_ref, acc, kt):
    size = x_ref.shape[0]
    nh = (x_ref.shape[1] - 2 * HD) // (3 * HD)
    w = nh * HD
    nb = size // BR
    jj = lax.broadcasted_iota(jnp.int32, (BR, BR), 0)
    ii = lax.broadcasted_iota(jnp.int32, (BR, BR), 1)
    below = (jj < ii).astype(jnp.bfloat16)
    above = (jj > ii).astype(jnp.bfloat16)
    ones = jnp.ones((8, HD), jnp.bfloat16)
    for h in range(nh + 1):
        lo = 3 * w + HD if h == nh else w + h * HD
        kt[h, :, :size] = jnp.transpose(x_ref[:, lo : lo + HD].astype(jnp.float32)).astype(
            jnp.bfloat16
        )
    later = [None] * nb
    for b in reversed(range(nb)):
        rows = pl.ds(b * BR, BR)
        q0 = x_ref[rows, 3 * w : 3 * w + HD] * 0.125
        pens, sigs, sums = [], [], [None] * (b + 1)
        for c in range(b + 1):
            sel = mm(x_ref[c * BR : (c + 1) * BR, 3 * w + HD : 3 * w + 2 * HD], q0, NT)
            small = jnp.exp(-jnp.abs(sel))
            sp = jnp.maximum(sel, 0.0) + jnp.log(1.0 + small)
            sig = jnp.where(sel >= 0, 1.0, small) / (1.0 + small)
            if c == b or c == 0:
                keep = None
                if c == b:
                    keep = ii > jj
                if c == 0:
                    keep = jj >= 1 if keep is None else jnp.logical_and(keep, jj >= 1)
                sp = jnp.where(keep, sp, 0.0)
                sig = jnp.where(keep, sig, 0.0)
            hi, lo = halves(sp)
            start = jnp.transpose(
                jnp.broadcast_to(carry_ref[b : b + 1, c * BR : (c + 1) * BR], (128, BR))
            )
            pen = mm(hi, below) + mm(lo, below) + start[:, :1]
            if c == b:
                pen = jnp.where(ii >= jj, pen, BIG)
            pens.append(pen)
            sigs.append(sig)
        for h in range(nh):
            qh = x_ref[rows, h * HD : (h + 1) * HD] * 0.125
            gh = g_ref[rows, h * HD : (h + 1) * HD]
            prod = gh.astype(jnp.float32) * o_ref[rows, h * HD : (h + 1) * HD].astype(jnp.float32)
            phi, plo = halves(prod)
            delta = (mm(ones, phi, NT) + mm(ones, plo, NT))[:1]
            lse = lse_ref[h : h + 1, rows]
            dqt = None
            for c in range(b + 1):
                cols = pl.ds(c * BR, BR)
                s = mm(x_ref[cols, w + h * HD : w + (h + 1) * HD], qh, NT)
                p = jnp.exp((s - pens[c]) - lse)
                dp = mm(x_ref[cols, 2 * w + h * HD : 2 * w + (h + 1) * HD], gh, NT)
                ds = p * (dp - delta)
                low = ds.astype(jnp.bfloat16)
                dk = mm(low, qh)
                dv = mm(p.astype(jnp.bfloat16), gh)
                part = mm(kt[h, :, c * BR : (c + 1) * BR], low)
                dqt = part if dqt is None else dqt + part
                if b == nb - 1:
                    acc[h, cols] = dk
                    acc[nh + h, cols] = dv
                else:
                    acc[h, cols] += dk
                    acc[nh + h, cols] += dv
                sums[c] = ds if sums[c] is None else sums[c] + ds
            d_ref[rows, h * HD : (h + 1) * HD] = jnp.transpose(dqt * 0.125).astype(jnp.bfloat16)
        dqt = None
        for c in range(b + 1):
            cols = pl.ds(c * BR, BR)
            hi, lo = halves(sums[c])
            grad = mm(hi, above) + mm(lo, above)
            full = grad[:, :1] + sums[c][:, :1]
            if later[c] is not None:
                grad = grad + later[c]
                full = full + later[c]
            later[c] = full
            low = (-(grad * sigs[c])).astype(jnp.bfloat16)
            dk = mm(low, q0)
            part = mm(kt[nh, :, c * BR : (c + 1) * BR], low)
            dqt = part if dqt is None else dqt + part
            if b == nb - 1:
                acc[2 * nh, cols] = dk
            else:
                acc[2 * nh, cols] += dk
        d_ref[rows, 3 * w : 3 * w + HD] = jnp.transpose(dqt * 0.125).astype(jnp.bfloat16)
        own = pl.ds(b * BR, BR)
    for h in range(nh):
        d_ref[:, w + h * HD : w + (h + 1) * HD] = acc[h, :size].astype(jnp.bfloat16)
        d_ref[:, 2 * w + h * HD : 2 * w + (h + 1) * HD] = acc[nh + h, :size].astype(jnp.bfloat16)
    d_ref[:, 3 * w + HD : 3 * w + 2 * HD] = acc[2 * nh, :size].astype(jnp.bfloat16)


VMEM = pl.BlockSpec(memory_space=pltpu.VMEM)
LIMIT = 48 * 1024 * 1024


def attend_fwd(x):
    size, w = x.shape[0], (x.shape[1] - 2 * HD) // 3
    return pl.pallas_call(
        fwd_one,
        out_shape=(
            jax.ShapeDtypeStruct((size, w), jnp.bfloat16),
            jax.ShapeDtypeStruct((8, size), jnp.float32),
            jax.ShapeDtypeStruct((8, size), jnp.float32),
        ),
        in_specs=[VMEM],
        out_specs=(VMEM,) * 3,
        compiler_params=pltpu.CompilerParams(vmem_limit_bytes=LIMIT),
        cost_estimate=pl.CostEstimate(
            flops=size * size * 64 * 40, bytes_accessed=size * 2000, transcendentals=size * size * 3
        ),
        name="attend_fwd",
    )(x)


def attend_bwd(x, g, o, lse, carry):
    size, w = x.shape[0], (x.shape[1] - 2 * HD) // 3
    nh = w // HD
    return pl.pallas_call(
        bwd_one,
        out_shape=jax.ShapeDtypeStruct(x.shape, jnp.bfloat16),
        in_specs=[VMEM] * 5,
        out_specs=VMEM,
        scratch_shapes=[
            pltpu.VMEM((2 * nh + 1, size, HD), jnp.float32),
            pltpu.VMEM((nh + 1, HD, size), jnp.bfloat16),
        ],
        compiler_params=pltpu.CompilerParams(vmem_limit_bytes=LIMIT),
        cost_estimate=pl.CostEstimate(
            flops=size * size * 64 * 80, bytes_accessed=size * 4000, transcendentals=size * size * 3
        ),
        name="attend_bwd",
    )(x, g, o, lse, carry)


EPS = 1e-05
F32 = jnp.float32
BF = jnp.bfloat16


def swap(v, *axes):
    count = 2 ** len(axes)
    return lax.ppermute(
        v, axes if len(axes) > 1 else axes[0], [(i, count - 1 - i) for i in range(count)]
    )


def ordered(own, other, index, axis):
    return jnp.where(
        index == 0,
        jnp.concatenate([own, other], axis=axis),
        jnp.concatenate([other, own], axis=axis),
    )


def pick(v, index, axis):
    return lax.dynamic_index_in_dim(v, index, axis, keepdims=False)


def normalize(v, gain, shift):
    mean = jnp.mean(v, axis=-1, keepdims=True)
    cen = v - mean
    var = jnp.mean(cen * cen, axis=-1, keepdims=True)
    inv = lax.rsqrt(var + EPS)
    hat = cen * inv
    return hat * gain + shift, hat, inv


def normalize_back(grad, hat, inv, gain):
    gh = grad * gain
    a = jnp.mean(gh, axis=-1, keepdims=True)
    b = jnp.mean(gh * hat, axis=-1, keepdims=True)
    return inv * (gh - a - hat * b), jnp.sum(grad * hat, axis=0), jnp.sum(grad, axis=0)


def gelu_both(u):
    k = 0.7978845608028654
    inner = k * (u + 0.044715 * u * u * u)
    t = jnp.tanh(inner)
    act = 0.5 * u * (1.0 + t)
    slope = 0.5 * (1.0 + t) + 0.5 * u * (1.0 - t * t) * k * (1.0 + 3 * 0.044715 * u * u)
    return act, slope


def dot(a, b, ca=1, cb=0):
    return lax.dot_general(a, b, (((ca,), (cb,)), ((), ())), preferred_element_type=F32)


class Plan:
    def __init__(self, dims, dp, mp):
        self.dims, self.dp, self.mp = dims, dp, mp
        self.core = dims[-1]
        self.plane = dims[:-1]
        self.c = lax.axis_index(self.core)
        self.zh = lax.axis_index("zh")
        self.zl = lax.axis_index("zl")
        self.z = lax.axis_index(("zh", "zl"))
        self.d = lax.axis_index(dims)

    def relabel(self, v):
        got = lax.ppermute(v, (self.core, "zh"), [(1, 2), (2, 1)])
        return jnp.where(self.c == self.zh, v, got)

    def ring(self, v, step):
        n = self.mp
        return lax.ppermute(v, ("zh", "zl"), [(i, (i + step) % n) for i in range(n)])

    def gather(self, v):
        v = ordered(v, swap(v, "zl"), self.zl, 0)
        return ordered(v, swap(v, self.core), self.c, 0)

    def scatter(self, v):
        rows = v.shape[0] // 4
        v = v.reshape(2, 2, rows, v.shape[1])
        got = swap(pick(v, 1 - self.c, 0), self.core)
        mine = pick(v, self.c, 0).astype(F32) + got.astype(F32)
        got = swap(pick(mine, 1 - self.zl, 0).astype(BF), "zl")
        return pick(mine, self.zl, 0) + got.astype(F32)

    def to_rows(self, o):
        rows = o.shape[0] // 4
        o = o.reshape(2, 2, rows, o.shape[1])
        got = []
        for dc in range(2):
            line = []
            for dz in range(2):
                part = pick(pick(o, self.c ^ dc, 0), self.zl ^ dz, 0)
                axes = ((self.core,) if dc else ()) + (("zl",) if dz else ())
                line.append(swap(part, *axes) if axes else part)
            got.append(ordered(line[0], line[1], self.zl, 1))
        return ordered(got[0], got[1], self.c, 1)

    def to_heads(self, g):
        rows, w = g.shape[0], g.shape[1] // 4
        g = g.reshape(rows, 2, 2, w)
        got = []
        for dc in range(2):
            line = []
            for dz in range(2):
                part = pick(pick(g, self.c ^ dc, 1), self.zl ^ dz, 1)
                axes = ((self.core,) if dc else ()) + (("zl",) if dz else ())
                line.append(swap(part, *axes) if axes else part)
            got.append(ordered(line[0], line[1], self.zl, 0))
        return ordered(got[0], got[1], self.c, 0)

    def piece(self, w):
        rows = w.shape[0] // self.dp
        return lax.dynamic_slice_in_dim(w, self.d * rows, rows, 0)

    def ring_gather(self, v):
        parts = []
        for _ in range(self.mp - 1):
            v = self.ring(v, 1)
            parts.append(v)
        return parts

    def plane_gather(self, v, axes):
        k, rows, n = v.shape
        have = []
        shape = [k]
        for ax in axes:
            pos = sum(self.dims.index(h) < self.dims.index(ax) for h in have)
            got = swap(v, ax)
            cur = v.reshape(k, *([2] * len(have)), rows, n)
            oth = got.reshape(cur.shape)
            a = jnp.stack([cur, oth], axis=1 + pos)
            b = jnp.stack([oth, cur], axis=1 + pos)
            v = jnp.where(lax.axis_index(ax) == 0, a, b)
            have.append(ax)
            v = v.reshape(k, -1, rows, n).reshape(k, -1, n)
            rows_all = v.shape[1]
            v = v.reshape(k, rows_all, n)
        return v.reshape(k, self.dp, rows, n)

    def plane_scatter(self, g, axes):
        n = g.shape[1]
        left = [ax for ax in self.dims]
        rows = g.shape[0] // self.dp
        v = g.reshape(*([2] * len(left)), rows, n)
        for ax in axes:
            pos = left.index(ax)
            i = lax.axis_index(ax)
            got = swap(pick(v, 1 - i, pos), ax)
            v = (pick(v, i, pos).astype(F32) + got.astype(F32)).astype(BF)
            left.remove(ax)
        return v.reshape(-1, n)

    def ring_scatter(self, chunks):
        t = chunks[-1]
        for r in range(self.mp - 2, -1, -1):
            got = self.ring(t, -1)
            t = chunks[r].astype(F32) + got.astype(F32)
            if r:
                t = t.astype(BF)
        return t


def body(
    dims, dp, mp,
    x_long, x_short, dy_long, dy_short, ln_gain, ln_bias, w_qkv, b_qv, w_out, b_out, w_up, b_up, w_down, b_down, threshold,
):
    plan = Plan(dims, dp, mp)
    layers = w_qkv.shape[0]
    d_model = x_long.shape[-1]
    heads_w = w_qkv.shape[-1]
    ffq = w_up.shape[-1]
    rl, rs = x_long.shape[1], x_short.shape[1]
    rows = rl + rs
    core_rest = tuple(plan.plane)
    fwd_axes = core_rest + (plan.core,)
    alt_axes = core_rest[::-1] + (plan.core,)
    gain = ln_gain.astype(F32)
    shift = ln_bias.astype(F32)

    x = jnp.concatenate([x_long[0], x_short[0]], axis=0)
    x = plan.relabel(x)

    small = jnp.concatenate([b_up.reshape(-1), b_qv.reshape(-1)])
    rel_small = jnp.stack([small] + plan.ring_gather(small))
    n_up = layers * ffq
    rel_bup = rel_small[:, :n_up].reshape(mp, layers, ffq).astype(F32)
    rel_bqv = rel_small[:, n_up:].reshape(mp, layers, 2, heads_w).astype(F32)
    mine = 2 * plan.c + plan.zl
    my_bqv = pick(rel_bqv, (plan.z - mine) % mp, 0)
    zero_bq = pick(rel_bqv, plan.z % mp, 0)[:, 0, :HD]

    exts = []
    for l in range(layers):
        quarter = plan.relabel(w_qkv[l].reshape(d_model, 3 * heads_w))
        head0 = w_qkv[l][:, :2, :HD].reshape(d_model, 2 * HD)
        got = lax.ppermute(head0, "zl", [(0, 1)])
        head0 = jnp.where(plan.zl == 0, head0, got)
        got = lax.ppermute(head0, "zh", [(0, 1)])
        head0 = jnp.where(plan.zh == 0, head0, got)
        exts.append(jnp.concatenate([quarter, head0], axis=1))

    ups, downs, outs = [], [], []
    for l in range(layers):
        po = plan.piece(w_out[l])
        pu = jnp.concatenate([plan.piece(w_up[l]), po], axis=0)
        pd = plan.piece(w_down[l])
        n_out, n_d = po.shape[0], pd.shape[0]
        both = plan.ring_gather(jnp.concatenate([pu, pd], axis=0))
        stacked = jnp.stack(both)
        n_u = pu.shape[0]
        gu = plan.plane_gather(stacked[:, :n_u], fwd_axes)
        gd = plan.plane_gather(stacked[:, n_u:], alt_axes)
        up = gu[:, :, : n_u - n_out].reshape(mp - 1, d_model, ffq)
        ups.append(jnp.concatenate([w_up[l]] + [up[r] for r in range(mp - 1)], axis=1))
        out = gu[:, :, n_u - n_out :].reshape(mp - 1, heads_w, d_model)
        out = jnp.concatenate([w_out[l][None], out], axis=0)
        outs.append(
            jnp.concatenate([pick(out, (plan.z - q) % mp, 0) for q in range(mp)], axis=0)
        )
        downs.append(
            jnp.concatenate([w_down[l], gd.reshape((mp - 1) * ffq, d_model)], axis=0)
        )

    dy = plan.relabel(jnp.concatenate([dy_long[0], dy_short[0]], axis=0))

    limits = threshold.astype(F32) / 64.0
    resid = x.astype(F32)
    saved = []
    shares = []
    for l in range(layers):
        normed, hat1, inv1 = normalize(resid, gain[l, 0], shift[l, 0])
        normed = normed.astype(BF)
        full = [plan.gather(normed[:rl]), plan.gather(normed[rl:])]
        bias = jnp.concatenate(
            [
                my_bqv[l, 0],
                jnp.zeros((heads_w,), F32),
                my_bqv[l, 1],
                zero_bq[l],
                jnp.zeros((HD,), F32),
            ]
        )
        proj = [(dot(n, exts[l]) + bias).astype(BF) for n in full]
        att = [attend_fwd(p) for p in proj]
        share = jnp.zeros((), F32)
        for p, a in zip(proj, att):
            size = p.shape[0]
            sel = a[2][size // BR]
            left = (size - 1 - lax.broadcasted_iota(jnp.int32, (size,), 0)).astype(F32)
            share = share + jnp.sum(
                jax.nn.sigmoid(4.0 * (sel / jnp.maximum(left, 1.0) - limits[l]))
            )
        shares.append(share)
        attended = jnp.concatenate([plan.to_rows(a[0]) for a in att], axis=0)
        middle = resid + dot(attended, outs[l]) + b_out[l].astype(F32)
        normed2, hat2, inv2 = normalize(middle, gain[l, 1], shift[l, 1])
        normed2 = normed2.astype(BF)
        upper = dot(normed2, ups[l]) + rel_bup[:, l].reshape(-1)
        active = gelu_both(upper)[0].astype(BF)
        saved.append((resid, middle, full, proj, att, attended, normed2, upper, active))
        resid = middle + dot(active, downs[l]) + b_down[l].astype(F32)

    y = plan.relabel(resid.astype(BF))

    g = dy.astype(F32)
    vec = {}
    weight_grads = [None] * layers
    for l in reversed(range(layers)):
        resid, middle, full, proj, att, attended, normed2, upper, active = saved[l]
        g_bdown = jnp.sum(g, axis=0)
        gm = g.astype(BF)
        gact = dot(gm, downs[l], 1, 1)
        slope = gelu_both(upper)[1]
        gu = (slope * gact).astype(BF)
        w_down_t = dot(gm, active, 0, 0).astype(BF)
        w_up_g = dot(normed2, gu, 0, 0).astype(BF)
        g_bup = jnp.sum(gu.astype(F32), axis=0)
        gn2 = dot(gu, ups[l], 1, 1)
        _, hat2, inv2 = normalize(middle, gain[l, 1], shift[l, 1])
        back, g_gain2, g_shift2 = normalize_back(gn2, hat2, inv2, gain[l, 1])
        gmid = g + back
        g_bout = jnp.sum(gmid, axis=0)
        ga = gmid.astype(BF)
        go = dot(ga, outs[l], 1, 1).astype(BF)
        w_out_t = dot(ga, attended, 0, 0).astype(BF)
        gh = [plan.to_heads(go[:rl]), plan.to_heads(go[rl:])]
        dext = [attend_bwd(p, h, a[0], a[1], a[2]) for p, h, a in zip(proj, gh, att)]
        gn1 = jnp.concatenate(
            [plan.scatter(dot(e, exts[l], 1, 1).astype(BF)) for e in dext], axis=0
        )
        w_ext_g = sum(dot(n, e, 0, 0) for n, e in zip(full, dext)).astype(BF)
        g_bext = sum(jnp.sum(e.astype(F32), axis=0) for e in dext)
        _, hat1, inv1 = normalize(resid, gain[l, 0], shift[l, 0])
        back, g_gain1, g_shift1 = normalize_back(gn1, hat1, inv1, gain[l, 0])
        g = gmid + back

        w_up_g = plan.plane_scatter(w_up_g, (plan.core,) + core_rest)
        w_up_g = plan.ring_scatter([w_up_g[:, r * ffq : (r + 1) * ffq] for r in range(mp)])
        w_down_t = plan.plane_scatter(w_down_t, (plan.core,) + core_rest[::-1])
        w_down_t = plan.ring_scatter([w_down_t[:, r * ffq : (r + 1) * ffq] for r in range(mp)])
        w_out_t = plan.plane_scatter(w_out_t, (plan.core,) + core_rest)
        w_out_t = w_out_t.reshape(-1, mp, heads_w)
        w_out_t = plan.ring_scatter([pick(w_out_t, (plan.z - r) % mp, 1) for r in range(mp)])
        w_ext_g = plan.plane_scatter(w_ext_g, core_rest[::-1])
        w_ext_g = w_ext_g.reshape(2, -1, w_ext_g.shape[1])
        part, zero = w_ext_g[..., : 3 * heads_w], w_ext_g[..., 3 * heads_w :]
        got = lax.ppermute(part, (plan.core, "zh"), [(1, 0), (2, 3)])
        part = part.astype(F32) + got.astype(F32)
        got = lax.ppermute(
            pick(part, 1 - plan.c, 0).astype(BF), (plan.core, "zh"), [(0, 2), (3, 1)]
        )
        w_qkv_g = jnp.where(plan.c == plan.zh, pick(part, plan.c, 0), got.astype(F32))
        got = swap(pick(zero, 1 - plan.c, 0), plan.core)
        zero = (pick(zero, plan.c, 0).astype(F32) + got.astype(F32)).astype(BF)
        zero = zero.astype(F32) + swap(zero, "zl").astype(F32)
        zero = zero + swap(zero.astype(BF), "zh").astype(F32)
        zero = jnp.where(plan.z == 0, zero, 0.0)
        w_qkv_g = w_qkv_g.reshape(-1, 3, heads_w)
        zero = zero.reshape(-1, 2, HD)
        w_qkv_g = w_qkv_g + jnp.pad(zero, ((0, 0), (0, 1), (0, heads_w - HD)))
        weight_grads[l] = (w_qkv_g, jnp.transpose(w_out_t), w_up_g, jnp.transpose(w_down_t))

        hot = (lax.broadcasted_iota(jnp.int32, (mp, 1), 0) == mine).astype(F32)
        gq = hot * g_bext[None, :heads_w]
        gv = hot * g_bext[None, 2 * heads_w : 3 * heads_w]
        gq = gq.reshape(-1).at[:HD].add(g_bext[3 * heads_w : 3 * heads_w + HD])
        g_bup = g_bup.reshape(mp, ffq)
        g_bup = jnp.stack([pick(g_bup, (plan.z - q) % mp, 0) for q in range(mp)])
        vec[l] = jnp.concatenate(
            [
                g_gain1, g_gain2, g_shift1, g_shift2, g_bout, g_bdown,
                gq, gv.reshape(-1), g_bup.reshape(-1), jnp.full((128,), shares[l] / mp),
            ]
        )

    dx = plan.relabel(g.astype(BF)).astype(F32)
    total = lax.psum(jnp.stack([vec[l] for l in range(layers)]), dims + ("zh", "zl"))
    n = d_model
    g_gain = total[:, : 2 * n].reshape(layers, 2, n)
    g_bias = total[:, 2 * n : 4 * n].reshape(layers, 2, n)
    g_bout = total[:, 4 * n : 5 * n]
    g_bdown = total[:, 5 * n : 6 * n]
    at = 6 * n
    g_bqv = total[:, at : at + 2 * mp * heads_w].reshape(layers, 2, mp, heads_w)
    at += 2 * mp * heads_w
    g_bup = total[:, at : at + mp * ffq].reshape(layers, mp, ffq)
    at += mp * ffq
    key_share = total[:, at] / (dp * (rows * mp))
    return (
        y[None, :rl],
        y[None, rl:],
        dx[None, :rl],
        dx[None, rl:],
        g_gain,
        g_bias,
        jnp.stack([weight_grads[l][0] for l in range(layers)]),
        pick(g_bqv, plan.z, 2),
        jnp.stack([weight_grads[l][1] for l in range(layers)]),
        g_bout,
        jnp.stack([weight_grads[l][2] for l in range(layers)]),
        pick(g_bup, plan.z, 1),
        jnp.stack([weight_grads[l][3] for l in range(layers)]),
        g_bdown,
        key_share,
    )


def solution(mesh):
    dp, mp = mesh.shape["dp"], mesh.shape["mp"]
    bits = dp.bit_length() - 1
    dims = tuple(f"d{i}" for i in range(bits))
    fine = Mesh(mesh.devices.reshape((2,) * bits + (2, mp // 2)), dims + ("zh", "zl"))
    z = ("zh", "zl")
    in_specs = (
        P(dims, z, None), P(dims, z, None), P(dims, z, None), P(dims, z, None),
        P(), P(), P(None, None, None, z), P(None, None, z), P(None, z, None), P(),
        P(None, None, z), P(None, z), P(None, z, None), P(), P(),
    )
    out_specs = (
        P(dims, z, None), P(dims, z, None), P(dims, z, None), P(dims, z, None),
        P(), P(), P(None, dims, None, z), P(None, None, z), P(None, z, dims), P(),
        P(None, dims, z), P(None, z), P(None, z, dims), P(), P(),
    )
    return jax.shard_map(
        functools.partial(body, dims, dp, mp), mesh=fine, in_specs=in_specs, out_specs=out_specs, check_vma=False
    )
```

```python
import functools

import jax, jax.numpy as jnp
from jax import lax
from jax.experimental import pallas as pl
from jax.experimental.pallas import tpu as pltpu
from jax.sharding import Mesh
from jax.sharding import PartitionSpec as P

HD = 64
BR = 256
BIG = 1e30
NT = (((1,), (1,)), ((), ()))
NN = (((1,), (0,)), ((), ()))


def mm(a, b, dims=NN):
    return lax.dot_general(a, b, dims, preferred_element_type=jnp.float32)


def halves(v):
    hi = v.astype(jnp.bfloat16)
    lo = (v - hi.astype(jnp.float32)).astype(jnp.bfloat16)
    return hi, lo


def softplus(v):
    return jnp.maximum(v, 0.0) + jnp.log(1.0 + jnp.exp(-jnp.abs(v)))


def fwd_one(x_ref, o_ref, lse_ref, carry_ref, done=None):
    size = x_ref.shape[0]
    nh = (x_ref.shape[1] - 2 * HD) // (3 * HD)
    w = nh * HD
    nb = size // BR
    first = lax.broadcasted_iota(jnp.int32, (BR, BR), 0)
    second = lax.broadcasted_iota(jnp.int32, (BR, BR), 1)
    tri = (first > second).astype(jnp.bfloat16)
    lanes = lax.broadcasted_iota(jnp.int32, (BR, 128), 1)
    lse_ref[...] = jnp.zeros_like(lse_ref)
    carry_ref[...] = jnp.zeros_like(carry_ref)
    for b in range(nb):
        rows = pl.ds(b * BR, BR)
        q0 = x_ref[rows, 3 * w : 3 * w + HD] * 0.125
        pens = []
        for c in range(b + 1):
            cols = pl.ds(c * BR, BR)
            sp = softplus(mm(q0, x_ref[cols, 3 * w + HD : 3 * w + 2 * HD], NT))
            if c == b:
                keep = first > second
                if c == 0:
                    keep = jnp.logical_and(keep, second >= 1)
                sp = jnp.where(keep, sp, 0.0)
            elif c == 0:
                sp = jnp.where(second >= 1, sp, 0.0)
            hi, lo = halves(sp)
            pen = mm(tri, hi) + mm(tri, lo) + carry_ref[b : b + 1, cols]
            carry_ref[b + 1 : b + 2, cols] = pen[BR - 1 :] + sp[BR - 1 :]
            if c == b:
                pen = jnp.where(first >= second, pen, BIG)
            pens.append(pen)
        stats = jnp.zeros((BR, 128), jnp.float32)
        for h in range(nh):
            qh = x_ref[rows, h * HD : (h + 1) * HD] * 0.125
            scores = [
                mm(qh, x_ref[c * BR : (c + 1) * BR, w + h * HD : w + (h + 1) * HD], NT) - pens[c]
                for c in range(b + 1)
            ]
            top = scores[0]
            for s in scores[1:]:
                top = jnp.maximum(top, s)
            top = jnp.max(top, axis=1, keepdims=True)
            total = None
            acc = None
            for c in range(b + 1):
                e = jnp.exp(scores[c] - top)
                total = e if total is None else total + e
                part = mm(
                    e.astype(jnp.bfloat16),
                    x_ref[c * BR : (c + 1) * BR, 2 * w + h * HD : 2 * w + (h + 1) * HD],
                )
                acc = part if acc is None else acc + part
            total = jnp.sum(total, axis=1, keepdims=True)
            o_ref[rows, h * HD : (h + 1) * HD] = (acc / total).astype(jnp.bfloat16)
            stats = jnp.where(lanes == h, top + jnp.log(total), stats)
        lse_ref[:, rows] = jnp.transpose(stats)[:8]
        if done is not None:
            done(b)


def bwd_one(x_ref, g_ref, o_ref, lse_ref, carry_ref, d_ref, acc, kt):
    size = x_ref.shape[0]
    nh = (x_ref.shape[1] - 2 * HD) // (3 * HD)
    w = nh * HD
    nb = size // BR
    jj = lax.broadcasted_iota(jnp.int32, (BR, BR), 0)
    ii = lax.broadcasted_iota(jnp.int32, (BR, BR), 1)
    below = (jj < ii).astype(jnp.bfloat16)
    above = (jj > ii).astype(jnp.bfloat16)
    ones = jnp.ones((8, HD), jnp.bfloat16)
    for h in range(nh + 1):
        lo = 3 * w + HD if h == nh else w + h * HD
        kt[h, :, :size] = jnp.transpose(x_ref[:, lo : lo + HD].astype(jnp.float32)).astype(
            jnp.bfloat16
        )
    later = [None] * nb
    for b in reversed(range(nb)):
        rows = pl.ds(b * BR, BR)
        q0 = x_ref[rows, 3 * w : 3 * w + HD] * 0.125
        pens, sigs, sums = [], [], [None] * (b + 1)
        for c in range(b + 1):
            sel = mm(x_ref[c * BR : (c + 1) * BR, 3 * w + HD : 3 * w + 2 * HD], q0, NT)
            small = jnp.exp(-jnp.abs(sel))
            sp = jnp.maximum(sel, 0.0) + jnp.log(1.0 + small)
            sig = jnp.where(sel >= 0, 1.0, small) / (1.0 + small)
            if c == b or c == 0:
                keep = None
                if c == b:
                    keep = ii > jj
                if c == 0:
                    keep = jj >= 1 if keep is None else jnp.logical_and(keep, jj >= 1)
                sp = jnp.where(keep, sp, 0.0)
                sig = jnp.where(keep, sig, 0.0)
            hi, lo = halves(sp)
            start = jnp.transpose(
                jnp.broadcast_to(carry_ref[b : b + 1, c * BR : (c + 1) * BR], (128, BR))
            )
            pen = mm(hi, below) + mm(lo, below) + start[:, :1]
            if c == b:
                pen = jnp.where(ii >= jj, pen, BIG)
            pens.append(pen)
            sigs.append(sig)
        for h in range(nh):
            qh = x_ref[rows, h * HD : (h + 1) * HD] * 0.125
            gh = g_ref[rows, h * HD : (h + 1) * HD]
            prod = gh.astype(jnp.float32) * o_ref[rows, h * HD : (h + 1) * HD].astype(jnp.float32)
            phi, plo = halves(prod)
            delta = (mm(ones, phi, NT) + mm(ones, plo, NT))[:1]
            lse = lse_ref[h : h + 1, rows]
            dqt = None
            for c in range(b + 1):
                cols = pl.ds(c * BR, BR)
                s = mm(x_ref[cols, w + h * HD : w + (h + 1) * HD], qh, NT)
                p = jnp.exp((s - pens[c]) - lse)
                dp = mm(x_ref[cols, 2 * w + h * HD : 2 * w + (h + 1) * HD], gh, NT)
                ds = p * (dp - delta)
                low = ds.astype(jnp.bfloat16)
                dk = mm(low, qh)
                dv = mm(p.astype(jnp.bfloat16), gh)
                part = mm(kt[h, :, c * BR : (c + 1) * BR], low)
                dqt = part if dqt is None else dqt + part
                if b == nb - 1:
                    acc[h, cols] = dk
                    acc[nh + h, cols] = dv
                else:
                    acc[h, cols] += dk
                    acc[nh + h, cols] += dv
                sums[c] = ds if sums[c] is None else sums[c] + ds
            d_ref[rows, h * HD : (h + 1) * HD] = jnp.transpose(dqt * 0.125).astype(jnp.bfloat16)
        dqt = None
        for c in range(b + 1):
            cols = pl.ds(c * BR, BR)
            hi, lo = halves(sums[c])
            grad = mm(hi, above) + mm(lo, above)
            full = grad[:, :1] + sums[c][:, :1]
            if later[c] is not None:
                grad = grad + later[c]
                full = full + later[c]
            later[c] = full
            low = (-(grad * sigs[c])).astype(jnp.bfloat16)
            dk = mm(low, q0)
            part = mm(kt[nh, :, c * BR : (c + 1) * BR], low)
            dqt = part if dqt is None else dqt + part
            if b == nb - 1:
                acc[2 * nh, cols] = dk
            else:
                acc[2 * nh, cols] += dk
        d_ref[rows, 3 * w : 3 * w + HD] = jnp.transpose(dqt * 0.125).astype(jnp.bfloat16)
        own = pl.ds(b * BR, BR)
    for h in range(nh):
        d_ref[:, w + h * HD : w + (h + 1) * HD] = acc[h, :size].astype(jnp.bfloat16)
        d_ref[:, 2 * w + h * HD : 2 * w + (h + 1) * HD] = acc[nh + h, :size].astype(jnp.bfloat16)
    d_ref[:, 3 * w + HD : 3 * w + 2 * HD] = acc[2 * nh, :size].astype(jnp.bfloat16)


VMEM = pl.BlockSpec(memory_space=pltpu.VMEM)
LIMIT = 48 * 1024 * 1024


def attend_fwd(x):
    size, w = x.shape[0], (x.shape[1] - 2 * HD) // 3
    return pl.pallas_call(
        fwd_one,
        out_shape=(
            jax.ShapeDtypeStruct((size, w), jnp.bfloat16),
            jax.ShapeDtypeStruct((8, size), jnp.float32),
            jax.ShapeDtypeStruct((8, size), jnp.float32),
        ),
        in_specs=[VMEM],
        out_specs=(VMEM,) * 3,
        compiler_params=pltpu.CompilerParams(vmem_limit_bytes=LIMIT),
        cost_estimate=pl.CostEstimate(
            flops=size * size * 64 * 40, bytes_accessed=size * 2000, transcendentals=size * size * 3
        ),
        name="attend_fwd",
    )(x)


def attend_bwd(x, g, o, lse, carry):
    size, w = x.shape[0], (x.shape[1] - 2 * HD) // 3
    nh = w // HD
    return pl.pallas_call(
        bwd_one,
        out_shape=jax.ShapeDtypeStruct(x.shape, jnp.bfloat16),
        in_specs=[VMEM] * 5,
        out_specs=VMEM,
        scratch_shapes=[
            pltpu.VMEM((2 * nh + 1, size, HD), jnp.float32),
            pltpu.VMEM((nh + 1, HD, size), jnp.bfloat16),
        ],
        compiler_params=pltpu.CompilerParams(vmem_limit_bytes=LIMIT),
        cost_estimate=pl.CostEstimate(
            flops=size * size * 64 * 80, bytes_accessed=size * 4000, transcendentals=size * size * 3
        ),
        name="attend_bwd",
    )(x, g, o, lse, carry)


class Group:
    def __init__(self, core):
        self.core = core
        self.c = lax.axis_index(core)
        self.zl = lax.axis_index("zl")
        self.me = 2 * self.c + self.zl

    def peer(self, delta):
        return {self.core: self.c ^ (delta >> 1), "zl": self.zl ^ (delta & 1)}

    def member(self, m):
        return {self.core: m >> 1, "zl": m & 1}

    def greet(self, deltas):
        barrier = pltpu.get_barrier_semaphore()
        for delta in deltas:
            pl.semaphore_signal(
                barrier, inc=1, device_id=self.peer(delta), device_id_type=pl.DeviceIdType.MESH
            )
        pl.semaphore_wait(barrier, len(deltas))


def send(src, dst, ssem, rsem, device):
    return pltpu.make_async_remote_copy(
        src_ref=src,
        dst_ref=dst,
        send_sem=ssem,
        recv_sem=rsem,
        device_id=device,
        device_id_type=pl.DeviceIdType.MESH,
    )


def fwd_x(core, xl, xs, att, ol, os, lsel, lses, cl, cs, land, ssem, rsem):
    group = Group(core)
    nl, ns = xl.shape[0] // 4, xs.shape[0] // 4
    group.greet((1, 2, 3))

    def copy(k, m):
        src, n, at = ((ol, nl, 0), (os, ns, nl))[k]
        return send(
            src.at[pl.ds(m * n, n)],
            land.at[group.me, pl.ds(at, n)],
            ssem.at[k, m],
            rsem.at[k, group.me],
            group.member(m),
        )

    def arrived(k, m):
        src, n, at = ((ol, nl, 0), (os, ns, nl))[k]
        return send(
            src.at[pl.ds(0, n)], land.at[m, pl.ds(at, n)], ssem.at[k, m], rsem.at[k, m], group.member(m)
        )

    def start(k, m):
        src, n, at = ((ol, nl, 0), (os, ns, nl))[k]

        @pl.when(group.me != m)
        def _():
            copy(k, m).start()

        @pl.when(group.me == m)
        def _():
            land[m, at : at + n] = src[m * n : (m + 1) * n]

    def started(k, n):
        def done(b):
            for m in range(b * BR // n, (b + 1) * BR // n):
                start(k, m)

        return done

    fwd_one(xs, os, lses, cs, started(1, ns))
    fwd_one(xl, ol, lsel, cl, started(0, nl))
    w = ol.shape[1]
    for m in range(4):

        @pl.when(group.me != m)
        def _():
            for k in range(2):
                copy(k, m).wait_send()
                arrived(k, m).wait_recv()

    for m in range(4):
        att[:, m * w : (m + 1) * w] = land[m]


def bwd_x(core, xl, xs, go, ol, os, lsel, lses, cl, cs, dl, ds, acc, kt, out, gl, gs, ssem, rsem):
    group = Group(core)
    nl, ns = xl.shape[0] // 4, xs.shape[0] // 4
    w = ol.shape[1]
    for m in range(4):
        out[m] = go[:, m * w : (m + 1) * w]
    group.greet((1, 2, 3))

    def part(k):
        return ((gl, nl, 0), (gs, ns, nl))[k]

    def copy(k, m):
        dst, n, at = part(k)
        return send(
            out.at[m, pl.ds(at, n)],
            dst.at[pl.ds(pl.multiple_of(group.me * n, 16), n)],
            ssem.at[k, m],
            rsem.at[k, group.me],
            group.member(m),
        )

    def arrived(k, m):
        dst, n, at = part(k)
        return send(
            out.at[m, pl.ds(at, n)], dst.at[pl.ds(m * n, n)], ssem.at[k, m], rsem.at[k, m], group.member(m)
        )

    for k in (1, 0):
        for m in range(4):
            dst, n, at = part(k)

            @pl.when(group.me != m)
            def _():
                copy(k, m).start()

            @pl.when(group.me == m)
            def _():
                dst[m * n : (m + 1) * n] = out[m, at : at + n]

    for k in (1, 0):
        for m in range(4):

            @pl.when(group.me != m)
            def _():
                arrived(k, m).wait_recv()

        if k:
            bwd_one(xs, gs, os, lses, cs, ds, acc, kt)
        else:
            bwd_one(xl, gl, ol, lsel, cl, dl, acc, kt)
    for m in range(4):

        @pl.when(group.me != m)
        def _():
            for k in range(2):
                copy(k, m).wait_send()


def norm_rows(v):
    mean = jnp.mean(v, axis=-1, keepdims=True)
    cen = v - mean
    inv = lax.rsqrt(jnp.mean(cen * cen, axis=-1, keepdims=True) + 1e-05)
    return cen * inv, inv


def project_x(core, resid, gain, shift, w, bias, nl_ref, ns_ref, pl_ref, ps_ref, ssem, rsem):
    group = Group(core)
    nl, ns = nl_ref.shape[0] // 4, ns_ref.shape[0] // 4
    half = nl // 2
    parts = ((ns_ref, ps_ref, ns, 0, ns, nl), (nl_ref, pl_ref, nl, 0, half, 0), (nl_ref, pl_ref, nl, half, half, half))

    def rows(k, m):
        ref, _, n, at, size, _ = parts[k]
        return ref.at[pl.ds(pl.multiple_of(m * n + at, 16), size)]

    def copy(k, j, m, delta):
        return send(rows(k, m), rows(k, m), ssem.at[k, j], rsem.at[k, j], group.peer(delta))

    def compute(k, m):
        ref, out, n, at, size, _ = parts[k]
        here = pl.ds(pl.multiple_of(m * n + at, 16), size)
        out[here] = (mm(ref[here], w[...]) + bias[...]).astype(jnp.bfloat16)

    me = group.me
    for k in range(3):
        ref, _, n, at, size, src = parts[k]
        hat, _ = norm_rows(resid[src : src + size])
        ref[pl.ds(pl.multiple_of(me * n + at, 16), size)] = (hat * gain[...] + shift[...]).astype(
            jnp.bfloat16
        )
        if k == 0:
            group.greet((1, 2))
        copy(k, 0, me, 1).start()
        copy(k, 1, me, 2).start()
    for k in range(3):
        compute(k, me)
    for k in range(3):
        copy(k, 1, me ^ 2, 2).wait_recv()
        compute(k, me ^ 2)
    for k in range(3):
        copy(k, 0, me ^ 1, 1).wait_recv()
        copy(k, 2, me ^ 1, 2).start()
        compute(k, me ^ 1)
    for k in range(3):
        copy(k, 2, me ^ 3, 2).wait_recv()
        compute(k, me ^ 3)
    for k in range(3):
        copy(k, 0, me, 1).wait_send()
        copy(k, 1, me, 2).wait_send()
        copy(k, 2, me ^ 1, 2).wait_send()


def collect_x(core, dl, ds, w, resid, gain, gmid, g_ref, sums, mine, out, got, ssem, rsem):
    group = Group(core)
    nl, ns = dl.shape[0] // 4, ds.shape[0] // 4
    me = group.me

    def partial(m):
        a = mm(dl[pl.ds(pl.multiple_of(m * nl, 16), nl)], w[...], NT)
        b = mm(ds[pl.ds(pl.multiple_of(m * ns, 16), ns)], w[...], NT)
        return jnp.concatenate([a, b], axis=0)

    def copy(k, delta):
        return send(out.at[k], got.at[k], ssem.at[k], rsem.at[k], group.peer(delta))

    out[0] = partial(me ^ 3).astype(jnp.bfloat16)
    group.greet((1, 2))
    copy(0, 2).start()
    mine[...] = partial(me ^ 1)
    copy(0, 2).wait_recv()
    out[1] = (mine[...] + got[0].astype(jnp.float32)).astype(jnp.bfloat16)
    copy(1, 1).start()
    out[2] = partial(me ^ 2).astype(jnp.bfloat16)
    copy(2, 2).start()
    mine[...] = partial(me)
    hat, inv = norm_rows(resid[...])
    copy(2, 2).wait_recv()
    copy(1, 1).wait_recv()
    grad = mine[...] + got[2].astype(jnp.float32) + got[1].astype(jnp.float32)
    gh = grad * gain[...]
    a = jnp.mean(gh, axis=-1, keepdims=True)
    b = jnp.mean(gh * hat, axis=-1, keepdims=True)
    g_ref[...] = gmid[...] + inv * (gh - a - hat * b)
    sums[0:1] = jnp.sum(grad * hat, axis=0, keepdims=True)
    sums[1:2] = jnp.sum(grad, axis=0, keepdims=True)
    copy(0, 2).wait_send()
    copy(1, 1).wait_send()
    copy(2, 2).wait_send()


def shape(dims, dtype):
    return jax.ShapeDtypeStruct(tuple(dims), dtype)


def remote(kernel, core, outs, scratch, ident, name, args, flops=10**9):
    return pl.pallas_call(
        functools.partial(kernel, core),
        out_shape=tuple(outs),
        in_specs=[VMEM] * len(args),
        out_specs=(VMEM,) * len(outs),
        scratch_shapes=scratch,
        compiler_params=pltpu.CompilerParams(
            vmem_limit_bytes=LIMIT, collective_id=ident, has_side_effects=True
        ),
        cost_estimate=pl.CostEstimate(flops=flops, bytes_accessed=10**7, transcendentals=10**6),
        name=name,
    )(*args)


DMA = pltpu.SemaphoreType.DMA


def attend_fwd_x(core, xl, xs):
    w = (xl.shape[1] - 2 * HD) // 3
    rows = (xl.shape[0] + xs.shape[0]) // 4
    outs = [shape((rows, 4 * w), jnp.bfloat16)]
    outs += [shape((x.shape[0], w), jnp.bfloat16) for x in (xl, xs)]
    outs += [shape((8, x.shape[0]), jnp.float32) for x in (xl, xs)] * 2
    scratch = [pltpu.VMEM((4, rows, w), jnp.bfloat16), DMA((2, 4)), DMA((2, 4))]
    return remote(fwd_x, core, outs, scratch, 1, "attend_fwd_x", (xl, xs), 10**10)


def attend_bwd_x(core, xl, xs, go, ol, os, lsel, lses, cl, cs):
    w = ol.shape[1]
    nh = w // HD
    size = xl.shape[0]
    outs = [shape(x.shape, jnp.bfloat16) for x in (xl, xs)]
    scratch = [
        pltpu.VMEM((2 * nh + 1, size, HD), jnp.float32),
        pltpu.VMEM((nh + 1, HD, size), jnp.bfloat16),
        pltpu.VMEM((4, go.shape[0], w), jnp.bfloat16),
        pltpu.VMEM(ol.shape, jnp.bfloat16),
        pltpu.VMEM(os.shape, jnp.bfloat16),
        DMA((2, 4)),
        DMA((2, 4)),
    ]
    args = (xl, xs, go, ol, os, lsel, lses, cl, cs)
    return remote(bwd_x, core, outs, scratch, 2, "attend_bwd_x", args, 2 * 10**10)


def project(core, resid, gain, shift, w, bias, nl, ns):
    d, n = w.shape
    outs = [shape((4 * nl, d), jnp.bfloat16), shape((4 * ns, d), jnp.bfloat16)]
    outs += [shape((4 * nl, n), jnp.bfloat16), shape((4 * ns, n), jnp.bfloat16)]
    args = (resid, gain[None], shift[None], w, bias[None])
    return remote(project_x, core, outs, [DMA((3, 3)), DMA((3, 3))], 3, "project_x", args)


def collect(core, dl, ds, w, resid, gain, gmid):
    outs = [shape(resid.shape, jnp.float32), shape((8, w.shape[0]), jnp.float32)]
    scratch = [
        pltpu.VMEM(resid.shape, jnp.float32),
        pltpu.VMEM((3,) + resid.shape, jnp.bfloat16),
        pltpu.VMEM((3,) + resid.shape, jnp.bfloat16),
        DMA((3,)),
        DMA((3,)),
    ]
    return remote(collect_x, core, outs, scratch, 4, "collect_x", (dl, ds, w, resid, gain[None], gmid))


def total_x(axes, v, out, land, ssem, rsem):
    barrier = pltpu.get_barrier_semaphore()
    peers = [{ax: 1 - lax.axis_index(ax)} for ax in axes]
    for peer in peers:
        pl.semaphore_signal(barrier, inc=1, device_id=peer, device_id_type=pl.DeviceIdType.MESH)
    pl.semaphore_wait(barrier, len(peers))
    land[0] = v[...]
    n = len(axes)
    for i, peer in enumerate(peers):
        copy = send(land.at[i], land.at[n + 1 + i], ssem.at[i], rsem.at[i], peer)
        copy.start()
        copy.wait()
        land[i + 1] = land[i] + land[n + 1 + i]
    out[...] = land[n]


def total(axes, v):
    n = len(axes)
    scratch = [pltpu.VMEM((2 * n + 1,) + v.shape, jnp.float32), DMA((n,)), DMA((n,))]
    return remote(total_x, axes, [shape(v.shape, jnp.float32)], scratch, 5, "total_x", (v,))[0]


EPS = 1e-05
F32 = jnp.float32
BF = jnp.bfloat16


def swap(v, *axes):
    count = 2 ** len(axes)
    return lax.ppermute(
        v, axes if len(axes) > 1 else axes[0], [(i, count - 1 - i) for i in range(count)]
    )


def ordered(own, other, index, axis):
    return jnp.where(
        index == 0,
        jnp.concatenate([own, other], axis=axis),
        jnp.concatenate([other, own], axis=axis),
    )


def pick(v, index, axis):
    return lax.dynamic_index_in_dim(v, index, axis, keepdims=False)


def normalize(v, gain, shift):
    mean = jnp.mean(v, axis=-1, keepdims=True)
    cen = v - mean
    var = jnp.mean(cen * cen, axis=-1, keepdims=True)
    inv = lax.rsqrt(var + EPS)
    hat = cen * inv
    return hat * gain + shift, hat, inv


def normalize_back(grad, hat, inv, gain):
    gh = grad * gain
    a = jnp.mean(gh, axis=-1, keepdims=True)
    b = jnp.mean(gh * hat, axis=-1, keepdims=True)
    return inv * (gh - a - hat * b), jnp.sum(grad * hat, axis=0), jnp.sum(grad, axis=0)


def gelu_both(u):
    k = 0.7978845608028654
    inner = k * (u + 0.044715 * u * u * u)
    t = jnp.tanh(inner)
    act = 0.5 * u * (1.0 + t)
    slope = 0.5 * (1.0 + t) + 0.5 * u * (1.0 - t * t) * k * (1.0 + 3 * 0.044715 * u * u)
    return act, slope


def dot(a, b, ca=1, cb=0):
    return lax.dot_general(a, b, (((ca,), (cb,)), ((), ())), preferred_element_type=F32)


class Plan:
    def __init__(self, dims, dp, mp):
        self.dims, self.dp, self.mp = dims, dp, mp
        self.core = dims[-1]
        self.plane = dims[:-1]
        self.c = lax.axis_index(self.core)
        self.zh = lax.axis_index("zh")
        self.zl = lax.axis_index("zl")
        self.z = lax.axis_index(("zh", "zl"))
        self.d = lax.axis_index(dims)

    def relabel(self, v):
        got = lax.ppermute(v, (self.core, "zh"), [(1, 2), (2, 1)])
        return jnp.where(self.c == self.zh, v, got)

    def ring(self, v, step):
        n = self.mp
        return lax.ppermute(v, ("zh", "zl"), [(i, (i + step) % n) for i in range(n)])

    def gather(self, v):
        v = ordered(v, swap(v, "zl"), self.zl, 0)
        return ordered(v, swap(v, self.core), self.c, 0)

    def scatter(self, v):
        rows = v.shape[0] // 4
        v = v.reshape(2, 2, rows, v.shape[1])
        got = swap(pick(v, 1 - self.c, 0), self.core)
        mine = pick(v, self.c, 0).astype(F32) + got.astype(F32)
        got = swap(pick(mine, 1 - self.zl, 0).astype(BF), "zl")
        return pick(mine, self.zl, 0) + got.astype(F32)

    def to_rows(self, o):
        rows = o.shape[0] // 4
        o = o.reshape(2, 2, rows, o.shape[1])
        got = []
        for dc in range(2):
            line = []
            for dz in range(2):
                part = pick(pick(o, self.c ^ dc, 0), self.zl ^ dz, 0)
                axes = ((self.core,) if dc else ()) + (("zl",) if dz else ())
                line.append(swap(part, *axes) if axes else part)
            got.append(ordered(line[0], line[1], self.zl, 1))
        return ordered(got[0], got[1], self.c, 1)

    def to_heads(self, g):
        rows, w = g.shape[0], g.shape[1] // 4
        g = g.reshape(rows, 2, 2, w)
        got = []
        for dc in range(2):
            line = []
            for dz in range(2):
                part = pick(pick(g, self.c ^ dc, 1), self.zl ^ dz, 1)
                axes = ((self.core,) if dc else ()) + (("zl",) if dz else ())
                line.append(swap(part, *axes) if axes else part)
            got.append(ordered(line[0], line[1], self.zl, 0))
        return ordered(got[0], got[1], self.c, 0)

    def piece(self, w):
        rows = w.shape[0] // self.dp
        return lax.dynamic_slice_in_dim(w, self.d * rows, rows, 0)

    def ring_gather(self, v):
        parts = []
        for _ in range(self.mp - 1):
            v = self.ring(v, 1)
            parts.append(v)
        return parts

    def plane_gather(self, v, axes):
        k, rows, n = v.shape
        have = []
        shape = [k]
        for ax in axes:
            pos = sum(self.dims.index(h) < self.dims.index(ax) for h in have)
            got = swap(v, ax)
            cur = v.reshape(k, *([2] * len(have)), rows, n)
            oth = got.reshape(cur.shape)
            a = jnp.stack([cur, oth], axis=1 + pos)
            b = jnp.stack([oth, cur], axis=1 + pos)
            v = jnp.where(lax.axis_index(ax) == 0, a, b)
            have.append(ax)
            v = v.reshape(k, -1, rows, n).reshape(k, -1, n)
            rows_all = v.shape[1]
            v = v.reshape(k, rows_all, n)
        return v.reshape(k, self.dp, rows, n)

    def plane_scatter(self, g, axes):
        n = g.shape[1]
        left = [ax for ax in self.dims]
        rows = g.shape[0] // self.dp
        v = g.reshape(*([2] * len(left)), rows, n)
        for ax in axes:
            pos = left.index(ax)
            i = lax.axis_index(ax)
            got = swap(pick(v, 1 - i, pos), ax)
            v = (pick(v, i, pos).astype(F32) + got.astype(F32)).astype(BF)
            left.remove(ax)
        return v.reshape(-1, n)

    def scatter_all(self, up, down, out):
        n, e = up.shape[1], out.shape[1]
        bits = len(self.dims)
        view = lambda v: v.reshape(*([2] * bits), -1, v.shape[1])
        mats = [view(up), view(down), view(out)]
        pos = bits - 1
        to_send = jnp.concatenate([pick(v, 1 - self.c, pos) for v in mats], axis=-1)
        got = swap(to_send, self.core)
        up, down, out = [
            (pick(v, self.c, pos).astype(F32) + got[..., at : at + v.shape[-1]].astype(F32)).astype(BF)
            for v, at in zip(mats, (0, n, 2 * n))
        ]
        down = jnp.concatenate([down, out], axis=-1)
        res = []
        for v, axes in ((up, self.plane), (down, self.plane[::-1])):
            left = list(self.plane)
            for ax in axes:
                i, p = lax.axis_index(ax), left.index(ax)
                got = swap(pick(v, 1 - i, p), ax)
                v = (pick(v, i, p).astype(F32) + got.astype(F32)).astype(BF)
                left.remove(ax)
            res.append(v)
        up, down = res
        rows = up.shape[0]
        cut = lambda v: v.reshape(rows, self.mp, -1)
        v = jnp.concatenate([cut(up), cut(down[:, :n]), cut(down[:, n:])], axis=-1)
        v = self.ring_scatter([pick(v, (self.z - r) % self.mp, 1) for r in range(self.mp)])
        q = n // self.mp
        return v[:, :q], v[:, q : 2 * q], v[:, 2 * q :]

    def ring_scatter(self, chunks):
        t = chunks[-1]
        for r in range(self.mp - 2, -1, -1):
            got = self.ring(t, -1)
            t = chunks[r].astype(F32) + got.astype(F32)
            if r:
                t = t.astype(BF)
        return t


def body(
    dims, dp, mp,
    x_long, x_short, dy_long, dy_short, ln_gain, ln_bias, w_qkv, b_qv, w_out, b_out, w_up, b_up, w_down, b_down, threshold,
):
    plan = Plan(dims, dp, mp)
    layers = w_qkv.shape[0]
    d_model = x_long.shape[-1]
    heads_w = w_qkv.shape[-1]
    ffq = w_up.shape[-1]
    rl, rs = x_long.shape[1], x_short.shape[1]
    rows = rl + rs
    core_rest = tuple(plan.plane)
    fwd_axes = core_rest + (plan.core,)
    alt_axes = core_rest[::-1] + (plan.core,)
    gain = ln_gain.astype(F32)
    shift = ln_bias.astype(F32)

    x = jnp.concatenate([x_long[0], x_short[0]], axis=0)
    x = plan.relabel(x)

    small = jnp.concatenate([b_up.reshape(-1), b_qv.reshape(-1)])
    rel_small = jnp.stack([small] + plan.ring_gather(small))
    n_up = layers * ffq
    rel_bup = rel_small[:, :n_up].reshape(mp, layers, ffq).astype(F32)
    bup = jnp.stack([pick(rel_bup, (plan.z - q) % mp, 0) for q in range(mp)])
    rel_bqv = rel_small[:, n_up:].reshape(mp, layers, 2, heads_w).astype(F32)
    mine = 2 * plan.c + plan.zl
    my_bqv = pick(rel_bqv, (plan.z - mine) % mp, 0)
    zero_bq = pick(rel_bqv, plan.z % mp, 0)[:, 0, :HD]

    exts = []
    for l in range(layers):
        quarter = plan.relabel(w_qkv[l].reshape(d_model, 3 * heads_w))
        head0 = w_qkv[l][:, :2, :HD].reshape(d_model, 2 * HD)
        got = lax.ppermute(head0, "zl", [(0, 1)])
        head0 = jnp.where(plan.zl == 0, head0, got)
        got = lax.ppermute(head0, "zh", [(0, 1)])
        head0 = jnp.where(plan.zh == 0, head0, got)
        exts.append(jnp.concatenate([quarter, head0], axis=1))

    ups, downs, outs = [], [], []
    order = ("zh", "zl") + dims
    for l in range(layers):
        outs.append(lax.all_gather(plan.piece(w_out[l]), order, axis=0, tiled=True))
        n_up = ffq // dp
        piece = lax.dynamic_slice_in_dim(w_up[l], plan.d * n_up, n_up, 1)
        ups.append(lax.all_gather(jnp.transpose(piece), order, axis=0, tiled=True))
        downs.append(lax.all_gather(plan.piece(w_down[l]), order, axis=0, tiled=True))

    dy = plan.relabel(jnp.concatenate([dy_long[0], dy_short[0]], axis=0))

    limits = threshold.astype(F32) / 64.0
    resid = x.astype(F32)
    saved = []
    shares = []
    for l in range(layers):
        bias = jnp.concatenate(
            [
                my_bqv[l, 0],
                jnp.zeros((heads_w,), F32),
                my_bqv[l, 1],
                zero_bq[l],
                jnp.zeros((HD,), F32),
            ]
        )
        full_l, full_s, pj_l, pj_s = project(
            plan.core, resid, gain[l, 0], shift[l, 0], exts[l], bias, rl, rs
        )
        full, proj = (full_l, full_s), (pj_l, pj_s)
        attended, *att = attend_fwd_x(plan.core, pj_l, pj_s)
        share = jnp.zeros((), F32)
        for carry in att[4:]:
            size = carry.shape[1]
            sel = carry[size // BR]
            left = (size - 1 - lax.broadcasted_iota(jnp.int32, (size,), 0)).astype(F32)
            share = share + jnp.sum(
                jax.nn.sigmoid(4.0 * (sel / jnp.maximum(left, 1.0) - limits[l]))
            )
        shares.append(share)
        middle = resid + dot(attended, outs[l]) + b_out[l].astype(F32)
        normed2, hat2, inv2 = normalize(middle, gain[l, 1], shift[l, 1])
        normed2 = normed2.astype(BF)
        upper = dot(normed2, ups[l], 1, 1) + bup[:, l].reshape(-1)
        active = gelu_both(upper)[0].astype(BF)
        saved.append((resid, middle, full, proj, att, attended, normed2, upper, active))
        resid = middle + dot(active, downs[l]) + b_down[l].astype(F32)

    y = plan.relabel(resid.astype(BF))

    g = dy.astype(F32)
    vec = {}
    weight_grads = [None] * layers
    for l in reversed(range(layers)):
        resid, middle, full, proj, att, attended, normed2, upper, active = saved[l]
        g_bdown = jnp.sum(g, axis=0)
        gm = g.astype(BF)
        gact = dot(gm, downs[l], 1, 1)
        slope = gelu_both(upper)[1]
        gu = (slope * gact).astype(BF)
        w_down_t = dot(gm, active, 0, 0).astype(BF)
        w_up_g = dot(normed2, gu, 0, 0).astype(BF)
        g_bup = jnp.sum(gu.astype(F32), axis=0)
        gn2 = dot(gu, ups[l])
        _, hat2, inv2 = normalize(middle, gain[l, 1], shift[l, 1])
        back, g_gain2, g_shift2 = normalize_back(gn2, hat2, inv2, gain[l, 1])
        gmid = g + back
        g_bout = jnp.sum(gmid, axis=0)
        ga = gmid.astype(BF)
        go = dot(ga, outs[l], 1, 1).astype(BF)
        w_out_t = dot(ga, attended, 0, 0).astype(BF)
        dext = attend_bwd_x(plan.core, *proj, go, *att)
        new_g, ln1 = collect(plan.core, *dext, exts[l], resid, gain[l, 0], gmid)
        g_gain1, g_shift1 = ln1[0], ln1[1]
        w_ext_g = sum(dot(n, e, 0, 0) for n, e in zip(full, dext)).astype(BF)
        g_bext = sum(jnp.sum(e.astype(F32), axis=0) for e in dext)
        g = new_g

        w_up_g, w_down_t, w_out_t = plan.scatter_all(w_up_g, w_down_t, w_out_t)
        w_ext_g = plan.plane_scatter(w_ext_g, core_rest[::-1])
        w_ext_g = w_ext_g.reshape(2, -1, w_ext_g.shape[1])
        part, zero = w_ext_g[..., : 3 * heads_w], w_ext_g[..., 3 * heads_w :]
        got = lax.ppermute(part, (plan.core, "zh"), [(1, 0), (2, 3)])
        part = part.astype(F32) + got.astype(F32)
        got = lax.ppermute(
            pick(part, 1 - plan.c, 0).astype(BF), (plan.core, "zh"), [(0, 2), (3, 1)]
        )
        w_qkv_g = jnp.where(plan.c == plan.zh, pick(part, plan.c, 0), got.astype(F32))
        got = swap(pick(zero, 1 - plan.c, 0), plan.core)
        zero = (pick(zero, plan.c, 0).astype(F32) + got.astype(F32)).astype(BF)
        zero = zero.astype(F32) + swap(zero, "zl").astype(F32)
        zero = zero + swap(zero.astype(BF), "zh").astype(F32)
        zero = jnp.where(plan.z == 0, zero, 0.0)
        w_qkv_g = w_qkv_g.reshape(-1, 3, heads_w)
        zero = zero.reshape(-1, 2, HD)
        w_qkv_g = w_qkv_g + jnp.pad(zero, ((0, 0), (0, 1), (0, heads_w - HD)))
        weight_grads[l] = (w_qkv_g, jnp.transpose(w_out_t), w_up_g, jnp.transpose(w_down_t))

        hot = (lax.broadcasted_iota(jnp.int32, (mp, 1), 0) == mine).astype(F32)
        gq = hot * g_bext[None, :heads_w]
        gv = hot * g_bext[None, 2 * heads_w : 3 * heads_w]
        gq = gq.reshape(-1).at[:HD].add(g_bext[3 * heads_w : 3 * heads_w + HD])
        vec[l] = jnp.concatenate(
            [
                g_gain1, g_gain2, g_shift1, g_shift2, g_bout, g_bdown,
                gq, gv.reshape(-1), g_bup.reshape(-1), jnp.full((128,), shares[l] / mp),
            ]
        )

    dx = plan.relabel(g.astype(BF)).astype(F32)
    total_v = jnp.stack([vec[l] for l in range(layers)])
    total_v = total(dims + ("zh", "zl"), total_v.reshape(-1, 128)).reshape(total_v.shape)
    n = d_model
    g_gain = total_v[:, : 2 * n].reshape(layers, 2, n)
    g_bias = total_v[:, 2 * n : 4 * n].reshape(layers, 2, n)
    g_bout = total_v[:, 4 * n : 5 * n]
    g_bdown = total_v[:, 5 * n : 6 * n]
    at = 6 * n
    g_bqv = total_v[:, at : at + 2 * mp * heads_w].reshape(layers, 2, mp, heads_w)
    at += 2 * mp * heads_w
    g_bup = total_v[:, at : at + mp * ffq].reshape(layers, mp, ffq)
    at += mp * ffq
    key_share = total_v[:, at] / (dp * (rows * mp))
    return (
        y[None, :rl],
        y[None, rl:],
        dx[None, :rl],
        dx[None, rl:],
        g_gain,
        g_bias,
        jnp.stack([weight_grads[l][0] for l in range(layers)]),
        pick(g_bqv, plan.z, 2),
        jnp.stack([weight_grads[l][1] for l in range(layers)]),
        g_bout,
        jnp.stack([weight_grads[l][2] for l in range(layers)]),
        pick(g_bup, plan.z, 1),
        jnp.stack([weight_grads[l][3] for l in range(layers)]),
        g_bdown,
        key_share,
    )


def solution(mesh):
    dp, mp = mesh.shape["dp"], mesh.shape["mp"]
    bits = dp.bit_length() - 1
    dims = tuple(f"d{i}" for i in range(bits))
    fine = Mesh(mesh.devices.reshape((2,) * bits + (2, mp // 2)), dims + ("zh", "zl"))
    z = ("zh", "zl")
    in_specs = (
        P(dims, z, None), P(dims, z, None), P(dims, z, None), P(dims, z, None),
        P(), P(), P(None, None, None, z), P(None, None, z), P(None, z, None), P(),
        P(None, None, z), P(None, z), P(None, z, None), P(), P(),
    )
    out_specs = (
        P(dims, z, None), P(dims, z, None), P(dims, z, None), P(dims, z, None),
        P(), P(), P(None, dims, None, z), P(None, None, z), P(None, z, dims), P(),
        P(None, dims, z), P(None, z), P(None, z, dims), P(), P(),
    )
    return jax.shard_map(
        functools.partial(body, dims, dp, mp), mesh=fine, in_specs=in_specs, out_specs=out_specs, check_vma=False
    )
```

```python
import functools

import jax, jax.numpy as jnp
from jax import lax
from jax.experimental import pallas as pl
from jax.experimental.pallas import tpu as pltpu
from jax.sharding import Mesh
from jax.sharding import PartitionSpec as P

HD = 64
BR = 256
BIG = 1e30
NT = (((1,), (1,)), ((), ()))
NN = (((1,), (0,)), ((), ()))


def mm(a, b, dims=NN):
    return lax.dot_general(a, b, dims, preferred_element_type=jnp.float32)


def halves(v):
    hi = v.astype(jnp.bfloat16)
    lo = (v - hi.astype(jnp.float32)).astype(jnp.bfloat16)
    return hi, lo


def softplus(v):
    return jnp.maximum(v, 0.0) + jnp.log(1.0 + jnp.exp(-jnp.abs(v)))


def fwd_one(x_ref, o_ref, lse_ref, carry_ref, done=None):
    size = x_ref.shape[0]
    nh = (x_ref.shape[1] - 2 * HD) // (3 * HD)
    w = nh * HD
    nb = size // BR
    first = lax.broadcasted_iota(jnp.int32, (BR, BR), 0)
    second = lax.broadcasted_iota(jnp.int32, (BR, BR), 1)
    tri = (first > second).astype(jnp.bfloat16)
    lanes = lax.broadcasted_iota(jnp.int32, (BR, 128), 1)
    lse_ref[...] = jnp.zeros_like(lse_ref)
    carry_ref[...] = jnp.zeros_like(carry_ref)
    for b in range(nb):
        rows = pl.ds(b * BR, BR)
        q0 = x_ref[rows, 3 * w : 3 * w + HD] * 0.125
        pens = []
        for c in range(b + 1):
            cols = pl.ds(c * BR, BR)
            sp = softplus(mm(q0, x_ref[cols, 3 * w + HD : 3 * w + 2 * HD], NT))
            if c == b:
                keep = first > second
                if c == 0:
                    keep = jnp.logical_and(keep, second >= 1)
                sp = jnp.where(keep, sp, 0.0)
            elif c == 0:
                sp = jnp.where(second >= 1, sp, 0.0)
            hi, lo = halves(sp)
            pen = mm(tri, hi) + mm(tri, lo) + carry_ref[b : b + 1, cols]
            carry_ref[b + 1 : b + 2, cols] = pen[BR - 1 :] + sp[BR - 1 :]
            if c == b:
                pen = jnp.where(first >= second, pen, BIG)
            pens.append(pen)
        stats = jnp.zeros((BR, 128), jnp.float32)
        for h in range(nh):
            qh = x_ref[rows, h * HD : (h + 1) * HD] * 0.125
            scores = [
                mm(qh, x_ref[c * BR : (c + 1) * BR, w + h * HD : w + (h + 1) * HD], NT) - pens[c]
                for c in range(b + 1)
            ]
            top = scores[0]
            for s in scores[1:]:
                top = jnp.maximum(top, s)
            top = jnp.max(top, axis=1, keepdims=True)
            total = None
            acc = None
            for c in range(b + 1):
                e = jnp.exp(scores[c] - top)
                total = e if total is None else total + e
                part = mm(
                    e.astype(jnp.bfloat16),
                    x_ref[c * BR : (c + 1) * BR, 2 * w + h * HD : 2 * w + (h + 1) * HD],
                )
                acc = part if acc is None else acc + part
            total = jnp.sum(total, axis=1, keepdims=True)
            o_ref[rows, h * HD : (h + 1) * HD] = (acc / total).astype(jnp.bfloat16)
            stats = jnp.where(lanes == h, top + jnp.log(total), stats)
        lse_ref[:, rows] = jnp.transpose(stats)[:8]
        if done is not None:
            done(b)


def bwd_one(x_ref, g_ref, o_ref, lse_ref, carry_ref, d_ref, acc, kt):
    size = x_ref.shape[0]
    nh = (x_ref.shape[1] - 2 * HD) // (3 * HD)
    w = nh * HD
    nb = size // BR
    jj = lax.broadcasted_iota(jnp.int32, (BR, BR), 0)
    ii = lax.broadcasted_iota(jnp.int32, (BR, BR), 1)
    below = (jj < ii).astype(jnp.bfloat16)
    above = (jj > ii).astype(jnp.bfloat16)
    ones = jnp.ones((8, HD), jnp.bfloat16)
    for h in range(nh + 1):
        lo = 3 * w + HD if h == nh else w + h * HD
        kt[h, :, :size] = jnp.transpose(x_ref[:, lo : lo + HD].astype(jnp.float32)).astype(
            jnp.bfloat16
        )
    later = [None] * nb
    for b in reversed(range(nb)):
        rows = pl.ds(b * BR, BR)
        q0 = x_ref[rows, 3 * w : 3 * w + HD] * 0.125
        pens, sigs, sums = [], [], [None] * (b + 1)
        for c in range(b + 1):
            sel = mm(x_ref[c * BR : (c + 1) * BR, 3 * w + HD : 3 * w + 2 * HD], q0, NT)
            small = jnp.exp(-jnp.abs(sel))
            sp = jnp.maximum(sel, 0.0) + jnp.log(1.0 + small)
            sig = jnp.where(sel >= 0, 1.0, small) / (1.0 + small)
            if c == b or c == 0:
                keep = None
                if c == b:
                    keep = ii > jj
                if c == 0:
                    keep = jj >= 1 if keep is None else jnp.logical_and(keep, jj >= 1)
                sp = jnp.where(keep, sp, 0.0)
                sig = jnp.where(keep, sig, 0.0)
            hi, lo = halves(sp)
            start = jnp.transpose(
                jnp.broadcast_to(carry_ref[b : b + 1, c * BR : (c + 1) * BR], (128, BR))
            )
            pen = mm(hi, below) + mm(lo, below) + start[:, :1]
            if c == b:
                pen = jnp.where(ii >= jj, pen, BIG)
            pens.append(pen)
            sigs.append(sig)
        for h in range(nh):
            qh = x_ref[rows, h * HD : (h + 1) * HD] * 0.125
            gh = g_ref[rows, h * HD : (h + 1) * HD]
            prod = gh.astype(jnp.float32) * o_ref[rows, h * HD : (h + 1) * HD].astype(jnp.float32)
            phi, plo = halves(prod)
            delta = (mm(ones, phi, NT) + mm(ones, plo, NT))[:1]
            lse = lse_ref[h : h + 1, rows]
            dqt = None
            for c in range(b + 1):
                cols = pl.ds(c * BR, BR)
                s = mm(x_ref[cols, w + h * HD : w + (h + 1) * HD], qh, NT)
                p = jnp.exp((s - pens[c]) - lse)
                dp = mm(x_ref[cols, 2 * w + h * HD : 2 * w + (h + 1) * HD], gh, NT)
                ds = p * (dp - delta)
                low = ds.astype(jnp.bfloat16)
                dk = mm(low, qh)
                dv = mm(p.astype(jnp.bfloat16), gh)
                part = mm(kt[h, :, c * BR : (c + 1) * BR], low)
                dqt = part if dqt is None else dqt + part
                if b == nb - 1:
                    acc[h, cols] = dk
                    acc[nh + h, cols] = dv
                else:
                    acc[h, cols] += dk
                    acc[nh + h, cols] += dv
                sums[c] = ds if sums[c] is None else sums[c] + ds
            d_ref[rows, h * HD : (h + 1) * HD] = jnp.transpose(dqt * 0.125).astype(jnp.bfloat16)
        dqt = None
        for c in range(b + 1):
            cols = pl.ds(c * BR, BR)
            hi, lo = halves(sums[c])
            grad = mm(hi, above) + mm(lo, above)
            full = grad[:, :1] + sums[c][:, :1]
            if later[c] is not None:
                grad = grad + later[c]
                full = full + later[c]
            later[c] = full
            low = (-(grad * sigs[c])).astype(jnp.bfloat16)
            dk = mm(low, q0)
            part = mm(kt[nh, :, c * BR : (c + 1) * BR], low)
            dqt = part if dqt is None else dqt + part
            if b == nb - 1:
                acc[2 * nh, cols] = dk
            else:
                acc[2 * nh, cols] += dk
        d_ref[rows, 3 * w : 3 * w + HD] = jnp.transpose(dqt * 0.125).astype(jnp.bfloat16)
        own = pl.ds(b * BR, BR)
    for h in range(nh):
        d_ref[:, w + h * HD : w + (h + 1) * HD] = acc[h, :size].astype(jnp.bfloat16)
        d_ref[:, 2 * w + h * HD : 2 * w + (h + 1) * HD] = acc[nh + h, :size].astype(jnp.bfloat16)
    d_ref[:, 3 * w + HD : 3 * w + 2 * HD] = acc[2 * nh, :size].astype(jnp.bfloat16)


VMEM = pl.BlockSpec(memory_space=pltpu.VMEM)
LIMIT = 48 * 1024 * 1024


def attend_fwd(x):
    size, w = x.shape[0], (x.shape[1] - 2 * HD) // 3
    return pl.pallas_call(
        fwd_one,
        out_shape=(
            jax.ShapeDtypeStruct((size, w), jnp.bfloat16),
            jax.ShapeDtypeStruct((8, size), jnp.float32),
            jax.ShapeDtypeStruct((8, size), jnp.float32),
        ),
        in_specs=[VMEM],
        out_specs=(VMEM,) * 3,
        compiler_params=pltpu.CompilerParams(vmem_limit_bytes=LIMIT),
        cost_estimate=pl.CostEstimate(
            flops=size * size * 64 * 40, bytes_accessed=size * 2000, transcendentals=size * size * 3
        ),
        name="attend_fwd",
    )(x)


def attend_bwd(x, g, o, lse, carry):
    size, w = x.shape[0], (x.shape[1] - 2 * HD) // 3
    nh = w // HD
    return pl.pallas_call(
        bwd_one,
        out_shape=jax.ShapeDtypeStruct(x.shape, jnp.bfloat16),
        in_specs=[VMEM] * 5,
        out_specs=VMEM,
        scratch_shapes=[
            pltpu.VMEM((2 * nh + 1, size, HD), jnp.float32),
            pltpu.VMEM((nh + 1, HD, size), jnp.bfloat16),
        ],
        compiler_params=pltpu.CompilerParams(vmem_limit_bytes=LIMIT),
        cost_estimate=pl.CostEstimate(
            flops=size * size * 64 * 80, bytes_accessed=size * 4000, transcendentals=size * size * 3
        ),
        name="attend_bwd",
    )(x, g, o, lse, carry)


class Group:
    def __init__(self, core):
        self.core = core
        self.c = lax.axis_index(core)
        self.zl = lax.axis_index("zl")
        self.me = 2 * self.c + self.zl

    def peer(self, delta):
        return {self.core: self.c ^ (delta >> 1), "zl": self.zl ^ (delta & 1)}

    def member(self, m):
        return {self.core: m >> 1, "zl": m & 1}

    def greet(self, deltas):
        barrier = pltpu.get_barrier_semaphore()
        for delta in deltas:
            pl.semaphore_signal(
                barrier, inc=1, device_id=self.peer(delta), device_id_type=pl.DeviceIdType.MESH
            )
        pl.semaphore_wait(barrier, len(deltas))


def send(src, dst, ssem, rsem, device):
    return pltpu.make_async_remote_copy(
        src_ref=src,
        dst_ref=dst,
        send_sem=ssem,
        recv_sem=rsem,
        device_id=device,
        device_id_type=pl.DeviceIdType.MESH,
    )


def fwd_x(core, xl, xs, att, ol, os, lsel, lses, cl, cs, land, ssem, rsem):
    group = Group(core)
    nl, ns = xl.shape[0] // 4, xs.shape[0] // 4
    group.greet((1, 2, 3))

    def copy(k, m):
        src, n, at = ((ol, nl, 0), (os, ns, nl))[k]
        return send(
            src.at[pl.ds(m * n, n)],
            land.at[group.me, pl.ds(at, n)],
            ssem.at[k, m],
            rsem.at[k, group.me],
            group.member(m),
        )

    def arrived(k, m):
        src, n, at = ((ol, nl, 0), (os, ns, nl))[k]
        return send(
            src.at[pl.ds(0, n)], land.at[m, pl.ds(at, n)], ssem.at[k, m], rsem.at[k, m], group.member(m)
        )

    def start(k, m):
        src, n, at = ((ol, nl, 0), (os, ns, nl))[k]

        @pl.when(group.me != m)
        def _():
            copy(k, m).start()

        @pl.when(group.me == m)
        def _():
            land[m, at : at + n] = src[m * n : (m + 1) * n]

    def started(k, n):
        def done(b):
            for m in range(b * BR // n, (b + 1) * BR // n):
                start(k, m)

        return done

    fwd_one(xs, os, lses, cs, started(1, ns))
    fwd_one(xl, ol, lsel, cl, started(0, nl))
    w = ol.shape[1]
    for m in range(4):

        @pl.when(group.me != m)
        def _():
            for k in range(2):
                copy(k, m).wait_send()
                arrived(k, m).wait_recv()

    for m in range(4):
        att[:, m * w : (m + 1) * w] = land[m]


def bwd_x(core, xl, xs, go, ol, os, lsel, lses, cl, cs, dl, ds, acc, kt, out, gl, gs, ssem, rsem):
    group = Group(core)
    nl, ns = xl.shape[0] // 4, xs.shape[0] // 4
    w = ol.shape[1]
    for m in range(4):
        out[m] = go[:, m * w : (m + 1) * w]
    group.greet((1, 2, 3))

    def part(k):
        return ((gl, nl, 0), (gs, ns, nl))[k]

    def copy(k, m):
        dst, n, at = part(k)
        return send(
            out.at[m, pl.ds(at, n)],
            dst.at[pl.ds(pl.multiple_of(group.me * n, 16), n)],
            ssem.at[k, m],
            rsem.at[k, group.me],
            group.member(m),
        )

    def arrived(k, m):
        dst, n, at = part(k)
        return send(
            out.at[m, pl.ds(at, n)], dst.at[pl.ds(m * n, n)], ssem.at[k, m], rsem.at[k, m], group.member(m)
        )

    for k in (1, 0):
        for m in range(4):
            dst, n, at = part(k)

            @pl.when(group.me != m)
            def _():
                copy(k, m).start()

            @pl.when(group.me == m)
            def _():
                dst[m * n : (m + 1) * n] = out[m, at : at + n]

    for k in (1, 0):
        for m in range(4):

            @pl.when(group.me != m)
            def _():
                arrived(k, m).wait_recv()

        if k:
            bwd_one(xs, gs, os, lses, cs, ds, acc, kt)
        else:
            bwd_one(xl, gl, ol, lsel, cl, dl, acc, kt)
    for m in range(4):

        @pl.when(group.me != m)
        def _():
            for k in range(2):
                copy(k, m).wait_send()


def norm_rows(v):
    mean = jnp.mean(v, axis=-1, keepdims=True)
    cen = v - mean
    inv = lax.rsqrt(jnp.mean(cen * cen, axis=-1, keepdims=True) + 1e-05)
    return cen * inv, inv


def project_x(core, resid, gain, shift, w, bias, nl_ref, ns_ref, pl_ref, ps_ref, ssem, rsem):
    group = Group(core)
    nl, ns = nl_ref.shape[0] // 4, ns_ref.shape[0] // 4
    half = nl // 2
    parts = ((ns_ref, ps_ref, ns, 0, ns, nl), (nl_ref, pl_ref, nl, 0, half, 0), (nl_ref, pl_ref, nl, half, half, half))

    def rows(k, m):
        ref, _, n, at, size, _ = parts[k]
        return ref.at[pl.ds(pl.multiple_of(m * n + at, 16), size)]

    def copy(k, j, m, delta):
        return send(rows(k, m), rows(k, m), ssem.at[k, j], rsem.at[k, j], group.peer(delta))

    def compute(k, m):
        ref, out, n, at, size, _ = parts[k]
        here = pl.ds(pl.multiple_of(m * n + at, 16), size)
        out[here] = (mm(ref[here], w[...]) + bias[...]).astype(jnp.bfloat16)

    me = group.me
    for k in range(3):
        ref, _, n, at, size, src = parts[k]
        hat, _ = norm_rows(resid[src : src + size])
        ref[pl.ds(pl.multiple_of(me * n + at, 16), size)] = (hat * gain[...] + shift[...]).astype(
            jnp.bfloat16
        )
        if k == 0:
            group.greet((1, 2))
        copy(k, 0, me, 1).start()
        copy(k, 1, me, 2).start()
    for k in range(3):
        compute(k, me)
    for k in range(3):
        copy(k, 1, me ^ 2, 2).wait_recv()
        compute(k, me ^ 2)
    for k in range(3):
        copy(k, 0, me ^ 1, 1).wait_recv()
        copy(k, 2, me ^ 1, 2).start()
        compute(k, me ^ 1)
    for k in range(3):
        copy(k, 2, me ^ 3, 2).wait_recv()
        compute(k, me ^ 3)
    for k in range(3):
        copy(k, 0, me, 1).wait_send()
        copy(k, 1, me, 2).wait_send()
        copy(k, 2, me ^ 1, 2).wait_send()


def collect_x(core, dl, ds, w, resid, gain, gmid, g_ref, sums, mine, out, got, ssem, rsem):
    group = Group(core)
    nl, ns = dl.shape[0] // 4, ds.shape[0] // 4
    me = group.me

    def partial(m):
        a = mm(dl[pl.ds(pl.multiple_of(m * nl, 16), nl)], w[...], NT)
        b = mm(ds[pl.ds(pl.multiple_of(m * ns, 16), ns)], w[...], NT)
        return jnp.concatenate([a, b], axis=0)

    def copy(k, delta):
        return send(out.at[k], got.at[k], ssem.at[k], rsem.at[k], group.peer(delta))

    out[0] = partial(me ^ 3).astype(jnp.bfloat16)
    group.greet((1, 2))
    copy(0, 2).start()
    mine[...] = partial(me ^ 1)
    copy(0, 2).wait_recv()
    out[1] = (mine[...] + got[0].astype(jnp.float32)).astype(jnp.bfloat16)
    copy(1, 1).start()
    out[2] = partial(me ^ 2).astype(jnp.bfloat16)
    copy(2, 2).start()
    mine[...] = partial(me)
    hat, inv = norm_rows(resid[...])
    copy(2, 2).wait_recv()
    copy(1, 1).wait_recv()
    grad = mine[...] + got[2].astype(jnp.float32) + got[1].astype(jnp.float32)
    gh = grad * gain[...]
    a = jnp.mean(gh, axis=-1, keepdims=True)
    b = jnp.mean(gh * hat, axis=-1, keepdims=True)
    g_ref[...] = gmid[...] + inv * (gh - a - hat * b)
    sums[0:1] = jnp.sum(grad * hat, axis=0, keepdims=True)
    sums[1:2] = jnp.sum(grad, axis=0, keepdims=True)
    copy(0, 2).wait_send()
    copy(1, 1).wait_send()
    copy(2, 2).wait_send()


def shape(dims, dtype):
    return jax.ShapeDtypeStruct(tuple(dims), dtype)


def remote(kernel, core, outs, scratch, ident, name, args, flops=10**9):
    return pl.pallas_call(
        functools.partial(kernel, core),
        out_shape=tuple(outs),
        in_specs=[VMEM] * len(args),
        out_specs=(VMEM,) * len(outs),
        scratch_shapes=scratch,
        compiler_params=pltpu.CompilerParams(
            vmem_limit_bytes=LIMIT, collective_id=ident, has_side_effects=True
        ),
        cost_estimate=pl.CostEstimate(flops=flops, bytes_accessed=10**7, transcendentals=10**6),
        name=name,
    )(*args)


DMA = pltpu.SemaphoreType.DMA


def attend_fwd_x(core, xl, xs):
    w = (xl.shape[1] - 2 * HD) // 3
    rows = (xl.shape[0] + xs.shape[0]) // 4
    outs = [shape((rows, 4 * w), jnp.bfloat16)]
    outs += [shape((x.shape[0], w), jnp.bfloat16) for x in (xl, xs)]
    outs += [shape((8, x.shape[0]), jnp.float32) for x in (xl, xs)] * 2
    scratch = [pltpu.VMEM((4, rows, w), jnp.bfloat16), DMA((2, 4)), DMA((2, 4))]
    return remote(fwd_x, core, outs, scratch, 1, "attend_fwd_x", (xl, xs), 10**10)


def attend_bwd_x(core, xl, xs, go, ol, os, lsel, lses, cl, cs):
    w = ol.shape[1]
    nh = w // HD
    size = xl.shape[0]
    outs = [shape(x.shape, jnp.bfloat16) for x in (xl, xs)]
    scratch = [
        pltpu.VMEM((2 * nh + 1, size, HD), jnp.float32),
        pltpu.VMEM((nh + 1, HD, size), jnp.bfloat16),
        pltpu.VMEM((4, go.shape[0], w), jnp.bfloat16),
        pltpu.VMEM(ol.shape, jnp.bfloat16),
        pltpu.VMEM(os.shape, jnp.bfloat16),
        DMA((2, 4)),
        DMA((2, 4)),
    ]
    args = (xl, xs, go, ol, os, lsel, lses, cl, cs)
    return remote(bwd_x, core, outs, scratch, 2, "attend_bwd_x", args, 2 * 10**10)


def project(core, resid, gain, shift, w, bias, nl, ns):
    d, n = w.shape
    outs = [shape((4 * nl, d), jnp.bfloat16), shape((4 * ns, d), jnp.bfloat16)]
    outs += [shape((4 * nl, n), jnp.bfloat16), shape((4 * ns, n), jnp.bfloat16)]
    args = (resid, gain[None], shift[None], w, bias[None])
    return remote(project_x, core, outs, [DMA((3, 3)), DMA((3, 3))], 3, "project_x", args)


def collect(core, dl, ds, w, resid, gain, gmid):
    outs = [shape(resid.shape, jnp.float32), shape((8, w.shape[0]), jnp.float32)]
    scratch = [
        pltpu.VMEM(resid.shape, jnp.float32),
        pltpu.VMEM((3,) + resid.shape, jnp.bfloat16),
        pltpu.VMEM((3,) + resid.shape, jnp.bfloat16),
        DMA((3,)),
        DMA((3,)),
    ]
    return remote(collect_x, core, outs, scratch, 4, "collect_x", (dl, ds, w, resid, gain[None], gmid))


def total_x(axes, v, out, land, ssem, rsem):
    barrier = pltpu.get_barrier_semaphore()
    peers = [{ax: 1 - lax.axis_index(ax)} for ax in axes]
    for peer in peers:
        pl.semaphore_signal(barrier, inc=1, device_id=peer, device_id_type=pl.DeviceIdType.MESH)
    pl.semaphore_wait(barrier, len(peers))
    land[0] = v[...]
    n = len(axes)
    for i, peer in enumerate(peers):
        copy = send(land.at[i], land.at[n + 1 + i], ssem.at[i], rsem.at[i], peer)
        copy.start()
        copy.wait()
        land[i + 1] = land[i] + land[n + 1 + i]
    out[...] = land[n]


def total(axes, v):
    n = len(axes)
    scratch = [pltpu.VMEM((2 * n + 1,) + v.shape, jnp.float32), DMA((n,)), DMA((n,))]
    return remote(total_x, axes, [shape(v.shape, jnp.float32)], scratch, 5, "total_x", (v,))[0]


EPS = 1e-05
F32 = jnp.float32
BF = jnp.bfloat16


def swap(v, *axes):
    count = 2 ** len(axes)
    return lax.ppermute(
        v, axes if len(axes) > 1 else axes[0], [(i, count - 1 - i) for i in range(count)]
    )


def ordered(own, other, index, axis):
    return jnp.where(
        index == 0,
        jnp.concatenate([own, other], axis=axis),
        jnp.concatenate([other, own], axis=axis),
    )


def pick(v, index, axis):
    return lax.dynamic_index_in_dim(v, index, axis, keepdims=False)


def normalize(v, gain, shift):
    mean = jnp.mean(v, axis=-1, keepdims=True)
    cen = v - mean
    var = jnp.mean(cen * cen, axis=-1, keepdims=True)
    inv = lax.rsqrt(var + EPS)
    hat = cen * inv
    return hat * gain + shift, hat, inv


def normalize_back(grad, hat, inv, gain):
    gh = grad * gain
    a = jnp.mean(gh, axis=-1, keepdims=True)
    b = jnp.mean(gh * hat, axis=-1, keepdims=True)
    return inv * (gh - a - hat * b), jnp.sum(grad * hat, axis=0), jnp.sum(grad, axis=0)


def gelu_both(u):
    k = 0.7978845608028654
    inner = k * (u + 0.044715 * u * u * u)
    t = jnp.tanh(inner)
    act = 0.5 * u * (1.0 + t)
    slope = 0.5 * (1.0 + t) + 0.5 * u * (1.0 - t * t) * k * (1.0 + 3 * 0.044715 * u * u)
    return act, slope


def dot(a, b, ca=1, cb=0):
    return lax.dot_general(a, b, (((ca,), (cb,)), ((), ())), preferred_element_type=F32)


class Plan:
    def __init__(self, dims, dp, mp):
        self.dims, self.dp, self.mp = dims, dp, mp
        self.core = dims[-1]
        self.plane = dims[:-1]
        self.c = lax.axis_index(self.core)
        self.zh = lax.axis_index("zh")
        self.zl = lax.axis_index("zl")
        self.z = lax.axis_index(("zh", "zl"))
        self.d = lax.axis_index(dims)

    def relabel(self, v):
        got = lax.ppermute(v, (self.core, "zh"), [(1, 2), (2, 1)])
        return jnp.where(self.c == self.zh, v, got)

    def ring(self, v, step):
        n = self.mp
        return lax.ppermute(v, ("zh", "zl"), [(i, (i + step) % n) for i in range(n)])

    def gather(self, v):
        v = ordered(v, swap(v, "zl"), self.zl, 0)
        return ordered(v, swap(v, self.core), self.c, 0)

    def scatter(self, v):
        rows = v.shape[0] // 4
        v = v.reshape(2, 2, rows, v.shape[1])
        got = swap(pick(v, 1 - self.c, 0), self.core)
        mine = pick(v, self.c, 0).astype(F32) + got.astype(F32)
        got = swap(pick(mine, 1 - self.zl, 0).astype(BF), "zl")
        return pick(mine, self.zl, 0) + got.astype(F32)

    def to_rows(self, o):
        rows = o.shape[0] // 4
        o = o.reshape(2, 2, rows, o.shape[1])
        got = []
        for dc in range(2):
            line = []
            for dz in range(2):
                part = pick(pick(o, self.c ^ dc, 0), self.zl ^ dz, 0)
                axes = ((self.core,) if dc else ()) + (("zl",) if dz else ())
                line.append(swap(part, *axes) if axes else part)
            got.append(ordered(line[0], line[1], self.zl, 1))
        return ordered(got[0], got[1], self.c, 1)

    def to_heads(self, g):
        rows, w = g.shape[0], g.shape[1] // 4
        g = g.reshape(rows, 2, 2, w)
        got = []
        for dc in range(2):
            line = []
            for dz in range(2):
                part = pick(pick(g, self.c ^ dc, 1), self.zl ^ dz, 1)
                axes = ((self.core,) if dc else ()) + (("zl",) if dz else ())
                line.append(swap(part, *axes) if axes else part)
            got.append(ordered(line[0], line[1], self.zl, 0))
        return ordered(got[0], got[1], self.c, 0)

    def piece(self, w):
        rows = w.shape[0] // self.dp
        return lax.dynamic_slice_in_dim(w, self.d * rows, rows, 0)

    def ring_gather(self, v):
        parts = []
        for _ in range(self.mp - 1):
            v = self.ring(v, 1)
            parts.append(v)
        return parts

    def plane_gather(self, v, axes):
        k, rows, n = v.shape
        have = []
        shape = [k]
        for ax in axes:
            pos = sum(self.dims.index(h) < self.dims.index(ax) for h in have)
            got = swap(v, ax)
            cur = v.reshape(k, *([2] * len(have)), rows, n)
            oth = got.reshape(cur.shape)
            a = jnp.stack([cur, oth], axis=1 + pos)
            b = jnp.stack([oth, cur], axis=1 + pos)
            v = jnp.where(lax.axis_index(ax) == 0, a, b)
            have.append(ax)
            v = v.reshape(k, -1, rows, n).reshape(k, -1, n)
            rows_all = v.shape[1]
            v = v.reshape(k, rows_all, n)
        return v.reshape(k, self.dp, rows, n)

    def plane_scatter(self, g, axes):
        n = g.shape[1]
        left = [ax for ax in self.dims]
        rows = g.shape[0] // self.dp
        v = g.reshape(*([2] * len(left)), rows, n)
        for ax in axes:
            pos = left.index(ax)
            i = lax.axis_index(ax)
            got = swap(pick(v, 1 - i, pos), ax)
            v = (pick(v, i, pos).astype(F32) + got.astype(F32)).astype(BF)
            left.remove(ax)
        return v.reshape(-1, n)

    def ring_scatter(self, chunks):
        t = chunks[-1]
        for r in range(self.mp - 2, -1, -1):
            got = self.ring(t, -1)
            t = chunks[r].astype(F32) + got.astype(F32)
            if r:
                t = t.astype(BF)
        return t


def body(
    dims, dp, mp,
    x_long, x_short, dy_long, dy_short, ln_gain, ln_bias, w_qkv, b_qv, w_out, b_out, w_up, b_up, w_down, b_down, threshold,
):
    plan = Plan(dims, dp, mp)
    layers = w_qkv.shape[0]
    d_model = x_long.shape[-1]
    heads_w = w_qkv.shape[-1]
    ffq = w_up.shape[-1]
    rl, rs = x_long.shape[1], x_short.shape[1]
    rows = rl + rs
    core_rest = tuple(plan.plane)
    fwd_axes = core_rest + (plan.core,)
    alt_axes = core_rest[::-1] + (plan.core,)
    gain = ln_gain.astype(F32)
    shift = ln_bias.astype(F32)

    x = jnp.concatenate([x_long[0], x_short[0]], axis=0)
    x = plan.relabel(x)

    small = jnp.concatenate([b_up.reshape(-1), b_qv.reshape(-1)])
    rel_small = jnp.stack([small] + plan.ring_gather(small))
    n_up = layers * ffq
    rel_bup = rel_small[:, :n_up].reshape(mp, layers, ffq).astype(F32)
    rel_bqv = rel_small[:, n_up:].reshape(mp, layers, 2, heads_w).astype(F32)
    mine = 2 * plan.c + plan.zl
    my_bqv = pick(rel_bqv, (plan.z - mine) % mp, 0)
    zero_bq = pick(rel_bqv, plan.z % mp, 0)[:, 0, :HD]

    exts = []
    for l in range(layers):
        quarter = plan.relabel(w_qkv[l].reshape(d_model, 3 * heads_w))
        head0 = w_qkv[l][:, :2, :HD].reshape(d_model, 2 * HD)
        got = lax.ppermute(head0, "zl", [(0, 1)])
        head0 = jnp.where(plan.zl == 0, head0, got)
        got = lax.ppermute(head0, "zh", [(0, 1)])
        head0 = jnp.where(plan.zh == 0, head0, got)
        exts.append(jnp.concatenate([quarter, head0], axis=1))

    ups, downs, outs = [], [], []
    for l in range(layers):
        po = plan.piece(w_out[l])
        pu = jnp.concatenate([plan.piece(w_up[l]), po], axis=0)
        pd = plan.piece(w_down[l])
        n_out, n_d = po.shape[0], pd.shape[0]
        both = plan.ring_gather(jnp.concatenate([pu, pd], axis=0))
        stacked = jnp.stack(both)
        n_u = pu.shape[0]
        gu = plan.plane_gather(stacked[:, :n_u], fwd_axes)
        gd = plan.plane_gather(stacked[:, n_u:], alt_axes)
        up = gu[:, :, : n_u - n_out].reshape(mp - 1, d_model, ffq)
        ups.append(jnp.concatenate([w_up[l]] + [up[r] for r in range(mp - 1)], axis=1))
        out = gu[:, :, n_u - n_out :].reshape(mp - 1, heads_w, d_model)
        out = jnp.concatenate([w_out[l][None], out], axis=0)
        outs.append(
            jnp.concatenate([pick(out, (plan.z - q) % mp, 0) for q in range(mp)], axis=0)
        )
        downs.append(
            jnp.concatenate([w_down[l], gd.reshape((mp - 1) * ffq, d_model)], axis=0)
        )

    dy = plan.relabel(jnp.concatenate([dy_long[0], dy_short[0]], axis=0))

    limits = threshold.astype(F32) / 64.0
    resid = x.astype(F32)
    saved = []
    shares = []
    for l in range(layers):
        normed, hat1, inv1 = normalize(resid, gain[l, 0], shift[l, 0])
        normed = normed.astype(BF)
        full = [plan.gather(normed[:rl]), plan.gather(normed[rl:])]
        bias = jnp.concatenate(
            [
                my_bqv[l, 0],
                jnp.zeros((heads_w,), F32),
                my_bqv[l, 1],
                zero_bq[l],
                jnp.zeros((HD,), F32),
            ]
        )
        proj = [(dot(n, exts[l]) + bias).astype(BF) for n in full]
        att = [attend_fwd(p) for p in proj]
        share = jnp.zeros((), F32)
        for p, a in zip(proj, att):
            size = p.shape[0]
            sel = a[2][size // BR]
            left = (size - 1 - lax.broadcasted_iota(jnp.int32, (size,), 0)).astype(F32)
            share = share + jnp.sum(
                jax.nn.sigmoid(4.0 * (sel / jnp.maximum(left, 1.0) - limits[l]))
            )
        shares.append(share)
        attended = jnp.concatenate([plan.to_rows(a[0]) for a in att], axis=0)
        middle = resid + dot(attended, outs[l]) + b_out[l].astype(F32)
        normed2, hat2, inv2 = normalize(middle, gain[l, 1], shift[l, 1])
        normed2 = normed2.astype(BF)
        upper = dot(normed2, ups[l]) + rel_bup[:, l].reshape(-1)
        active = gelu_both(upper)[0].astype(BF)
        saved.append((resid, middle, full, proj, att, attended, normed2, upper, active))
        resid = middle + dot(active, downs[l]) + b_down[l].astype(F32)

    y = plan.relabel(resid.astype(BF))

    g = dy.astype(F32)
    vec = {}
    weight_grads = [None] * layers
    for l in reversed(range(layers)):
        resid, middle, full, proj, att, attended, normed2, upper, active = saved[l]
        g_bdown = jnp.sum(g, axis=0)
        gm = g.astype(BF)
        gact = dot(gm, downs[l], 1, 1)
        slope = gelu_both(upper)[1]
        gu = (slope * gact).astype(BF)
        w_down_t = dot(gm, active, 0, 0).astype(BF)
        w_up_g = dot(normed2, gu, 0, 0).astype(BF)
        g_bup = jnp.sum(gu.astype(F32), axis=0)
        gn2 = dot(gu, ups[l], 1, 1)
        _, hat2, inv2 = normalize(middle, gain[l, 1], shift[l, 1])
        back, g_gain2, g_shift2 = normalize_back(gn2, hat2, inv2, gain[l, 1])
        gmid = g + back
        g_bout = jnp.sum(gmid, axis=0)
        ga = gmid.astype(BF)
        go = dot(ga, outs[l], 1, 1).astype(BF)
        w_out_t = dot(ga, attended, 0, 0).astype(BF)
        gh = [plan.to_heads(go[:rl]), plan.to_heads(go[rl:])]
        dext = [attend_bwd(p, h, a[0], a[1], a[2]) for p, h, a in zip(proj, gh, att)]
        gn1 = jnp.concatenate(
            [plan.scatter(dot(e, exts[l], 1, 1).astype(BF)) for e in dext], axis=0
        )
        w_ext_g = sum(dot(n, e, 0, 0) for n, e in zip(full, dext)).astype(BF)
        g_bext = sum(jnp.sum(e.astype(F32), axis=0) for e in dext)
        _, hat1, inv1 = normalize(resid, gain[l, 0], shift[l, 0])
        back, g_gain1, g_shift1 = normalize_back(gn1, hat1, inv1, gain[l, 0])
        g = gmid + back

        w_up_g = plan.plane_scatter(w_up_g, (plan.core,) + core_rest)
        w_up_g = plan.ring_scatter([w_up_g[:, r * ffq : (r + 1) * ffq] for r in range(mp)])
        w_down_t = plan.plane_scatter(w_down_t, (plan.core,) + core_rest[::-1])
        w_down_t = plan.ring_scatter([w_down_t[:, r * ffq : (r + 1) * ffq] for r in range(mp)])
        w_out_t = plan.plane_scatter(w_out_t, (plan.core,) + core_rest)
        w_out_t = w_out_t.reshape(-1, mp, heads_w)
        w_out_t = plan.ring_scatter([pick(w_out_t, (plan.z - r) % mp, 1) for r in range(mp)])
        w_ext_g = plan.plane_scatter(w_ext_g, core_rest[::-1])
        w_ext_g = w_ext_g.reshape(2, -1, w_ext_g.shape[1])
        part, zero = w_ext_g[..., : 3 * heads_w], w_ext_g[..., 3 * heads_w :]
        got = lax.ppermute(part, (plan.core, "zh"), [(1, 0), (2, 3)])
        part = part.astype(F32) + got.astype(F32)
        got = lax.ppermute(
            pick(part, 1 - plan.c, 0).astype(BF), (plan.core, "zh"), [(0, 2), (3, 1)]
        )
        w_qkv_g = jnp.where(plan.c == plan.zh, pick(part, plan.c, 0), got.astype(F32))
        got = swap(pick(zero, 1 - plan.c, 0), plan.core)
        zero = (pick(zero, plan.c, 0).astype(F32) + got.astype(F32)).astype(BF)
        zero = zero.astype(F32) + swap(zero, "zl").astype(F32)
        zero = zero + swap(zero.astype(BF), "zh").astype(F32)
        zero = jnp.where(plan.z == 0, zero, 0.0)
        w_qkv_g = w_qkv_g.reshape(-1, 3, heads_w)
        zero = zero.reshape(-1, 2, HD)
        w_qkv_g = w_qkv_g + jnp.pad(zero, ((0, 0), (0, 1), (0, heads_w - HD)))
        weight_grads[l] = (w_qkv_g, jnp.transpose(w_out_t), w_up_g, jnp.transpose(w_down_t))

        hot = (lax.broadcasted_iota(jnp.int32, (mp, 1), 0) == mine).astype(F32)
        gq = hot * g_bext[None, :heads_w]
        gv = hot * g_bext[None, 2 * heads_w : 3 * heads_w]
        gq = gq.reshape(-1).at[:HD].add(g_bext[3 * heads_w : 3 * heads_w + HD])
        g_bup = g_bup.reshape(mp, ffq)
        g_bup = jnp.stack([pick(g_bup, (plan.z - q) % mp, 0) for q in range(mp)])
        vec[l] = jnp.concatenate(
            [
                g_gain1, g_gain2, g_shift1, g_shift2, g_bout, g_bdown,
                gq, gv.reshape(-1), g_bup.reshape(-1), jnp.full((128,), shares[l] / mp),
            ]
        )

    dx = plan.relabel(g.astype(BF)).astype(F32)
    total = lax.psum(jnp.stack([vec[l] for l in range(layers)]), dims + ("zh", "zl"))
    n = d_model
    g_gain = total[:, : 2 * n].reshape(layers, 2, n)
    g_bias = total[:, 2 * n : 4 * n].reshape(layers, 2, n)
    g_bout = total[:, 4 * n : 5 * n]
    g_bdown = total[:, 5 * n : 6 * n]
    at = 6 * n
    g_bqv = total[:, at : at + 2 * mp * heads_w].reshape(layers, 2, mp, heads_w)
    at += 2 * mp * heads_w
    g_bup = total[:, at : at + mp * ffq].reshape(layers, mp, ffq)
    at += mp * ffq
    key_share = total[:, at] / (dp * (rows * mp))
    return (
        y[None, :rl],
        y[None, rl:],
        dx[None, :rl],
        dx[None, rl:],
        g_gain,
        g_bias,
        jnp.stack([weight_grads[l][0] for l in range(layers)]),
        pick(g_bqv, plan.z, 2),
        jnp.stack([weight_grads[l][1] for l in range(layers)]),
        g_bout,
        jnp.stack([weight_grads[l][2] for l in range(layers)]),
        pick(g_bup, plan.z, 1),
        jnp.stack([weight_grads[l][3] for l in range(layers)]),
        g_bdown,
        key_share,
    )


MESH = pl.DeviceIdType.MESH
ANY = pl.BlockSpec(memory_space=pl.ANY)


class Net:
    def __init__(self, dims):
        self.dims = dims
        self.y, self.x, self.c = (lax.axis_index(ax) for ax in dims)
        self.zh, self.zl = lax.axis_index("zh"), lax.axis_index("zl")
        self.z = 2 * self.zh + self.zl
        self.yx = 2 * self.y + self.x
        self.me = 2 * self.c + self.zl
        self.moves = self.c != self.zh

    def group(self, delta):
        return {self.dims[2]: self.c ^ (delta >> 1), "zl": self.zl ^ (delta & 1)}

    def member(self, m):
        return {self.dims[2]: m >> 1, "zl": m & 1}

    def plane(self, e):
        return {self.dims[0]: self.y ^ (e >> 1), self.dims[1]: self.x ^ (e & 1)}

    def line(self, r):
        to = (self.z + r) % 4
        return {"zh": to // 2, "zl": to % 2}

    def partner(self):
        return {self.dims[2]: 1 - self.c, "zh": 1 - self.zh}

    def greet(self, peers):
        barrier = pltpu.get_barrier_semaphore()
        for peer in peers:
            pl.semaphore_signal(barrier, inc=1, device_id=peer, device_id_type=MESH)
        pl.semaphore_wait(barrier, len(peers))


class Sems:
    def __init__(self, ssem, rsem):
        self.ssem, self.rsem, self.used = ssem, rsem, 0

    def copy(self, src, dst, device):
        i = self.used
        self.used += 1
        return send(src, dst, self.ssem.at[i], self.rsem.at[i], device)


class Batch:
    def __init__(self, copies, when=None):
        self.copies, self.when = copies, when

    def _do(self, f):
        if self.when is None:
            f()
        else:
            pl.when(self.when)(f)

    def start(self):
        self._do(lambda: [c.start() for c in self.copies] and None)

    def recv(self):
        self._do(lambda: [c.wait_recv() for c in self.copies] and None)

    def sent(self):
        self._do(lambda: [c.wait_send() for c in self.copies] and None)

    def end(self):
        self.recv()
        self.sent()


def aligned(v, n=16):
    return pl.multiple_of(v, n)


def z_weights(net, sems, layer, w_up, w_down, zup, zdn):
    rows, n = zup.shape[1], zup.shape[2]
    part = zdn.shape[1]
    out = []
    for r in (1, 2, 3):
        dev, slot = net.line(r), 3 - r
        src = w_up.at[layer, pl.ds(aligned(net.yx * rows), rows), pl.ds(aligned(net.c * n, 128), n)]
        out.append(sems.copy(src, zup.at[slot], dev))
        src = w_down.at[layer, pl.ds(aligned(net.c * n + net.yx * part), part)]
        out.append(sems.copy(src, zdn.at[slot], dev))
    return Batch(out)


def plane_weights(net, sems, lsem, layer, w_up, w_down, zup, zdn, wup, wdn):
    rows, n = zup.shape[1], zup.shape[2]
    part = zdn.shape[1]
    at_up = pl.ds(aligned(net.yx * rows), rows)
    at_dn = pl.ds(aligned(net.yx * part), part)
    out = []
    for e in (1, 2, 3):
        out.append(sems.copy(zup, wup.at[pl.ds(1, 3), at_up], net.plane(e)))
        out.append(sems.copy(zdn, wdn.at[pl.ds(1, 3), at_dn], net.plane(e)))
    cols = pl.ds(aligned(net.c * n, 128), n)
    local = [
        pltpu.make_async_copy(zup, wup.at[pl.ds(1, 3), at_up], lsem.at[0]),
        pltpu.make_async_copy(zdn, wdn.at[pl.ds(1, 3), at_dn], lsem.at[1]),
        pltpu.make_async_copy(w_up.at[layer, :, cols], wup.at[0], lsem.at[2]),
        pltpu.make_async_copy(w_down.at[layer, pl.ds(aligned(net.c * n), n)], wdn.at[0], lsem.at[3]),
    ]
    return Batch(out), local


class Projections:
    def __init__(self, net, sems, wq, w0, qland, zland, ext):
        self.net, self.wq, self.w0, self.qland, self.zland, self.ext = net, wq, w0, qland, zland, ext
        rows = qland.shape[1]
        here = pl.ds(aligned(net.yx * rows), rows)
        at = net.yx
        self.q1 = Batch([sems.copy(wq.at[here], qland.at[at], net.partner())], net.moves)
        self.q2 = Batch([sems.copy(qland.at[at], qland.at[at], net.plane(e)) for e in (1, 2, 3)], net.moves)
        self.h1 = []
        for r in (1, 2, 3):
            copy = sems.copy(w0.at[here], zland.at[at], net.line(r))
            self.h1.append(copy)
        self.h2 = Batch([sems.copy(zland.at[at], zland.at[at], net.plane(e)) for e in (1, 2, 3)], net.z != 0)

    def start(self):
        self.q1.start()

        @pl.when(self.net.z == 0)
        def _():
            for copy in self.h1:
                copy.start()

    def forward(self):
        self.q1.recv()
        self.q2.start()
        for r in (1, 2, 3):
            pl.when(self.net.z == r)(lambda: self.h1[r - 1].wait_recv())
        self.h2.start()

    def finish(self):
        rows, n = self.qland.shape[1:]
        self.q2.recv()
        self.h2.recv()

        @pl.when(self.net.moves)
        def _():
            for k in range(4):
                self.ext[k * rows : (k + 1) * rows, :n] = self.qland[k]

        @pl.when(jnp.logical_not(self.net.moves))
        def _():
            self.ext[:, :n] = self.wq[...]

        @pl.when(self.net.z != 0)
        def _():
            for k in range(4):
                self.ext[k * rows : (k + 1) * rows, n:] = self.zland[k]

        @pl.when(self.net.z == 0)
        def _():
            self.ext[:, n:] = self.w0[...]

        self.q1.sent()
        self.q2.sent()
        self.h2.sent()

        @pl.when(self.net.z == 0)
        def _():
            for copy in self.h1:
                copy.wait_send()


def first_x(dims, x, wq, w0, small, w_up, w_down, xr, ext, smalls, zup, zdn, qland, zland, lsem, ssem, rsem):
    net, sems = Net(dims), Sems(ssem, rsem)
    moved = Batch([sems.copy(x, xr, net.partner())], net.moves)
    proj = Projections(net, sems, wq, w0, qland, zland, ext)
    tiny = Batch([sems.copy(small, smalls.at[4 - r], net.line(r)) for r in (1, 2, 3)])
    weights = z_weights(net, sems, 0, w_up, w_down, zup, zdn)
    net.greet([net.partner()] + [net.line(r) for r in (1, 2, 3)] + [net.plane(e) for e in (1, 2, 3)])
    proj.start()
    moved.start()
    tiny.start()
    weights.start()
    smalls[0] = small[...]

    @pl.when(jnp.logical_not(net.moves))
    def _():
        xr[...] = x[...]

    proj.forward()
    proj.finish()
    moved.end()
    tiny.end()
    weights.end()


def project_part(net, sems, resid, gain, shift, w, bias, fl, fs, pj_l, pj_s):
    nl, ns = fl.shape[0] // 4, fs.shape[0] // 4
    half = nl // 2
    parts = ((fs, pj_s, ns, 0, ns, nl), (fl, pj_l, nl, 0, half, 0), (fl, pj_l, nl, half, half, half))
    me = net.me

    def rows(k, m):
        ref, _, n, at, size, _ = parts[k]
        return ref.at[pl.ds(aligned(m * n + at), size)]

    def compute(k, m):
        ref, out, n, at, size, _ = parts[k]
        here = pl.ds(aligned(m * n + at), size)
        out[here] = (mm(ref[here], w[...]) + bias[...]).astype(jnp.bfloat16)

    chip = [sems.copy(rows(k, me), rows(k, me), net.group(1)) for k in range(3)]
    core = [sems.copy(rows(k, me), rows(k, me), net.group(2)) for k in range(3)]
    over = [sems.copy(rows(k, me ^ 1), rows(k, me ^ 1), net.group(2)) for k in range(3)]
    for k in range(3):
        ref, _, n, at, size, src = parts[k]
        hat, _ = norm_rows(resid[src : src + size].astype(jnp.float32))
        ref[pl.ds(aligned(me * n + at), size)] = (hat * gain[...] + shift[...]).astype(jnp.bfloat16)
        chip[k].start()
        core[k].start()
    for k in range(3):
        compute(k, me)
    for k in range(3):
        core[k].wait_recv()
        compute(k, me ^ 2)
    for k in range(3):
        chip[k].wait_recv()
        over[k].start()
        compute(k, me ^ 1)
    for k in range(3):
        over[k].wait_recv()
        compute(k, me ^ 3)
    return chip + core + over


def attend_part(net, sems, xl, xs, att, ol, os, lsel, lses, cl, cs, land):
    nl, ns = xl.shape[0] // 4, xs.shape[0] // 4
    w = ol.shape[1]
    base = sems.used
    sems.used += 8

    def part(k):
        return ((ol, nl, 0), (os, ns, nl))[k]

    def copy(k, m):
        src, n, at = part(k)
        return send(
            src.at[pl.ds(m * n, n)],
            land.at[net.me, pl.ds(at, n)],
            sems.ssem.at[base + 4 * k + m],
            sems.rsem.at[base + 4 * k + net.me],
            net.member(m),
        )

    def arrived(k, m):
        src, n, at = part(k)
        i = base + 4 * k + m
        return send(src.at[pl.ds(0, n)], land.at[m, pl.ds(at, n)], sems.ssem.at[i], sems.rsem.at[i], net.member(m))

    def start(k, m):
        src, n, at = part(k)

        @pl.when(net.me != m)
        def _():
            copy(k, m).start()

        @pl.when(net.me == m)
        def _():
            land[m, at : at + n] = src[m * n : (m + 1) * n]

    def started(k, n):
        def done(b):
            for m in range(b * BR // n, (b + 1) * BR // n):
                start(k, m)

        return done

    fwd_one(xs, os, lses, cs, started(1, ns))
    fwd_one(xl, ol, lsel, cl, started(0, nl))
    for m in range(4):

        @pl.when(net.me != m)
        def _():
            for k in range(2):
                copy(k, m).wait_send()
                arrived(k, m).wait_recv()

    for m in range(4):
        att[:, m * w : (m + 1) * w] = land[m]


def layer_x(
    dims, first, resid, gain, shift, w, bias, w_up, w_down, zup, zdn, *rest
):
    net = Net(dims)
    if first:
        wq, w0, *rest = rest
    else:
        dy, *rest = rest
    att, fl, fs, pj_l, pj_s, ol, os, lsel, lses, cl, cs, wup, wdn, extra, *rest = rest
    land, lsem, ssem, rsem, *rest = rest
    sems = Sems(ssem, rsem)
    weights, local = plane_weights(net, sems, lsem, 0 if first else 1, w_up, w_down, zup, zdn, wup, wdn)
    peers = [net.group(2), net.group(3), net.partner()]
    peers += [net.plane(e) for e in (1, 2, 3)] + [net.line(r) for r in (1, 2, 3)]
    if first:
        qland, zland = rest
        proj = Projections(net, sems, wq, w0, qland, zland, extra)
    else:
        moved = Batch([sems.copy(dy, extra, net.partner())], net.moves)
    net.greet(peers)
    weights.start()
    for copy in local:
        copy.start()
    pending = project_part(net, sems, resid, gain, shift, w, bias, fl, fs, pj_l, pj_s)
    if first:
        proj.start()
    else:
        moved.start()

        @pl.when(jnp.logical_not(net.moves))
        def _():
            extra[...] = dy[...]

    attend_part(net, sems, pj_l, pj_s, att, ol, os, lsel, lses, cl, cs, land)
    if first:
        proj.forward()
    for copy in pending:
        copy.wait_send()
    if first:
        proj.finish()
    else:
        moved.end()
    for copy in local:
        copy.wait()
    weights.end()


def gelu_pair(u):
    k = 0.7978845608028654
    sq = u * u
    t = jnp.tanh(u * (k + k * 0.044715 * sq))
    h = 0.5 * (1.0 + t)
    act = u * h
    slope = h + act * (1.0 - t) * (k + 3 * k * 0.044715 * sq)
    return act, slope


def mlp_x(
    dims, last, att, resid, wout, bout, gain, shift, wup, wdn, bup, bdown, w_up, w_down, *rest
):
    net = Net(dims)
    if last:
        middle, n2, act, slope, new, out, got, ssem, rsem = rest
    else:
        middle, n2, act, slope, new, zup, zdn, out, got, ssem, rsem = rest
    sems = Sems(ssem, rsem)
    n = att.shape[0]
    f = wup.shape[2]
    there = sems.copy(n2.at[pl.ds(0, n)], n2.at[pl.ds(n, n)], net.group(2))
    back = sems.copy(out, got, net.group(2))
    peers = [net.group(2)]
    if not last:
        weights = z_weights(net, sems, 1, w_up, w_down, zup, zdn)
        peers += [net.line(r) for r in (1, 2, 3)]
    net.greet(peers)
    if not last:
        weights.start()
    half = n // 2
    for i in range(2):
        at = slice(i * half, (i + 1) * half)
        middle[at] = resid[at].astype(jnp.float32) + mm(att[at], wout[...]) + bout[...]
        hat, _ = norm_rows(middle[at])
        n2[at] = (hat * gain[...] + shift[...]).astype(jnp.bfloat16)
    there.start()

    def hidden(at):
        for r in range(4):
            cols = slice(r * f, (r + 1) * f)
            u = mm(n2[at], wup[r]) + bup[r : r + 1]
            a, s = gelu_pair(u)
            act[at, cols] = a.astype(jnp.bfloat16)
            slope[at, cols] = s.astype(jnp.bfloat16)

    def down(at):
        total = mm(act[at, :f], wdn[0])
        for r in range(1, 4):
            total = total + mm(act[at, r * f : (r + 1) * f], wdn[r])
        return total

    quarter = n // 4
    for i in range(4):
        hidden(slice(i * quarter, (i + 1) * quarter))
    there.wait_recv()
    for i in range(4):
        hidden(slice(n + i * quarter, n + (i + 1) * quarter))
    for i in range(2):
        out[i * half : (i + 1) * half] = down(slice(n + i * half, n + (i + 1) * half)).astype(
            jnp.bfloat16
        )
    back.start()
    for i in range(2):
        at = slice(i * half, (i + 1) * half)
        new[at] = middle[at] + down(at) + bdown[...]
    back.wait_recv()
    new[...] += got[...].astype(jnp.float32)
    there.wait_send()
    back.wait_send()
    if not last:
        weights.end()


TN = (((0,), (0,)), ((), ()))


def ext_scatter(net, sems, dw, land):
    return [sems.copy(dw.at[net.yx ^ e], land.at[e - 1], net.plane(e)) for e in (1, 2, 3)]


def mlp_back_x(
    dims, last, g, att, wout, gain, wup, wdn, middle, n2, act, slope, *rest
):
    net = Net(dims)
    if last:
        ins = ()
    else:
        s_in, so_in, dq_in, d0_in, *rest = rest
    gmid, go, dup, ddn, dout, sums, sums_up, *rest = rest
    if not last:
        f_out, fo_out, q_out, z_out, *rest = rest
    gm, gu, gact, out, got, oself, olands, *rest = rest
    if not last:
        land, oland, qland, zland, *rest = rest
    ssem, rsem = rest
    sems = Sems(ssem, rsem)
    n, d = g.shape
    f = wup.shape[2]
    there = sems.copy(gm.at[pl.ds(0, n)], gm.at[pl.ds(n, n)], net.group(2))
    back = sems.copy(out, got, net.group(2))
    cross = sems.copy(oself, olands, net.group(2))
    peers = [net.group(2)]
    if not last:
        carry = FinishLine(net, sems, s_in, so_in, land, oland)
        ext = Batch(ext_scatter(net, sems, dq_in, qland) + ext_scatter(net, sems, d0_in, zland))
        peers += [net.line(r) for r in (1, 2, 3)] + [net.plane(e) for e in (1, 2, 3)]
    gm[:n] = g[...].astype(jnp.bfloat16)
    net.greet(peers)
    there.start()
    if not last:
        carry.start()
        ext.start()
    sums[...] = jnp.zeros_like(sums)
    sums[0:1] = jnp.sum(g[...], axis=0, keepdims=True)
    quarter = n // 4

    def hidden(at):
        for r in range(4):
            cols = slice(r * f, (r + 1) * f)
            u = mm(gm[at], wdn[r], NT)
            gu[at, cols] = (u * slope[at, cols].astype(jnp.float32)).astype(jnp.bfloat16)

    def up(at):
        total = mm(gu[at, :f], wup[0], NT)
        for r in range(1, 4):
            total = total + mm(gu[at, r * f : (r + 1) * f], wup[r], NT)
        return total

    for i in range(4):
        hidden(slice(i * quarter, (i + 1) * quarter))
    there.wait_recv()
    for i in range(4):
        hidden(slice(n + i * quarter, n + (i + 1) * quarter))
    half = n // 2
    for i in range(2):
        out[i * half : (i + 1) * half] = up(slice(n + i * half, n + (i + 1) * half)).astype(
            jnp.bfloat16
        )
    back.start()
    for i in range(2):
        at = slice(i * half, (i + 1) * half)
        gact[at] = up(at)
    chunk = d // 4

    def products(left, right, dst):
        for k in range(4):
            for r in range(4):
                dst[k, r] = mm(
                    left[:, k * chunk : (k + 1) * chunk], right[:, r * f : (r + 1) * f], TN
                ).astype(jnp.bfloat16)

    products(gm, act, ddn)
    back.wait_recv()
    gn = gact[...] + got[...].astype(jnp.float32)
    hat, inv = norm_rows(middle[...])
    gh = gn * gain[...]
    a = jnp.mean(gh, axis=-1, keepdims=True)
    b = jnp.mean(gh * hat, axis=-1, keepdims=True)
    gmid[...] = g[...] + inv * (gh - a - hat * b)
    sums[1:2] = jnp.sum(gn * hat, axis=0, keepdims=True)
    sums[2:3] = jnp.sum(gn, axis=0, keepdims=True)
    sums[3:4] = jnp.sum(gmid[...], axis=0, keepdims=True)
    ga = gmid[...].astype(jnp.bfloat16)
    go[...] = mm(ga, wout[...], NT).astype(jnp.bfloat16)
    e = att.shape[1] // 2
    other = att[:, pl.ds(aligned((1 - net.c) * e, 128), e)]
    oself[...] = mm(ga, other, TN).astype(jnp.bfloat16)
    cross.start()
    products(n2, gu, dup)
    sums_up[...] = jnp.zeros_like(sums_up)
    sums_up[0:1] = jnp.sum(gu[...].astype(jnp.float32), axis=0, keepdims=True)
    mine = mm(ga, att[:, pl.ds(aligned(net.c * e, 128), e)], TN)
    cross.wait_recv()
    mine = mine + olands[...].astype(jnp.float32)
    for k in range(4):
        dout[k] = mine[k * chunk : (k + 1) * chunk].astype(jnp.bfloat16)
    there.wait_send()
    back.wait_send()
    cross.wait_send()
    if not last:
        carry.finish(f_out, fo_out)
        ext.recv()
        for own, lands, dst in ((dq_in, qland, q_out), (d0_in, zland, z_out)):
            t = own[net.yx].astype(jnp.float32)
            for e in range(3):
                t = t + lands[e].astype(jnp.float32)
            dst[...] = t.astype(jnp.bfloat16)
        ext.sent()


class FinishLine:
    def __init__(self, net, sems, s, so, land, oland):
        self.net, self.s, self.so, self.land, self.oland = net, s, so, land, oland
        self.main = Batch([sems.copy(s.at[r], land.at[3 - r], net.line(r)) for r in (1, 2, 3)])
        self.out = []
        for r in (1, 2, 3):
            to = (net.z + r) % 4
            copy = sems.copy(so.at[to % 2], oland.at[3 - r], net.line(r))
            self.out.append((copy, to // 2 == net.c))
        self.owner = net.zh == net.c

    def start(self):
        self.main.start()
        for copy, use in self.out:
            pl.when(use)(copy.start)

    def finish(self, f_out, fo_out):
        self.main.recv()
        f_out[...] = (
            self.s[0].astype(jnp.float32)
            + self.land[0].astype(jnp.float32)
            + self.land[1].astype(jnp.float32)
            + self.land[2].astype(jnp.float32)
        ).astype(f_out.dtype)

        @pl.when(self.owner)
        def _():
            for copy, _ in self.out:
                copy.wait_recv()
            fo_out[...] = (
                self.so[self.net.zl].astype(jnp.float32)
                + self.oland[0].astype(jnp.float32)
                + self.oland[1].astype(jnp.float32)
                + self.oland[2].astype(jnp.float32)
            ).astype(fo_out.dtype)

        @pl.when(jnp.logical_not(self.owner))
        def _():
            fo_out[...] = jnp.zeros_like(fo_out)

        self.main.sent()
        for copy, use in self.out:
            pl.when(use)(copy.wait_send)


def layer_back_x(
    dims, xl, xs, go, ol, os, lsel, lses, cl, cs, w, resid, gain, gmid, fl, fs, dup, ddn, dout,
    g_ref, sums, bsum, dq, d0, s, so,
    dl, ds, acc, kt, outg, gl, gs, mine, out, got, rup, rdn, rout, ssem, rsem,
):
    net, sems = Net(dims), Sems(ssem, rsem)
    nl, ns = xl.shape[0] // 4, xs.shape[0] // 4
    wid = ol.shape[1]
    me = net.me
    base = sems.used
    sems.used += 8
    big = []
    for e in (1, 2, 3):
        at = net.yx ^ e
        big.append(sems.copy(ddn.at[at], rdn.at[e - 1], net.plane(e)))
        big.append(sems.copy(dup.at[at], rup.at[e - 1], net.plane(e)))
        big.append(sems.copy(dout.at[at], rout.at[e - 1], net.plane(e)))
    big = Batch(big)
    for m in range(4):
        outg[m] = go[:, m * wid : (m + 1) * wid]
    net.greet([net.group(d) for d in (1, 2, 3)] + [net.plane(e) for e in (1, 2, 3)])

    def part(k):
        return ((gl, nl, 0), (gs, ns, nl))[k]

    def copy(k, m):
        dst, n, at = part(k)
        return send(
            outg.at[m, pl.ds(at, n)],
            dst.at[pl.ds(aligned(me * n), n)],
            sems.ssem.at[base + 4 * k + m],
            sems.rsem.at[base + 4 * k + me],
            net.member(m),
        )

    def arrived(k, m):
        dst, n, at = part(k)
        i = base + 4 * k + m
        return send(outg.at[m, pl.ds(at, n)], dst.at[pl.ds(m * n, n)], sems.ssem.at[i], sems.rsem.at[i], net.member(m))

    for k in (1, 0):
        for m in range(4):
            dst, n, at = part(k)

            @pl.when(me != m)
            def _():
                copy(k, m).start()

            @pl.when(me == m)
            def _():
                dst[m * n : (m + 1) * n] = outg[m, at : at + n]

    big.start()
    for k in (1, 0):
        for m in range(4):

            @pl.when(me != m)
            def _():
                arrived(k, m).wait_recv()

        if k:
            bwd_one(xs, gs, os, lses, cs, ds, acc, kt)
        else:
            bwd_one(xl, gl, ol, lsel, cl, dl, acc, kt)
    for m in range(4):

        @pl.when(me != m)
        def _():
            for k in range(2):
                copy(k, m).wait_send()

    def partial(m):
        a = mm(dl[pl.ds(aligned(m * nl), nl)], w[...], NT)
        b = mm(ds[pl.ds(aligned(m * ns), ns)], w[...], NT)
        return jnp.concatenate([a, b], axis=0)

    to_core = [sems.copy(out.at[k], got.at[k], net.group(2)) for k in (0, 1)]
    to_chip = sems.copy(out.at[2], got.at[2], net.group(1))
    out[0] = partial(me ^ 3).astype(jnp.bfloat16)
    to_core[0].start()
    mine[...] = partial(me ^ 1)
    to_core[0].wait_recv()
    out[2] = (mine[...] + got[0].astype(jnp.float32)).astype(jnp.bfloat16)
    to_chip.start()
    out[1] = partial(me ^ 2).astype(jnp.bfloat16)
    to_core[1].start()
    mine[...] = partial(me)
    chunk = w.shape[0] // 4
    nq = dq.shape[2]
    for k in range(4):
        at = slice(k * chunk, (k + 1) * chunk)
        both = mm(fl[:, at], dl[...], TN) + mm(fs[:, at], ds[...], TN)
        dq[k] = both[:, :nq].astype(jnp.bfloat16)
        d0[k] = both[:, nq:].astype(jnp.bfloat16)
    bsum[...] = jnp.zeros_like(bsum)
    bsum[0:1] = jnp.sum(dl[...].astype(jnp.float32), axis=0, keepdims=True) + jnp.sum(
        ds[...].astype(jnp.float32), axis=0, keepdims=True
    )
    hat, inv = norm_rows(resid[...].astype(jnp.float32))
    to_core[1].wait_recv()
    to_chip.wait_recv()
    grad = mine[...] + got[1].astype(jnp.float32) + got[2].astype(jnp.float32)
    gh = grad * gain[...]
    a = jnp.mean(gh, axis=-1, keepdims=True)
    b = jnp.mean(gh * hat, axis=-1, keepdims=True)
    g_ref[...] = gmid[...] + inv * (gh - a - hat * b)
    sums[...] = jnp.zeros_like(sums)
    sums[0:1] = jnp.sum(grad * hat, axis=0, keepdims=True)
    sums[1:2] = jnp.sum(grad, axis=0, keepdims=True)
    for c in to_core + [to_chip]:
        c.wait_send()
    big.recv()
    yx = net.yx
    for r in range(4):
        for i, (own, land) in enumerate(((dup, rup), (ddn, rdn))):
            t = own[yx, r].astype(jnp.float32)
            for e in range(3):
                t = t + land[e, r].astype(jnp.float32)
            s[r, i] = t.astype(jnp.bfloat16)
    t = dout[yx].astype(jnp.float32)
    for e in range(3):
        t = t + rout[e].astype(jnp.float32)
    n = so.shape[2]
    for i in range(2):
        so[i] = t[:, i * n : (i + 1) * n].astype(jnp.bfloat16)
    big.sent()


def tail_x(
    axes, s, so, dq, d0, f1, fo1, q1, z1, vec, dx,
    gup, gdn, gout, gqkv, dxr, total_ref,
    land, oland, f0, fo0, qland, zland, qs, zs, qline, zline, fself, fland, oself, olands, qself, qlands, zself, zlands, vland,
    ssem, rsem,
):
    dims = axes[:-2]
    net, sems = Net(dims), Sems(ssem, rsem)
    moved = Batch([sems.copy(dx, dxr, net.partner())], net.moves)
    line = FinishLine(net, sems, s, so, land, oland)
    ext = Batch(ext_scatter(net, sems, dq, qland) + ext_scatter(net, sems, d0, zland))
    rounds = [{ax: 1 - lax.axis_index(ax)} for ax in axes]
    nv = len(axes)
    steps = [sems.copy(vland.at[i], vland.at[nv + 1 + i], peer) for i, peer in enumerate(rounds)]
    qsend = Batch([sems.copy(qs, qline, net.line(2))], net.moves)
    qrecv = jnp.logical_not(net.moves)
    zsend = [sems.copy(zs, zline.at[r - 1], net.line(r)) for r in (1, 2, 3)]
    cross = Batch([sems.copy(fself, fland, net.group(2)), sems.copy(zself, zlands, net.group(2))])
    owned = Batch([sems.copy(oself, olands, net.group(2)), sems.copy(qself, qlands, net.group(2))])
    net.greet(
        [net.partner(), net.group(2)]
        + [net.line(r) for r in (1, 2, 3)]
        + [net.plane(e) for e in (1, 2, 3)]
    )
    f32 = jnp.float32
    ext.start()
    moved.start()
    line.start()

    @pl.when(jnp.logical_not(net.moves))
    def _():
        dxr[...] = dx[...]

    vland[0] = vec[...]
    for i in range(nv):
        steps[i].start()
        steps[i].wait()
        vland[i + 1] = vland[i] + vland[nv + 1 + i]
    total_ref[...] = vland[nv]

    ext.recv()
    yx = net.yx
    for own, lands, dst in ((dq, qland, qs), (d0, zland, zs)):
        t = own[yx].astype(f32)
        for e in range(3):
            t = t + lands[e].astype(f32)
        dst[0] = t.astype(jnp.bfloat16)
    qs[1] = q1[...]
    zs[1] = z1[...]
    qsend.start()
    for r in (1, 2, 3):
        pl.when(net.z == 4 - r)(zsend[r - 1].start)
    line.finish(f0, fo0)
    half = f0.shape[1] // 2
    theirs = pl.ds(aligned((1 - net.c) * half), half)
    ours = pl.ds(aligned(net.c * half), half)

    @pl.when(qrecv)
    def _():
        qsend.copies[0].wait_recv()
        for l in range(2):
            qself[l] = (qs[l, theirs].astype(f32) + qline[l, theirs].astype(f32)).astype(jnp.bfloat16)
            gqkv[l] = qs[l, ours].astype(f32) + qline[l, ours].astype(f32)
        for l, fo in ((0, fo0), (1, fo1)):
            oself[l] = fo[theirs].astype(jnp.bfloat16)
            gout[l] = fo[ours].astype(f32)
        for c in owned.copies:
            c.start()

    @pl.when(net.z == 0)
    def _():
        for r in (1, 2, 3):
            zsend[r - 1].wait_recv()
        for l in range(2):
            t = zs[l].astype(f32)
            for r in range(3):
                t = t + zline[r, l].astype(f32)
            zs[l] = t.astype(jnp.bfloat16)

    for l, f in ((0, f0), (1, f1)):
        for i in range(2):
            fself[l, i] = f[i, theirs].astype(jnp.bfloat16)
        zself[l] = zs[l, theirs]
    cross.start()
    cross.recv()
    n = f0.shape[2]

    @pl.when(net.moves)
    def _():
        for c in owned.copies:
            c.wait_recv()
        gqkv[...] = qlands[...].astype(f32)
        gout[...] = olands[...].astype(f32)

    for c in range(2):

        @pl.when(net.c == c)
        def _():
            for l, f in ((0, f0), (1, f1)):
                for i, dst in ((0, gup), (1, gdn)):
                    dst[l, :, c * n : (c + 1) * n] = f[i, ours].astype(f32)
                    dst[l, :, (1 - c) * n : (2 - c) * n] = fland[l, i].astype(f32)

    @pl.when(net.z == 0)
    def _():
        wid = gout.shape[2]
        for l in range(2):
            t = zs[l, ours].astype(f32) + zlands[l].astype(f32)
            gqkv[l, :, :HD] += t[:, :HD]
            gqkv[l, :, wid : wid + HD] += t[:, HD:]

    pl.when(qrecv)(lambda: [c.wait_send() for c in owned.copies] and None)
    cross.sent()
    qsend.sent()
    for r in (1, 2, 3):
        pl.when(net.z == 4 - r)(zsend[r - 1].wait_send)
    ext.sent()
    moved.end()


def call(kernel, static, args, outs, scratch, ident, name, flops):
    return pl.pallas_call(
        functools.partial(kernel, *static),
        out_shape=tuple(jax.ShapeDtypeStruct(tuple(s), t) for s, t, _ in outs),
        in_specs=[VMEM if v else ANY for _, v in args],
        out_specs=tuple(VMEM if v else ANY for _, _, v in outs),
        scratch_shapes=scratch,
        compiler_params=pltpu.CompilerParams(
            vmem_limit_bytes=56 * 1024 * 1024, collective_id=ident, has_side_effects=True
        ),
        cost_estimate=pl.CostEstimate(flops=flops, bytes_accessed=10**7, transcendentals=10**6),
        name=name,
    )(*[a for a, _ in args])


def sems_of(n):
    return [DMA((n,)), DMA((n,))]


def fast_body(
    dims, x_long, x_short, dy_long, dy_short, ln_gain, ln_bias, w_qkv, b_qv, w_out, b_out, w_up, b_up, w_down, b_down, threshold
):
    bf, f32 = jnp.bfloat16, jnp.float32
    layers, d = w_qkv.shape[0], w_qkv.shape[1]
    wid, ffq = w_qkv.shape[3], w_up.shape[2]
    rl, rs = x_long.shape[1], x_short.shape[1]
    rows = rl + rs
    nq, nx = 3 * wid, 3 * wid + 2 * HD
    f = ffq // 2
    chunk, part = d // 4, f // 4
    net = Net(dims)
    axes = dims + ("zh", "zl")
    vm = lambda *s: pltpu.VMEM(tuple(s), bf)
    vf = lambda *s: pltpu.VMEM(tuple(s), f32)

    x = jnp.concatenate([x_long[0], x_short[0]], axis=0)
    dy = jnp.concatenate([dy_long[0], dy_short[0]], axis=0)
    wqs = [w_qkv[l].reshape(d, nq) for l in range(layers)]
    w0s = [w_qkv[l][:, :2, :HD].reshape(d, 2 * HD) for l in range(layers)]
    flat = jnp.concatenate([b_up.reshape(-1), b_qv.reshape(-1)])
    flat = jnp.pad(flat, (0, -flat.shape[0] % 4096)).reshape(16, -1)
    order = ("zh", "zl") + dims
    share_rows = wid // 8
    wo = lax.dynamic_slice_in_dim(w_out, (4 * net.y + 2 * net.x + net.c) * share_rows, share_rows, 1)
    wo = lax.all_gather(wo, order, axis=0, tiled=False)
    wo = jnp.moveaxis(wo, 1, 0).reshape(layers, 4 * wid, d)

    lands = [vm(4, chunk, nq), vm(4, chunk, 2 * HD)]
    xr, ext0, smalls, zup, zdn = call(
        first_x,
        (dims,),
        [(x, 1), (wqs[0], 1), (w0s[0], 1), (flat, 1), (w_up, 0), (w_down, 0)],
        [((rows, d), bf, 1), ((d, nx), bf, 1), ((4,) + flat.shape, bf, 1), ((3, chunk, f), bf, 0), ((3, part, d), bf, 0)],
        lands + [DMA((1,))] + sems_of(24),
        1,
        "first_x",
        10**9,
    )
    n_up = layers * ffq
    smalls = smalls.reshape(4, -1)
    rel_bup = smalls[:, :n_up].reshape(4, layers, 2, f).astype(f32)
    rel_bup = lax.dynamic_index_in_dim(rel_bup, net.c, 2, keepdims=False)
    rel_bqv = smalls[:, n_up : n_up + layers * 2 * wid].reshape(4, layers, 2, wid).astype(f32)
    my_bqv = lax.dynamic_index_in_dim(rel_bqv, (net.me - net.z) % 4, 0, keepdims=False)
    zero_bq = lax.dynamic_index_in_dim(rel_bqv, (0 - net.z) % 4, 0, keepdims=False)[:, 0, :HD]
    none = jnp.zeros((layers, wid), f32)
    bias = jnp.concatenate([my_bqv[:, 0], none, my_bqv[:, 1], zero_bq, none[:, :HD]], axis=1)
    gain, shift = ln_gain.astype(f32), ln_bias.astype(f32)
    bo, bd = b_out.astype(f32), b_down.astype(f32)
    limits = threshold.astype(f32) / 64.0

    resid = xr
    exts = [ext0, None]
    saved, shares = [], []
    for l in range(layers):
        first = l == 0
        extra = [(wqs[1], 1), (w0s[1], 1)] if first else [(dy, 1)]
        extra_out = ((d, nx), bf, 1) if first else ((rows, d), bf, 1)
        size = ((4 * rl), (4 * rs))
        att, fl, fs, pj_l, pj_s, ol, os, lsel, lses, cl, cs, wup, wdn, got = call(
            layer_x,
            (dims, first),
            [
                (resid, 1), (gain[l, :1], 1), (shift[l, :1], 1), (exts[l], 1), (bias[l : l + 1], 1),
                (w_up, 0), (w_down, 0), (zup, 0), (zdn, 0),
            ] + extra,
            [((rows, 4 * wid), bf, 1)]
            + [((n, d), bf, 1) for n in size]
            + [((n, nx), bf, 1) for n in size]
            + [((n, wid), bf, 1) for n in size]
            + [((8, n), f32, 1) for n in size] * 2
            + [((4, d, f), bf, 0), ((4, f, d), bf, 0), extra_out],
            [vm(4, rows, wid), DMA((4,))] + sems_of(40) + (lands if first else []),
            2 + l,
            "layer_x",
            10**10,
        )
        if first:
            exts[1] = got
        else:
            dyr = got
        share = jnp.zeros((), f32)
        for carry in (cl, cs):
            n = carry.shape[1]
            left = (n - 1 - lax.broadcasted_iota(jnp.int32, (n,), 0)).astype(f32)
            ratio = carry[n // BR] / jnp.maximum(left, 1.0)
            share = share + jnp.sum(jax.nn.sigmoid(4.0 * (ratio - limits[l])))
        shares.append(share)
        last = l == layers - 1
        outs = [
            ((rows, d), f32, 1), ((2 * rows, d), bf, 1), ((2 * rows, 4 * f), bf, 1), ((2 * rows, 4 * f), bf, 1),
            ((rows, d), f32, 1),
        ]
        if not last:
            outs += [((3, chunk, f), bf, 0), ((3, part, d), bf, 0)]
        middle, n2, act, slope, new, *z = call(
            mlp_x,
            (dims, last),
            [
                (att, 1), (resid, 1), (wo[l], 1), (bo[l : l + 1], 1), (gain[l, 1:], 1), (shift[l, 1:], 1),
                (wup, 1), (wdn, 1), (rel_bup[:, l], 1), (bd[l : l + 1], 1), (w_up, 0), (w_down, 0),
            ],
            outs,
            [vm(rows, d), vm(rows, d)] + sems_of(10),
            4 + l,
            "mlp_x",
            10**10,
        )
        if not last:
            zup, zdn = z
        saved.append((resid, middle, n2, act, slope, att, fl, fs, pj_l, pj_s, ol, os, lsel, lses, cl, cs, wup, wdn))
        resid = new

    y = Plan(dims, 8, 4).relabel(resid.astype(bf))
    g = dyr.astype(f32)
    vec = [None] * layers
    carried = []
    for l in reversed(range(layers)):
        resid, middle, n2, act, slope, att, fl, fs, pj_l, pj_s, ol, os, lsel, lses, cl, cs, wup, wdn = saved[l]
        last = l == layers - 1
        outs = [
            ((rows, d), f32, 1), ((rows, d), bf, 1), ((4, 4, chunk, f), bf, 1), ((4, 4, chunk, f), bf, 1),
            ((4, chunk, 2 * wid), bf, 1), ((8, d), f32, 1), ((8, 4 * f), f32, 1),
        ]
        scratch = [
            vm(2 * rows, d), vm(2 * rows, 4 * f), vf(rows, d), vm(rows, d), vm(rows, d), vm(d, 2 * wid), vm(d, 2 * wid)
        ]
        args = [
            (g, 1), (att, 1), (wo[l], 1), (gain[l, 1:], 1), (wup, 1), (wdn, 1), (middle, 1), (n2, 1), (act, 1), (slope, 1)
        ]
        if not last:
            args += [(v, 1) for v in carried]
            outs += [((2, chunk, f), bf, 1), ((chunk, wid), bf, 1), ((chunk, nq), bf, 1), ((chunk, 2 * HD), bf, 1)]
            scratch += [vm(3, 2, chunk, f), vm(3, chunk, wid), vm(3, chunk, nq), vm(3, chunk, 2 * HD)]
        gmid, go, dup, ddn, dout, sums2, sums_up, *done = call(
            mlp_back_x, (dims, last), args, outs, scratch + sems_of(20), 6 + l, "mlp_back_x", 10**10
        )
        size = ((4 * rl), (4 * rs))
        g, sums1, bsum, dq, d0, s, so = call(
            layer_back_x,
            (dims,),
            [
                (v, 1)
                for v in (
                    pj_l, pj_s, go, ol, os, lsel, lses, cl, cs, exts[l], resid, gain[l, :1], gmid, fl, fs, dup, ddn, dout
                )
            ],
            [
                ((rows, d), f32, 1), ((8, d), f32, 1), ((8, nx), f32, 1), ((4, chunk, nq), bf, 1),
                ((4, chunk, 2 * HD), bf, 1), ((4, 2, chunk, f), bf, 1), ((2, chunk, wid), bf, 1),
            ],
            [
                vm(size[0], nx), vm(size[1], nx), vf(2 * (wid // HD) + 1, size[0], HD), vm(wid // HD + 1, HD, size[0]),
                vm(4, rows, wid), vm(size[0], wid), vm(size[1], wid), vf(rows, d), vm(3, rows, d), vm(3, rows, d),
                vm(3, 4, chunk, f), vm(3, 4, chunk, f), vm(3, chunk, 2 * wid),
            ] + sems_of(24),
            8 + l,
            "layer_back_x",
            2 * 10**10,
        )
        carried = [s, so, dq, d0]
        hot = (lax.broadcasted_iota(jnp.int32, (4, 1), 0) == net.me).astype(f32)
        b = bsum[0]
        gq = (hot * b[None, :wid]).reshape(-1).at[:HD].add(b[nq : nq + HD])
        gv = (hot * b[None, 2 * wid : nq]).reshape(-1)
        up = sums_up[0].reshape(4, f)
        up = jnp.stack([lax.dynamic_index_in_dim(up, (q - net.z) % 4, 0, keepdims=False) for q in range(4)])
        side = (lax.broadcasted_iota(jnp.int32, (1, 2, 1), 1) == net.c).astype(f32)
        up = (up[:, None] * side).reshape(-1)
        vec[l] = jnp.concatenate(
            [
                sums1[0], sums2[1], sums1[1], sums2[2], sums2[3], sums2[0], gq, gv, up,
                jnp.full((128,), shares[l] / 4),
            ]
        )

    v = jnp.stack(vec)
    flat_v = v.reshape(-1, 128)
    pad = -flat_v.shape[0] % 8
    flat_v = jnp.pad(flat_v, ((0, pad), (0, 0)))
    f1, fo1, q1, z1 = done
    s, so, dq, d0 = carried
    half = chunk // 2
    nv = len(axes)
    gup, gdn, gout, gqkv, dx, tot = call(
        tail_x,
        (axes,),
        [(a, 1) for a in (s, so, dq, d0, f1, fo1, q1, z1, flat_v, g.astype(bf))],
        [
            ((2, half, ffq), f32, 1), ((2, half, ffq), f32, 1), ((2, half, wid), f32, 1), ((2, half, nq), f32, 1),
            ((rows, d), bf, 1), (flat_v.shape, f32, 1),
        ],
        [
            vm(3, 2, chunk, f), vm(3, chunk, wid), vf(2, chunk, f), vf(chunk, wid),
            vm(3, chunk, nq), vm(3, chunk, 2 * HD), vm(2, chunk, nq), vm(2, chunk, 2 * HD), vm(2, chunk, nq),
            vm(3, 2, chunk, 2 * HD), vm(2, 2, half, f), vm(2, 2, half, f), vm(2, half, wid), vm(2, half, wid),
            vm(2, half, nq), vm(2, half, nq), vm(2, half, 2 * HD), vm(2, half, 2 * HD), vf(2 * nv + 1, *flat_v.shape),
        ] + sems_of(32),
        10,
        "tail_x",
        10**9,
    )
    tot = tot[: flat_v.shape[0] - pad].reshape(v.shape) if pad else tot.reshape(v.shape)
    dx = dx.astype(f32)
    at = 6 * d
    g_bqv = tot[:, at : at + 8 * wid].reshape(layers, 2, 4, wid)
    at += 8 * wid
    g_bup = tot[:, at : at + 4 * ffq].reshape(layers, 4, ffq)
    at += 4 * ffq
    return (
        y[None, :rl],
        y[None, rl:],
        dx[None, :rl],
        dx[None, rl:],
        tot[:, : 2 * d].reshape(layers, 2, d),
        tot[:, 2 * d : 4 * d].reshape(layers, 2, d),
        gqkv.reshape(layers, half, 3, wid),
        pick(g_bqv, net.z, 2),
        jnp.swapaxes(gout, 1, 2),
        tot[:, 4 * d : 5 * d],
        gup,
        pick(g_bup, net.z, 1),
        jnp.swapaxes(gdn, 1, 2),
        tot[:, 5 * d : 6 * d],
        tot[:, at] / (8 * 4 * rows),
    )


def solution(mesh):
    dp, mp = mesh.shape["dp"], mesh.shape["mp"]
    bits = dp.bit_length() - 1
    dims = tuple(f"d{i}" for i in range(bits))
    fine = Mesh(mesh.devices.reshape((2,) * bits + (2, mp // 2)), dims + ("zh", "zl"))
    z = ("zh", "zl")
    in_specs = (
        P(dims, z, None), P(dims, z, None), P(dims, z, None), P(dims, z, None),
        P(), P(), P(None, None, None, z), P(None, None, z), P(None, z, None), P(),
        P(None, None, z), P(None, z), P(None, z, None), P(), P(),
    )
    out_specs = (
        P(dims, z, None), P(dims, z, None), P(dims, z, None), P(dims, z, None),
        P(), P(), P(None, dims, None, z), P(None, None, z), P(None, z, dims), P(),
        P(None, dims, z), P(None, z), P(None, z, dims), P(), P(),
    )
    run = functools.partial(fast_body, dims) if dp == 8 else functools.partial(body, dims, dp, mp)
    return jax.shard_map(
        run, mesh=fine, in_specs=in_specs, out_specs=out_specs, check_vma=False
    )
```

```python
import functools
import types

import jax, jax.numpy as jnp
from jax import lax
from jax.experimental import pallas as pl
from jax.experimental.pallas import tpu as pltpu
from jax.sharding import Mesh
from jax.sharding import PartitionSpec as P

HD = 64
BR = 256
BIG = 1e30
NT = (((1,), (1,)), ((), ()))
NN = (((1,), (0,)), ((), ()))


def mm(a, b, dims=NN):
    return lax.dot_general(a, b, dims, preferred_element_type=jnp.float32)


def halves(v):
    hi = v.astype(jnp.bfloat16)
    lo = (v - hi.astype(jnp.float32)).astype(jnp.bfloat16)
    return hi, lo


def softplus(v):
    return jnp.maximum(v, 0.0) + jnp.log(1.0 + jnp.exp(-jnp.abs(v)))


def fwd_one(x_ref, o_ref, lse_ref, carry_ref, done=None):
    size = x_ref.shape[0]
    nh = (x_ref.shape[1] - 2 * HD) // (3 * HD)
    w = nh * HD
    nb = size // BR
    first = lax.broadcasted_iota(jnp.int32, (BR, BR), 0)
    second = lax.broadcasted_iota(jnp.int32, (BR, BR), 1)
    tri = (first > second).astype(jnp.bfloat16)
    lanes = lax.broadcasted_iota(jnp.int32, (BR, 128), 1)
    lse_ref[...] = jnp.zeros_like(lse_ref)
    carry_ref[...] = jnp.zeros_like(carry_ref)
    for b in range(nb):
        rows = pl.ds(b * BR, BR)
        q0 = x_ref[rows, 3 * w : 3 * w + HD] * 0.125
        pens = []
        for c in range(b + 1):
            cols = pl.ds(c * BR, BR)
            sp = softplus(mm(q0, x_ref[cols, 3 * w + HD : 3 * w + 2 * HD], NT))
            if c == b:
                keep = first > second
                if c == 0:
                    keep = jnp.logical_and(keep, second >= 1)
                sp = jnp.where(keep, sp, 0.0)
            elif c == 0:
                sp = jnp.where(second >= 1, sp, 0.0)
            hi, lo = halves(sp)
            pen = mm(tri, hi) + mm(tri, lo) + carry_ref[b : b + 1, cols]
            carry_ref[b + 1 : b + 2, cols] = pen[BR - 1 :] + sp[BR - 1 :]
            if c == b:
                pen = jnp.where(first >= second, pen, BIG)
            pens.append(pen)
        stats = jnp.zeros((BR, 128), jnp.float32)
        for h in range(nh):
            qh = x_ref[rows, h * HD : (h + 1) * HD] * 0.125
            scores = [
                mm(qh, x_ref[c * BR : (c + 1) * BR, w + h * HD : w + (h + 1) * HD], NT) - pens[c]
                for c in range(b + 1)
            ]
            top = scores[0]
            for s in scores[1:]:
                top = jnp.maximum(top, s)
            top = jnp.max(top, axis=1, keepdims=True)
            total = None
            acc = None
            for c in range(b + 1):
                e = jnp.exp(scores[c] - top)
                total = e if total is None else total + e
                part = mm(
                    e.astype(jnp.bfloat16),
                    x_ref[c * BR : (c + 1) * BR, 2 * w + h * HD : 2 * w + (h + 1) * HD],
                )
                acc = part if acc is None else acc + part
            total = jnp.sum(total, axis=1, keepdims=True)
            o_ref[rows, h * HD : (h + 1) * HD] = (acc / total).astype(jnp.bfloat16)
            stats = jnp.where(lanes == h, top + jnp.log(total), stats)
        lse_ref[:, rows] = jnp.transpose(stats)[:8]
        if done is not None:
            done(b)


def bwd_one(x_ref, g_ref, o_ref, lse_ref, carry_ref, d_ref, acc, kt):
    size = x_ref.shape[0]
    nh = (x_ref.shape[1] - 2 * HD) // (3 * HD)
    w = nh * HD
    nb = size // BR
    jj = lax.broadcasted_iota(jnp.int32, (BR, BR), 0)
    ii = lax.broadcasted_iota(jnp.int32, (BR, BR), 1)
    below = (jj < ii).astype(jnp.bfloat16)
    above = (jj > ii).astype(jnp.bfloat16)
    ones = jnp.ones((8, HD), jnp.bfloat16)
    for h in range(nh + 1):
        lo = 3 * w + HD if h == nh else w + h * HD
        kt[h, :, :size] = jnp.transpose(x_ref[:, lo : lo + HD].astype(jnp.float32)).astype(
            jnp.bfloat16
        )
    later = [None] * nb
    for b in reversed(range(nb)):
        rows = pl.ds(b * BR, BR)
        q0 = x_ref[rows, 3 * w : 3 * w + HD] * 0.125
        pens, sigs, sums = [], [], [None] * (b + 1)
        for c in range(b + 1):
            sel = mm(x_ref[c * BR : (c + 1) * BR, 3 * w + HD : 3 * w + 2 * HD], q0, NT)
            small = jnp.exp(-jnp.abs(sel))
            sp = jnp.maximum(sel, 0.0) + jnp.log(1.0 + small)
            sig = jnp.where(sel >= 0, 1.0, small) / (1.0 + small)
            if c == b or c == 0:
                keep = None
                if c == b:
                    keep = ii > jj
                if c == 0:
                    keep = jj >= 1 if keep is None else jnp.logical_and(keep, jj >= 1)
                sp = jnp.where(keep, sp, 0.0)
                sig = jnp.where(keep, sig, 0.0)
            hi, lo = halves(sp)
            start = jnp.transpose(
                jnp.broadcast_to(carry_ref[b : b + 1, c * BR : (c + 1) * BR], (128, BR))
            )
            pen = mm(hi, below) + mm(lo, below) + start[:, :1]
            if c == b:
                pen = jnp.where(ii >= jj, pen, BIG)
            pens.append(pen)
            sigs.append(sig)
        for h in range(nh):
            qh = x_ref[rows, h * HD : (h + 1) * HD] * 0.125
            gh = g_ref[rows, h * HD : (h + 1) * HD]
            prod = gh.astype(jnp.float32) * o_ref[rows, h * HD : (h + 1) * HD].astype(jnp.float32)
            phi, plo = halves(prod)
            delta = (mm(ones, phi, NT) + mm(ones, plo, NT))[:1]
            lse = lse_ref[h : h + 1, rows]
            dqt = None
            for c in range(b + 1):
                cols = pl.ds(c * BR, BR)
                s = mm(x_ref[cols, w + h * HD : w + (h + 1) * HD], qh, NT)
                p = jnp.exp((s - pens[c]) - lse)
                dp = mm(x_ref[cols, 2 * w + h * HD : 2 * w + (h + 1) * HD], gh, NT)
                ds = p * (dp - delta)
                low = ds.astype(jnp.bfloat16)
                dk = mm(low, qh)
                dv = mm(p.astype(jnp.bfloat16), gh)
                part = mm(kt[h, :, c * BR : (c + 1) * BR], low)
                dqt = part if dqt is None else dqt + part
                if b == nb - 1:
                    acc[h, cols] = dk
                    acc[nh + h, cols] = dv
                else:
                    acc[h, cols] += dk
                    acc[nh + h, cols] += dv
                sums[c] = ds if sums[c] is None else sums[c] + ds
            d_ref[rows, h * HD : (h + 1) * HD] = jnp.transpose(dqt * 0.125).astype(jnp.bfloat16)
        dqt = None
        for c in range(b + 1):
            cols = pl.ds(c * BR, BR)
            hi, lo = halves(sums[c])
            grad = mm(hi, above) + mm(lo, above)
            full = grad[:, :1] + sums[c][:, :1]
            if later[c] is not None:
                grad = grad + later[c]
                full = full + later[c]
            later[c] = full
            low = (-(grad * sigs[c])).astype(jnp.bfloat16)
            dk = mm(low, q0)
            part = mm(kt[nh, :, c * BR : (c + 1) * BR], low)
            dqt = part if dqt is None else dqt + part
            if b == nb - 1:
                acc[2 * nh, cols] = dk
            else:
                acc[2 * nh, cols] += dk
        d_ref[rows, 3 * w : 3 * w + HD] = jnp.transpose(dqt * 0.125).astype(jnp.bfloat16)
        own = pl.ds(b * BR, BR)
    for h in range(nh):
        d_ref[:, w + h * HD : w + (h + 1) * HD] = acc[h, :size].astype(jnp.bfloat16)
        d_ref[:, 2 * w + h * HD : 2 * w + (h + 1) * HD] = acc[nh + h, :size].astype(jnp.bfloat16)
    d_ref[:, 3 * w + HD : 3 * w + 2 * HD] = acc[2 * nh, :size].astype(jnp.bfloat16)


VMEM = pl.BlockSpec(memory_space=pltpu.VMEM)
LIMIT = 48 * 1024 * 1024


def attend_fwd(x):
    size, w = x.shape[0], (x.shape[1] - 2 * HD) // 3
    return pl.pallas_call(
        fwd_one,
        out_shape=(
            jax.ShapeDtypeStruct((size, w), jnp.bfloat16),
            jax.ShapeDtypeStruct((8, size), jnp.float32),
            jax.ShapeDtypeStruct((8, size), jnp.float32),
        ),
        in_specs=[VMEM],
        out_specs=(VMEM,) * 3,
        compiler_params=pltpu.CompilerParams(vmem_limit_bytes=LIMIT),
        cost_estimate=pl.CostEstimate(
            flops=size * size * 64 * 40, bytes_accessed=size * 2000, transcendentals=size * size * 3
        ),
        name="attend_fwd",
    )(x)


def attend_bwd(x, g, o, lse, carry):
    size, w = x.shape[0], (x.shape[1] - 2 * HD) // 3
    nh = w // HD
    return pl.pallas_call(
        bwd_one,
        out_shape=jax.ShapeDtypeStruct(x.shape, jnp.bfloat16),
        in_specs=[VMEM] * 5,
        out_specs=VMEM,
        scratch_shapes=[
            pltpu.VMEM((2 * nh + 1, size, HD), jnp.float32),
            pltpu.VMEM((nh + 1, HD, size), jnp.bfloat16),
        ],
        compiler_params=pltpu.CompilerParams(vmem_limit_bytes=LIMIT),
        cost_estimate=pl.CostEstimate(
            flops=size * size * 64 * 80, bytes_accessed=size * 4000, transcendentals=size * size * 3
        ),
        name="attend_bwd",
    )(x, g, o, lse, carry)


class Group:
    def __init__(self, core):
        self.core = core
        self.c = lax.axis_index(core)
        self.zl = lax.axis_index("zl")
        self.me = 2 * self.c + self.zl

    def peer(self, delta):
        return {self.core: self.c ^ (delta >> 1), "zl": self.zl ^ (delta & 1)}

    def member(self, m):
        return {self.core: m >> 1, "zl": m & 1}

    def greet(self, deltas):
        barrier = pltpu.get_barrier_semaphore()
        for delta in deltas:
            pl.semaphore_signal(
                barrier, inc=1, device_id=self.peer(delta), device_id_type=pl.DeviceIdType.MESH
            )
        pl.semaphore_wait(barrier, len(deltas))


def send(src, dst, ssem, rsem, device):
    return pltpu.make_async_remote_copy(
        src_ref=src,
        dst_ref=dst,
        send_sem=ssem,
        recv_sem=rsem,
        device_id=device,
        device_id_type=pl.DeviceIdType.MESH,
    )


def fwd_x(core, xl, xs, att, ol, os, lsel, lses, cl, cs, land, ssem, rsem):
    group = Group(core)
    nl, ns = xl.shape[0] // 4, xs.shape[0] // 4
    group.greet((1, 2, 3))

    def copy(k, m):
        src, n, at = ((ol, nl, 0), (os, ns, nl))[k]
        return send(
            src.at[pl.ds(m * n, n)],
            land.at[group.me, pl.ds(at, n)],
            ssem.at[k, m],
            rsem.at[k, group.me],
            group.member(m),
        )

    def arrived(k, m):
        src, n, at = ((ol, nl, 0), (os, ns, nl))[k]
        return send(
            src.at[pl.ds(0, n)], land.at[m, pl.ds(at, n)], ssem.at[k, m], rsem.at[k, m], group.member(m)
        )

    def start(k, m):
        src, n, at = ((ol, nl, 0), (os, ns, nl))[k]

        @pl.when(group.me != m)
        def _():
            copy(k, m).start()

        @pl.when(group.me == m)
        def _():
            land[m, at : at + n] = src[m * n : (m + 1) * n]

    def started(k, n):
        def done(b):
            for m in range(b * BR // n, (b + 1) * BR // n):
                start(k, m)

        return done

    fwd_one(xs, os, lses, cs, started(1, ns))
    fwd_one(xl, ol, lsel, cl, started(0, nl))
    w = ol.shape[1]
    for m in range(4):

        @pl.when(group.me != m)
        def _():
            for k in range(2):
                copy(k, m).wait_send()
                arrived(k, m).wait_recv()

    for m in range(4):
        att[:, m * w : (m + 1) * w] = land[m]


def bwd_x(core, xl, xs, go, ol, os, lsel, lses, cl, cs, dl, ds, acc, kt, out, gl, gs, ssem, rsem):
    group = Group(core)
    nl, ns = xl.shape[0] // 4, xs.shape[0] // 4
    w = ol.shape[1]
    for m in range(4):
        out[m] = go[:, m * w : (m + 1) * w]
    group.greet((1, 2, 3))

    def part(k):
        return ((gl, nl, 0), (gs, ns, nl))[k]

    def copy(k, m):
        dst, n, at = part(k)
        return send(
            out.at[m, pl.ds(at, n)],
            dst.at[pl.ds(pl.multiple_of(group.me * n, 16), n)],
            ssem.at[k, m],
            rsem.at[k, group.me],
            group.member(m),
        )

    def arrived(k, m):
        dst, n, at = part(k)
        return send(
            out.at[m, pl.ds(at, n)], dst.at[pl.ds(m * n, n)], ssem.at[k, m], rsem.at[k, m], group.member(m)
        )

    for k in (1, 0):
        for m in range(4):
            dst, n, at = part(k)

            @pl.when(group.me != m)
            def _():
                copy(k, m).start()

            @pl.when(group.me == m)
            def _():
                dst[m * n : (m + 1) * n] = out[m, at : at + n]

    for k in (1, 0):
        for m in range(4):

            @pl.when(group.me != m)
            def _():
                arrived(k, m).wait_recv()

        if k:
            bwd_one(xs, gs, os, lses, cs, ds, acc, kt)
        else:
            bwd_one(xl, gl, ol, lsel, cl, dl, acc, kt)
    for m in range(4):

        @pl.when(group.me != m)
        def _():
            for k in range(2):
                copy(k, m).wait_send()


def norm_rows(v):
    mean = jnp.mean(v, axis=-1, keepdims=True)
    cen = v - mean
    inv = lax.rsqrt(jnp.mean(cen * cen, axis=-1, keepdims=True) + 1e-05)
    return cen * inv, inv


def project_x(core, resid, gain, shift, w, bias, nl_ref, ns_ref, pl_ref, ps_ref, ssem, rsem):
    group = Group(core)
    nl, ns = nl_ref.shape[0] // 4, ns_ref.shape[0] // 4
    half = nl // 2
    parts = ((ns_ref, ps_ref, ns, 0, ns, nl), (nl_ref, pl_ref, nl, 0, half, 0), (nl_ref, pl_ref, nl, half, half, half))

    def rows(k, m):
        ref, _, n, at, size, _ = parts[k]
        return ref.at[pl.ds(pl.multiple_of(m * n + at, 16), size)]

    def copy(k, j, m, delta):
        return send(rows(k, m), rows(k, m), ssem.at[k, j], rsem.at[k, j], group.peer(delta))

    def compute(k, m):
        ref, out, n, at, size, _ = parts[k]
        here = pl.ds(pl.multiple_of(m * n + at, 16), size)
        out[here] = (mm(ref[here], w[...]) + bias[...]).astype(jnp.bfloat16)

    me = group.me
    for k in range(3):
        ref, _, n, at, size, src = parts[k]
        hat, _ = norm_rows(resid[src : src + size])
        ref[pl.ds(pl.multiple_of(me * n + at, 16), size)] = (hat * gain[...] + shift[...]).astype(
            jnp.bfloat16
        )
        if k == 0:
            group.greet((1, 2))
        copy(k, 0, me, 1).start()
        copy(k, 1, me, 2).start()
    for k in range(3):
        compute(k, me)
    for k in range(3):
        copy(k, 1, me ^ 2, 2).wait_recv()
        compute(k, me ^ 2)
    for k in range(3):
        copy(k, 0, me ^ 1, 1).wait_recv()
        copy(k, 2, me ^ 1, 2).start()
        compute(k, me ^ 1)
    for k in range(3):
        copy(k, 2, me ^ 3, 2).wait_recv()
        compute(k, me ^ 3)
    for k in range(3):
        copy(k, 0, me, 1).wait_send()
        copy(k, 1, me, 2).wait_send()
        copy(k, 2, me ^ 1, 2).wait_send()


def collect_x(core, dl, ds, w, resid, gain, gmid, g_ref, sums, mine, out, got, ssem, rsem):
    group = Group(core)
    nl, ns = dl.shape[0] // 4, ds.shape[0] // 4
    me = group.me

    def partial(m):
        a = mm(dl[pl.ds(pl.multiple_of(m * nl, 16), nl)], w[...], NT)
        b = mm(ds[pl.ds(pl.multiple_of(m * ns, 16), ns)], w[...], NT)
        return jnp.concatenate([a, b], axis=0)

    def copy(k, delta):
        return send(out.at[k], got.at[k], ssem.at[k], rsem.at[k], group.peer(delta))

    out[0] = partial(me ^ 3).astype(jnp.bfloat16)
    group.greet((1, 2))
    copy(0, 2).start()
    mine[...] = partial(me ^ 1)
    copy(0, 2).wait_recv()
    out[1] = (mine[...] + got[0].astype(jnp.float32)).astype(jnp.bfloat16)
    copy(1, 1).start()
    out[2] = partial(me ^ 2).astype(jnp.bfloat16)
    copy(2, 2).start()
    mine[...] = partial(me)
    hat, inv = norm_rows(resid[...])
    copy(2, 2).wait_recv()
    copy(1, 1).wait_recv()
    grad = mine[...] + got[2].astype(jnp.float32) + got[1].astype(jnp.float32)
    gh = grad * gain[...]
    a = jnp.mean(gh, axis=-1, keepdims=True)
    b = jnp.mean(gh * hat, axis=-1, keepdims=True)
    g_ref[...] = gmid[...] + inv * (gh - a - hat * b)
    sums[0:1] = jnp.sum(grad * hat, axis=0, keepdims=True)
    sums[1:2] = jnp.sum(grad, axis=0, keepdims=True)
    copy(0, 2).wait_send()
    copy(1, 1).wait_send()
    copy(2, 2).wait_send()


def shape(dims, dtype):
    return jax.ShapeDtypeStruct(tuple(dims), dtype)


def remote(kernel, core, outs, scratch, ident, name, args, flops=10**9):
    return pl.pallas_call(
        functools.partial(kernel, core),
        out_shape=tuple(outs),
        in_specs=[VMEM] * len(args),
        out_specs=(VMEM,) * len(outs),
        scratch_shapes=scratch,
        compiler_params=pltpu.CompilerParams(
            vmem_limit_bytes=LIMIT, collective_id=ident, has_side_effects=True
        ),
        cost_estimate=pl.CostEstimate(flops=flops, bytes_accessed=10**7, transcendentals=10**6),
        name=name,
    )(*args)


DMA = pltpu.SemaphoreType.DMA


def attend_fwd_x(core, xl, xs):
    w = (xl.shape[1] - 2 * HD) // 3
    rows = (xl.shape[0] + xs.shape[0]) // 4
    outs = [shape((rows, 4 * w), jnp.bfloat16)]
    outs += [shape((x.shape[0], w), jnp.bfloat16) for x in (xl, xs)]
    outs += [shape((8, x.shape[0]), jnp.float32) for x in (xl, xs)] * 2
    scratch = [pltpu.VMEM((4, rows, w), jnp.bfloat16), DMA((2, 4)), DMA((2, 4))]
    return remote(fwd_x, core, outs, scratch, 1, "attend_fwd_x", (xl, xs), 10**10)


def attend_bwd_x(core, xl, xs, go, ol, os, lsel, lses, cl, cs):
    w = ol.shape[1]
    nh = w // HD
    size = xl.shape[0]
    outs = [shape(x.shape, jnp.bfloat16) for x in (xl, xs)]
    scratch = [
        pltpu.VMEM((2 * nh + 1, size, HD), jnp.float32),
        pltpu.VMEM((nh + 1, HD, size), jnp.bfloat16),
        pltpu.VMEM((4, go.shape[0], w), jnp.bfloat16),
        pltpu.VMEM(ol.shape, jnp.bfloat16),
        pltpu.VMEM(os.shape, jnp.bfloat16),
        DMA((2, 4)),
        DMA((2, 4)),
    ]
    args = (xl, xs, go, ol, os, lsel, lses, cl, cs)
    return remote(bwd_x, core, outs, scratch, 2, "attend_bwd_x", args, 2 * 10**10)


def project(core, resid, gain, shift, w, bias, nl, ns):
    d, n = w.shape
    outs = [shape((4 * nl, d), jnp.bfloat16), shape((4 * ns, d), jnp.bfloat16)]
    outs += [shape((4 * nl, n), jnp.bfloat16), shape((4 * ns, n), jnp.bfloat16)]
    args = (resid, gain[None], shift[None], w, bias[None])
    return remote(project_x, core, outs, [DMA((3, 3)), DMA((3, 3))], 3, "project_x", args)


def collect(core, dl, ds, w, resid, gain, gmid):
    outs = [shape(resid.shape, jnp.float32), shape((8, w.shape[0]), jnp.float32)]
    scratch = [
        pltpu.VMEM(resid.shape, jnp.float32),
        pltpu.VMEM((3,) + resid.shape, jnp.bfloat16),
        pltpu.VMEM((3,) + resid.shape, jnp.bfloat16),
        DMA((3,)),
        DMA((3,)),
    ]
    return remote(collect_x, core, outs, scratch, 4, "collect_x", (dl, ds, w, resid, gain[None], gmid))


def total_x(axes, v, out, land, ssem, rsem):
    barrier = pltpu.get_barrier_semaphore()
    peers = [{ax: 1 - lax.axis_index(ax)} for ax in axes]
    for peer in peers:
        pl.semaphore_signal(barrier, inc=1, device_id=peer, device_id_type=pl.DeviceIdType.MESH)
    pl.semaphore_wait(barrier, len(peers))
    land[0] = v[...]
    n = len(axes)
    for i, peer in enumerate(peers):
        copy = send(land.at[i], land.at[n + 1 + i], ssem.at[i], rsem.at[i], peer)
        copy.start()
        copy.wait()
        land[i + 1] = land[i] + land[n + 1 + i]
    out[...] = land[n]


def total(axes, v):
    n = len(axes)
    scratch = [pltpu.VMEM((2 * n + 1,) + v.shape, jnp.float32), DMA((n,)), DMA((n,))]
    return remote(total_x, axes, [shape(v.shape, jnp.float32)], scratch, 5, "total_x", (v,))[0]


EPS = 1e-05
F32 = jnp.float32
BF = jnp.bfloat16


def swap(v, *axes):
    count = 2 ** len(axes)
    return lax.ppermute(
        v, axes if len(axes) > 1 else axes[0], [(i, count - 1 - i) for i in range(count)]
    )


def ordered(own, other, index, axis):
    return jnp.where(
        index == 0,
        jnp.concatenate([own, other], axis=axis),
        jnp.concatenate([other, own], axis=axis),
    )


def pick(v, index, axis):
    return lax.dynamic_index_in_dim(v, index, axis, keepdims=False)


def normalize(v, gain, shift):
    mean = jnp.mean(v, axis=-1, keepdims=True)
    cen = v - mean
    var = jnp.mean(cen * cen, axis=-1, keepdims=True)
    inv = lax.rsqrt(var + EPS)
    hat = cen * inv
    return hat * gain + shift, hat, inv


def normalize_back(grad, hat, inv, gain):
    gh = grad * gain
    a = jnp.mean(gh, axis=-1, keepdims=True)
    b = jnp.mean(gh * hat, axis=-1, keepdims=True)
    return inv * (gh - a - hat * b), jnp.sum(grad * hat, axis=0), jnp.sum(grad, axis=0)


def gelu_both(u):
    k = 0.7978845608028654
    inner = k * (u + 0.044715 * u * u * u)
    t = jnp.tanh(inner)
    act = 0.5 * u * (1.0 + t)
    slope = 0.5 * (1.0 + t) + 0.5 * u * (1.0 - t * t) * k * (1.0 + 3 * 0.044715 * u * u)
    return act, slope


def dot(a, b, ca=1, cb=0):
    return lax.dot_general(a, b, (((ca,), (cb,)), ((), ())), preferred_element_type=F32)


class Plan:
    def __init__(self, dims, dp, mp):
        self.dims, self.dp, self.mp = dims, dp, mp
        self.core = dims[-1]
        self.plane = dims[:-1]
        self.c = lax.axis_index(self.core)
        self.zh = lax.axis_index("zh")
        self.zl = lax.axis_index("zl")
        self.z = lax.axis_index(("zh", "zl"))
        self.d = lax.axis_index(dims)

    def relabel(self, v):
        got = lax.ppermute(v, (self.core, "zh"), [(1, 2), (2, 1)])
        return jnp.where(self.c == self.zh, v, got)

    def ring(self, v, step):
        n = self.mp
        return lax.ppermute(v, ("zh", "zl"), [(i, (i + step) % n) for i in range(n)])

    def gather(self, v):
        v = ordered(v, swap(v, "zl"), self.zl, 0)
        return ordered(v, swap(v, self.core), self.c, 0)

    def scatter(self, v):
        rows = v.shape[0] // 4
        v = v.reshape(2, 2, rows, v.shape[1])
        got = swap(pick(v, 1 - self.c, 0), self.core)
        mine = pick(v, self.c, 0).astype(F32) + got.astype(F32)
        got = swap(pick(mine, 1 - self.zl, 0).astype(BF), "zl")
        return pick(mine, self.zl, 0) + got.astype(F32)

    def to_rows(self, o):
        rows = o.shape[0] // 4
        o = o.reshape(2, 2, rows, o.shape[1])
        got = []
        for dc in range(2):
            line = []
            for dz in range(2):
                part = pick(pick(o, self.c ^ dc, 0), self.zl ^ dz, 0)
                axes = ((self.core,) if dc else ()) + (("zl",) if dz else ())
                line.append(swap(part, *axes) if axes else part)
            got.append(ordered(line[0], line[1], self.zl, 1))
        return ordered(got[0], got[1], self.c, 1)

    def to_heads(self, g):
        rows, w = g.shape[0], g.shape[1] // 4
        g = g.reshape(rows, 2, 2, w)
        got = []
        for dc in range(2):
            line = []
            for dz in range(2):
                part = pick(pick(g, self.c ^ dc, 1), self.zl ^ dz, 1)
                axes = ((self.core,) if dc else ()) + (("zl",) if dz else ())
                line.append(swap(part, *axes) if axes else part)
            got.append(ordered(line[0], line[1], self.zl, 0))
        return ordered(got[0], got[1], self.c, 0)

    def piece(self, w):
        rows = w.shape[0] // self.dp
        return lax.dynamic_slice_in_dim(w, self.d * rows, rows, 0)

    def ring_gather(self, v):
        parts = []
        for _ in range(self.mp - 1):
            v = self.ring(v, 1)
            parts.append(v)
        return parts

    def plane_gather(self, v, axes):
        k, rows, n = v.shape
        have = []
        shape = [k]
        for ax in axes:
            pos = sum(self.dims.index(h) < self.dims.index(ax) for h in have)
            got = swap(v, ax)
            cur = v.reshape(k, *([2] * len(have)), rows, n)
            oth = got.reshape(cur.shape)
            a = jnp.stack([cur, oth], axis=1 + pos)
            b = jnp.stack([oth, cur], axis=1 + pos)
            v = jnp.where(lax.axis_index(ax) == 0, a, b)
            have.append(ax)
            v = v.reshape(k, -1, rows, n).reshape(k, -1, n)
            rows_all = v.shape[1]
            v = v.reshape(k, rows_all, n)
        return v.reshape(k, self.dp, rows, n)

    def plane_scatter(self, g, axes):
        n = g.shape[1]
        left = [ax for ax in self.dims]
        rows = g.shape[0] // self.dp
        v = g.reshape(*([2] * len(left)), rows, n)
        for ax in axes:
            pos = left.index(ax)
            i = lax.axis_index(ax)
            got = swap(pick(v, 1 - i, pos), ax)
            v = (pick(v, i, pos).astype(F32) + got.astype(F32)).astype(BF)
            left.remove(ax)
        return v.reshape(-1, n)

    def ring_scatter(self, chunks):
        t = chunks[-1]
        for r in range(self.mp - 2, -1, -1):
            got = self.ring(t, -1)
            t = chunks[r].astype(F32) + got.astype(F32)
            if r:
                t = t.astype(BF)
        return t


def body(
    dims, dp, mp,
    x_long, x_short, dy_long, dy_short, ln_gain, ln_bias, w_qkv, b_qv, w_out, b_out, w_up, b_up, w_down, b_down, threshold,
):
    plan = Plan(dims, dp, mp)
    layers = w_qkv.shape[0]
    d_model = x_long.shape[-1]
    heads_w = w_qkv.shape[-1]
    ffq = w_up.shape[-1]
    rl, rs = x_long.shape[1], x_short.shape[1]
    rows = rl + rs
    core_rest = tuple(plan.plane)
    fwd_axes = core_rest + (plan.core,)
    alt_axes = core_rest[::-1] + (plan.core,)
    gain = ln_gain.astype(F32)
    shift = ln_bias.astype(F32)

    x = jnp.concatenate([x_long[0], x_short[0]], axis=0)
    x = plan.relabel(x)

    small = jnp.concatenate([b_up.reshape(-1), b_qv.reshape(-1)])
    rel_small = jnp.stack([small] + plan.ring_gather(small))
    n_up = layers * ffq
    rel_bup = rel_small[:, :n_up].reshape(mp, layers, ffq).astype(F32)
    rel_bqv = rel_small[:, n_up:].reshape(mp, layers, 2, heads_w).astype(F32)
    mine = 2 * plan.c + plan.zl
    my_bqv = pick(rel_bqv, (plan.z - mine) % mp, 0)
    zero_bq = pick(rel_bqv, plan.z % mp, 0)[:, 0, :HD]

    exts = []
    for l in range(layers):
        quarter = plan.relabel(w_qkv[l].reshape(d_model, 3 * heads_w))
        head0 = w_qkv[l][:, :2, :HD].reshape(d_model, 2 * HD)
        got = lax.ppermute(head0, "zl", [(0, 1)])
        head0 = jnp.where(plan.zl == 0, head0, got)
        got = lax.ppermute(head0, "zh", [(0, 1)])
        head0 = jnp.where(plan.zh == 0, head0, got)
        exts.append(jnp.concatenate([quarter, head0], axis=1))

    ups, downs, outs = [], [], []
    for l in range(layers):
        po = plan.piece(w_out[l])
        pu = jnp.concatenate([plan.piece(w_up[l]), po], axis=0)
        pd = plan.piece(w_down[l])
        n_out, n_d = po.shape[0], pd.shape[0]
        both = plan.ring_gather(jnp.concatenate([pu, pd], axis=0))
        stacked = jnp.stack(both)
        n_u = pu.shape[0]
        gu = plan.plane_gather(stacked[:, :n_u], fwd_axes)
        gd = plan.plane_gather(stacked[:, n_u:], alt_axes)
        up = gu[:, :, : n_u - n_out].reshape(mp - 1, d_model, ffq)
        ups.append(jnp.concatenate([w_up[l]] + [up[r] for r in range(mp - 1)], axis=1))
        out = gu[:, :, n_u - n_out :].reshape(mp - 1, heads_w, d_model)
        out = jnp.concatenate([w_out[l][None], out], axis=0)
        outs.append(
            jnp.concatenate([pick(out, (plan.z - q) % mp, 0) for q in range(mp)], axis=0)
        )
        downs.append(
            jnp.concatenate([w_down[l], gd.reshape((mp - 1) * ffq, d_model)], axis=0)
        )

    dy = plan.relabel(jnp.concatenate([dy_long[0], dy_short[0]], axis=0))

    limits = threshold.astype(F32) / 64.0
    resid = x.astype(F32)
    saved = []
    shares = []
    for l in range(layers):
        normed, hat1, inv1 = normalize(resid, gain[l, 0], shift[l, 0])
        normed = normed.astype(BF)
        full = [plan.gather(normed[:rl]), plan.gather(normed[rl:])]
        bias = jnp.concatenate(
            [
                my_bqv[l, 0],
                jnp.zeros((heads_w,), F32),
                my_bqv[l, 1],
                zero_bq[l],
                jnp.zeros((HD,), F32),
            ]
        )
        proj = [(dot(n, exts[l]) + bias).astype(BF) for n in full]
        att = [attend_fwd(p) for p in proj]
        share = jnp.zeros((), F32)
        for p, a in zip(proj, att):
            size = p.shape[0]
            sel = a[2][size // BR]
            left = (size - 1 - lax.broadcasted_iota(jnp.int32, (size,), 0)).astype(F32)
            share = share + jnp.sum(
                jax.nn.sigmoid(4.0 * (sel / jnp.maximum(left, 1.0) - limits[l]))
            )
        shares.append(share)
        attended = jnp.concatenate([plan.to_rows(a[0]) for a in att], axis=0)
        middle = resid + dot(attended, outs[l]) + b_out[l].astype(F32)
        normed2, hat2, inv2 = normalize(middle, gain[l, 1], shift[l, 1])
        normed2 = normed2.astype(BF)
        upper = dot(normed2, ups[l]) + rel_bup[:, l].reshape(-1)
        active = gelu_both(upper)[0].astype(BF)
        saved.append((resid, middle, full, proj, att, attended, normed2, upper, active))
        resid = middle + dot(active, downs[l]) + b_down[l].astype(F32)

    y = plan.relabel(resid.astype(BF))

    g = dy.astype(F32)
    vec = {}
    weight_grads = [None] * layers
    for l in reversed(range(layers)):
        resid, middle, full, proj, att, attended, normed2, upper, active = saved[l]
        g_bdown = jnp.sum(g, axis=0)
        gm = g.astype(BF)
        gact = dot(gm, downs[l], 1, 1)
        slope = gelu_both(upper)[1]
        gu = (slope * gact).astype(BF)
        w_down_t = dot(gm, active, 0, 0).astype(BF)
        w_up_g = dot(normed2, gu, 0, 0).astype(BF)
        g_bup = jnp.sum(gu.astype(F32), axis=0)
        gn2 = dot(gu, ups[l], 1, 1)
        _, hat2, inv2 = normalize(middle, gain[l, 1], shift[l, 1])
        back, g_gain2, g_shift2 = normalize_back(gn2, hat2, inv2, gain[l, 1])
        gmid = g + back
        g_bout = jnp.sum(gmid, axis=0)
        ga = gmid.astype(BF)
        go = dot(ga, outs[l], 1, 1).astype(BF)
        w_out_t = dot(ga, attended, 0, 0).astype(BF)
        gh = [plan.to_heads(go[:rl]), plan.to_heads(go[rl:])]
        dext = [attend_bwd(p, h, a[0], a[1], a[2]) for p, h, a in zip(proj, gh, att)]
        gn1 = jnp.concatenate(
            [plan.scatter(dot(e, exts[l], 1, 1).astype(BF)) for e in dext], axis=0
        )
        w_ext_g = sum(dot(n, e, 0, 0) for n, e in zip(full, dext)).astype(BF)
        g_bext = sum(jnp.sum(e.astype(F32), axis=0) for e in dext)
        _, hat1, inv1 = normalize(resid, gain[l, 0], shift[l, 0])
        back, g_gain1, g_shift1 = normalize_back(gn1, hat1, inv1, gain[l, 0])
        g = gmid + back

        w_up_g = plan.plane_scatter(w_up_g, (plan.core,) + core_rest)
        w_up_g = plan.ring_scatter([w_up_g[:, r * ffq : (r + 1) * ffq] for r in range(mp)])
        w_down_t = plan.plane_scatter(w_down_t, (plan.core,) + core_rest[::-1])
        w_down_t = plan.ring_scatter([w_down_t[:, r * ffq : (r + 1) * ffq] for r in range(mp)])
        w_out_t = plan.plane_scatter(w_out_t, (plan.core,) + core_rest)
        w_out_t = w_out_t.reshape(-1, mp, heads_w)
        w_out_t = plan.ring_scatter([pick(w_out_t, (plan.z - r) % mp, 1) for r in range(mp)])
        w_ext_g = plan.plane_scatter(w_ext_g, core_rest[::-1])
        w_ext_g = w_ext_g.reshape(2, -1, w_ext_g.shape[1])
        part, zero = w_ext_g[..., : 3 * heads_w], w_ext_g[..., 3 * heads_w :]
        got = lax.ppermute(part, (plan.core, "zh"), [(1, 0), (2, 3)])
        part = part.astype(F32) + got.astype(F32)
        got = lax.ppermute(
            pick(part, 1 - plan.c, 0).astype(BF), (plan.core, "zh"), [(0, 2), (3, 1)]
        )
        w_qkv_g = jnp.where(plan.c == plan.zh, pick(part, plan.c, 0), got.astype(F32))
        got = swap(pick(zero, 1 - plan.c, 0), plan.core)
        zero = (pick(zero, plan.c, 0).astype(F32) + got.astype(F32)).astype(BF)
        zero = zero.astype(F32) + swap(zero, "zl").astype(F32)
        zero = zero + swap(zero.astype(BF), "zh").astype(F32)
        zero = jnp.where(plan.z == 0, zero, 0.0)
        w_qkv_g = w_qkv_g.reshape(-1, 3, heads_w)
        zero = zero.reshape(-1, 2, HD)
        w_qkv_g = w_qkv_g + jnp.pad(zero, ((0, 0), (0, 1), (0, heads_w - HD)))
        weight_grads[l] = (w_qkv_g, jnp.transpose(w_out_t), w_up_g, jnp.transpose(w_down_t))

        hot = (lax.broadcasted_iota(jnp.int32, (mp, 1), 0) == mine).astype(F32)
        gq = hot * g_bext[None, :heads_w]
        gv = hot * g_bext[None, 2 * heads_w : 3 * heads_w]
        gq = gq.reshape(-1).at[:HD].add(g_bext[3 * heads_w : 3 * heads_w + HD])
        g_bup = g_bup.reshape(mp, ffq)
        g_bup = jnp.stack([pick(g_bup, (plan.z - q) % mp, 0) for q in range(mp)])
        vec[l] = jnp.concatenate(
            [
                g_gain1, g_gain2, g_shift1, g_shift2, g_bout, g_bdown,
                gq, gv.reshape(-1), g_bup.reshape(-1), jnp.full((128,), shares[l] / mp),
            ]
        )

    dx = plan.relabel(g.astype(BF)).astype(F32)
    total = lax.psum(jnp.stack([vec[l] for l in range(layers)]), dims + ("zh", "zl"))
    n = d_model
    g_gain = total[:, : 2 * n].reshape(layers, 2, n)
    g_bias = total[:, 2 * n : 4 * n].reshape(layers, 2, n)
    g_bout = total[:, 4 * n : 5 * n]
    g_bdown = total[:, 5 * n : 6 * n]
    at = 6 * n
    g_bqv = total[:, at : at + 2 * mp * heads_w].reshape(layers, 2, mp, heads_w)
    at += 2 * mp * heads_w
    g_bup = total[:, at : at + mp * ffq].reshape(layers, mp, ffq)
    at += mp * ffq
    key_share = total[:, at] / (dp * (rows * mp))
    return (
        y[None, :rl],
        y[None, rl:],
        dx[None, :rl],
        dx[None, rl:],
        g_gain,
        g_bias,
        jnp.stack([weight_grads[l][0] for l in range(layers)]),
        pick(g_bqv, plan.z, 2),
        jnp.stack([weight_grads[l][1] for l in range(layers)]),
        g_bout,
        jnp.stack([weight_grads[l][2] for l in range(layers)]),
        pick(g_bup, plan.z, 1),
        jnp.stack([weight_grads[l][3] for l in range(layers)]),
        g_bdown,
        key_share,
    )


MESH = pl.DeviceIdType.MESH
ANY = pl.BlockSpec(memory_space=pl.ANY)


class Net:
    def __init__(self, dims):
        self.dims = dims
        self.y, self.x, self.c = (lax.axis_index(ax) for ax in dims)
        self.zh, self.zl = lax.axis_index("zh"), lax.axis_index("zl")
        self.z = 2 * self.zh + self.zl
        self.yx = 2 * self.y + self.x
        self.me = 2 * self.c + self.zl
        self.moves = self.c != self.zh

    def group(self, delta):
        return {self.dims[2]: self.c ^ (delta >> 1), "zl": self.zl ^ (delta & 1)}

    def member(self, m):
        return {self.dims[2]: m >> 1, "zl": m & 1}

    def plane(self, e):
        return {self.dims[0]: self.y ^ (e >> 1), self.dims[1]: self.x ^ (e & 1)}

    def line(self, r):
        to = (self.z + r) % 4
        return {"zh": to // 2, "zl": to % 2}

    def partner(self):
        return {self.dims[2]: 1 - self.c, "zh": 1 - self.zh}

    def greet(self, peers):
        barrier = pltpu.get_barrier_semaphore()
        for peer in peers:
            pl.semaphore_signal(barrier, inc=1, device_id=peer, device_id_type=MESH)
        pl.semaphore_wait(barrier, len(peers))


class Sems:
    def __init__(self, ssem, rsem):
        self.ssem, self.rsem, self.used = ssem, rsem, 0

    def copy(self, src, dst, device):
        i = self.used
        self.used += 1
        return send(src, dst, self.ssem.at[i], self.rsem.at[i], device)


class Batch:
    def __init__(self, copies, when=None):
        self.copies, self.when = copies, when

    def _do(self, f):
        if self.when is None:
            f()
        else:
            pl.when(self.when)(f)

    def start(self):
        self._do(lambda: [c.start() for c in self.copies] and None)

    def recv(self):
        self._do(lambda: [c.wait_recv() for c in self.copies] and None)

    def sent(self):
        self._do(lambda: [c.wait_send() for c in self.copies] and None)

    def end(self):
        self.recv()
        self.sent()


def aligned(v, n=16):
    return pl.multiple_of(v, n)


class Projections:
    def __init__(self, net, sems, wq, w0, qland, zland, ext):
        self.net, self.wq, self.w0, self.qland, self.zland, self.ext = net, wq, w0, qland, zland, ext
        rows = qland.shape[1]
        here = pl.ds(aligned(net.yx * rows), rows)
        at = net.yx
        self.q1 = Batch([sems.copy(wq.at[here], qland.at[at], net.partner())], net.moves)
        self.q2 = Batch([sems.copy(qland.at[at], qland.at[at], net.plane(e)) for e in (1, 2, 3)], net.moves)
        self.h1 = []
        for r in (1, 2, 3):
            copy = sems.copy(w0.at[here], zland.at[at], net.line(r))
            self.h1.append(copy)
        self.h2 = Batch([sems.copy(zland.at[at], zland.at[at], net.plane(e)) for e in (1, 2, 3)], net.z != 0)

    def start(self):
        self.q1.start()

        @pl.when(self.net.z == 0)
        def _():
            for copy in self.h1:
                copy.start()

    def forward(self):
        self.q1.recv()
        self.q2.start()
        for r in (1, 2, 3):
            pl.when(self.net.z == r)(lambda: self.h1[r - 1].wait_recv())
        self.h2.start()

    def finish(self):
        rows, n = self.qland.shape[1:]
        self.q2.recv()
        self.h2.recv()

        @pl.when(self.net.moves)
        def _():
            for k in range(4):
                self.ext[k * rows : (k + 1) * rows, :n] = self.qland[k]

        @pl.when(jnp.logical_not(self.net.moves))
        def _():
            self.ext[:, :n] = self.wq[...]

        @pl.when(self.net.z != 0)
        def _():
            for k in range(4):
                self.ext[k * rows : (k + 1) * rows, n:] = self.zland[k]

        @pl.when(self.net.z == 0)
        def _():
            self.ext[:, n:] = self.w0[...]

        self.q1.sent()
        self.q2.sent()
        self.h2.sent()

        @pl.when(self.net.z == 0)
        def _():
            for copy in self.h1:
                copy.wait_send()


def project_part(net, sems, resid, gain, shift, w, bias, fl, fs, pj_l, pj_s):
    nl, ns = fl.shape[0] // 4, fs.shape[0] // 4
    half = nl // 2
    parts = ((fs, pj_s, ns, 0, ns, nl), (fl, pj_l, nl, 0, half, 0), (fl, pj_l, nl, half, half, half))
    me = net.me

    def rows(k, m):
        ref, _, n, at, size, _ = parts[k]
        return ref.at[pl.ds(aligned(m * n + at), size)]

    def compute(k, m):
        ref, out, n, at, size, _ = parts[k]
        here = pl.ds(aligned(m * n + at), size)
        out[here] = (mm(ref[here], w[...]) + bias[...]).astype(jnp.bfloat16)

    chip = [sems.copy(rows(k, me), rows(k, me), net.group(1)) for k in range(3)]
    core = [sems.copy(rows(k, me), rows(k, me), net.group(2)) for k in range(3)]
    over = [sems.copy(rows(k, me ^ 1), rows(k, me ^ 1), net.group(2)) for k in range(3)]
    for k in range(3):
        ref, _, n, at, size, src = parts[k]
        hat, _ = norm_rows(resid[src : src + size].astype(jnp.float32))
        ref[pl.ds(aligned(me * n + at), size)] = (hat * gain[...] + shift[...]).astype(jnp.bfloat16)
        chip[k].start()
        core[k].start()
    for k in range(3):
        compute(k, me)
    for k in range(3):
        core[k].wait_recv()
        compute(k, me ^ 2)
    for k in range(3):
        chip[k].wait_recv()
        over[k].start()
        compute(k, me ^ 1)
    for k in range(3):
        over[k].wait_recv()
        compute(k, me ^ 3)
    return chip + core + over


def attend_part(net, sems, xl, xs, att, ol, os, lsel, lses, cl, cs, land):
    nl, ns = xl.shape[0] // 4, xs.shape[0] // 4
    w = ol.shape[1]
    base = sems.used
    sems.used += 8

    def part(k):
        return ((ol, nl, 0), (os, ns, nl))[k]

    def copy(k, m):
        src, n, at = part(k)
        return send(
            src.at[pl.ds(m * n, n)],
            land.at[net.me, pl.ds(at, n)],
            sems.ssem.at[base + 4 * k + m],
            sems.rsem.at[base + 4 * k + net.me],
            net.member(m),
        )

    def arrived(k, m):
        src, n, at = part(k)
        i = base + 4 * k + m
        return send(src.at[pl.ds(0, n)], land.at[m, pl.ds(at, n)], sems.ssem.at[i], sems.rsem.at[i], net.member(m))

    def start(k, m):
        src, n, at = part(k)

        @pl.when(net.me != m)
        def _():
            copy(k, m).start()

        @pl.when(net.me == m)
        def _():
            land[m, at : at + n] = src[m * n : (m + 1) * n]

    def started(k, n):
        def done(b):
            for m in range(b * BR // n, (b + 1) * BR // n):
                start(k, m)

        return done

    fwd_one(xs, os, lses, cs, started(1, ns))
    fwd_one(xl, ol, lsel, cl, started(0, nl))
    for m in range(4):

        @pl.when(net.me != m)
        def _():
            for k in range(2):
                copy(k, m).wait_send()
                arrived(k, m).wait_recv()

    for m in range(4):
        att[:, m * w : (m + 1) * w] = land[m]


def gelu_pair(u):
    k = 0.7978845608028654
    sq = u * u
    t = jnp.tanh(u * (k + k * 0.044715 * sq))
    h = 0.5 * (1.0 + t)
    act = u * h
    slope = h + act * (1.0 - t) * (k + 3 * k * 0.044715 * sq)
    return act, slope


TN = (((0,), (0,)), ((), ()))


def ext_scatter(net, sems, dw, land):
    return [sems.copy(dw.at[net.yx ^ e], land.at[e - 1], net.plane(e)) for e in (1, 2, 3)]


class FinishLine:
    def __init__(self, net, sems, s, so, land, oland, own=None):
        self.own = s.at[0] if own is None else own
        self.net, self.s, self.so, self.land, self.oland = net, s, so, land, oland
        self.main = Batch([sems.copy(s.at[r], land.at[3 - r], net.line(r)) for r in (1, 2, 3)])
        self.out = []
        for r in (1, 2, 3):
            to = (net.z + r) % 4
            copy = sems.copy(so.at[to % 2], oland.at[3 - r], net.line(r))
            self.out.append((copy, to // 2 == net.c))
        self.owner = net.zh == net.c

    def start(self):
        self.main.start()
        for copy, use in self.out:
            pl.when(use)(copy.start)

    def finish(self, f_out, fo_out):
        self.main.recv()
        f_out[...] = (
            self.own[...].astype(jnp.float32)
            + self.land[0].astype(jnp.float32)
            + self.land[1].astype(jnp.float32)
            + self.land[2].astype(jnp.float32)
        ).astype(f_out.dtype)

        @pl.when(self.owner)
        def _():
            for copy, _ in self.out:
                copy.wait_recv()
            fo_out[...] = (
                self.so[self.net.zl].astype(jnp.float32)
                + self.oland[0].astype(jnp.float32)
                + self.oland[1].astype(jnp.float32)
                + self.oland[2].astype(jnp.float32)
            ).astype(fo_out.dtype)

        @pl.when(jnp.logical_not(self.owner))
        def _():
            fo_out[...] = jnp.zeros_like(fo_out)

        self.main.sent()
        for copy, use in self.out:
            pl.when(use)(copy.wait_send)


class Local:
    def __init__(self, sem):
        self.sem, self.copies = sem, []

    def start(self, src, dst):
        copy = pltpu.make_async_copy(src, dst, self.sem.at[len(self.copies)])
        self.copies.append(copy)
        copy.start()
        return copy


def z_weights(net, sems, layer, w_up, w_down, zup, zdn):
    rows, n = zup.shape[0], zup.shape[1] // 3
    part = zdn.shape[1]
    out = []
    for r in (1, 2, 3):
        dev, slot = net.line(r), 3 - r
        src = w_up.at[layer, pl.ds(aligned(net.yx * rows), rows), pl.ds(aligned(net.c * n, 128), n)]
        out.append(sems.copy(src, zup.at[:, pl.ds(slot * n, n)], dev))
        src = w_down.at[layer, pl.ds(aligned(net.c * n + net.yx * part), part)]
        out.append(sems.copy(src, zdn.at[slot], dev))
    return Batch(out)


def plane_weights(net, sems, zup, zdn, wup, wdn):
    rows, n = zup.shape[0], zup.shape[1] // 3
    part = zdn.shape[1]
    at_up = pl.ds(aligned(net.yx * rows), rows)
    at_dn = pl.ds(aligned(net.yx * part), part)
    out = []
    for e in (1, 2, 3):
        out.append(sems.copy(zup, wup.at[at_up, pl.ds(n, 3 * n)], net.plane(e)))
        out.append(sems.copy(zdn, wdn.at[pl.ds(1, 3), at_dn], net.plane(e)))
    return Batch(out)


def first_x(dims, R):
    net, sems = Net(dims), Sems(R.ssem, R.rsem)
    nl = R.xl.shape[0]
    moved = Batch(
        [
            sems.copy(R.xl, R.xr.at[pl.ds(0, nl)], net.partner()),
            sems.copy(R.xs, R.xr.at[pl.ds(nl, R.xs.shape[0])], net.partner()),
        ],
        net.moves,
    )
    proj = Projections(net, sems, R.wq, R.w0, R.qland, R.zland, R.ext)
    tiny = Batch([sems.copy(R.small, R.smalls.at[4 - r], net.line(r)) for r in (1, 2, 3)])
    weights = z_weights(net, sems, 0, R.w_up, R.w_down, R.zup, R.zdn)
    net.greet([net.partner()] + [net.line(r) for r in (1, 2, 3)] + [net.plane(e) for e in (1, 2, 3)])
    proj.start()
    moved.start()
    tiny.start()
    weights.start()
    R.smalls[0] = R.small[...]

    @pl.when(jnp.logical_not(net.moves))
    def _():
        R.xr[:nl] = R.xl[...]
        R.xr[nl:] = R.xs[...]

    proj.forward()
    proj.finish()
    moved.end()
    tiny.end()
    weights.end()


def forward_x(dims, first, last, R):
    net, sems, loc = Net(dims), Sems(R.ssem, R.rsem), Local(R.lsem)
    n, d = R.resid.shape
    f = R.own_up.shape[1]
    weights = plane_weights(net, sems, R.zup, R.zdn, R.wup, R.wdn)
    peers = [net.group(2), net.group(3), net.partner()]
    peers += [net.plane(e) for e in (1, 2, 3)] + [net.line(r) for r in (1, 2, 3)]
    if first:
        proj = Projections(net, sems, R.wq, R.w0, R.qland, R.zland, R.ext_next)
        later = z_weights(net, sems, 1, R.w_up, R.w_down, R.zup_next, R.zdn_next)
    else:
        nl = R.dl.shape[0]
        moved = Batch(
            [
                sems.copy(R.dl, R.dyr.at[pl.ds(0, nl)], net.partner()),
                sems.copy(R.ds, R.dyr.at[pl.ds(nl, R.ds.shape[0])], net.partner()),
            ],
            net.moves,
        )
    there = sems.copy(R.n2.at[pl.ds(0, n)], R.n2.at[pl.ds(n, n)], net.group(2))
    back = sems.copy(R.out, R.got, net.group(2))
    net.greet(peers)
    weights.start()
    pending = project_part(
        net, sems, R.resid, R.gain1, R.shift1, R.ext, R.bias, R.fl, R.fs, R.pj_l, R.pj_s
    )
    if first:
        proj.start()
    else:
        moved.start()

        @pl.when(jnp.logical_not(net.moves))
        def _():
            R.dyr[:nl] = R.dl[...]
            R.dyr[nl:] = R.ds[...]

    for src, dst in ((R.fl, R.fl_o), (R.fs, R.fs_o), (R.pj_l, R.pjl_o), (R.pj_s, R.pjs_o)):
        loc.start(src, dst)
    R.wup[:, :f] = R.own_up[...]
    R.wdn[0] = R.own_dn[...]
    rows, part = R.zup.shape[0], R.zdn.shape[1]
    R.wup[pl.ds(aligned(net.yx * rows), rows), f:] = R.zup[...]
    for k in range(3):
        R.wdn[k + 1, pl.ds(aligned(net.yx * part), part)] = R.zdn[k]
    if first:
        later.start()
    attend_part(
        net, sems, R.pj_l, R.pj_s, R.att, R.ol, R.os, R.lsel, R.lses, R.cl, R.cs, R.land
    )
    if first:
        proj.forward()
    share = jnp.zeros((1, 1), jnp.float32)
    for carry in (R.cl, R.cs):
        size = carry.shape[1]
        left = (size - 1 - lax.broadcasted_iota(jnp.int32, (1, size), 1)).astype(jnp.float32)
        ratio = carry[size // BR : size // BR + 1] / jnp.maximum(left, 1.0)
        t = 4.0 * (ratio - R.limit[:1, :1])
        share = share + jnp.sum(1.0 / (1.0 + jnp.exp(-t)), axis=1, keepdims=True)
    R.share[...] = jnp.broadcast_to(share * 0.25, R.share.shape)
    half = n // 2
    for i in range(2):
        at = slice(i * half, (i + 1) * half)
        R.middle[at] = R.resid[at].astype(jnp.float32) + mm(R.att[at], R.wout[...]) + R.bout[...]
        hat, _ = norm_rows(R.middle[at])
        R.n2[at] = (hat * R.gain2[...] + R.shift2[...]).astype(jnp.bfloat16)
    there.start()
    weights.recv()
    for src, dst in ((R.wup, R.wup_o), (R.wdn, R.wdn_o)):
        loc.start(src, dst)

    def hidden(at):
        u = mm(R.n2[at], R.wup[...]) + R.bup[...]
        a, s = gelu_pair(u)
        low = a.astype(jnp.bfloat16)
        for i in range(2):
            R.act[i, at] = low[:, 2 * i * f : 2 * (i + 1) * f]
            loc.start(R.act.at[i, at], R.act_o.at[i, at])
        R.slope[at] = s.astype(jnp.bfloat16)
        loc.start(R.slope.at[at], R.slope_o.at[at])

    def down(at):
        return mm(R.act[0, at], R.wdn[0:2].reshape(2 * f, d)) + mm(
            R.act[1, at], R.wdn[2:4].reshape(2 * f, d)
        )

    quarter = n // 2
    for i in range(2):
        hidden(slice(i * quarter, (i + 1) * quarter))
    there.wait_recv()
    for i in range(2):
        hidden(slice(n + i * quarter, n + (i + 1) * quarter))
    for i in range(2):
        R.out[i * half : (i + 1) * half] = down(slice(n + i * half, n + (i + 1) * half)).astype(
            jnp.bfloat16
        )
    back.start()
    for i in range(2):
        at = slice(i * half, (i + 1) * half)
        R.new[at] = R.middle[at] + down(at) + R.bdown[...]
    back.wait_recv()
    R.new[...] += R.got[...].astype(jnp.float32)
    if last:
        R.y[...] = R.new[...].astype(jnp.bfloat16)
    there.wait_send()
    back.wait_send()
    for copy in pending:
        copy.wait_send()
    weights.sent()
    if first:
        proj.finish()
        later.end()
    else:
        moved.end()
    for copy in loc.copies:
        copy.wait()


def backward_x(dims, last, R):
    net, sems, loc = Net(dims), Sems(R.ssem, R.rsem), Local(R.lsem)
    f32, bf = jnp.float32, jnp.bfloat16
    n, d = R.g.shape
    f = R.wup.shape[1] // 4
    nl, ns = R.pj_l.shape[0] // 4, R.pj_s.shape[0] // 4
    wid = R.ol.shape[1]
    me, yx = net.me, net.yx
    there = sems.copy(R.gm.at[pl.ds(0, n)], R.gm.at[pl.ds(n, n)], net.group(2))
    back = sems.copy(R.out.at[0], R.got.at[0], net.group(2))
    cross = sems.copy(R.oself, R.olands, net.group(2))
    big_dn = Batch([sems.copy(R.ddn.at[yx ^ e], R.rdn.at[e - 1], net.plane(e)) for e in (1, 2, 3)])
    big_up = Batch(
        [sems.copy(R.dup.at[yx ^ e], R.rup.at[e - 1], net.plane(e)) for e in (1, 2, 3)]
        + [sems.copy(R.dout.at[yx ^ e], R.rout.at[e - 1], net.plane(e)) for e in (1, 2, 3)]
    )
    base = sems.used
    sems.used += 8
    peers = [net.group(d_) for d_ in (1, 2, 3)] + [net.plane(e) for e in (1, 2, 3)]
    if last:
        moved = Batch([sems.copy(R.y, R.yr, net.partner())], net.moves)
        peers += [net.partner()]
    else:
        carry = FinishLine(net, sems, R.s_in, R.so_in, R.fland, R.foland, R.s_own)
        ext = Batch(ext_scatter(net, sems, R.dq_in, R.qland) + ext_scatter(net, sems, R.d0_in, R.zland))
        peers += [net.line(2), net.line(4 - net.zl * 2 - 1)]
    R.gm[:n] = R.g[...].astype(bf)
    net.greet(peers)
    there.start()
    fetched = [loc.start(R.act.at[i], R.buf.at[pl.ds(i * 2 * n, 2 * n)]) for i in range(2)]
    for src, dst in ((R.pjl_i, R.pj_l), (R.pjs_i, R.pj_s), (R.ext_i, R.ext)):
        loc.start(src, dst)
    if last:
        moved.start()

        @pl.when(jnp.logical_not(net.moves))
        def _():
            R.yr[...] = R.y[...]

    else:
        ext.start()
        carry.start()
        for src, dst in ((R.s_in.at[0], R.s_own), (R.dq_in.at[yx], R.dq_own), (R.d0_in.at[yx], R.d0_own)):
            loc.start(src, dst)
    R.rows[...] = jnp.zeros_like(R.rows)
    R.rows[5:6] = jnp.sum(R.g[...].astype(f32), axis=0, keepdims=True)
    half = n // 2
    wdn2 = lambda: R.wdn[...].reshape(4 * f, d)

    def hidden(at):
        u = mm(R.gm[at], wdn2(), NT)
        R.gu[at] = (u * R.slope[at].astype(f32)).astype(bf)

    for i in range(2):
        hidden(slice(i * half, (i + 1) * half))
    there.wait_recv()
    for i in range(2):
        hidden(slice(n + i * half, n + (i + 1) * half))
    for i in range(2):
        R.out[0, i * half : (i + 1) * half] = mm(
            R.gu[n + i * half : n + (i + 1) * half], R.wup[...], NT
        ).astype(bf)
    back.start()
    for i in range(2):
        R.mine[i * half : (i + 1) * half] = mm(R.gu[i * half : (i + 1) * half], R.wup[...], NT)
    chunk = d // 4

    for c in fetched:
        c.wait()
    for k in range(4):
        for i in range(2):
            t = mm(R.gm[:, k * chunk : (k + 1) * chunk], R.buf[i * 2 * n : (i + 1) * 2 * n], TN)
            t = t.astype(bf)
            R.ddn[k, 2 * i] = t[:, :f]
            R.ddn[k, 2 * i + 1] = t[:, f:]
    big_dn.start()
    fl, fs = R.buf.at[pl.ds(0, 4 * nl)], R.buf.at[pl.ds(4 * nl, 4 * ns)]
    late = [loc.start(R.fl_i, fl), loc.start(R.fs_i, fs)]
    back.wait_recv()
    gn = R.mine[...] + R.got[0].astype(f32)
    hat, inv = norm_rows(R.middle[...])
    gh = gn * R.gain2[...]
    a = jnp.mean(gh, axis=-1, keepdims=True)
    b = jnp.mean(gh * hat, axis=-1, keepdims=True)
    R.gmid[...] = R.g[...].astype(f32) + inv * (gh - a - hat * b)
    R.rows[1:2] = jnp.sum(gn * hat, axis=0, keepdims=True)
    R.rows[3:4] = jnp.sum(gn, axis=0, keepdims=True)
    R.rows[4:5] = jnp.sum(R.gmid[...], axis=0, keepdims=True)
    R.ga[...] = R.gmid[...].astype(bf)
    go = mm(R.ga[...], R.wout[...], NT).astype(bf)
    for m in range(4):
        R.outg[m] = go[:, m * wid : (m + 1) * wid]

    def part(k):
        return ((R.gl, nl, 0), (R.gs, ns, nl))[k]

    def copy(k, m):
        dst, size, at = part(k)
        return send(
            R.outg.at[m, pl.ds(at, size)],
            dst.at[pl.ds(aligned(me * size), size)],
            sems.ssem.at[base + 4 * k + m],
            sems.rsem.at[base + 4 * k + me],
            net.member(m),
        )

    def arrived(k, m):
        dst, size, at = part(k)
        i = base + 4 * k + m
        return send(
            R.outg.at[m, pl.ds(at, size)], dst.at[pl.ds(m * size, size)], sems.ssem.at[i], sems.rsem.at[i], net.member(m)
        )

    for k in (1, 0):
        for m in range(4):
            dst, size, at = part(k)

            @pl.when(me != m)
            def _():
                copy(k, m).start()

            @pl.when(me == m)
            def _():
                dst[m * size : (m + 1) * size] = R.outg[m, at : at + size]

    e = R.att.shape[1] // 2
    other = R.att[:, pl.ds(aligned((1 - net.c) * e, 128), e)]
    R.oself[...] = mm(R.ga[...], other, TN).astype(bf)
    cross.start()
    for k in range(4):
        t = mm(R.n2[:, k * chunk : (k + 1) * chunk], R.gu[...], TN).astype(bf)
        for r in range(4):
            R.dup[k, r] = t[:, r * f : (r + 1) * f]
    bup = jnp.sum(R.gu[...].astype(f32), axis=0, keepdims=True)
    for c in range(2):

        @pl.when(net.c == c)
        def _():
            for r in range(4):
                R.rows[pl.ds(16 + (net.z + r) % 4, 1), c * f : (c + 1) * f] = bup[:, r * f : (r + 1) * f]

    own = mm(R.ga[...], R.att[:, pl.ds(aligned(net.c * e, 128), e)], TN)
    cross.wait_recv()
    own = (own + R.olands[...].astype(f32)).astype(bf)
    for k in range(4):
        R.dout[k] = own[k * chunk : (k + 1) * chunk]
    big_up.start()
    done = [id(c) for c in fetched + late]
    for c in loc.copies:
        if id(c) not in done:
            c.wait()
    for k in (1, 0):
        for m in range(4):

            @pl.when(me != m)
            def _():
                arrived(k, m).wait_recv()

        if k:
            bwd_one(R.pj_s, R.gs, R.os, R.lses, R.cs, R.ds, R.acc, R.kt)
        else:
            bwd_one(R.pj_l, R.gl, R.ol, R.lsel, R.cl, R.dl, R.acc, R.kt)

    def partial(m):
        a = mm(R.dl[pl.ds(aligned(m * nl), nl)], R.ext[...], NT)
        b = mm(R.ds[pl.ds(aligned(m * ns), ns)], R.ext[...], NT)
        return jnp.concatenate([a, b], axis=0)

    back.wait_send()
    to_core = [sems.copy(R.out.at[k], R.got.at[k + 1], net.group(2)) for k in (0, 1)]
    to_chip = sems.copy(R.out.at[2], R.got.at[3], net.group(1))
    R.out[0] = partial(me ^ 3).astype(bf)
    to_core[0].start()
    R.mine[...] = partial(me ^ 1)
    to_core[0].wait_recv()
    R.out[2] = (R.mine[...] + R.got[1].astype(f32)).astype(bf)
    to_chip.start()
    R.out[1] = partial(me ^ 2).astype(bf)
    to_core[1].start()
    R.mine[...] = partial(me)
    nq = R.dq.shape[2]
    for c in late:
        c.wait()
    for k in range(4):
        at = slice(k * chunk, (k + 1) * chunk)
        both = mm(fl[:, at], R.dl[...], TN) + mm(fs[:, at], R.ds[...], TN)
        R.dq[k] = both[:, :nq].astype(bf)
        R.d0[k] = both[:, nq:].astype(bf)
    bsum = jnp.sum(R.dl[...].astype(f32), axis=0, keepdims=True) + jnp.sum(
        R.ds[...].astype(f32), axis=0, keepdims=True
    )
    R.rows[pl.ds(8 + me, 1), :wid] = bsum[:, :wid]
    R.rows[pl.ds(12 + me, 1), :wid] = bsum[:, 2 * wid : 3 * wid]
    R.rows[8:9, :HD] += bsum[:, nq : nq + HD]
    hat, inv = norm_rows(R.resid[...].astype(f32))
    to_core[1].wait_recv()
    to_chip.wait_recv()
    grad = R.mine[...] + R.got[2].astype(f32) + R.got[3].astype(f32)
    gh = grad * R.gain1[...]
    a = jnp.mean(gh, axis=-1, keepdims=True)
    b = jnp.mean(gh * hat, axis=-1, keepdims=True)
    R.g_new[...] = (R.gmid[...] + inv * (gh - a - hat * b)).astype(R.g_new.dtype)
    R.rows[0:1] = jnp.sum(grad * hat, axis=0, keepdims=True)
    R.rows[2:3] = jnp.sum(grad, axis=0, keepdims=True)
    for c in to_core + [to_chip, there, cross]:
        c.wait_send()
    for m in range(4):

        @pl.when(me != m)
        def _():
            for k in range(2):
                copy(k, m).wait_send()

    if last:
        moved.end()
    else:
        ext.recv()
        for own, lands, dst in ((R.dq_own, R.qland, R.q_out), (R.d0_own, R.zland, R.z_out)):
            t = own[...].astype(f32)
            for i in range(3):
                t = t + lands[i].astype(f32)
            dst[...] = t.astype(bf)
        carry.finish(R.f_out, R.fo_out)
        ext.sent()

    def add_up(own, land, i):
        for r in range(4):
            t = own[yx, r].astype(f32)
            for k in range(3):
                t = t + land[k, r].astype(f32)
            R.s[r, i] = t.astype(bf)

    big_dn.recv()
    add_up(R.ddn, R.rdn, 1)
    big_up.recv()
    add_up(R.dup, R.rup, 0)
    t = R.dout[yx].astype(f32)
    for k in range(3):
        t = t + R.rout[k].astype(f32)
    for i in range(2):
        R.so[i] = t[:, i * wid : (i + 1) * wid].astype(bf)
    big_dn.sent()
    big_up.sent()


def tail_x(axes, R):
    dims = axes[:-2]
    net, sems = Net(dims), Sems(R.ssem, R.rsem)
    f32, bf = jnp.float32, jnp.bfloat16
    moved = Batch([sems.copy(R.dx, R.dxr, net.partner())], net.moves)
    line = FinishLine(net, sems, R.s, R.so, R.land, R.oland)
    ext = Batch(ext_scatter(net, sems, R.dq, R.qland) + ext_scatter(net, sems, R.d0, R.zland))
    nv = len(axes)
    rounds = [{ax: 1 - lax.axis_index(ax)} for ax in axes]
    steps = [sems.copy(R.vland.at[i], R.vland.at[nv + 1 + i], peer) for i, peer in enumerate(rounds)]
    qsend = Batch([sems.copy(R.qs, R.qline, net.line(2))], net.moves)
    qrecv = jnp.logical_not(net.moves)
    zsend = [sems.copy(R.zs, R.zline.at[r - 1], net.line(r)) for r in (1, 2, 3)]
    cross = Batch(
        [sems.copy(R.fself, R.fland, net.group(2)), sems.copy(R.zself, R.zlands, net.group(2))]
    )
    owned = Batch(
        [sems.copy(R.oself, R.olands, net.group(2)), sems.copy(R.qself, R.qlands, net.group(2))],
        None,
    )
    net.greet(
        [net.partner(), net.group(2)]
        + [net.line(r) for r in (1, 2, 3)]
        + [net.plane(e) for e in (1, 2, 3)]
    )
    ext.start()
    line.start()
    moved.start()
    nr = R.rows0.shape[0]
    R.vland[0, :nr] = R.rows0[...]
    R.vland[0, nr:] = R.rows1[...]
    R.vland[0, 6:7] = jnp.broadcast_to(R.share0[:1, :1], (1, R.rows0.shape[1]))
    R.vland[0, nr + 6 : nr + 7] = jnp.broadcast_to(R.share1[:1, :1], (1, R.rows0.shape[1]))

    def step(i):
        steps[i].wait()
        R.vland[i + 1] = R.vland[i] + R.vland[nv + 1 + i]
        if i + 1 < nv:
            steps[i + 1].start()

    steps[0].start()
    step(0)
    step(1)
    ext.recv()
    yx = net.yx
    for own, lands, dst in ((R.dq, R.qland, R.qs), (R.d0, R.zland, R.zs)):
        t = own[yx].astype(f32)
        for e in range(3):
            t = t + lands[e].astype(f32)
        dst[0] = t.astype(bf)
    R.qs[1] = R.q1[...]
    R.zs[1] = R.z1[...]
    qsend.start()
    for r in (1, 2, 3):
        pl.when(net.z == 4 - r)(zsend[r - 1].start)
    step(2)
    step(3)
    step(4)
    nl = R.dx_l.shape[0]
    half = R.f0.shape[1] // 2
    theirs = pl.ds(aligned((1 - net.c) * half), half)
    ours = pl.ds(aligned(net.c * half), half)

    @pl.when(qrecv)
    def _():
        R.dx_l[...] = R.dx[:nl].astype(f32)
        R.dx_s[...] = R.dx[nl:].astype(f32)
        qsend.copies[0].wait_recv()
        for l in range(2):
            R.qself[l] = (R.qs[l, theirs].astype(f32) + R.qline[l, theirs].astype(f32)).astype(bf)
            R.gqkv[l] = R.qs[l, ours].astype(f32) + R.qline[l, ours].astype(f32)

    @pl.when(net.z == 0)
    def _():
        for r in (1, 2, 3):
            zsend[r - 1].wait_recv()
        for l in range(2):
            t = R.zs[l].astype(f32)
            for r in range(3):
                t = t + R.zline[r, l].astype(f32)
            R.zs[l] = t.astype(bf)

    tot = R.vland.at[nv]
    for l in range(2):
        at = l * nr
        for i in range(2):
            R.g_gain[l, i : i + 1] = tot[at + i : at + i + 1]
            R.g_bias[l, i : i + 1] = tot[at + 2 + i : at + 3 + i]
            R.g_bqv[l, i : i + 1] = tot[pl.ds(at + 8 + 4 * i + net.z, 1), : R.g_bqv.shape[2]]
        R.g_bout[l : l + 1] = tot[at + 4 : at + 5]
        R.g_bdown[l : l + 1] = tot[at + 5 : at + 6]
        R.g_bup[l : l + 1] = tot[pl.ds(at + 16 + net.z, 1)]
        R.shares[l : l + 1] = tot[at + 6 : at + 7, :128]
    line.finish(R.f0, R.fo0)

    @pl.when(qrecv)
    def _():
        for l, fo in ((0, R.fo0), (1, R.fo1)):
            R.oself[l] = fo[theirs].astype(bf)
            R.gout[l] = jnp.transpose(fo[ours].astype(f32))
        for c in owned.copies:
            c.start()

    for l, f in ((0, R.f0), (1, R.f1)):
        for i in range(2):
            R.fself[l, i] = f[i, theirs].astype(bf)
        R.zself[l] = R.zs[l, theirs]
    cross.start()
    n = R.f0.shape[2]
    for c in range(2):

        @pl.when(net.c == c)
        def _():
            for l, f in ((0, R.f0), (1, R.f1)):
                R.gup[l, :, c * n : (c + 1) * n] = f[0, ours].astype(f32)
                R.gdn[l, c * n : (c + 1) * n] = jnp.transpose(f[1, ours].astype(f32))

    cross.recv()
    for c in range(2):

        @pl.when(net.c != c)
        def _():
            for l in range(2):
                R.gup[l, :, c * n : (c + 1) * n] = R.fland[l, 0].astype(f32)
                R.gdn[l, c * n : (c + 1) * n] = jnp.transpose(R.fland[l, 1].astype(f32))

    @pl.when(net.moves)
    def _():
        for c in owned.copies:
            c.wait_recv()
        R.gqkv[...] = R.qlands[...].astype(f32)
        for l in range(2):
            R.gout[l] = jnp.transpose(R.olands[l].astype(f32))

    @pl.when(net.z == 0)
    def _():
        wid = R.gout.shape[1]
        for l in range(2):
            t = R.zs[l, ours].astype(f32) + R.zlands[l].astype(f32)
            R.gqkv[l, :, :HD] += t[:, :HD]
            R.gqkv[l, :, wid : wid + HD] += t[:, HD:]

    moved.recv()

    @pl.when(net.moves)
    def _():
        R.dx_l[...] = R.dxr[:nl].astype(f32)
        R.dx_s[...] = R.dxr[nl:].astype(f32)

    pl.when(qrecv)(lambda: [c.wait_send() for c in owned.copies] and None)
    cross.sent()
    qsend.sent()
    for r in (1, 2, 3):
        pl.when(net.z == 4 - r)(zsend[r - 1].wait_send)
    ext.sent()
    moved.sent()


def run(kernel, static, ins, outs, scratch, ident, name, flops):
    names = list(ins) + list(outs) + list(scratch)

    def body_of(*refs):
        kernel(*static, types.SimpleNamespace(**dict(zip(names, refs))))

    res = pl.pallas_call(
        body_of,
        out_shape=tuple(jax.ShapeDtypeStruct(tuple(s), t) for s, t, _ in outs.values()),
        in_specs=[VMEM if v else ANY for _, v in ins.values()],
        out_specs=tuple(VMEM if v else ANY for _, _, v in outs.values()),
        scratch_shapes=list(scratch.values()),
        compiler_params=pltpu.CompilerParams(
            vmem_limit_bytes=60 * 1024 * 1024, collective_id=ident, has_side_effects=True
        ),
        cost_estimate=pl.CostEstimate(flops=flops, bytes_accessed=10**7, transcendentals=10**6),
        name=name,
    )(*[a for a, _ in ins.values()])
    return types.SimpleNamespace(**dict(zip(outs, res)))


def fast_body(
    dims, x_long, x_short, dy_long, dy_short, ln_gain, ln_bias, w_qkv, b_qv, w_out, b_out, w_up, b_up, w_down, b_down, threshold
):
    bf, f32 = jnp.bfloat16, jnp.float32
    layers, d = w_qkv.shape[0], w_qkv.shape[1]
    wid, ffq = w_qkv.shape[3], w_up.shape[2]
    rl, rs = x_long.shape[1], x_short.shape[1]
    n = rl + rs
    sl, ss = 4 * rl, 4 * rs
    nq, nx, n0 = 3 * wid, 3 * wid + 2 * HD, 2 * HD
    nh = wid // HD
    f = ffq // 2
    ff = 4 * f
    chunk, part = d // 4, f // 4
    half = chunk // 2
    net = Net(dims)
    axes = dims + ("zh", "zl")
    vm = lambda *s: pltpu.VMEM(tuple(s), bf)
    vf = lambda *s: pltpu.VMEM(tuple(s), f32)
    sem2 = lambda k: dict(ssem=DMA((k,)), rsem=DMA((k,)))

    wqs = [w_qkv[l].reshape(d, nq) for l in range(layers)]
    w0s = [w_qkv[l][:, :2, :HD].reshape(d, n0) for l in range(layers)]
    flat = jnp.concatenate([b_up.reshape(-1), b_qv.reshape(-1)])
    flat = jnp.pad(flat, (0, -flat.shape[0] % 4096)).reshape(16, -1)
    share_rows = wid // 8
    wo = lax.dynamic_slice_in_dim(w_out, (4 * net.y + 2 * net.x + net.c) * share_rows, share_rows, 1)
    wo = [lax.all_gather(wo[l], ("zh", "zl") + dims, axis=0, tiled=True) for l in range(layers)]
    own_up = [lax.dynamic_slice_in_dim(w_up[l], net.c * f, f, 1) for l in range(layers)]
    own_dn = [lax.dynamic_slice_in_dim(w_down[l], net.c * f, f, 0) for l in range(layers)]

    lands = dict(qland=vm(4, chunk, nq), zland=vm(4, chunk, n0))
    P0 = run(
        first_x,
        (dims,),
        dict(xl=(x_long[0], 1), xs=(x_short[0], 1), wq=(wqs[0], 1), w0=(w0s[0], 1), small=(flat, 1), w_up=(w_up, 0), w_down=(w_down, 0)),
        dict(
            xr=((n, d), bf, 1), ext=((d, nx), bf, 1), smalls=((4,) + flat.shape, bf, 1),
            zup=((chunk, 3 * f), bf, 0), zdn=((3, part, d), bf, 0),
        ),
        dict(**lands, **sem2(24)),
        1,
        "first_x",
        10**9,
    )
    n_up = layers * ffq
    smalls = P0.smalls.reshape(4, -1)
    rel_bup = smalls[:, :n_up].reshape(4, layers, 2, f).astype(f32)
    rel_bup = lax.dynamic_index_in_dim(rel_bup, net.c, 2, keepdims=False)
    rel_bup = jnp.swapaxes(rel_bup, 0, 1).reshape(layers, ff)
    rel_bqv = smalls[:, n_up : n_up + layers * 2 * wid].reshape(4, layers, 2, wid).astype(f32)
    my_bqv = lax.dynamic_index_in_dim(rel_bqv, (net.me - net.z) % 4, 0, keepdims=False)
    zero_bq = lax.dynamic_index_in_dim(rel_bqv, (0 - net.z) % 4, 0, keepdims=False)[:, 0, :HD]
    none = jnp.zeros((layers, wid), f32)
    bias = jnp.concatenate([my_bqv[:, 0], none, my_bqv[:, 1], zero_bq, none[:, :HD]], axis=1)
    gain, shift = ln_gain.astype(f32), ln_bias.astype(f32)
    bo, bd = b_out.astype(f32), b_down.astype(f32)
    limits = jnp.broadcast_to((threshold.astype(f32) / 64.0)[:, None, None], (layers, 8, 128))

    resid, zup, zdn = P0.xr, P0.zup, P0.zdn
    exts = [P0.ext]
    saved = []
    for l in range(layers):
        first, last = l == 0, l == layers - 1
        ins = dict(
            resid=(resid, 1), gain1=(gain[l, :1], 1), shift1=(shift[l, :1], 1), gain2=(gain[l, 1:], 1), shift2=(shift[l, 1:], 1),
            ext=(exts[l], 1), bias=(bias[l : l + 1], 1), own_up=(own_up[l], 1), own_dn=(own_dn[l], 1), zup=(zup, 1), zdn=(zdn, 1),
            wout=(wo[l], 1), bout=(bo[l : l + 1], 1), bup=(rel_bup[l : l + 1], 1), bdown=(bd[l : l + 1], 1), limit=(limits[l], 1),
        )
        outs = dict(
            fl_o=((sl, d), bf, 0), fs_o=((ss, d), bf, 0), pjl_o=((sl, nx), bf, 0), pjs_o=((ss, nx), bf, 0),
            att=((n, 4 * wid), bf, 1), ol=((sl, wid), bf, 1), os=((ss, wid), bf, 1),
            lsel=((8, sl), f32, 1), lses=((8, ss), f32, 1), cl=((8, sl), f32, 1), cs=((8, ss), f32, 1),
            wup_o=((d, ff), bf, 0), wdn_o=((4, f, d), bf, 0), middle=((n, d), f32, 1), n2=((2 * n, d), bf, 1),
            act_o=((2, 2 * n, 2 * f), bf, 0), slope_o=((2 * n, ff), bf, 0), new=((n, d), f32, 1), share=((8, 128), f32, 1),
        )
        scratch = dict(
            fl=vm(sl, d), fs=vm(ss, d), pj_l=vm(sl, nx), pj_s=vm(ss, nx), wup=vm(d, ff), wdn=vm(4, f, d),
            act=vm(2, 2 * n, 2 * f), slope=vm(2 * n, ff), land=vm(4, n, wid), out=vm(n, d), got=vm(n, d), lsem=DMA((24,)),
            **sem2(48),
        )
        if first:
            ins.update(wq=(wqs[1], 1), w0=(w0s[1], 1), w_up=(w_up, 0), w_down=(w_down, 0))
            outs.update(ext_next=((d, nx), bf, 1), zup_next=((chunk, 3 * f), bf, 0), zdn_next=((3, part, d), bf, 0))
            scratch.update(lands)
        else:
            ins.update(dl=(dy_long[0], 1), ds=(dy_short[0], 1))
            outs.update(dyr=((n, d), bf, 1))
        if last:
            outs.update(y=((n, d), bf, 1))
        A = run(forward_x, (dims, first, last), ins, outs, scratch, 2 + l, "forward_x", 10**10)
        A.resid = resid
        saved.append(A)
        resid = A.new
        if first:
            exts.append(A.ext_next)
            zup, zdn = A.zup_next, A.zdn_next

    g = saved[-1].dyr
    back = [None] * layers
    B = None
    for l in reversed(range(layers)):
        A = saved[l]
        last = l == layers - 1
        ins = dict(
            g=(g, 1), att=(A.att, 1), wout=(wo[l], 1), gain1=(gain[l, :1], 1), gain2=(gain[l, 1:], 1), wup=(A.wup_o, 1), wdn=(A.wdn_o, 1),
            middle=(A.middle, 1), n2=(A.n2, 1), act=(A.act_o, 0), slope=(A.slope_o, 1), resid=(A.resid, 1),
            pjl_i=(A.pjl_o, 0), pjs_i=(A.pjs_o, 0), ext_i=(exts[l], 0), fl_i=(A.fl_o, 0), fs_i=(A.fs_o, 0),
            ol=(A.ol, 1), os=(A.os, 1), lsel=(A.lsel, 1), lses=(A.lses, 1), cl=(A.cl, 1), cs=(A.cs, 1),
        )
        outs = dict(
            g_new=((n, d), f32 if l else bf, 1), rows=((24, d), f32, 1), dq=((4, chunk, nq), bf, 1), d0=((4, chunk, n0), bf, 1),
            s=((4, 2, chunk, f), bf, 1), so=((2, chunk, wid), bf, 1),
        )
        scratch = dict(
            gm=vm(2 * n, d), gu=vm(2 * n, ff), mine=vf(n, d), out=vm(3, n, d), got=vm(4, n, d), gmid=vf(n, d), ga=vm(n, d),
            oself=vm(d, 2 * wid), olands=vm(d, 2 * wid), dup=vm(4, 4, chunk, f), ddn=vm(4, 4, chunk, f), dout=vm(4, chunk, 2 * wid),
            rup=vm(3, 4, chunk, f), rdn=vm(3, 4, chunk, f), rout=vm(3, chunk, 2 * wid),
            outg=vm(4, n, wid), gl=vm(sl, wid), gs=vm(ss, wid), pj_l=vm(sl, nx), pj_s=vm(ss, nx), ext=vm(d, nx),
            buf=vm(sl + ss, d), dl=vm(sl, nx), ds=vm(ss, nx), acc=vf(2 * nh + 1, sl, HD), kt=vm(nh + 1, HD, sl),
            lsem=DMA((12,)), **sem2(48),
        )
        if last:
            ins.update(y=(A.y, 1))
            outs.update(yr=((n, d), bf, 1))
        else:
            ins.update(s_in=(B.s, 0), so_in=(B.so, 1), dq_in=(B.dq, 0), d0_in=(B.d0, 0))
            outs.update(
                f_out=((2, chunk, f), bf, 1), fo_out=((chunk, wid), bf, 1), q_out=((chunk, nq), bf, 1), z_out=((chunk, n0), bf, 1)
            )
            scratch.update(
                s_own=vm(2, chunk, f), dq_own=vm(chunk, nq), d0_own=vm(chunk, n0), fland=vm(3, 2, chunk, f), foland=vm(3, chunk, wid), qland=vm(3, chunk, nq), zland=vm(3, chunk, n0))
        B = run(backward_x, (dims, last), ins, outs, scratch, 6 + l, "backward_x", 2 * 10**10)
        back[l] = B
        g = B.g_new
        if last:
            y = B.yr

    nv = len(axes)
    T = run(
        tail_x,
        (axes,),
        dict(
            s=(B.s, 1), so=(B.so, 1), dq=(B.dq, 1), d0=(B.d0, 1), f1=(B.f_out, 1), fo1=(B.fo_out, 1), q1=(B.q_out, 1), z1=(B.z_out, 1),
            rows0=(back[0].rows, 1), rows1=(back[1].rows, 1), share0=(saved[0].share, 1), share1=(saved[1].share, 1), dx=(g, 1),
        ),
        dict(
            gup=((2, half, ffq), f32, 1), gdn=((2, ffq, half), f32, 1), gout=((2, wid, half), f32, 1), gqkv=((2, half, nq), f32, 1),
            dx_l=((rl, d), f32, 1), dx_s=((rs, d), f32, 1), g_gain=((2, 2, d), f32, 1), g_bias=((2, 2, d), f32, 1),
            g_bqv=((2, 2, wid), f32, 1), g_bout=((2, d), f32, 1), g_bdown=((2, d), f32, 1), g_bup=((2, ffq), f32, 1),
            shares=((2, 128), f32, 1),
        ),
        dict(
            land=vm(3, 2, chunk, f), oland=vm(3, chunk, wid), f0=vf(2, chunk, f), fo0=vf(chunk, wid),
            qland=vm(3, chunk, nq), zland=vm(3, chunk, n0), qs=vm(2, chunk, nq), zs=vm(2, chunk, n0), qline=vm(2, chunk, nq),
            zline=vm(3, 2, chunk, n0), fself=vm(2, 2, half, f), fland=vm(2, 2, half, f), oself=vm(2, half, wid),
            olands=vm(2, half, wid), qself=vm(2, half, nq), qlands=vm(2, half, nq), zself=vm(2, half, n0), zlands=vm(2, half, n0),
            vland=vf(2 * nv + 1, 48, d), dxr=vm(n, d), **sem2(32),
        ),
        10,
        "tail_x",
        10**9,
    )
    return (
        y[None, :rl],
        y[None, rl:],
        T.dx_l[None],
        T.dx_s[None],
        T.g_gain,
        T.g_bias,
        T.gqkv.reshape(layers, half, 3, wid),
        T.g_bqv,
        T.gout,
        T.g_bout,
        T.gup,
        T.g_bup,
        T.gdn,
        T.g_bdown,
        T.shares[:, 0] / (8 * 4 * n),
    )


def solution(mesh):
    dp, mp = mesh.shape["dp"], mesh.shape["mp"]
    bits = dp.bit_length() - 1
    dims = tuple(f"d{i}" for i in range(bits))
    fine = Mesh(mesh.devices.reshape((2,) * bits + (2, mp // 2)), dims + ("zh", "zl"))
    z = ("zh", "zl")
    in_specs = (
        P(dims, z, None), P(dims, z, None), P(dims, z, None), P(dims, z, None),
        P(), P(), P(None, None, None, z), P(None, None, z), P(None, z, None), P(),
        P(None, None, z), P(None, z), P(None, z, None), P(), P(),
    )
    out_specs = (
        P(dims, z, None), P(dims, z, None), P(dims, z, None), P(dims, z, None),
        P(), P(), P(None, dims, None, z), P(None, None, z), P(None, z, dims), P(),
        P(None, dims, z), P(None, z), P(None, z, dims), P(), P(),
    )
    run = functools.partial(fast_body, dims) if dp == 8 else functools.partial(body, dims, dp, mp)
    return jax.shard_map(
        run, mesh=fine, in_specs=in_specs, out_specs=out_specs, check_vma=False
    )
```

```python
import functools
import types

import jax, jax.numpy as jnp
from jax import lax
from jax.experimental import pallas as pl
from jax.experimental.pallas import tpu as pltpu
from jax.sharding import Mesh
from jax.sharding import PartitionSpec as P

HD = 64
BR = 256
BIG = 1e30
NT = (((1,), (1,)), ((), ()))
NN = (((1,), (0,)), ((), ()))


def mm(a, b, dims=NN):
    return lax.dot_general(a, b, dims, preferred_element_type=jnp.float32)


def halves(v):
    hi = v.astype(jnp.bfloat16)
    lo = (v - hi.astype(jnp.float32)).astype(jnp.bfloat16)
    return hi, lo


def softplus(v):
    return jnp.maximum(v, 0.0) + jnp.log(1.0 + jnp.exp(-jnp.abs(v)))


def fwd_one(x_ref, o_ref, lse_ref, carry_ref, done=None):
    size = x_ref.shape[0]
    nh = (x_ref.shape[1] - 2 * HD) // (3 * HD)
    w = nh * HD
    nb = size // BR
    first = lax.broadcasted_iota(jnp.int32, (BR, BR), 0)
    second = lax.broadcasted_iota(jnp.int32, (BR, BR), 1)
    tri = (first > second).astype(jnp.bfloat16)
    lanes = lax.broadcasted_iota(jnp.int32, (BR, 128), 1)
    lse_ref[...] = jnp.zeros_like(lse_ref)
    carry_ref[...] = jnp.zeros_like(carry_ref)
    for b in range(nb):
        rows = pl.ds(b * BR, BR)
        q0 = x_ref[rows, 3 * w : 3 * w + HD] * 0.125
        pens = []
        for c in range(b + 1):
            cols = pl.ds(c * BR, BR)
            sp = softplus(mm(q0, x_ref[cols, 3 * w + HD : 3 * w + 2 * HD], NT))
            if c == b:
                keep = first > second
                if c == 0:
                    keep = jnp.logical_and(keep, second >= 1)
                sp = jnp.where(keep, sp, 0.0)
            elif c == 0:
                sp = jnp.where(second >= 1, sp, 0.0)
            hi, lo = halves(sp)
            pen = mm(tri, hi) + mm(tri, lo) + carry_ref[b : b + 1, cols]
            carry_ref[b + 1 : b + 2, cols] = pen[BR - 1 :] + sp[BR - 1 :]
            if c == b:
                pen = jnp.where(first >= second, pen, BIG)
            pens.append(pen)
        stats = jnp.zeros((BR, 128), jnp.float32)
        for h in range(nh):
            qh = x_ref[rows, h * HD : (h + 1) * HD] * 0.125
            scores = [
                mm(qh, x_ref[c * BR : (c + 1) * BR, w + h * HD : w + (h + 1) * HD], NT) - pens[c]
                for c in range(b + 1)
            ]
            top = scores[0]
            for s in scores[1:]:
                top = jnp.maximum(top, s)
            top = jnp.max(top, axis=1, keepdims=True)
            total = None
            acc = None
            for c in range(b + 1):
                e = jnp.exp(scores[c] - top)
                total = e if total is None else total + e
                part = mm(
                    e.astype(jnp.bfloat16),
                    x_ref[c * BR : (c + 1) * BR, 2 * w + h * HD : 2 * w + (h + 1) * HD],
                )
                acc = part if acc is None else acc + part
            total = jnp.sum(total, axis=1, keepdims=True)
            o_ref[rows, h * HD : (h + 1) * HD] = (acc / total).astype(jnp.bfloat16)
            stats = jnp.where(lanes == h, top + jnp.log(total), stats)
        lse_ref[:, rows] = jnp.transpose(stats)[:8]
        if done is not None:
            done(b)


def bwd_one(x_ref, g_ref, o_ref, lse_ref, carry_ref, d_ref, acc, kt):
    size = x_ref.shape[0]
    nh = (x_ref.shape[1] - 2 * HD) // (3 * HD)
    w = nh * HD
    nb = size // BR
    jj = lax.broadcasted_iota(jnp.int32, (BR, BR), 0)
    ii = lax.broadcasted_iota(jnp.int32, (BR, BR), 1)
    below = (jj < ii).astype(jnp.bfloat16)
    above = (jj > ii).astype(jnp.bfloat16)
    ones = jnp.ones((8, HD), jnp.bfloat16)
    for h in range(nh + 1):
        lo = 3 * w + HD if h == nh else w + h * HD
        kt[h, :, :size] = jnp.transpose(x_ref[:, lo : lo + HD].astype(jnp.float32)).astype(
            jnp.bfloat16
        )
    later = [None] * nb
    for b in reversed(range(nb)):
        rows = pl.ds(b * BR, BR)
        q0 = x_ref[rows, 3 * w : 3 * w + HD] * 0.125
        pens, sigs, sums = [], [], [None] * (b + 1)
        for c in range(b + 1):
            sel = mm(x_ref[c * BR : (c + 1) * BR, 3 * w + HD : 3 * w + 2 * HD], q0, NT)
            small = jnp.exp(-jnp.abs(sel))
            sp = jnp.maximum(sel, 0.0) + jnp.log(1.0 + small)
            sig = jnp.where(sel >= 0, 1.0, small) / (1.0 + small)
            if c == b or c == 0:
                keep = None
                if c == b:
                    keep = ii > jj
                if c == 0:
                    keep = jj >= 1 if keep is None else jnp.logical_and(keep, jj >= 1)
                sp = jnp.where(keep, sp, 0.0)
                sig = jnp.where(keep, sig, 0.0)
            hi, lo = halves(sp)
            start = jnp.transpose(
                jnp.broadcast_to(carry_ref[b : b + 1, c * BR : (c + 1) * BR], (128, BR))
            )
            pen = mm(hi, below) + mm(lo, below) + start[:, :1]
            if c == b:
                pen = jnp.where(ii >= jj, pen, BIG)
            pens.append(pen)
            sigs.append(sig)
        for h in range(nh):
            qh = x_ref[rows, h * HD : (h + 1) * HD] * 0.125
            gh = g_ref[rows, h * HD : (h + 1) * HD]
            prod = gh.astype(jnp.float32) * o_ref[rows, h * HD : (h + 1) * HD].astype(jnp.float32)
            phi, plo = halves(prod)
            delta = (mm(ones, phi, NT) + mm(ones, plo, NT))[:1]
            lse = lse_ref[h : h + 1, rows]
            dqt = None
            for c in range(b + 1):
                cols = pl.ds(c * BR, BR)
                s = mm(x_ref[cols, w + h * HD : w + (h + 1) * HD], qh, NT)
                p = jnp.exp((s - pens[c]) - lse)
                dp = mm(x_ref[cols, 2 * w + h * HD : 2 * w + (h + 1) * HD], gh, NT)
                ds = p * (dp - delta)
                low = ds.astype(jnp.bfloat16)
                dk = mm(low, qh)
                dv = mm(p.astype(jnp.bfloat16), gh)
                part = mm(kt[h, :, c * BR : (c + 1) * BR], low)
                dqt = part if dqt is None else dqt + part
                if b == nb - 1:
                    acc[h, cols] = dk
                    acc[nh + h, cols] = dv
                else:
                    acc[h, cols] += dk
                    acc[nh + h, cols] += dv
                sums[c] = ds if sums[c] is None else sums[c] + ds
            d_ref[rows, h * HD : (h + 1) * HD] = jnp.transpose(dqt * 0.125).astype(jnp.bfloat16)
        dqt = None
        for c in range(b + 1):
            cols = pl.ds(c * BR, BR)
            hi, lo = halves(sums[c])
            grad = mm(hi, above) + mm(lo, above)
            full = grad[:, :1] + sums[c][:, :1]
            if later[c] is not None:
                grad = grad + later[c]
                full = full + later[c]
            later[c] = full
            low = (-(grad * sigs[c])).astype(jnp.bfloat16)
            dk = mm(low, q0)
            part = mm(kt[nh, :, c * BR : (c + 1) * BR], low)
            dqt = part if dqt is None else dqt + part
            if b == nb - 1:
                acc[2 * nh, cols] = dk
            else:
                acc[2 * nh, cols] += dk
        d_ref[rows, 3 * w : 3 * w + HD] = jnp.transpose(dqt * 0.125).astype(jnp.bfloat16)
        own = pl.ds(b * BR, BR)
    for h in range(nh):
        d_ref[:, w + h * HD : w + (h + 1) * HD] = acc[h, :size].astype(jnp.bfloat16)
        d_ref[:, 2 * w + h * HD : 2 * w + (h + 1) * HD] = acc[nh + h, :size].astype(jnp.bfloat16)
    d_ref[:, 3 * w + HD : 3 * w + 2 * HD] = acc[2 * nh, :size].astype(jnp.bfloat16)


VMEM = pl.BlockSpec(memory_space=pltpu.VMEM)
LIMIT = 48 * 1024 * 1024


def attend_fwd(x):
    size, w = x.shape[0], (x.shape[1] - 2 * HD) // 3
    return pl.pallas_call(
        fwd_one,
        out_shape=(
            jax.ShapeDtypeStruct((size, w), jnp.bfloat16),
            jax.ShapeDtypeStruct((8, size), jnp.float32),
            jax.ShapeDtypeStruct((8, size), jnp.float32),
        ),
        in_specs=[VMEM],
        out_specs=(VMEM,) * 3,
        compiler_params=pltpu.CompilerParams(vmem_limit_bytes=LIMIT),
        cost_estimate=pl.CostEstimate(
            flops=size * size * 64 * 40, bytes_accessed=size * 2000, transcendentals=size * size * 3
        ),
        name="attend_fwd",
    )(x)


def attend_bwd(x, g, o, lse, carry):
    size, w = x.shape[0], (x.shape[1] - 2 * HD) // 3
    nh = w // HD
    return pl.pallas_call(
        bwd_one,
        out_shape=jax.ShapeDtypeStruct(x.shape, jnp.bfloat16),
        in_specs=[VMEM] * 5,
        out_specs=VMEM,
        scratch_shapes=[
            pltpu.VMEM((2 * nh + 1, size, HD), jnp.float32),
            pltpu.VMEM((nh + 1, HD, size), jnp.bfloat16),
        ],
        compiler_params=pltpu.CompilerParams(vmem_limit_bytes=LIMIT),
        cost_estimate=pl.CostEstimate(
            flops=size * size * 64 * 80, bytes_accessed=size * 4000, transcendentals=size * size * 3
        ),
        name="attend_bwd",
    )(x, g, o, lse, carry)


class Group:
    def __init__(self, core):
        self.core = core
        self.c = lax.axis_index(core)
        self.zl = lax.axis_index("zl")
        self.me = 2 * self.c + self.zl

    def peer(self, delta):
        return {self.core: self.c ^ (delta >> 1), "zl": self.zl ^ (delta & 1)}

    def member(self, m):
        return {self.core: m >> 1, "zl": m & 1}

    def greet(self, deltas):
        barrier = pltpu.get_barrier_semaphore()
        for delta in deltas:
            pl.semaphore_signal(
                barrier, inc=1, device_id=self.peer(delta), device_id_type=pl.DeviceIdType.MESH
            )
        pl.semaphore_wait(barrier, len(deltas))


def send(src, dst, ssem, rsem, device):
    return pltpu.make_async_remote_copy(
        src_ref=src,
        dst_ref=dst,
        send_sem=ssem,
        recv_sem=rsem,
        device_id=device,
        device_id_type=pl.DeviceIdType.MESH,
    )


def fwd_x(core, xl, xs, att, ol, os, lsel, lses, cl, cs, land, ssem, rsem):
    group = Group(core)
    nl, ns = xl.shape[0] // 4, xs.shape[0] // 4
    group.greet((1, 2, 3))

    def copy(k, m):
        src, n, at = ((ol, nl, 0), (os, ns, nl))[k]
        return send(
            src.at[pl.ds(m * n, n)],
            land.at[group.me, pl.ds(at, n)],
            ssem.at[k, m],
            rsem.at[k, group.me],
            group.member(m),
        )

    def arrived(k, m):
        src, n, at = ((ol, nl, 0), (os, ns, nl))[k]
        return send(
            src.at[pl.ds(0, n)], land.at[m, pl.ds(at, n)], ssem.at[k, m], rsem.at[k, m], group.member(m)
        )

    def start(k, m):
        src, n, at = ((ol, nl, 0), (os, ns, nl))[k]

        @pl.when(group.me != m)
        def _():
            copy(k, m).start()

        @pl.when(group.me == m)
        def _():
            land[m, at : at + n] = src[m * n : (m + 1) * n]

    def started(k, n):
        def done(b):
            for m in range(b * BR // n, (b + 1) * BR // n):
                start(k, m)

        return done

    fwd_one(xs, os, lses, cs, started(1, ns))
    fwd_one(xl, ol, lsel, cl, started(0, nl))
    w = ol.shape[1]
    for m in range(4):

        @pl.when(group.me != m)
        def _():
            for k in range(2):
                copy(k, m).wait_send()
                arrived(k, m).wait_recv()

    for m in range(4):
        att[:, m * w : (m + 1) * w] = land[m]


def bwd_x(core, xl, xs, go, ol, os, lsel, lses, cl, cs, dl, ds, acc, kt, out, gl, gs, ssem, rsem):
    group = Group(core)
    nl, ns = xl.shape[0] // 4, xs.shape[0] // 4
    w = ol.shape[1]
    for m in range(4):
        out[m] = go[:, m * w : (m + 1) * w]
    group.greet((1, 2, 3))

    def part(k):
        return ((gl, nl, 0), (gs, ns, nl))[k]

    def copy(k, m):
        dst, n, at = part(k)
        return send(
            out.at[m, pl.ds(at, n)],
            dst.at[pl.ds(pl.multiple_of(group.me * n, 16), n)],
            ssem.at[k, m],
            rsem.at[k, group.me],
            group.member(m),
        )

    def arrived(k, m):
        dst, n, at = part(k)
        return send(
            out.at[m, pl.ds(at, n)], dst.at[pl.ds(m * n, n)], ssem.at[k, m], rsem.at[k, m], group.member(m)
        )

    for k in (1, 0):
        for m in range(4):
            dst, n, at = part(k)

            @pl.when(group.me != m)
            def _():
                copy(k, m).start()

            @pl.when(group.me == m)
            def _():
                dst[m * n : (m + 1) * n] = out[m, at : at + n]

    for k in (1, 0):
        for m in range(4):

            @pl.when(group.me != m)
            def _():
                arrived(k, m).wait_recv()

        if k:
            bwd_one(xs, gs, os, lses, cs, ds, acc, kt)
        else:
            bwd_one(xl, gl, ol, lsel, cl, dl, acc, kt)
    for m in range(4):

        @pl.when(group.me != m)
        def _():
            for k in range(2):
                copy(k, m).wait_send()


def norm_rows(v):
    mean = jnp.mean(v, axis=-1, keepdims=True)
    cen = v - mean
    inv = lax.rsqrt(jnp.mean(cen * cen, axis=-1, keepdims=True) + 1e-05)
    return cen * inv, inv


def project_x(core, resid, gain, shift, w, bias, nl_ref, ns_ref, pl_ref, ps_ref, ssem, rsem):
    group = Group(core)
    nl, ns = nl_ref.shape[0] // 4, ns_ref.shape[0] // 4
    half = nl // 2
    parts = ((ns_ref, ps_ref, ns, 0, ns, nl), (nl_ref, pl_ref, nl, 0, half, 0), (nl_ref, pl_ref, nl, half, half, half))

    def rows(k, m):
        ref, _, n, at, size, _ = parts[k]
        return ref.at[pl.ds(pl.multiple_of(m * n + at, 16), size)]

    def copy(k, j, m, delta):
        return send(rows(k, m), rows(k, m), ssem.at[k, j], rsem.at[k, j], group.peer(delta))

    def compute(k, m):
        ref, out, n, at, size, _ = parts[k]
        here = pl.ds(pl.multiple_of(m * n + at, 16), size)
        out[here] = (mm(ref[here], w[...]) + bias[...]).astype(jnp.bfloat16)

    me = group.me
    for k in range(3):
        ref, _, n, at, size, src = parts[k]
        hat, _ = norm_rows(resid[src : src + size])
        ref[pl.ds(pl.multiple_of(me * n + at, 16), size)] = (hat * gain[...] + shift[...]).astype(
            jnp.bfloat16
        )
        if k == 0:
            group.greet((1, 2))
        copy(k, 0, me, 1).start()
        copy(k, 1, me, 2).start()
    for k in range(3):
        compute(k, me)
    for k in range(3):
        copy(k, 1, me ^ 2, 2).wait_recv()
        compute(k, me ^ 2)
    for k in range(3):
        copy(k, 0, me ^ 1, 1).wait_recv()
        copy(k, 2, me ^ 1, 2).start()
        compute(k, me ^ 1)
    for k in range(3):
        copy(k, 2, me ^ 3, 2).wait_recv()
        compute(k, me ^ 3)
    for k in range(3):
        copy(k, 0, me, 1).wait_send()
        copy(k, 1, me, 2).wait_send()
        copy(k, 2, me ^ 1, 2).wait_send()


def collect_x(core, dl, ds, w, resid, gain, gmid, g_ref, sums, mine, out, got, ssem, rsem):
    group = Group(core)
    nl, ns = dl.shape[0] // 4, ds.shape[0] // 4
    me = group.me

    def partial(m):
        a = mm(dl[pl.ds(pl.multiple_of(m * nl, 16), nl)], w[...], NT)
        b = mm(ds[pl.ds(pl.multiple_of(m * ns, 16), ns)], w[...], NT)
        return jnp.concatenate([a, b], axis=0)

    def copy(k, delta):
        return send(out.at[k], got.at[k], ssem.at[k], rsem.at[k], group.peer(delta))

    out[0] = partial(me ^ 3).astype(jnp.bfloat16)
    group.greet((1, 2))
    copy(0, 2).start()
    mine[...] = partial(me ^ 1)
    copy(0, 2).wait_recv()
    out[1] = (mine[...] + got[0].astype(jnp.float32)).astype(jnp.bfloat16)
    copy(1, 1).start()
    out[2] = partial(me ^ 2).astype(jnp.bfloat16)
    copy(2, 2).start()
    mine[...] = partial(me)
    hat, inv = norm_rows(resid[...])
    copy(2, 2).wait_recv()
    copy(1, 1).wait_recv()
    grad = mine[...] + got[2].astype(jnp.float32) + got[1].astype(jnp.float32)
    gh = grad * gain[...]
    a = jnp.mean(gh, axis=-1, keepdims=True)
    b = jnp.mean(gh * hat, axis=-1, keepdims=True)
    g_ref[...] = gmid[...] + inv * (gh - a - hat * b)
    sums[0:1] = jnp.sum(grad * hat, axis=0, keepdims=True)
    sums[1:2] = jnp.sum(grad, axis=0, keepdims=True)
    copy(0, 2).wait_send()
    copy(1, 1).wait_send()
    copy(2, 2).wait_send()


def shape(dims, dtype):
    return jax.ShapeDtypeStruct(tuple(dims), dtype)


def remote(kernel, core, outs, scratch, ident, name, args, flops=10**9):
    return pl.pallas_call(
        functools.partial(kernel, core),
        out_shape=tuple(outs),
        in_specs=[VMEM] * len(args),
        out_specs=(VMEM,) * len(outs),
        scratch_shapes=scratch,
        compiler_params=pltpu.CompilerParams(
            vmem_limit_bytes=LIMIT, collective_id=ident, has_side_effects=True
        ),
        cost_estimate=pl.CostEstimate(flops=flops, bytes_accessed=10**7, transcendentals=10**6),
        name=name,
    )(*args)


DMA = pltpu.SemaphoreType.DMA


def attend_fwd_x(core, xl, xs):
    w = (xl.shape[1] - 2 * HD) // 3
    rows = (xl.shape[0] + xs.shape[0]) // 4
    outs = [shape((rows, 4 * w), jnp.bfloat16)]
    outs += [shape((x.shape[0], w), jnp.bfloat16) for x in (xl, xs)]
    outs += [shape((8, x.shape[0]), jnp.float32) for x in (xl, xs)] * 2
    scratch = [pltpu.VMEM((4, rows, w), jnp.bfloat16), DMA((2, 4)), DMA((2, 4))]
    return remote(fwd_x, core, outs, scratch, 1, "attend_fwd_x", (xl, xs), 10**10)


def attend_bwd_x(core, xl, xs, go, ol, os, lsel, lses, cl, cs):
    w = ol.shape[1]
    nh = w // HD
    size = xl.shape[0]
    outs = [shape(x.shape, jnp.bfloat16) for x in (xl, xs)]
    scratch = [
        pltpu.VMEM((2 * nh + 1, size, HD), jnp.float32),
        pltpu.VMEM((nh + 1, HD, size), jnp.bfloat16),
        pltpu.VMEM((4, go.shape[0], w), jnp.bfloat16),
        pltpu.VMEM(ol.shape, jnp.bfloat16),
        pltpu.VMEM(os.shape, jnp.bfloat16),
        DMA((2, 4)),
        DMA((2, 4)),
    ]
    args = (xl, xs, go, ol, os, lsel, lses, cl, cs)
    return remote(bwd_x, core, outs, scratch, 2, "attend_bwd_x", args, 2 * 10**10)


def project(core, resid, gain, shift, w, bias, nl, ns):
    d, n = w.shape
    outs = [shape((4 * nl, d), jnp.bfloat16), shape((4 * ns, d), jnp.bfloat16)]
    outs += [shape((4 * nl, n), jnp.bfloat16), shape((4 * ns, n), jnp.bfloat16)]
    args = (resid, gain[None], shift[None], w, bias[None])
    return remote(project_x, core, outs, [DMA((3, 3)), DMA((3, 3))], 3, "project_x", args)


def collect(core, dl, ds, w, resid, gain, gmid):
    outs = [shape(resid.shape, jnp.float32), shape((8, w.shape[0]), jnp.float32)]
    scratch = [
        pltpu.VMEM(resid.shape, jnp.float32),
        pltpu.VMEM((3,) + resid.shape, jnp.bfloat16),
        pltpu.VMEM((3,) + resid.shape, jnp.bfloat16),
        DMA((3,)),
        DMA((3,)),
    ]
    return remote(collect_x, core, outs, scratch, 4, "collect_x", (dl, ds, w, resid, gain[None], gmid))


def total_x(axes, v, out, land, ssem, rsem):
    barrier = pltpu.get_barrier_semaphore()
    peers = [{ax: 1 - lax.axis_index(ax)} for ax in axes]
    for peer in peers:
        pl.semaphore_signal(barrier, inc=1, device_id=peer, device_id_type=pl.DeviceIdType.MESH)
    pl.semaphore_wait(barrier, len(peers))
    land[0] = v[...]
    n = len(axes)
    for i, peer in enumerate(peers):
        copy = send(land.at[i], land.at[n + 1 + i], ssem.at[i], rsem.at[i], peer)
        copy.start()
        copy.wait()
        land[i + 1] = land[i] + land[n + 1 + i]
    out[...] = land[n]


def total(axes, v):
    n = len(axes)
    scratch = [pltpu.VMEM((2 * n + 1,) + v.shape, jnp.float32), DMA((n,)), DMA((n,))]
    return remote(total_x, axes, [shape(v.shape, jnp.float32)], scratch, 5, "total_x", (v,))[0]


EPS = 1e-05
F32 = jnp.float32
BF = jnp.bfloat16


def swap(v, *axes):
    count = 2 ** len(axes)
    return lax.ppermute(
        v, axes if len(axes) > 1 else axes[0], [(i, count - 1 - i) for i in range(count)]
    )


def ordered(own, other, index, axis):
    return jnp.where(
        index == 0,
        jnp.concatenate([own, other], axis=axis),
        jnp.concatenate([other, own], axis=axis),
    )


def pick(v, index, axis):
    return lax.dynamic_index_in_dim(v, index, axis, keepdims=False)


def normalize(v, gain, shift):
    mean = jnp.mean(v, axis=-1, keepdims=True)
    cen = v - mean
    var = jnp.mean(cen * cen, axis=-1, keepdims=True)
    inv = lax.rsqrt(var + EPS)
    hat = cen * inv
    return hat * gain + shift, hat, inv


def normalize_back(grad, hat, inv, gain):
    gh = grad * gain
    a = jnp.mean(gh, axis=-1, keepdims=True)
    b = jnp.mean(gh * hat, axis=-1, keepdims=True)
    return inv * (gh - a - hat * b), jnp.sum(grad * hat, axis=0), jnp.sum(grad, axis=0)


def gelu_both(u):
    k = 0.7978845608028654
    inner = k * (u + 0.044715 * u * u * u)
    t = jnp.tanh(inner)
    act = 0.5 * u * (1.0 + t)
    slope = 0.5 * (1.0 + t) + 0.5 * u * (1.0 - t * t) * k * (1.0 + 3 * 0.044715 * u * u)
    return act, slope


def dot(a, b, ca=1, cb=0):
    return lax.dot_general(a, b, (((ca,), (cb,)), ((), ())), preferred_element_type=F32)


class Plan:
    def __init__(self, dims, dp, mp):
        self.dims, self.dp, self.mp = dims, dp, mp
        self.core = dims[-1]
        self.plane = dims[:-1]
        self.c = lax.axis_index(self.core)
        self.zh = lax.axis_index("zh")
        self.zl = lax.axis_index("zl")
        self.z = lax.axis_index(("zh", "zl"))
        self.d = lax.axis_index(dims)

    def relabel(self, v):
        got = lax.ppermute(v, (self.core, "zh"), [(1, 2), (2, 1)])
        return jnp.where(self.c == self.zh, v, got)

    def ring(self, v, step):
        n = self.mp
        return lax.ppermute(v, ("zh", "zl"), [(i, (i + step) % n) for i in range(n)])

    def gather(self, v):
        v = ordered(v, swap(v, "zl"), self.zl, 0)
        return ordered(v, swap(v, self.core), self.c, 0)

    def scatter(self, v):
        rows = v.shape[0] // 4
        v = v.reshape(2, 2, rows, v.shape[1])
        got = swap(pick(v, 1 - self.c, 0), self.core)
        mine = pick(v, self.c, 0).astype(F32) + got.astype(F32)
        got = swap(pick(mine, 1 - self.zl, 0).astype(BF), "zl")
        return pick(mine, self.zl, 0) + got.astype(F32)

    def to_rows(self, o):
        rows = o.shape[0] // 4
        o = o.reshape(2, 2, rows, o.shape[1])
        got = []
        for dc in range(2):
            line = []
            for dz in range(2):
                part = pick(pick(o, self.c ^ dc, 0), self.zl ^ dz, 0)
                axes = ((self.core,) if dc else ()) + (("zl",) if dz else ())
                line.append(swap(part, *axes) if axes else part)
            got.append(ordered(line[0], line[1], self.zl, 1))
        return ordered(got[0], got[1], self.c, 1)

    def to_heads(self, g):
        rows, w = g.shape[0], g.shape[1] // 4
        g = g.reshape(rows, 2, 2, w)
        got = []
        for dc in range(2):
            line = []
            for dz in range(2):
                part = pick(pick(g, self.c ^ dc, 1), self.zl ^ dz, 1)
                axes = ((self.core,) if dc else ()) + (("zl",) if dz else ())
                line.append(swap(part, *axes) if axes else part)
            got.append(ordered(line[0], line[1], self.zl, 0))
        return ordered(got[0], got[1], self.c, 0)

    def piece(self, w):
        rows = w.shape[0] // self.dp
        return lax.dynamic_slice_in_dim(w, self.d * rows, rows, 0)

    def ring_gather(self, v):
        parts = []
        for _ in range(self.mp - 1):
            v = self.ring(v, 1)
            parts.append(v)
        return parts

    def plane_gather(self, v, axes):
        k, rows, n = v.shape
        have = []
        shape = [k]
        for ax in axes:
            pos = sum(self.dims.index(h) < self.dims.index(ax) for h in have)
            got = swap(v, ax)
            cur = v.reshape(k, *([2] * len(have)), rows, n)
            oth = got.reshape(cur.shape)
            a = jnp.stack([cur, oth], axis=1 + pos)
            b = jnp.stack([oth, cur], axis=1 + pos)
            v = jnp.where(lax.axis_index(ax) == 0, a, b)
            have.append(ax)
            v = v.reshape(k, -1, rows, n).reshape(k, -1, n)
            rows_all = v.shape[1]
            v = v.reshape(k, rows_all, n)
        return v.reshape(k, self.dp, rows, n)

    def plane_scatter(self, g, axes):
        n = g.shape[1]
        left = [ax for ax in self.dims]
        rows = g.shape[0] // self.dp
        v = g.reshape(*([2] * len(left)), rows, n)
        for ax in axes:
            pos = left.index(ax)
            i = lax.axis_index(ax)
            got = swap(pick(v, 1 - i, pos), ax)
            v = (pick(v, i, pos).astype(F32) + got.astype(F32)).astype(BF)
            left.remove(ax)
        return v.reshape(-1, n)

    def ring_scatter(self, chunks):
        t = chunks[-1]
        for r in range(self.mp - 2, -1, -1):
            got = self.ring(t, -1)
            t = chunks[r].astype(F32) + got.astype(F32)
            if r:
                t = t.astype(BF)
        return t


def body(
    dims, dp, mp,
    x_long, x_short, dy_long, dy_short, ln_gain, ln_bias, w_qkv, b_qv, w_out, b_out, w_up, b_up, w_down, b_down, threshold,
):
    plan = Plan(dims, dp, mp)
    layers = w_qkv.shape[0]
    d_model = x_long.shape[-1]
    heads_w = w_qkv.shape[-1]
    ffq = w_up.shape[-1]
    rl, rs = x_long.shape[1], x_short.shape[1]
    rows = rl + rs
    core_rest = tuple(plan.plane)
    fwd_axes = core_rest + (plan.core,)
    alt_axes = core_rest[::-1] + (plan.core,)
    gain = ln_gain.astype(F32)
    shift = ln_bias.astype(F32)

    x = jnp.concatenate([x_long[0], x_short[0]], axis=0)
    x = plan.relabel(x)

    small = jnp.concatenate([b_up.reshape(-1), b_qv.reshape(-1)])
    rel_small = jnp.stack([small] + plan.ring_gather(small))
    n_up = layers * ffq
    rel_bup = rel_small[:, :n_up].reshape(mp, layers, ffq).astype(F32)
    rel_bqv = rel_small[:, n_up:].reshape(mp, layers, 2, heads_w).astype(F32)
    mine = 2 * plan.c + plan.zl
    my_bqv = pick(rel_bqv, (plan.z - mine) % mp, 0)
    zero_bq = pick(rel_bqv, plan.z % mp, 0)[:, 0, :HD]

    exts = []
    for l in range(layers):
        quarter = plan.relabel(w_qkv[l].reshape(d_model, 3 * heads_w))
        head0 = w_qkv[l][:, :2, :HD].reshape(d_model, 2 * HD)
        got = lax.ppermute(head0, "zl", [(0, 1)])
        head0 = jnp.where(plan.zl == 0, head0, got)
        got = lax.ppermute(head0, "zh", [(0, 1)])
        head0 = jnp.where(plan.zh == 0, head0, got)
        exts.append(jnp.concatenate([quarter, head0], axis=1))

    ups, downs, outs = [], [], []
    for l in range(layers):
        po = plan.piece(w_out[l])
        pu = jnp.concatenate([plan.piece(w_up[l]), po], axis=0)
        pd = plan.piece(w_down[l])
        n_out, n_d = po.shape[0], pd.shape[0]
        both = plan.ring_gather(jnp.concatenate([pu, pd], axis=0))
        stacked = jnp.stack(both)
        n_u = pu.shape[0]
        gu = plan.plane_gather(stacked[:, :n_u], fwd_axes)
        gd = plan.plane_gather(stacked[:, n_u:], alt_axes)
        up = gu[:, :, : n_u - n_out].reshape(mp - 1, d_model, ffq)
        ups.append(jnp.concatenate([w_up[l]] + [up[r] for r in range(mp - 1)], axis=1))
        out = gu[:, :, n_u - n_out :].reshape(mp - 1, heads_w, d_model)
        out = jnp.concatenate([w_out[l][None], out], axis=0)
        outs.append(
            jnp.concatenate([pick(out, (plan.z - q) % mp, 0) for q in range(mp)], axis=0)
        )
        downs.append(
            jnp.concatenate([w_down[l], gd.reshape((mp - 1) * ffq, d_model)], axis=0)
        )

    dy = plan.relabel(jnp.concatenate([dy_long[0], dy_short[0]], axis=0))

    limits = threshold.astype(F32) / 64.0
    resid = x.astype(F32)
    saved = []
    shares = []
    for l in range(layers):
        normed, hat1, inv1 = normalize(resid, gain[l, 0], shift[l, 0])
        normed = normed.astype(BF)
        full = [plan.gather(normed[:rl]), plan.gather(normed[rl:])]
        bias = jnp.concatenate(
            [
                my_bqv[l, 0],
                jnp.zeros((heads_w,), F32),
                my_bqv[l, 1],
                zero_bq[l],
                jnp.zeros((HD,), F32),
            ]
        )
        proj = [(dot(n, exts[l]) + bias).astype(BF) for n in full]
        att = [attend_fwd(p) for p in proj]
        share = jnp.zeros((), F32)
        for p, a in zip(proj, att):
            size = p.shape[0]
            sel = a[2][size // BR]
            left = (size - 1 - lax.broadcasted_iota(jnp.int32, (size,), 0)).astype(F32)
            share = share + jnp.sum(
                jax.nn.sigmoid(4.0 * (sel / jnp.maximum(left, 1.0) - limits[l]))
            )
        shares.append(share)
        attended = jnp.concatenate([plan.to_rows(a[0]) for a in att], axis=0)
        middle = resid + dot(attended, outs[l]) + b_out[l].astype(F32)
        normed2, hat2, inv2 = normalize(middle, gain[l, 1], shift[l, 1])
        normed2 = normed2.astype(BF)
        upper = dot(normed2, ups[l]) + rel_bup[:, l].reshape(-1)
        active = gelu_both(upper)[0].astype(BF)
        saved.append((resid, middle, full, proj, att, attended, normed2, upper, active))
        resid = middle + dot(active, downs[l]) + b_down[l].astype(F32)

    y = plan.relabel(resid.astype(BF))

    g = dy.astype(F32)
    vec = {}
    weight_grads = [None] * layers
    for l in reversed(range(layers)):
        resid, middle, full, proj, att, attended, normed2, upper, active = saved[l]
        g_bdown = jnp.sum(g, axis=0)
        gm = g.astype(BF)
        gact = dot(gm, downs[l], 1, 1)
        slope = gelu_both(upper)[1]
        gu = (slope * gact).astype(BF)
        w_down_t = dot(gm, active, 0, 0).astype(BF)
        w_up_g = dot(normed2, gu, 0, 0).astype(BF)
        g_bup = jnp.sum(gu.astype(F32), axis=0)
        gn2 = dot(gu, ups[l], 1, 1)
        _, hat2, inv2 = normalize(middle, gain[l, 1], shift[l, 1])
        back, g_gain2, g_shift2 = normalize_back(gn2, hat2, inv2, gain[l, 1])
        gmid = g + back
        g_bout = jnp.sum(gmid, axis=0)
        ga = gmid.astype(BF)
        go = dot(ga, outs[l], 1, 1).astype(BF)
        w_out_t = dot(ga, attended, 0, 0).astype(BF)
        gh = [plan.to_heads(go[:rl]), plan.to_heads(go[rl:])]
        dext = [attend_bwd(p, h, a[0], a[1], a[2]) for p, h, a in zip(proj, gh, att)]
        gn1 = jnp.concatenate(
            [plan.scatter(dot(e, exts[l], 1, 1).astype(BF)) for e in dext], axis=0
        )
        w_ext_g = sum(dot(n, e, 0, 0) for n, e in zip(full, dext)).astype(BF)
        g_bext = sum(jnp.sum(e.astype(F32), axis=0) for e in dext)
        _, hat1, inv1 = normalize(resid, gain[l, 0], shift[l, 0])
        back, g_gain1, g_shift1 = normalize_back(gn1, hat1, inv1, gain[l, 0])
        g = gmid + back

        w_up_g = plan.plane_scatter(w_up_g, (plan.core,) + core_rest)
        w_up_g = plan.ring_scatter([w_up_g[:, r * ffq : (r + 1) * ffq] for r in range(mp)])
        w_down_t = plan.plane_scatter(w_down_t, (plan.core,) + core_rest[::-1])
        w_down_t = plan.ring_scatter([w_down_t[:, r * ffq : (r + 1) * ffq] for r in range(mp)])
        w_out_t = plan.plane_scatter(w_out_t, (plan.core,) + core_rest)
        w_out_t = w_out_t.reshape(-1, mp, heads_w)
        w_out_t = plan.ring_scatter([pick(w_out_t, (plan.z - r) % mp, 1) for r in range(mp)])
        w_ext_g = plan.plane_scatter(w_ext_g, core_rest[::-1])
        w_ext_g = w_ext_g.reshape(2, -1, w_ext_g.shape[1])
        part, zero = w_ext_g[..., : 3 * heads_w], w_ext_g[..., 3 * heads_w :]
        got = lax.ppermute(part, (plan.core, "zh"), [(1, 0), (2, 3)])
        part = part.astype(F32) + got.astype(F32)
        got = lax.ppermute(
            pick(part, 1 - plan.c, 0).astype(BF), (plan.core, "zh"), [(0, 2), (3, 1)]
        )
        w_qkv_g = jnp.where(plan.c == plan.zh, pick(part, plan.c, 0), got.astype(F32))
        got = swap(pick(zero, 1 - plan.c, 0), plan.core)
        zero = (pick(zero, plan.c, 0).astype(F32) + got.astype(F32)).astype(BF)
        zero = zero.astype(F32) + swap(zero, "zl").astype(F32)
        zero = zero + swap(zero.astype(BF), "zh").astype(F32)
        zero = jnp.where(plan.z == 0, zero, 0.0)
        w_qkv_g = w_qkv_g.reshape(-1, 3, heads_w)
        zero = zero.reshape(-1, 2, HD)
        w_qkv_g = w_qkv_g + jnp.pad(zero, ((0, 0), (0, 1), (0, heads_w - HD)))
        weight_grads[l] = (w_qkv_g, jnp.transpose(w_out_t), w_up_g, jnp.transpose(w_down_t))

        hot = (lax.broadcasted_iota(jnp.int32, (mp, 1), 0) == mine).astype(F32)
        gq = hot * g_bext[None, :heads_w]
        gv = hot * g_bext[None, 2 * heads_w : 3 * heads_w]
        gq = gq.reshape(-1).at[:HD].add(g_bext[3 * heads_w : 3 * heads_w + HD])
        g_bup = g_bup.reshape(mp, ffq)
        g_bup = jnp.stack([pick(g_bup, (plan.z - q) % mp, 0) for q in range(mp)])
        vec[l] = jnp.concatenate(
            [
                g_gain1, g_gain2, g_shift1, g_shift2, g_bout, g_bdown,
                gq, gv.reshape(-1), g_bup.reshape(-1), jnp.full((128,), shares[l] / mp),
            ]
        )

    dx = plan.relabel(g.astype(BF)).astype(F32)
    total = lax.psum(jnp.stack([vec[l] for l in range(layers)]), dims + ("zh", "zl"))
    n = d_model
    g_gain = total[:, : 2 * n].reshape(layers, 2, n)
    g_bias = total[:, 2 * n : 4 * n].reshape(layers, 2, n)
    g_bout = total[:, 4 * n : 5 * n]
    g_bdown = total[:, 5 * n : 6 * n]
    at = 6 * n
    g_bqv = total[:, at : at + 2 * mp * heads_w].reshape(layers, 2, mp, heads_w)
    at += 2 * mp * heads_w
    g_bup = total[:, at : at + mp * ffq].reshape(layers, mp, ffq)
    at += mp * ffq
    key_share = total[:, at] / (dp * (rows * mp))
    return (
        y[None, :rl],
        y[None, rl:],
        dx[None, :rl],
        dx[None, rl:],
        g_gain,
        g_bias,
        jnp.stack([weight_grads[l][0] for l in range(layers)]),
        pick(g_bqv, plan.z, 2),
        jnp.stack([weight_grads[l][1] for l in range(layers)]),
        g_bout,
        jnp.stack([weight_grads[l][2] for l in range(layers)]),
        pick(g_bup, plan.z, 1),
        jnp.stack([weight_grads[l][3] for l in range(layers)]),
        g_bdown,
        key_share,
    )


MESH = pl.DeviceIdType.MESH
ANY = pl.BlockSpec(memory_space=pl.ANY)


class Net:
    def __init__(self, dims):
        self.dims = dims
        self.y, self.x, self.c = (lax.axis_index(ax) for ax in dims)
        self.zh, self.zl = lax.axis_index("zh"), lax.axis_index("zl")
        self.z = 2 * self.zh + self.zl
        self.yx = 2 * self.y + self.x
        self.me = 2 * self.c + self.zl
        self.moves = self.c != self.zh

    def group(self, delta):
        return {self.dims[2]: self.c ^ (delta >> 1), "zl": self.zl ^ (delta & 1)}

    def member(self, m):
        return {self.dims[2]: m >> 1, "zl": m & 1}

    def plane(self, e):
        return {self.dims[0]: self.y ^ (e >> 1), self.dims[1]: self.x ^ (e & 1)}

    def line(self, r):
        to = (self.z + r) % 4
        return {"zh": to // 2, "zl": to % 2}

    def partner(self):
        return {self.dims[2]: 1 - self.c, "zh": 1 - self.zh}

    def greet(self, peers):
        barrier = pltpu.get_barrier_semaphore()
        for peer in peers:
            pl.semaphore_signal(barrier, inc=1, device_id=peer, device_id_type=MESH)
        pl.semaphore_wait(barrier, len(peers))


class Sems:
    def __init__(self, ssem, rsem):
        self.ssem, self.rsem, self.used = ssem, rsem, 0

    def copy(self, src, dst, device):
        i = self.used
        self.used += 1
        assert i < self.ssem.shape[0]
        return send(src, dst, self.ssem.at[i], self.rsem.at[i], device)


class Batch:
    def __init__(self, copies, when=None):
        self.copies, self.when = copies, when

    def _do(self, f):
        if self.when is None:
            f()
        else:
            pl.when(self.when)(f)

    def start(self):
        self._do(lambda: [c.start() for c in self.copies] and None)

    def recv(self):
        self._do(lambda: [c.wait_recv() for c in self.copies] and None)

    def sent(self):
        self._do(lambda: [c.wait_send() for c in self.copies] and None)

    def end(self):
        self.recv()
        self.sent()


def aligned(v, n=16):
    return pl.multiple_of(v, n)


class Projections:
    def __init__(self, net, sems, wq, w0, qland, zland, ext):
        self.net, self.wq, self.w0, self.qland, self.zland, self.ext = net, wq, w0, qland, zland, ext
        rows = qland.shape[1]
        here = pl.ds(aligned(net.yx * rows), rows)
        at = net.yx
        self.q1 = Batch([sems.copy(wq.at[here], qland.at[at], net.partner())], net.moves)
        self.q2 = Batch([sems.copy(qland.at[at], qland.at[at], net.plane(e)) for e in (1, 2, 3)], net.moves)
        self.h1 = []
        for r in (1, 2, 3):
            copy = sems.copy(w0.at[here], zland.at[at], net.line(r))
            self.h1.append(copy)
        self.h2 = Batch([sems.copy(zland.at[at], zland.at[at], net.plane(e)) for e in (1, 2, 3)], net.z != 0)

    def start(self):
        self.q1.start()

        @pl.when(self.net.z == 0)
        def _():
            for copy in self.h1:
                copy.start()

    def forward(self):
        self.q1.recv()
        self.q2.start()
        for r in (1, 2, 3):
            pl.when(self.net.z == r)(lambda: self.h1[r - 1].wait_recv())
        self.h2.start()

    def finish(self):
        rows, n = self.qland.shape[1:]
        self.q2.recv()
        self.h2.recv()

        @pl.when(self.net.moves)
        def _():
            for k in range(4):
                self.ext[k * rows : (k + 1) * rows, :n] = self.qland[k]

        @pl.when(jnp.logical_not(self.net.moves))
        def _():
            self.ext[:, :n] = self.wq[...]

        @pl.when(self.net.z != 0)
        def _():
            for k in range(4):
                self.ext[k * rows : (k + 1) * rows, n:] = self.zland[k]

        @pl.when(self.net.z == 0)
        def _():
            self.ext[:, n:] = self.w0[...]

        self.q1.sent()
        self.q2.sent()
        self.h2.sent()

        @pl.when(self.net.z == 0)
        def _():
            for copy in self.h1:
                copy.wait_send()


def project_part(net, sems, resid, gain, shift, w, bias, fl, fs, pj_l, pj_s):
    nl, ns = fl.shape[0] // 4, fs.shape[0] // 4
    half = nl // 2
    parts = ((fs, pj_s, ns, 0, ns, nl), (fl, pj_l, nl, 0, half, 0), (fl, pj_l, nl, half, half, half))
    me = net.me

    def rows(k, m):
        ref, _, n, at, size, _ = parts[k]
        return ref.at[pl.ds(aligned(m * n + at), size)]

    def compute(k, m):
        ref, out, n, at, size, _ = parts[k]
        here = pl.ds(aligned(m * n + at), size)
        out[here] = (mm(ref[here], w[...]) + bias[...]).astype(jnp.bfloat16)

    chip = [sems.copy(rows(k, me), rows(k, me), net.group(1)) for k in range(3)]
    core = [sems.copy(rows(k, me), rows(k, me), net.group(2)) for k in range(3)]
    over = [sems.copy(rows(k, me ^ 1), rows(k, me ^ 1), net.group(2)) for k in range(3)]
    for k in range(3):
        ref, _, n, at, size, src = parts[k]
        hat, _ = norm_rows(resid[src : src + size].astype(jnp.float32))
        ref[pl.ds(aligned(me * n + at), size)] = (hat * gain[...] + shift[...]).astype(jnp.bfloat16)
        chip[k].start()
        core[k].start()
    for k in range(3):
        compute(k, me)
    for k in range(3):
        core[k].wait_recv()
        compute(k, me ^ 2)
    for k in range(3):
        chip[k].wait_recv()
        over[k].start()
        compute(k, me ^ 1)
    for k in range(3):
        over[k].wait_recv()
        compute(k, me ^ 3)
    return chip + core + over


def attend_part(net, sems, xl, xs, att, ol, os, lsel, lses, cl, cs, land):
    nl, ns = xl.shape[0] // 4, xs.shape[0] // 4
    w = ol.shape[1]
    base = sems.used
    sems.used += 8

    def part(k):
        return ((ol, nl, 0), (os, ns, nl))[k]

    def copy(k, m):
        src, n, at = part(k)
        return send(
            src.at[pl.ds(m * n, n)],
            land.at[net.me, pl.ds(at, n)],
            sems.ssem.at[base + 4 * k + m],
            sems.rsem.at[base + 4 * k + net.me],
            net.member(m),
        )

    def arrived(k, m):
        src, n, at = part(k)
        i = base + 4 * k + m
        return send(src.at[pl.ds(0, n)], land.at[m, pl.ds(at, n)], sems.ssem.at[i], sems.rsem.at[i], net.member(m))

    def start(k, m):
        src, n, at = part(k)

        @pl.when(net.me != m)
        def _():
            copy(k, m).start()

        @pl.when(net.me == m)
        def _():
            land[m, at : at + n] = src[m * n : (m + 1) * n]

    def started(k, n):
        def done(b):
            for m in range(b * BR // n, (b + 1) * BR // n):
                start(k, m)

        return done

    fwd_one(xs, os, lses, cs, started(1, ns))
    fwd_one(xl, ol, lsel, cl, started(0, nl))
    for m in range(4):

        @pl.when(net.me != m)
        def _():
            for k in range(2):
                copy(k, m).wait_send()
                arrived(k, m).wait_recv()

    for m in range(4):
        att[:, m * w : (m + 1) * w] = land[m]


def gelu_pair(u):
    k = 0.7978845608028654
    sq = u * u
    t = jnp.tanh(u * (k + k * 0.044715 * sq))
    h = 0.5 * (1.0 + t)
    act = u * h
    slope = h + act * (1.0 - t) * (k + 3 * k * 0.044715 * sq)
    return act, slope


TN = (((0,), (0,)), ((), ()))


def ext_scatter(net, sems, dw, land):
    return [sems.copy(dw.at[net.yx ^ e], land.at[e - 1], net.plane(e)) for e in (1, 2, 3)]


class FinishLine:
    def __init__(self, net, sems, s, so, land, oland, own=None):
        self.own = s.at[0] if own is None else own
        self.net, self.s, self.so, self.land, self.oland = net, s, so, land, oland
        self.main = Batch([sems.copy(s.at[r], land.at[3 - r], net.line(r)) for r in (1, 2, 3)])
        self.out = []
        for r in (1, 2, 3):
            to = (net.z + r) % 4
            copy = sems.copy(so.at[to % 2], oland.at[3 - r], net.line(r))
            self.out.append((copy, to // 2 == net.c))
        self.owner = net.zh == net.c

    def start(self):
        self.main.start()
        for copy, use in self.out:
            pl.when(use)(copy.start)

    def finish(self, f_out, fo_out):
        self.main.recv()
        f_out[...] = (
            self.own[...].astype(jnp.float32)
            + self.land[0].astype(jnp.float32)
            + self.land[1].astype(jnp.float32)
            + self.land[2].astype(jnp.float32)
        ).astype(f_out.dtype)

        @pl.when(self.owner)
        def _():
            for copy, _ in self.out:
                copy.wait_recv()
            fo_out[...] = (
                self.so[self.net.zl].astype(jnp.float32)
                + self.oland[0].astype(jnp.float32)
                + self.oland[1].astype(jnp.float32)
                + self.oland[2].astype(jnp.float32)
            ).astype(fo_out.dtype)

        @pl.when(jnp.logical_not(self.owner))
        def _():
            fo_out[...] = jnp.zeros_like(fo_out)

        self.main.sent()
        for copy, use in self.out:
            pl.when(use)(copy.wait_send)


class Local:
    def __init__(self, sem):
        self.sem, self.copies = sem, []

    def start(self, src, dst):
        assert len(self.copies) < self.sem.shape[0]
        copy = pltpu.make_async_copy(src, dst, self.sem.at[len(self.copies)])
        self.copies.append(copy)
        copy.start()
        return copy


class LineWeights:
    def __init__(self, net, sems, layer, w_up, w_down, zup, zdn):
        rows, n = zup.shape[0], zup.shape[1] // 3
        part = zdn.shape[1]
        own = (
            w_up.at[layer, pl.ds(aligned(net.yx * rows), rows), pl.ds(aligned(net.c * n, 128), n)],
            w_down.at[layer, pl.ds(aligned(net.c * n + net.yx * part), part)],
        )

        def slot(k):
            return (zup.at[:, pl.ds(k * n, n)], zdn.at[k])

        self.steps = []
        for s in (1, 2, 3):
            up_src = own if s == 1 else slot(4 - s)
            dn_src = own if s == 1 else slot(s - 2)
            up = [sems.copy(up_src[i], slot(3 - s)[i], net.line(1)) for i in range(2)]
            dn = [sems.copy(dn_src[i], slot(s - 1)[i], net.line(3)) for i in range(2)]
            sends_up = jnp.logical_and(net.z >= s - 1, net.z <= 2)
            sends_dn = jnp.logical_and(net.z <= 4 - s, net.z >= 1)
            self.steps.append(((up, sends_up, net.z >= s), (dn, sends_dn, net.z + s <= 3)))

    def start(self, s):
        for copies, sends, _ in self.steps[s]:
            Batch(copies, sends).start()

    def recv(self, s):
        for copies, _, gets in self.steps[s]:
            Batch(copies, gets).recv()

    def sent(self):
        for step in self.steps:
            for copies, sends, _ in step:
                Batch(copies, sends).sent()


def plane_weights(net, sems, zup, zdn, wup, wdn):
    rows, n = zup.shape[0], zup.shape[1] // 3
    part = zdn.shape[1]
    at_up = pl.ds(aligned(net.yx * rows), rows)
    at_dn = pl.ds(aligned(net.yx * part), part)
    out = []
    for e in (1, 2, 3):
        out.append(sems.copy(zup, wup.at[at_up, pl.ds(n, 3 * n)], net.plane(e)))
        out.append(sems.copy(zdn, wdn.at[pl.ds(1, 3), at_dn], net.plane(e)))
    return Batch(out)


def first_x(dims, R):
    net, sems = Net(dims), Sems(R.ssem, R.rsem)
    nl = R.xl.shape[0]
    moved = Batch(
        [
            sems.copy(R.xl, R.xr.at[pl.ds(0, nl)], net.partner()),
            sems.copy(R.xs, R.xr.at[pl.ds(nl, R.xs.shape[0])], net.partner()),
        ],
        net.moves,
    )
    proj = Projections(net, sems, R.wq, R.w0, R.qland, R.zland, R.ext)
    tiny = Batch([sems.copy(R.small, R.smalls.at[4 - r], net.line(r)) for r in (1, 2, 3)])
    weights = LineWeights(net, sems, 0, R.w_up, R.w_down, R.zup, R.zdn)
    net.greet([net.partner()] + [net.line(r) for r in (1, 2, 3)] + [net.plane(e) for e in (1, 2, 3)])
    proj.start()
    moved.start()
    tiny.start()
    weights.start(0)
    R.smalls[0] = R.small[...]

    @pl.when(jnp.logical_not(net.moves))
    def _():
        R.xr[:nl] = R.xl[...]
        R.xr[nl:] = R.xs[...]

    proj.forward()
    weights.recv(0)
    weights.start(1)
    proj.finish()
    weights.recv(1)
    weights.start(2)
    moved.end()
    tiny.end()
    weights.recv(2)
    weights.sent()


def forward_x(dims, first, last, R):
    net, sems, loc = Net(dims), Sems(R.ssem, R.rsem), Local(R.lsem)
    n, d = R.resid.shape
    f = R.wup.shape[1] // 4
    layer = 0 if first else 1
    weights = plane_weights(net, sems, R.zup, R.zdn, R.wup, R.wdn)
    peers = [net.group(2), net.group(3), net.partner()]
    peers += [net.plane(e) for e in (1, 2, 3)] + [net.line(r) for r in (1, 2, 3)]
    if first:
        proj = Projections(net, sems, R.wq, R.w0, R.qland, R.zland, R.ext_next)
        later = LineWeights(net, sems, 1, R.w_up, R.w_down, R.zup_next, R.zdn_next)
    else:
        nl = R.dl.shape[0]
        moved = Batch(
            [
                sems.copy(R.dl, R.dyr.at[pl.ds(0, nl)], net.partner()),
                sems.copy(R.ds, R.dyr.at[pl.ds(nl, R.ds.shape[0])], net.partner()),
            ],
            net.moves,
        )
    there = sems.copy(R.n2.at[pl.ds(0, n)], R.n2.at[pl.ds(n, n)], net.group(2))
    back = sems.copy(R.out, R.got, net.group(2))
    net.greet(peers)
    weights.start()
    own = [
        loc.start(R.w_up.at[layer, :, pl.ds(aligned(net.c * f, 128), f)], R.wup.at[:, pl.ds(0, f)]),
        loc.start(R.w_down.at[layer, pl.ds(aligned(net.c * f), f)], R.wdn.at[0]),
    ]
    pending = project_part(
        net, sems, R.resid, R.gain1, R.shift1, R.ext, R.bias, R.fl, R.fs, R.pj_l, R.pj_s
    )
    if first:
        proj.start()
    else:
        moved.start()

        @pl.when(jnp.logical_not(net.moves))
        def _():
            R.dyr[:nl] = R.dl[...]
            R.dyr[nl:] = R.ds[...]

    for src, dst in ((R.fl, R.fl_o), (R.fs, R.fs_o), (R.pj_l, R.pjl_o), (R.pj_s, R.pjs_o)):
        loc.start(src, dst)
    rows, part = R.zup.shape[0], R.zdn.shape[1]
    R.wup[pl.ds(aligned(net.yx * rows), rows), f:] = R.zup[...]
    for k in range(3):
        R.wdn[k + 1, pl.ds(aligned(net.yx * part), part)] = R.zdn[k]
    if first:
        later.start(0)
    attend_part(
        net, sems, R.pj_l, R.pj_s, R.att, R.ol, R.os, R.lsel, R.lses, R.cl, R.cs, R.land
    )
    if first:
        later.recv(0)
        later.start(1)
        proj.forward()
    share = jnp.zeros((1, 1), jnp.float32)
    for carry in (R.cl, R.cs):
        size = carry.shape[1]
        left = (size - 1 - lax.broadcasted_iota(jnp.int32, (1, size), 1)).astype(jnp.float32)
        ratio = carry[size // BR : size // BR + 1] / jnp.maximum(left, 1.0)
        t = 4.0 * (ratio - R.limit[:1, :1])
        share = share + jnp.sum(1.0 / (1.0 + jnp.exp(-t)), axis=1, keepdims=True)
    R.share[...] = jnp.broadcast_to(share * 0.25, R.share.shape)
    half = n // 2
    for i in range(2):
        at = slice(i * half, (i + 1) * half)
        R.middle[at] = R.resid[at].astype(jnp.float32) + mm(R.att[at], R.wout[...]) + R.bout[...]
        hat, _ = norm_rows(R.middle[at])
        R.n2[at] = (hat * R.gain2[...] + R.shift2[...]).astype(jnp.bfloat16)
    there.start()
    weights.recv()
    for copy in own:
        copy.wait()
    for src, dst in ((R.wup, R.wup_o), (R.wdn, R.wdn_o)):
        loc.start(src, dst)

    def hidden(at):
        u = mm(R.n2[at], R.wup[...]) + R.bup[...]
        a, s = gelu_pair(u)
        low = a.astype(jnp.bfloat16)
        for i in range(2):
            R.act[i, at] = low[:, 2 * i * f : 2 * (i + 1) * f]
            loc.start(R.act.at[i, at], R.act_o.at[i, at])
        R.slope[at] = s.astype(jnp.bfloat16)
        loc.start(R.slope.at[at], R.slope_o.at[at])

    def down(at):
        return mm(R.act[0, at], R.wdn[0:2].reshape(2 * f, d)) + mm(
            R.act[1, at], R.wdn[2:4].reshape(2 * f, d)
        )

    quarter = n // 2
    for i in range(2):
        hidden(slice(i * quarter, (i + 1) * quarter))
    if first:
        later.recv(1)
        later.start(2)
    there.wait_recv()
    for i in range(2):
        hidden(slice(n + i * quarter, n + (i + 1) * quarter))
    for i in range(2):
        R.out[i * half : (i + 1) * half] = down(slice(n + i * half, n + (i + 1) * half)).astype(
            jnp.bfloat16
        )
    back.start()
    for i in range(2):
        at = slice(i * half, (i + 1) * half)
        R.new[at] = R.middle[at] + down(at) + R.bdown[...]
    back.wait_recv()
    R.new[...] += R.got[...].astype(jnp.float32)
    if last:
        R.y[...] = R.new[...].astype(jnp.bfloat16)
    there.wait_send()
    back.wait_send()
    for copy in pending:
        copy.wait_send()
    weights.sent()
    if first:
        proj.finish()
        later.recv(2)
        later.sent()
    else:
        moved.end()
    for copy in loc.copies[2:]:
        copy.wait()


def backward_x(dims, last, R):
    net, sems, loc = Net(dims), Sems(R.ssem, R.rsem), Local(R.lsem)
    f32, bf = jnp.float32, jnp.bfloat16
    n, d = R.g.shape
    f = R.wup.shape[1] // 4
    nl, ns = R.pj_l.shape[0] // 4, R.pj_s.shape[0] // 4
    wid = R.ol.shape[1]
    me, yx = net.me, net.yx
    there = sems.copy(R.gm.at[pl.ds(0, n)], R.gm.at[pl.ds(n, n)], net.group(2))
    back = sems.copy(R.out.at[0], R.got.at[0], net.group(2))
    cross = sems.copy(R.oself, R.olands, net.group(2))
    big_dn = Batch([sems.copy(R.ddn.at[yx ^ e], R.rdn.at[e - 1], net.plane(e)) for e in (1, 2, 3)])
    big_up = Batch([sems.copy(R.dup.at[yx ^ e], R.rup.at[e - 1], net.plane(e)) for e in (1, 2, 3)])
    big_out = Batch([sems.copy(R.dout.at[yx ^ e], R.rout.at[e - 1], net.plane(e)) for e in (1, 2, 3)])
    base = sems.used
    sems.used += 8
    peers = [net.group(d_) for d_ in (1, 2, 3)] + [net.plane(e) for e in (1, 2, 3)]
    if last:
        moved = Batch([sems.copy(R.y, R.yr, net.partner())], net.moves)
        peers += [net.partner()]
    else:
        carry = FinishLine(net, sems, R.s_in, R.so_in, R.fland, R.foland, R.s_own)
        ext = Batch(ext_scatter(net, sems, R.dq_in, R.qland) + ext_scatter(net, sems, R.d0_in, R.zland))
        ext_line = ExtLine(net, sems, R.q_sum, R.z_sum, R.qline, R.zline)
        low = Batch([sems.copy(R.s.at[r, 1], R.dnland.at[3 - r], net.line(r)) for r in (1, 2, 3)])
        peers += [net.line(2), net.line(4 - net.zl * 2 - 1)]
    R.gm[:n] = R.g[...].astype(bf)
    net.greet(peers)
    there.start()
    fetched = [loc.start(R.act.at[i], R.buf.at[pl.ds(i * 2 * n, 2 * n)]) for i in range(2)]
    for src, dst in ((R.pjl_i, R.pj_l), (R.pjs_i, R.pj_s), (R.ext_i, R.ext)):
        loc.start(src, dst)
    if last:
        moved.start()

        @pl.when(jnp.logical_not(net.moves))
        def _():
            R.yr[...] = R.y[...]

    else:
        ext.start()
        carry.start()
        for src, dst in ((R.s_in.at[0], R.s_own), (R.dq_in.at[yx], R.dq_own), (R.d0_in.at[yx], R.d0_own)):
            loc.start(src, dst)
    R.rows[...] = jnp.zeros_like(R.rows)
    R.rows[5:6] = jnp.sum(R.g[...].astype(f32), axis=0, keepdims=True)
    half = n // 2
    wdn2 = lambda: R.wdn[...].reshape(4 * f, d)

    def hidden(at):
        u = mm(R.gm[at], wdn2(), NT)
        R.gu[at] = (u * R.slope[at].astype(f32)).astype(bf)

    for i in range(2):
        hidden(slice(i * half, (i + 1) * half))
    there.wait_recv()
    for i in range(2):
        hidden(slice(n + i * half, n + (i + 1) * half))
    for i in range(2):
        R.out[0, i * half : (i + 1) * half] = mm(
            R.gu[n + i * half : n + (i + 1) * half], R.wup[...], NT
        ).astype(bf)
    back.start()
    for i in range(2):
        R.mine[i * half : (i + 1) * half] = mm(R.gu[i * half : (i + 1) * half], R.wup[...], NT)
    chunk = d // 4

    for c in fetched:
        c.wait()
    for k in range(4):
        for i in range(2):
            t = mm(R.gm[:, k * chunk : (k + 1) * chunk], R.buf[i * 2 * n : (i + 1) * 2 * n], TN)
            t = t.astype(bf)
            R.ddn[k, 2 * i] = t[:, :f]
            R.ddn[k, 2 * i + 1] = t[:, f:]
    big_dn.start()
    fl, fs = R.buf.at[pl.ds(0, 4 * nl)], R.buf.at[pl.ds(4 * nl, 4 * ns)]
    late = [loc.start(R.fl_i, fl), loc.start(R.fs_i, fs)]
    back.wait_recv()
    gn = R.mine[...] + R.got[0].astype(f32)
    hat, inv = norm_rows(R.middle[...])
    gh = gn * R.gain2[...]
    a = jnp.mean(gh, axis=-1, keepdims=True)
    b = jnp.mean(gh * hat, axis=-1, keepdims=True)
    R.gmid[...] = R.g[...].astype(f32) + inv * (gh - a - hat * b)
    R.rows[1:2] = jnp.sum(gn * hat, axis=0, keepdims=True)
    R.rows[3:4] = jnp.sum(gn, axis=0, keepdims=True)
    R.rows[4:5] = jnp.sum(R.gmid[...], axis=0, keepdims=True)
    R.ga[...] = R.gmid[...].astype(bf)
    go = mm(R.ga[...], R.wout[...], NT).astype(bf)
    for m in range(4):
        R.outg[m] = go[:, m * wid : (m + 1) * wid]

    def part(k):
        return ((R.gl, nl, 0), (R.gs, ns, nl))[k]

    def copy(k, m):
        dst, size, at = part(k)
        return send(
            R.outg.at[m, pl.ds(at, size)],
            dst.at[pl.ds(aligned(me * size), size)],
            sems.ssem.at[base + 4 * k + m],
            sems.rsem.at[base + 4 * k + me],
            net.member(m),
        )

    def arrived(k, m):
        dst, size, at = part(k)
        i = base + 4 * k + m
        return send(
            R.outg.at[m, pl.ds(at, size)], dst.at[pl.ds(m * size, size)], sems.ssem.at[i], sems.rsem.at[i], net.member(m)
        )

    for k in (1, 0):
        for m in range(4):
            dst, size, at = part(k)

            @pl.when(me != m)
            def _():
                copy(k, m).start()

            @pl.when(me == m)
            def _():
                dst[m * size : (m + 1) * size] = R.outg[m, at : at + size]

    e = R.att.shape[1] // 2
    other = R.att[:, pl.ds(aligned((1 - net.c) * e, 128), e)]
    R.oself[...] = mm(R.ga[...], other, TN).astype(bf)
    cross.start()
    for k in range(4):
        t = mm(R.n2[:, k * chunk : (k + 1) * chunk], R.gu[...], TN).astype(bf)
        for r in range(4):
            R.dup[k, r] = t[:, r * f : (r + 1) * f]
    big_up.start()
    bup = jnp.sum(R.gu[...].astype(f32), axis=0, keepdims=True)
    for c in range(2):

        @pl.when(net.c == c)
        def _():
            for r in range(4):
                R.rows[pl.ds(16 + (net.z + r) % 4, 1), c * f : (c + 1) * f] = bup[:, r * f : (r + 1) * f]

    own = mm(R.ga[...], R.att[:, pl.ds(aligned(net.c * e, 128), e)], TN)
    cross.wait_recv()
    own = (own + R.olands[...].astype(f32)).astype(bf)
    for k in range(4):
        R.dout[k] = own[k * chunk : (k + 1) * chunk]
    big_out.start()
    if not last:
        late.append(loc.start(R.resid, R.ga))
    done = [id(c) for c in fetched + late]
    for c in loc.copies:
        if id(c) not in done:
            c.wait()
    for k in (1, 0):
        for m in range(4):

            @pl.when(me != m)
            def _():
                arrived(k, m).wait_recv()

        if k:
            bwd_one(R.pj_s, R.gs, R.os, R.lses, R.cs, R.ds, R.acc, R.kt)
            if not last:
                ext.recv()
                for own_, lands, dst in ((R.dq_own, R.qland, R.q_sum), (R.d0_own, R.zland, R.z_sum)):
                    t = own_[...].astype(f32)
                    for i in range(3):
                        t = t + lands[i].astype(f32)
                    dst[...] = t.astype(bf)
                ext_line.start()
        else:
            bwd_one(R.pj_l, R.gl, R.ol, R.lsel, R.cl, R.dl, R.acc, R.kt)

    def add_up(own, land, i):
        for r in range(4):
            t = own[yx, r].astype(f32)
            for k in range(3):
                t = t + land[k, r].astype(f32)
            R.s[r, i] = t.astype(bf)

    big_dn.recv()
    add_up(R.ddn, R.rdn, 1)
    if not last:
        low.start()

    def partial(m):
        a = mm(R.dl[pl.ds(aligned(m * nl), nl)], R.ext[...], NT)
        b = mm(R.ds[pl.ds(aligned(m * ns), ns)], R.ext[...], NT)
        return jnp.concatenate([a, b], axis=0)

    back.wait_send()
    to_core = [sems.copy(R.out.at[k], R.got.at[k + 1], net.group(2)) for k in (0, 1)]
    to_chip = sems.copy(R.out.at[2], R.got.at[3], net.group(1))
    R.out[0] = partial(me ^ 3).astype(bf)
    to_core[0].start()
    R.mine[...] = partial(me ^ 1)
    to_core[0].wait_recv()
    R.out[2] = (R.mine[...] + R.got[1].astype(f32)).astype(bf)
    to_chip.start()
    R.out[1] = partial(me ^ 2).astype(bf)
    to_core[1].start()
    R.mine[...] = partial(me)
    nq = R.dq.shape[2]
    for c in late:
        c.wait()
    for k in range(4):
        at = slice(k * chunk, (k + 1) * chunk)
        both = mm(fl[:, at], R.dl[...], TN) + mm(fs[:, at], R.ds[...], TN)
        R.dq[k] = both[:, :nq].astype(bf)
        R.d0[k] = both[:, nq:].astype(bf)
    bsum = jnp.sum(R.dl[...].astype(f32), axis=0, keepdims=True) + jnp.sum(
        R.ds[...].astype(f32), axis=0, keepdims=True
    )
    R.rows[pl.ds(8 + me, 1), :wid] = bsum[:, :wid]
    R.rows[pl.ds(12 + me, 1), :wid] = bsum[:, 2 * wid : 3 * wid]
    R.rows[8:9, :HD] += bsum[:, nq : nq + HD]
    hat, inv = norm_rows(R.resid[...] if last else R.ga[...].astype(f32))
    to_core[1].wait_recv()
    to_chip.wait_recv()
    grad = R.mine[...] + R.got[2].astype(f32) + R.got[3].astype(f32)
    gh = grad * R.gain1[...]
    a = jnp.mean(gh, axis=-1, keepdims=True)
    b = jnp.mean(gh * hat, axis=-1, keepdims=True)
    R.g_new[...] = (R.gmid[...] + inv * (gh - a - hat * b)).astype(R.g_new.dtype)
    R.rows[0:1] = jnp.sum(grad * hat, axis=0, keepdims=True)
    R.rows[2:3] = jnp.sum(grad, axis=0, keepdims=True)
    for c in to_core + [to_chip, there, cross]:
        c.wait_send()
    for m in range(4):

        @pl.when(me != m)
        def _():
            for k in range(2):
                copy(k, m).wait_send()

    if last:
        moved.end()
    else:
        carry.finish(R.f_out, R.fo_out)
        ext.sent()
        ext_line.finish(R.q_out, R.z_out)
        low.recv()
        t = R.s[0, 1].astype(f32)
        for k in range(3):
            t = t + R.dnland[k].astype(f32)
        R.dn_out[...] = t.astype(bf)
        low.sent()

    big_up.recv()
    add_up(R.dup, R.rup, 0)
    big_out.recv()
    t = R.dout[yx].astype(f32)
    for k in range(3):
        t = t + R.rout[k].astype(f32)
    for i in range(2):
        R.so[i] = t[:, i * wid : (i + 1) * wid].astype(bf)
    big_dn.sent()
    big_up.sent()
    big_out.sent()


class ExtLine:
    def __init__(self, net, sems, q, z, qline, zline):
        self.net, self.q, self.z, self.qline, self.zline = net, q, z, qline, zline
        self.qsend = Batch([sems.copy(q, qline, net.line(2))], net.moves)
        self.stays = jnp.logical_not(net.moves)
        self.zsend = [sems.copy(z, zline.at[r - 1], net.line(r)) for r in (1, 2, 3)]

    def start(self):
        self.qsend.start()
        for r in (1, 2, 3):
            pl.when(self.net.z == 4 - r)(self.zsend[r - 1].start)

    def finish(self, q_out, z_out):
        f32 = jnp.float32
        q_out[...] = self.q[...].astype(q_out.dtype)
        z_out[...] = self.z[...].astype(z_out.dtype)

        @pl.when(self.stays)
        def _():
            self.qsend.copies[0].wait_recv()
            q_out[...] = (self.q[...].astype(f32) + self.qline[...].astype(f32)).astype(q_out.dtype)

        @pl.when(self.net.z == 0)
        def _():
            t = self.z[...].astype(f32)
            for r in (1, 2, 3):
                self.zsend[r - 1].wait_recv()
                t = t + self.zline[r - 1].astype(f32)
            z_out[...] = t.astype(z_out.dtype)

        self.qsend.sent()
        for r in (1, 2, 3):
            pl.when(self.net.z == 4 - r)(self.zsend[r - 1].wait_send)


def tail_x(axes, R):
    dims = axes[:-2]
    net, sems = Net(dims), Sems(R.ssem, R.rsem)
    f32, bf = jnp.float32, jnp.bfloat16
    moved = Batch([sems.copy(R.dx, R.dxr, net.partner())], net.moves)
    line = FinishLine(net, sems, R.s.at[:, pl.ds(0, 1)], R.so, R.land, R.oland)
    ext = Batch(ext_scatter(net, sems, R.dq, R.qland) + ext_scatter(net, sems, R.d0, R.zland))
    nv = len(axes)
    rounds = [{ax: 1 - lax.axis_index(ax)} for ax in axes]
    steps = [sems.copy(R.vland.at[i], R.vland.at[nv + 1 + i], peer) for i, peer in enumerate(rounds)]
    ext_line = ExtLine(net, sems, R.q_sum, R.z_sum, R.qline, R.zline)
    qrecv = jnp.logical_not(net.moves)
    cross = Batch(
        [sems.copy(R.fself, R.fland, net.group(2)), sems.copy(R.zself, R.zlands, net.group(2))]
    )
    owned = Batch(
        [sems.copy(R.oself, R.olands, net.group(2)), sems.copy(R.qself, R.qlands, net.group(2))],
        None,
    )
    net.greet(
        [net.partner(), net.group(2)]
        + [net.line(r) for r in (1, 2, 3)]
        + [net.plane(e) for e in (1, 2, 3)]
    )
    ext.start()
    line.start()
    moved.start()
    nr = R.rows0.shape[0]
    R.vland[0, :nr] = R.rows0[...]
    R.vland[0, nr:] = R.rows1[...]
    R.vland[0, 6:7] = jnp.broadcast_to(R.share0[:1, :1], (1, R.rows0.shape[1]))
    R.vland[0, nr + 6 : nr + 7] = jnp.broadcast_to(R.share1[:1, :1], (1, R.rows0.shape[1]))

    def step(i):
        steps[i].wait()
        R.vland[i + 1] = R.vland[i] + R.vland[nv + 1 + i]
        if i + 1 < nv:
            steps[i + 1].start()

    steps[0].start()
    step(0)
    step(1)
    ext.recv()
    yx = net.yx
    for own, lands, dst in ((R.dq, R.qland, R.q_sum), (R.d0, R.zland, R.z_sum)):
        t = own[yx].astype(f32)
        for e in range(3):
            t = t + lands[e].astype(f32)
        dst[...] = t.astype(bf)
    ext_line.start()
    step(2)
    step(3)
    step(4)
    nl = R.dx_l.shape[0]
    half = R.f0.shape[1] // 2
    theirs = pl.ds(aligned((1 - net.c) * half), half)
    ours = pl.ds(aligned(net.c * half), half)

    @pl.when(qrecv)
    def _():
        R.dx_l[...] = R.dx[:nl].astype(f32)
        R.dx_s[...] = R.dx[nl:].astype(f32)

    ext_line.finish(R.q0, R.z0)

    @pl.when(qrecv)
    def _():
        for l, q in ((0, R.q0), (1, R.q1)):
            R.qself[l] = q[theirs].astype(bf)
            R.gqkv[l] = q[ours].astype(f32)

    tot = R.vland.at[nv]
    for l in range(2):
        at = l * nr
        for i in range(2):
            R.g_gain[l, i : i + 1] = tot[at + i : at + i + 1]
            R.g_bias[l, i : i + 1] = tot[at + 2 + i : at + 3 + i]
            R.g_bqv[l, i : i + 1] = tot[pl.ds(at + 8 + 4 * i + net.z, 1), : R.g_bqv.shape[2]]
        R.g_bout[l : l + 1] = tot[at + 4 : at + 5]
        R.g_bdown[l : l + 1] = tot[at + 5 : at + 6]
        R.g_bup[l : l + 1] = tot[pl.ds(at + 16 + net.z, 1)]
        R.shares[l : l + 1] = tot[at + 6 : at + 7, :128]
    line.finish(R.f0, R.fo0)

    @pl.when(qrecv)
    def _():
        for l, fo in ((0, R.fo0), (1, R.fo1)):
            R.oself[l] = fo[theirs].astype(bf)
            R.gout[l] = jnp.transpose(fo[ours].astype(f32))
        for c in owned.copies:
            c.start()

    for l, fs in ((0, (R.f0.at[0], R.dn0)), (1, (R.f1.at[0], R.f1.at[1]))):
        for i in range(2):
            R.fself[l, i] = fs[i][theirs].astype(bf)
    for l, z in ((0, R.z0), (1, R.z1)):
        R.zself[l] = z[theirs].astype(bf)
    cross.start()
    n = R.f0.shape[2]
    for c in range(2):

        @pl.when(net.c == c)
        def _():
            for l, fs in ((0, (R.f0.at[0], R.dn0)), (1, (R.f1.at[0], R.f1.at[1]))):
                R.gup[l, :, c * n : (c + 1) * n] = fs[0][ours].astype(f32)
                R.gdn[l, c * n : (c + 1) * n] = jnp.transpose(fs[1][ours].astype(f32))

    cross.recv()
    for c in range(2):

        @pl.when(net.c != c)
        def _():
            for l in range(2):
                R.gup[l, :, c * n : (c + 1) * n] = R.fland[l, 0].astype(f32)
                R.gdn[l, c * n : (c + 1) * n] = jnp.transpose(R.fland[l, 1].astype(f32))

    @pl.when(net.moves)
    def _():
        for c in owned.copies:
            c.wait_recv()
        R.gqkv[...] = R.qlands[...].astype(f32)
        for l in range(2):
            R.gout[l] = jnp.transpose(R.olands[l].astype(f32))

    @pl.when(net.z == 0)
    def _():
        wid = R.gout.shape[1]
        for l, z in ((0, R.z0), (1, R.z1)):
            t = z[ours].astype(f32) + R.zlands[l].astype(f32)
            R.gqkv[l, :, :HD] += t[:, :HD]
            R.gqkv[l, :, wid : wid + HD] += t[:, HD:]

    moved.recv()

    @pl.when(net.moves)
    def _():
        R.dx_l[...] = R.dxr[:nl].astype(f32)
        R.dx_s[...] = R.dxr[nl:].astype(f32)

    pl.when(qrecv)(lambda: [c.wait_send() for c in owned.copies] and None)
    cross.sent()
    ext.sent()
    moved.sent()


def results_k(*refs):
    k = len(refs) // 2
    for src, dst in zip(refs[:k], refs[k:]):
        dst[...] = src[...]


def results(arrays):
    return pl.pallas_call(
        results_k,
        out_shape=tuple(jax.ShapeDtypeStruct(a.shape, a.dtype) for a in arrays),
        in_specs=[VMEM] * len(arrays),
        out_specs=(VMEM,) * len(arrays),
        compiler_params=pltpu.CompilerParams(vmem_limit_bytes=40 * 1024 * 1024),
        name="results_k",
    )(*arrays)


def run(kernel, static, ins, outs, scratch, ident, name, flops):
    names = list(ins) + list(outs) + list(scratch)

    def body_of(*refs):
        kernel(*static, types.SimpleNamespace(**dict(zip(names, refs))))

    res = pl.pallas_call(
        body_of,
        out_shape=tuple(jax.ShapeDtypeStruct(tuple(s), t) for s, t, _ in outs.values()),
        in_specs=[VMEM if v else ANY for _, v in ins.values()],
        out_specs=tuple(VMEM if v else ANY for _, _, v in outs.values()),
        scratch_shapes=list(scratch.values()),
        compiler_params=pltpu.CompilerParams(
            vmem_limit_bytes=60 * 1024 * 1024, collective_id=ident, has_side_effects=True
        ),
        cost_estimate=pl.CostEstimate(flops=flops, bytes_accessed=10**7, transcendentals=10**6),
        name=name,
    )(*[a for a, _ in ins.values()])
    return types.SimpleNamespace(**dict(zip(outs, res)))


def fast_body(
    dims, x_long, x_short, dy_long, dy_short, ln_gain, ln_bias, w_qkv, b_qv, w_out, b_out, w_up, b_up, w_down, b_down, threshold
):
    bf, f32 = jnp.bfloat16, jnp.float32
    layers, d = w_qkv.shape[0], w_qkv.shape[1]
    wid, ffq = w_qkv.shape[3], w_up.shape[2]
    rl, rs = x_long.shape[1], x_short.shape[1]
    n = rl + rs
    sl, ss = 4 * rl, 4 * rs
    nq, nx, n0 = 3 * wid, 3 * wid + 2 * HD, 2 * HD
    nh = wid // HD
    f = ffq // 2
    ff = 4 * f
    chunk, part = d // 4, f // 4
    half = chunk // 2
    net = Net(dims)
    axes = dims + ("zh", "zl")
    vm = lambda *s: pltpu.VMEM(tuple(s), bf)
    vf = lambda *s: pltpu.VMEM(tuple(s), f32)
    sem2 = lambda k: dict(ssem=DMA((k,)), rsem=DMA((k,)))

    wqs = [w_qkv[l].reshape(d, nq) for l in range(layers)]
    w0s = [w_qkv[l][:, :2, :HD].reshape(d, n0) for l in range(layers)]
    flat = jnp.concatenate([b_up.reshape(-1), b_qv.reshape(-1)])
    flat = jnp.pad(flat, (0, -flat.shape[0] % 4096)).reshape(16, -1)
    share_rows = wid // 8
    wo = lax.dynamic_slice_in_dim(w_out, (4 * net.y + 2 * net.x + net.c) * share_rows, share_rows, 1)
    wo = [lax.all_gather(wo[l], ("zh", "zl") + dims, axis=0, tiled=True) for l in range(layers)]

    lands = dict(qland=vm(4, chunk, nq), zland=vm(4, chunk, n0))
    P0 = run(
        first_x,
        (dims,),
        dict(xl=(x_long[0], 1), xs=(x_short[0], 1), wq=(wqs[0], 1), w0=(w0s[0], 1), small=(flat, 1), w_up=(w_up, 0), w_down=(w_down, 0)),
        dict(
            xr=((n, d), bf, 1), ext=((d, nx), bf, 1), smalls=((4,) + flat.shape, bf, 1),
            zup=((chunk, 3 * f), bf, 0), zdn=((3, part, d), bf, 0),
        ),
        dict(**lands, **sem2(32)),
        1,
        "first_x",
        10**9,
    )
    n_up = layers * ffq
    smalls = P0.smalls.reshape(4, -1)
    rel_bup = smalls[:, :n_up].reshape(4, layers, 2, f).astype(f32)
    rel_bup = lax.dynamic_index_in_dim(rel_bup, net.c, 2, keepdims=False)
    rel_bup = jnp.swapaxes(rel_bup, 0, 1).reshape(layers, ff)
    rel_bqv = smalls[:, n_up : n_up + layers * 2 * wid].reshape(4, layers, 2, wid).astype(f32)
    my_bqv = lax.dynamic_index_in_dim(rel_bqv, (net.me - net.z) % 4, 0, keepdims=False)
    zero_bq = lax.dynamic_index_in_dim(rel_bqv, (0 - net.z) % 4, 0, keepdims=False)[:, 0, :HD]
    none = jnp.zeros((layers, wid), f32)
    bias = jnp.concatenate([my_bqv[:, 0], none, my_bqv[:, 1], zero_bq, none[:, :HD]], axis=1)
    gain, shift = ln_gain.astype(f32), ln_bias.astype(f32)
    bo, bd = b_out.astype(f32), b_down.astype(f32)
    limits = jnp.broadcast_to((threshold.astype(f32) / 64.0)[:, None, None], (layers, 8, 128))

    resid, zup, zdn = P0.xr, P0.zup, P0.zdn
    exts = [P0.ext]
    saved = []
    for l in range(layers):
        first, last = l == 0, l == layers - 1
        ins = dict(
            resid=(resid, 1), gain1=(gain[l, :1], 1), shift1=(shift[l, :1], 1), gain2=(gain[l, 1:], 1), shift2=(shift[l, 1:], 1),
            ext=(exts[l], 1), bias=(bias[l : l + 1], 1), w_up=(w_up, 0), w_down=(w_down, 0), zup=(zup, 1), zdn=(zdn, 1),
            wout=(wo[l], 1), bout=(bo[l : l + 1], 1), bup=(rel_bup[l : l + 1], 1), bdown=(bd[l : l + 1], 1), limit=(limits[l], 1),
        )
        outs = dict(
            fl_o=((sl, d), bf, 0), fs_o=((ss, d), bf, 0), pjl_o=((sl, nx), bf, 0), pjs_o=((ss, nx), bf, 0),
            att=((n, 4 * wid), bf, 1), ol=((sl, wid), bf, 1), os=((ss, wid), bf, 1),
            lsel=((8, sl), f32, 1), lses=((8, ss), f32, 1), cl=((8, sl), f32, 1), cs=((8, ss), f32, 1),
            wup_o=((d, ff), bf, 0), wdn_o=((4, f, d), bf, 0), middle=((n, d), f32, 1), n2=((2 * n, d), bf, 1),
            act_o=((2, 2 * n, 2 * f), bf, 0), slope_o=((2 * n, ff), bf, 0), new=((n, d), f32, 1), share=((8, 128), f32, 1),
        )
        scratch = dict(
            fl=vm(sl, d), fs=vm(ss, d), pj_l=vm(sl, nx), pj_s=vm(ss, nx), wup=vm(d, ff), wdn=vm(4, f, d),
            act=vm(2, 2 * n, 2 * f), slope=vm(2 * n, ff), land=vm(4, n, wid), out=vm(n, d), got=vm(n, d), lsem=DMA((24,)),
            **sem2(48),
        )
        if first:
            ins.update(wq=(wqs[1], 1), w0=(w0s[1], 1))
            outs.update(ext_next=((d, nx), bf, 1), zup_next=((chunk, 3 * f), bf, 0), zdn_next=((3, part, d), bf, 0))
            scratch.update(lands)
        else:
            ins.update(dl=(dy_long[0], 1), ds=(dy_short[0], 1))
            outs.update(dyr=((n, d), bf, 1))
        if last:
            outs.update(y=((n, d), bf, 1))
        A = run(forward_x, (dims, first, last), ins, outs, scratch, 2 + l, "forward_x", 10**10)
        A.resid = resid
        saved.append(A)
        resid = A.new
        if first:
            exts.append(A.ext_next)
            zup, zdn = A.zup_next, A.zdn_next

    g = saved[-1].dyr
    back = [None] * layers
    B = None
    for l in reversed(range(layers)):
        A = saved[l]
        last = l == layers - 1
        ins = dict(
            g=(g, 1), att=(A.att, 1), wout=(wo[l], 1), gain1=(gain[l, :1], 1), gain2=(gain[l, 1:], 1), wup=(A.wup_o, 1), wdn=(A.wdn_o, 1),
            middle=(A.middle, 1), n2=(A.n2, 1), act=(A.act_o, 0), slope=(A.slope_o, 1), resid=(A.resid, int(last)),
            pjl_i=(A.pjl_o, 0), pjs_i=(A.pjs_o, 0), ext_i=(exts[l], 0), fl_i=(A.fl_o, 0), fs_i=(A.fs_o, 0),
            ol=(A.ol, 1), os=(A.os, 1), lsel=(A.lsel, 1), lses=(A.lses, 1), cl=(A.cl, 1), cs=(A.cs, 1),
        )
        outs = dict(
            g_new=((n, d), f32 if l else bf, 1), rows=((24, d), f32, 1), dq=((4, chunk, nq), bf, 1), d0=((4, chunk, n0), bf, 1),
            s=((4, 2, chunk, f), bf, 1), so=((2, chunk, wid), bf, 1),
        )
        scratch = dict(
            gm=vm(2 * n, d), gu=vm(2 * n, ff), mine=vf(n, d), out=vm(3, n, d), got=vm(4, n, d), gmid=vf(n, d), ga=vm(n, d),
            oself=vm(d, 2 * wid), olands=vm(d, 2 * wid), dup=vm(4, 4, chunk, f), ddn=vm(4, 4, chunk, f), dout=vm(4, chunk, 2 * wid),
            rup=vm(3, 4, chunk, f), rdn=vm(3, 4, chunk, f), rout=vm(3, chunk, 2 * wid),
            outg=vm(4, n, wid), gl=vm(sl, wid), gs=vm(ss, wid), pj_l=vm(sl, nx), pj_s=vm(ss, nx), ext=vm(d, nx),
            buf=vm(sl + ss, d), dl=vm(sl, nx), ds=vm(ss, nx), acc=vf(2 * nh + 1, sl, HD), kt=vm(nh + 1, HD, sl),
            lsem=DMA((12,)), **sem2(48),
        )
        if last:
            ins.update(y=(A.y, 1))
            outs.update(yr=((n, d), bf, 1))
        else:
            ins.update(s_in=(B.s, 0), so_in=(B.so, 1), dq_in=(B.dq, 0), d0_in=(B.d0, 0))
            outs.update(
                dn_out=((chunk, f), bf, 1), f_out=((2, chunk, f), bf, 1), fo_out=((chunk, wid), bf, 1), q_out=((chunk, nq), bf, 1), z_out=((chunk, n0), bf, 1)
            )
            scratch.update(
                q_sum=vm(chunk, nq), z_sum=vm(chunk, n0), qline=vm(chunk, nq), zline=vm(3, chunk, n0), dnland=vm(3, chunk, f),
                s_own=vm(2, chunk, f), dq_own=vm(chunk, nq), d0_own=vm(chunk, n0), fland=vm(3, 2, chunk, f), foland=vm(3, chunk, wid), qland=vm(3, chunk, nq), zland=vm(3, chunk, n0))
        B = run(backward_x, (dims, last), ins, outs, scratch, 6 + l, "backward_x", 2 * 10**10)
        back[l] = B
        g = B.g_new
        if last:
            y = B.yr

    nv = len(axes)
    T = run(
        tail_x,
        (axes,),
        dict(
            s=(B.s, 1), so=(B.so, 1), dq=(B.dq, 1), d0=(B.d0, 1), f1=(B.f_out, 1), fo1=(B.fo_out, 1), q1=(B.q_out, 1), z1=(B.z_out, 1),
            rows0=(back[0].rows, 1), dn0=(B.dn_out, 1), rows1=(back[1].rows, 1), share0=(saved[0].share, 1), share1=(saved[1].share, 1), dx=(g, 1),
        ),
        dict(
            gup=((2, half, ffq), f32, 1), gdn=((2, ffq, half), f32, 1), gout=((2, wid, half), f32, 1), gqkv=((2, half, nq), f32, 1),
            dx_l=((rl, d), f32, 1), dx_s=((rs, d), f32, 1), g_gain=((2, 2, d), f32, 1), g_bias=((2, 2, d), f32, 1),
            g_bqv=((2, 2, wid), f32, 1), g_bout=((2, d), f32, 1), g_bdown=((2, d), f32, 1), g_bup=((2, ffq), f32, 1),
            shares=((2, 128), f32, 1),
        ),
        dict(
            land=vm(3, 1, chunk, f), oland=vm(3, chunk, wid), f0=vf(1, chunk, f), fo0=vf(chunk, wid), q0=vf(chunk, nq), z0=vf(chunk, n0),
            qland=vm(3, chunk, nq), zland=vm(3, chunk, n0), q_sum=vm(chunk, nq), z_sum=vm(chunk, n0), qline=vm(chunk, nq),
            zline=vm(3, chunk, n0), fself=vm(2, 2, half, f), fland=vm(2, 2, half, f), oself=vm(2, half, wid),
            olands=vm(2, half, wid), qself=vm(2, half, nq), qlands=vm(2, half, nq), zself=vm(2, half, n0), zlands=vm(2, half, n0),
            vland=vf(2 * nv + 1, 48, d), dxr=vm(n, d), **sem2(32),
        ),
        10,
        "tail_x",
        10**9,
    )
    done = results(
        (
            T.dx_l, T.dx_s, T.g_gain, T.g_bias, T.g_bqv, T.gout, T.g_bout, T.gup, T.g_bup, T.gdn, T.g_bdown
        )
    )
    dx_l, dx_s, g_gain, g_bias, g_bqv, gout, g_bout, gup, g_bup, gdn, g_bdown = done
    return (
        y[None, :rl], y[None, rl:], dx_l[None], dx_s[None], g_gain, g_bias, T.gqkv.reshape(layers, half, 3, wid),
        g_bqv, gout, g_bout, gup, g_bup, gdn, g_bdown, T.shares[:, 0] / (8 * 4 * n),
    )


def solution(mesh):
    dp, mp = mesh.shape["dp"], mesh.shape["mp"]
    bits = dp.bit_length() - 1
    dims = tuple(f"d{i}" for i in range(bits))
    fine = Mesh(mesh.devices.reshape((2,) * bits + (2, mp // 2)), dims + ("zh", "zl"))
    z = ("zh", "zl")
    in_specs = (
        P(dims, z, None), P(dims, z, None), P(dims, z, None), P(dims, z, None),
        P(), P(), P(None, None, None, z), P(None, None, z), P(None, z, None), P(),
        P(None, None, z), P(None, z), P(None, z, None), P(), P(),
    )
    out_specs = (
        P(dims, z, None), P(dims, z, None), P(dims, z, None), P(dims, z, None),
        P(), P(), P(None, dims, None, z), P(None, None, z), P(None, z, dims), P(),
        P(None, dims, z), P(None, z), P(None, z, dims), P(), P(),
    )
    run = functools.partial(fast_body, dims) if dp == 8 else functools.partial(body, dims, dp, mp)
    return jax.shard_map(
        run, mesh=fine, in_specs=in_specs, out_specs=out_specs, check_vma=False
    )
```

```python
import functools
import types

import jax, jax.numpy as jnp
from jax import lax
from jax.experimental import pallas as pl
from jax.experimental.pallas import tpu as pltpu
from jax.sharding import Mesh
from jax.sharding import PartitionSpec as P

HD = 64
BR = 256
BIG = 1e30
NT = (((1,), (1,)), ((), ()))
NN = (((1,), (0,)), ((), ()))


def mm(a, b, dims=NN):
    return lax.dot_general(a, b, dims, preferred_element_type=jnp.float32)


def halves(v):
    hi = v.astype(jnp.bfloat16)
    lo = (v - hi.astype(jnp.float32)).astype(jnp.bfloat16)
    return hi, lo


def softplus(v):
    return jnp.maximum(v, 0.0) + jnp.log(1.0 + jnp.exp(-jnp.abs(v)))


def fwd_one(x_ref, o_ref, lse_ref, carry_ref, done=None):
    size = x_ref.shape[0]
    nh = (x_ref.shape[1] - 2 * HD) // (3 * HD)
    w = nh * HD
    nb = size // BR
    first = lax.broadcasted_iota(jnp.int32, (BR, BR), 0)
    second = lax.broadcasted_iota(jnp.int32, (BR, BR), 1)
    tri = (first > second).astype(jnp.bfloat16)
    lanes = lax.broadcasted_iota(jnp.int32, (BR, 128), 1)
    lse_ref[...] = jnp.zeros_like(lse_ref)
    carry_ref[...] = jnp.zeros_like(carry_ref)
    for b in range(nb):
        rows = pl.ds(b * BR, BR)
        q0 = x_ref[rows, 3 * w : 3 * w + HD] * 0.125
        pens = []
        for c in range(b + 1):
            cols = pl.ds(c * BR, BR)
            sp = softplus(mm(q0, x_ref[cols, 3 * w + HD : 3 * w + 2 * HD], NT))
            if c == b:
                keep = first > second
                if c == 0:
                    keep = jnp.logical_and(keep, second >= 1)
                sp = jnp.where(keep, sp, 0.0)
            elif c == 0:
                sp = jnp.where(second >= 1, sp, 0.0)
            hi, lo = halves(sp)
            pen = mm(tri, hi) + mm(tri, lo) + carry_ref[b : b + 1, cols]
            carry_ref[b + 1 : b + 2, cols] = pen[BR - 1 :] + sp[BR - 1 :]
            if c == b:
                pen = jnp.where(first >= second, pen, BIG)
            pens.append(pen)
        stats = jnp.zeros((BR, 128), jnp.float32)
        for h in range(nh):
            qh = x_ref[rows, h * HD : (h + 1) * HD] * 0.125
            scores = [
                mm(qh, x_ref[c * BR : (c + 1) * BR, w + h * HD : w + (h + 1) * HD], NT) - pens[c]
                for c in range(b + 1)
            ]
            top = scores[0]
            for s in scores[1:]:
                top = jnp.maximum(top, s)
            top = jnp.max(top, axis=1, keepdims=True)
            total = None
            acc = None
            for c in range(b + 1):
                e = jnp.exp(scores[c] - top)
                total = e if total is None else total + e
                part = mm(
                    e.astype(jnp.bfloat16),
                    x_ref[c * BR : (c + 1) * BR, 2 * w + h * HD : 2 * w + (h + 1) * HD],
                )
                acc = part if acc is None else acc + part
            total = jnp.sum(total, axis=1, keepdims=True)
            o_ref[rows, h * HD : (h + 1) * HD] = (acc / total).astype(jnp.bfloat16)
            stats = jnp.where(lanes == h, top + jnp.log(total), stats)
        lse_ref[:, rows] = jnp.transpose(stats)[:8]
        if done is not None:
            done(b)


def bwd_one(x_ref, g_ref, o_ref, lse_ref, carry_ref, d_ref, acc, kt, midway=None):
    size = x_ref.shape[0]
    nh = (x_ref.shape[1] - 2 * HD) // (3 * HD)
    w = nh * HD
    nb = size // BR
    jj = lax.broadcasted_iota(jnp.int32, (BR, BR), 0)
    ii = lax.broadcasted_iota(jnp.int32, (BR, BR), 1)
    below = (jj < ii).astype(jnp.bfloat16)
    above = (jj > ii).astype(jnp.bfloat16)
    ones = jnp.ones((8, HD), jnp.bfloat16)
    for h in range(nh + 1):
        lo = 3 * w + HD if h == nh else w + h * HD
        kt[h, :, :size] = jnp.transpose(x_ref[:, lo : lo + HD].astype(jnp.float32)).astype(
            jnp.bfloat16
        )
    later = [None] * nb
    for b in reversed(range(nb)):
        rows = pl.ds(b * BR, BR)
        q0 = x_ref[rows, 3 * w : 3 * w + HD] * 0.125
        pens, sigs, sums = [], [], [None] * (b + 1)
        for c in range(b + 1):
            sel = mm(x_ref[c * BR : (c + 1) * BR, 3 * w + HD : 3 * w + 2 * HD], q0, NT)
            small = jnp.exp(-jnp.abs(sel))
            sp = jnp.maximum(sel, 0.0) + jnp.log(1.0 + small)
            sig = jnp.where(sel >= 0, 1.0, small) / (1.0 + small)
            if c == b or c == 0:
                keep = None
                if c == b:
                    keep = ii > jj
                if c == 0:
                    keep = jj >= 1 if keep is None else jnp.logical_and(keep, jj >= 1)
                sp = jnp.where(keep, sp, 0.0)
                sig = jnp.where(keep, sig, 0.0)
            hi, lo = halves(sp)
            start = jnp.transpose(
                jnp.broadcast_to(carry_ref[b : b + 1, c * BR : (c + 1) * BR], (128, BR))
            )
            pen = mm(hi, below) + mm(lo, below) + start[:, :1]
            if c == b:
                pen = jnp.where(ii >= jj, pen, BIG)
            pens.append(pen)
            sigs.append(sig)
        for h in range(nh):
            qh = x_ref[rows, h * HD : (h + 1) * HD] * 0.125
            gh = g_ref[rows, h * HD : (h + 1) * HD]
            prod = gh.astype(jnp.float32) * o_ref[rows, h * HD : (h + 1) * HD].astype(jnp.float32)
            phi, plo = halves(prod)
            delta = (mm(ones, phi, NT) + mm(ones, plo, NT))[:1]
            lse = lse_ref[h : h + 1, rows]
            dqt = None
            for c in range(b + 1):
                cols = pl.ds(c * BR, BR)
                s = mm(x_ref[cols, w + h * HD : w + (h + 1) * HD], qh, NT)
                p = jnp.exp((s - pens[c]) - lse)
                dp = mm(x_ref[cols, 2 * w + h * HD : 2 * w + (h + 1) * HD], gh, NT)
                ds = p * (dp - delta)
                low = ds.astype(jnp.bfloat16)
                dk = mm(low, qh)
                dv = mm(p.astype(jnp.bfloat16), gh)
                part = mm(kt[h, :, c * BR : (c + 1) * BR], low)
                dqt = part if dqt is None else dqt + part
                if b == nb - 1:
                    acc[h, cols] = dk
                    acc[nh + h, cols] = dv
                else:
                    acc[h, cols] += dk
                    acc[nh + h, cols] += dv
                sums[c] = ds if sums[c] is None else sums[c] + ds
            d_ref[rows, h * HD : (h + 1) * HD] = jnp.transpose(dqt * 0.125).astype(jnp.bfloat16)
        dqt = None
        for c in range(b + 1):
            cols = pl.ds(c * BR, BR)
            hi, lo = halves(sums[c])
            grad = mm(hi, above) + mm(lo, above)
            full = grad[:, :1] + sums[c][:, :1]
            if later[c] is not None:
                grad = grad + later[c]
                full = full + later[c]
            later[c] = full
            low = (-(grad * sigs[c])).astype(jnp.bfloat16)
            dk = mm(low, q0)
            part = mm(kt[nh, :, c * BR : (c + 1) * BR], low)
            dqt = part if dqt is None else dqt + part
            if b == nb - 1:
                acc[2 * nh, cols] = dk
            else:
                acc[2 * nh, cols] += dk
        d_ref[rows, 3 * w : 3 * w + HD] = jnp.transpose(dqt * 0.125).astype(jnp.bfloat16)
        if midway is not None:
            midway(b)
    for h in range(nh):
        d_ref[:, w + h * HD : w + (h + 1) * HD] = acc[h, :size].astype(jnp.bfloat16)
        d_ref[:, 2 * w + h * HD : 2 * w + (h + 1) * HD] = acc[nh + h, :size].astype(jnp.bfloat16)
    d_ref[:, 3 * w + HD : 3 * w + 2 * HD] = acc[2 * nh, :size].astype(jnp.bfloat16)


VMEM = pl.BlockSpec(memory_space=pltpu.VMEM)
LIMIT = 48 * 1024 * 1024


def attend_fwd(x):
    size, w = x.shape[0], (x.shape[1] - 2 * HD) // 3
    return pl.pallas_call(
        fwd_one,
        out_shape=(
            jax.ShapeDtypeStruct((size, w), jnp.bfloat16),
            jax.ShapeDtypeStruct((8, size), jnp.float32),
            jax.ShapeDtypeStruct((8, size), jnp.float32),
        ),
        in_specs=[VMEM],
        out_specs=(VMEM,) * 3,
        compiler_params=pltpu.CompilerParams(vmem_limit_bytes=LIMIT),
        cost_estimate=pl.CostEstimate(
            flops=size * size * 64 * 40, bytes_accessed=size * 2000, transcendentals=size * size * 3
        ),
        name="attend_fwd",
    )(x)


def attend_bwd(x, g, o, lse, carry):
    size, w = x.shape[0], (x.shape[1] - 2 * HD) // 3
    nh = w // HD
    return pl.pallas_call(
        bwd_one,
        out_shape=jax.ShapeDtypeStruct(x.shape, jnp.bfloat16),
        in_specs=[VMEM] * 5,
        out_specs=VMEM,
        scratch_shapes=[
            pltpu.VMEM((2 * nh + 1, size, HD), jnp.float32),
            pltpu.VMEM((nh + 1, HD, size), jnp.bfloat16),
        ],
        compiler_params=pltpu.CompilerParams(vmem_limit_bytes=LIMIT),
        cost_estimate=pl.CostEstimate(
            flops=size * size * 64 * 80, bytes_accessed=size * 4000, transcendentals=size * size * 3
        ),
        name="attend_bwd",
    )(x, g, o, lse, carry)


class Group:
    def __init__(self, core):
        self.core = core
        self.c = lax.axis_index(core)
        self.zl = lax.axis_index("zl")
        self.me = 2 * self.c + self.zl

    def peer(self, delta):
        return {self.core: self.c ^ (delta >> 1), "zl": self.zl ^ (delta & 1)}

    def member(self, m):
        return {self.core: m >> 1, "zl": m & 1}

    def greet(self, deltas):
        barrier = pltpu.get_barrier_semaphore()
        for delta in deltas:
            pl.semaphore_signal(
                barrier, inc=1, device_id=self.peer(delta), device_id_type=pl.DeviceIdType.MESH
            )
        pl.semaphore_wait(barrier, len(deltas))


def send(src, dst, ssem, rsem, device):
    return pltpu.make_async_remote_copy(
        src_ref=src,
        dst_ref=dst,
        send_sem=ssem,
        recv_sem=rsem,
        device_id=device,
        device_id_type=pl.DeviceIdType.MESH,
    )


def fwd_x(core, xl, xs, att, ol, os, lsel, lses, cl, cs, land, ssem, rsem):
    group = Group(core)
    nl, ns = xl.shape[0] // 4, xs.shape[0] // 4
    group.greet((1, 2, 3))

    def copy(k, m):
        src, n, at = ((ol, nl, 0), (os, ns, nl))[k]
        return send(
            src.at[pl.ds(m * n, n)],
            land.at[group.me, pl.ds(at, n)],
            ssem.at[k, m],
            rsem.at[k, group.me],
            group.member(m),
        )

    def arrived(k, m):
        src, n, at = ((ol, nl, 0), (os, ns, nl))[k]
        return send(
            src.at[pl.ds(0, n)], land.at[m, pl.ds(at, n)], ssem.at[k, m], rsem.at[k, m], group.member(m)
        )

    def start(k, m):
        src, n, at = ((ol, nl, 0), (os, ns, nl))[k]

        @pl.when(group.me != m)
        def _():
            copy(k, m).start()

        @pl.when(group.me == m)
        def _():
            land[m, at : at + n] = src[m * n : (m + 1) * n]

    def started(k, n):
        def done(b):
            for m in range(b * BR // n, (b + 1) * BR // n):
                start(k, m)

        return done

    fwd_one(xs, os, lses, cs, started(1, ns))
    fwd_one(xl, ol, lsel, cl, started(0, nl))
    w = ol.shape[1]
    for m in range(4):

        @pl.when(group.me != m)
        def _():
            for k in range(2):
                copy(k, m).wait_send()
                arrived(k, m).wait_recv()

    for m in range(4):
        att[:, m * w : (m + 1) * w] = land[m]


def bwd_x(core, xl, xs, go, ol, os, lsel, lses, cl, cs, dl, ds, acc, kt, out, gl, gs, ssem, rsem):
    group = Group(core)
    nl, ns = xl.shape[0] // 4, xs.shape[0] // 4
    w = ol.shape[1]
    for m in range(4):
        out[m] = go[:, m * w : (m + 1) * w]
    group.greet((1, 2, 3))

    def part(k):
        return ((gl, nl, 0), (gs, ns, nl))[k]

    def copy(k, m):
        dst, n, at = part(k)
        return send(
            out.at[m, pl.ds(at, n)],
            dst.at[pl.ds(pl.multiple_of(group.me * n, 16), n)],
            ssem.at[k, m],
            rsem.at[k, group.me],
            group.member(m),
        )

    def arrived(k, m):
        dst, n, at = part(k)
        return send(
            out.at[m, pl.ds(at, n)], dst.at[pl.ds(m * n, n)], ssem.at[k, m], rsem.at[k, m], group.member(m)
        )

    for k in (1, 0):
        for m in range(4):
            dst, n, at = part(k)

            @pl.when(group.me != m)
            def _():
                copy(k, m).start()

            @pl.when(group.me == m)
            def _():
                dst[m * n : (m + 1) * n] = out[m, at : at + n]

    for k in (1, 0):
        for m in range(4):

            @pl.when(group.me != m)
            def _():
                arrived(k, m).wait_recv()

        if k:
            bwd_one(xs, gs, os, lses, cs, ds, acc, kt)
        else:
            bwd_one(xl, gl, ol, lsel, cl, dl, acc, kt)
    for m in range(4):

        @pl.when(group.me != m)
        def _():
            for k in range(2):
                copy(k, m).wait_send()


def norm_rows(v):
    mean = jnp.mean(v, axis=-1, keepdims=True)
    cen = v - mean
    inv = lax.rsqrt(jnp.mean(cen * cen, axis=-1, keepdims=True) + 1e-05)
    return cen * inv, inv


def project_x(core, resid, gain, shift, w, bias, nl_ref, ns_ref, pl_ref, ps_ref, ssem, rsem):
    group = Group(core)
    nl, ns = nl_ref.shape[0] // 4, ns_ref.shape[0] // 4
    half = nl // 2
    parts = ((ns_ref, ps_ref, ns, 0, ns, nl), (nl_ref, pl_ref, nl, 0, half, 0), (nl_ref, pl_ref, nl, half, half, half))

    def rows(k, m):
        ref, _, n, at, size, _ = parts[k]
        return ref.at[pl.ds(pl.multiple_of(m * n + at, 16), size)]

    def copy(k, j, m, delta):
        return send(rows(k, m), rows(k, m), ssem.at[k, j], rsem.at[k, j], group.peer(delta))

    def compute(k, m):
        ref, out, n, at, size, _ = parts[k]
        here = pl.ds(pl.multiple_of(m * n + at, 16), size)
        out[here] = (mm(ref[here], w[...]) + bias[...]).astype(jnp.bfloat16)

    me = group.me
    for k in range(3):
        ref, _, n, at, size, src = parts[k]
        hat, _ = norm_rows(resid[src : src + size])
        ref[pl.ds(pl.multiple_of(me * n + at, 16), size)] = (hat * gain[...] + shift[...]).astype(
            jnp.bfloat16
        )
        if k == 0:
            group.greet((1, 2))
        copy(k, 0, me, 1).start()
        copy(k, 1, me, 2).start()
    for k in range(3):
        compute(k, me)
    for k in range(3):
        copy(k, 1, me ^ 2, 2).wait_recv()
        compute(k, me ^ 2)
    for k in range(3):
        copy(k, 0, me ^ 1, 1).wait_recv()
        copy(k, 2, me ^ 1, 2).start()
        compute(k, me ^ 1)
    for k in range(3):
        copy(k, 2, me ^ 3, 2).wait_recv()
        compute(k, me ^ 3)
    for k in range(3):
        copy(k, 0, me, 1).wait_send()
        copy(k, 1, me, 2).wait_send()
        copy(k, 2, me ^ 1, 2).wait_send()


def collect_x(core, dl, ds, w, resid, gain, gmid, g_ref, sums, mine, out, got, ssem, rsem):
    group = Group(core)
    nl, ns = dl.shape[0] // 4, ds.shape[0] // 4
    me = group.me

    def partial(m):
        a = mm(dl[pl.ds(pl.multiple_of(m * nl, 16), nl)], w[...], NT)
        b = mm(ds[pl.ds(pl.multiple_of(m * ns, 16), ns)], w[...], NT)
        return jnp.concatenate([a, b], axis=0)

    def copy(k, delta):
        return send(out.at[k], got.at[k], ssem.at[k], rsem.at[k], group.peer(delta))

    out[0] = partial(me ^ 3).astype(jnp.bfloat16)
    group.greet((1, 2))
    copy(0, 2).start()
    mine[...] = partial(me ^ 1)
    copy(0, 2).wait_recv()
    out[1] = (mine[...] + got[0].astype(jnp.float32)).astype(jnp.bfloat16)
    copy(1, 1).start()
    out[2] = partial(me ^ 2).astype(jnp.bfloat16)
    copy(2, 2).start()
    mine[...] = partial(me)
    hat, inv = norm_rows(resid[...])
    copy(2, 2).wait_recv()
    copy(1, 1).wait_recv()
    grad = mine[...] + got[2].astype(jnp.float32) + got[1].astype(jnp.float32)
    gh = grad * gain[...]
    a = jnp.mean(gh, axis=-1, keepdims=True)
    b = jnp.mean(gh * hat, axis=-1, keepdims=True)
    g_ref[...] = gmid[...] + inv * (gh - a - hat * b)
    sums[0:1] = jnp.sum(grad * hat, axis=0, keepdims=True)
    sums[1:2] = jnp.sum(grad, axis=0, keepdims=True)
    copy(0, 2).wait_send()
    copy(1, 1).wait_send()
    copy(2, 2).wait_send()


def shape(dims, dtype):
    return jax.ShapeDtypeStruct(tuple(dims), dtype)


def remote(kernel, core, outs, scratch, ident, name, args, flops=10**9):
    return pl.pallas_call(
        functools.partial(kernel, core),
        out_shape=tuple(outs),
        in_specs=[VMEM] * len(args),
        out_specs=(VMEM,) * len(outs),
        scratch_shapes=scratch,
        compiler_params=pltpu.CompilerParams(
            vmem_limit_bytes=LIMIT, collective_id=ident, has_side_effects=True
        ),
        cost_estimate=pl.CostEstimate(flops=flops, bytes_accessed=10**7, transcendentals=10**6),
        name=name,
    )(*args)


DMA = pltpu.SemaphoreType.DMA


def attend_fwd_x(core, xl, xs):
    w = (xl.shape[1] - 2 * HD) // 3
    rows = (xl.shape[0] + xs.shape[0]) // 4
    outs = [shape((rows, 4 * w), jnp.bfloat16)]
    outs += [shape((x.shape[0], w), jnp.bfloat16) for x in (xl, xs)]
    outs += [shape((8, x.shape[0]), jnp.float32) for x in (xl, xs)] * 2
    scratch = [pltpu.VMEM((4, rows, w), jnp.bfloat16), DMA((2, 4)), DMA((2, 4))]
    return remote(fwd_x, core, outs, scratch, 1, "attend_fwd_x", (xl, xs), 10**10)


def attend_bwd_x(core, xl, xs, go, ol, os, lsel, lses, cl, cs):
    w = ol.shape[1]
    nh = w // HD
    size = xl.shape[0]
    outs = [shape(x.shape, jnp.bfloat16) for x in (xl, xs)]
    scratch = [
        pltpu.VMEM((2 * nh + 1, size, HD), jnp.float32),
        pltpu.VMEM((nh + 1, HD, size), jnp.bfloat16),
        pltpu.VMEM((4, go.shape[0], w), jnp.bfloat16),
        pltpu.VMEM(ol.shape, jnp.bfloat16),
        pltpu.VMEM(os.shape, jnp.bfloat16),
        DMA((2, 4)),
        DMA((2, 4)),
    ]
    args = (xl, xs, go, ol, os, lsel, lses, cl, cs)
    return remote(bwd_x, core, outs, scratch, 2, "attend_bwd_x", args, 2 * 10**10)


def project(core, resid, gain, shift, w, bias, nl, ns):
    d, n = w.shape
    outs = [shape((4 * nl, d), jnp.bfloat16), shape((4 * ns, d), jnp.bfloat16)]
    outs += [shape((4 * nl, n), jnp.bfloat16), shape((4 * ns, n), jnp.bfloat16)]
    args = (resid, gain[None], shift[None], w, bias[None])
    return remote(project_x, core, outs, [DMA((3, 3)), DMA((3, 3))], 3, "project_x", args)


def collect(core, dl, ds, w, resid, gain, gmid):
    outs = [shape(resid.shape, jnp.float32), shape((8, w.shape[0]), jnp.float32)]
    scratch = [
        pltpu.VMEM(resid.shape, jnp.float32),
        pltpu.VMEM((3,) + resid.shape, jnp.bfloat16),
        pltpu.VMEM((3,) + resid.shape, jnp.bfloat16),
        DMA((3,)),
        DMA((3,)),
    ]
    return remote(collect_x, core, outs, scratch, 4, "collect_x", (dl, ds, w, resid, gain[None], gmid))


def total_x(axes, v, out, land, ssem, rsem):
    barrier = pltpu.get_barrier_semaphore()
    peers = [{ax: 1 - lax.axis_index(ax)} for ax in axes]
    for peer in peers:
        pl.semaphore_signal(barrier, inc=1, device_id=peer, device_id_type=pl.DeviceIdType.MESH)
    pl.semaphore_wait(barrier, len(peers))
    land[0] = v[...]
    n = len(axes)
    for i, peer in enumerate(peers):
        copy = send(land.at[i], land.at[n + 1 + i], ssem.at[i], rsem.at[i], peer)
        copy.start()
        copy.wait()
        land[i + 1] = land[i] + land[n + 1 + i]
    out[...] = land[n]


def total(axes, v):
    n = len(axes)
    scratch = [pltpu.VMEM((2 * n + 1,) + v.shape, jnp.float32), DMA((n,)), DMA((n,))]
    return remote(total_x, axes, [shape(v.shape, jnp.float32)], scratch, 5, "total_x", (v,))[0]


EPS = 1e-05
F32 = jnp.float32
BF = jnp.bfloat16


def swap(v, *axes):
    count = 2 ** len(axes)
    return lax.ppermute(
        v, axes if len(axes) > 1 else axes[0], [(i, count - 1 - i) for i in range(count)]
    )


def ordered(own, other, index, axis):
    return jnp.where(
        index == 0,
        jnp.concatenate([own, other], axis=axis),
        jnp.concatenate([other, own], axis=axis),
    )


def pick(v, index, axis):
    return lax.dynamic_index_in_dim(v, index, axis, keepdims=False)


def normalize(v, gain, shift):
    mean = jnp.mean(v, axis=-1, keepdims=True)
    cen = v - mean
    var = jnp.mean(cen * cen, axis=-1, keepdims=True)
    inv = lax.rsqrt(var + EPS)
    hat = cen * inv
    return hat * gain + shift, hat, inv


def normalize_back(grad, hat, inv, gain):
    gh = grad * gain
    a = jnp.mean(gh, axis=-1, keepdims=True)
    b = jnp.mean(gh * hat, axis=-1, keepdims=True)
    return inv * (gh - a - hat * b), jnp.sum(grad * hat, axis=0), jnp.sum(grad, axis=0)


def gelu_both(u):
    k = 0.7978845608028654
    inner = k * (u + 0.044715 * u * u * u)
    t = jnp.tanh(inner)
    act = 0.5 * u * (1.0 + t)
    slope = 0.5 * (1.0 + t) + 0.5 * u * (1.0 - t * t) * k * (1.0 + 3 * 0.044715 * u * u)
    return act, slope


def dot(a, b, ca=1, cb=0):
    return lax.dot_general(a, b, (((ca,), (cb,)), ((), ())), preferred_element_type=F32)


class Plan:
    def __init__(self, dims, dp, mp):
        self.dims, self.dp, self.mp = dims, dp, mp
        self.core = dims[-1]
        self.plane = dims[:-1]
        self.c = lax.axis_index(self.core)
        self.zh = lax.axis_index("zh")
        self.zl = lax.axis_index("zl")
        self.z = lax.axis_index(("zh", "zl"))
        self.d = lax.axis_index(dims)

    def relabel(self, v):
        got = lax.ppermute(v, (self.core, "zh"), [(1, 2), (2, 1)])
        return jnp.where(self.c == self.zh, v, got)

    def ring(self, v, step):
        n = self.mp
        return lax.ppermute(v, ("zh", "zl"), [(i, (i + step) % n) for i in range(n)])

    def gather(self, v):
        v = ordered(v, swap(v, "zl"), self.zl, 0)
        return ordered(v, swap(v, self.core), self.c, 0)

    def scatter(self, v):
        rows = v.shape[0] // 4
        v = v.reshape(2, 2, rows, v.shape[1])
        got = swap(pick(v, 1 - self.c, 0), self.core)
        mine = pick(v, self.c, 0).astype(F32) + got.astype(F32)
        got = swap(pick(mine, 1 - self.zl, 0).astype(BF), "zl")
        return pick(mine, self.zl, 0) + got.astype(F32)

    def to_rows(self, o):
        rows = o.shape[0] // 4
        o = o.reshape(2, 2, rows, o.shape[1])
        got = []
        for dc in range(2):
            line = []
            for dz in range(2):
                part = pick(pick(o, self.c ^ dc, 0), self.zl ^ dz, 0)
                axes = ((self.core,) if dc else ()) + (("zl",) if dz else ())
                line.append(swap(part, *axes) if axes else part)
            got.append(ordered(line[0], line[1], self.zl, 1))
        return ordered(got[0], got[1], self.c, 1)

    def to_heads(self, g):
        rows, w = g.shape[0], g.shape[1] // 4
        g = g.reshape(rows, 2, 2, w)
        got = []
        for dc in range(2):
            line = []
            for dz in range(2):
                part = pick(pick(g, self.c ^ dc, 1), self.zl ^ dz, 1)
                axes = ((self.core,) if dc else ()) + (("zl",) if dz else ())
                line.append(swap(part, *axes) if axes else part)
            got.append(ordered(line[0], line[1], self.zl, 0))
        return ordered(got[0], got[1], self.c, 0)

    def piece(self, w):
        rows = w.shape[0] // self.dp
        return lax.dynamic_slice_in_dim(w, self.d * rows, rows, 0)

    def ring_gather(self, v):
        parts = []
        for _ in range(self.mp - 1):
            v = self.ring(v, 1)
            parts.append(v)
        return parts

    def plane_gather(self, v, axes):
        k, rows, n = v.shape
        have = []
        shape = [k]
        for ax in axes:
            pos = sum(self.dims.index(h) < self.dims.index(ax) for h in have)
            got = swap(v, ax)
            cur = v.reshape(k, *([2] * len(have)), rows, n)
            oth = got.reshape(cur.shape)
            a = jnp.stack([cur, oth], axis=1 + pos)
            b = jnp.stack([oth, cur], axis=1 + pos)
            v = jnp.where(lax.axis_index(ax) == 0, a, b)
            have.append(ax)
            v = v.reshape(k, -1, rows, n).reshape(k, -1, n)
            rows_all = v.shape[1]
            v = v.reshape(k, rows_all, n)
        return v.reshape(k, self.dp, rows, n)

    def plane_scatter(self, g, axes):
        n = g.shape[1]
        left = [ax for ax in self.dims]
        rows = g.shape[0] // self.dp
        v = g.reshape(*([2] * len(left)), rows, n)
        for ax in axes:
            pos = left.index(ax)
            i = lax.axis_index(ax)
            got = swap(pick(v, 1 - i, pos), ax)
            v = (pick(v, i, pos).astype(F32) + got.astype(F32)).astype(BF)
            left.remove(ax)
        return v.reshape(-1, n)

    def ring_scatter(self, chunks):
        t = chunks[-1]
        for r in range(self.mp - 2, -1, -1):
            got = self.ring(t, -1)
            t = chunks[r].astype(F32) + got.astype(F32)
            if r:
                t = t.astype(BF)
        return t


def body(
    dims, dp, mp,
    x_long, x_short, dy_long, dy_short, ln_gain, ln_bias, w_qkv, b_qv, w_out, b_out, w_up, b_up, w_down, b_down, threshold,
):
    plan = Plan(dims, dp, mp)
    layers = w_qkv.shape[0]
    d_model = x_long.shape[-1]
    heads_w = w_qkv.shape[-1]
    ffq = w_up.shape[-1]
    rl, rs = x_long.shape[1], x_short.shape[1]
    rows = rl + rs
    core_rest = tuple(plan.plane)
    fwd_axes = core_rest + (plan.core,)
    alt_axes = core_rest[::-1] + (plan.core,)
    gain = ln_gain.astype(F32)
    shift = ln_bias.astype(F32)

    x = jnp.concatenate([x_long[0], x_short[0]], axis=0)
    x = plan.relabel(x)

    small = jnp.concatenate([b_up.reshape(-1), b_qv.reshape(-1)])
    rel_small = jnp.stack([small] + plan.ring_gather(small))
    n_up = layers * ffq
    rel_bup = rel_small[:, :n_up].reshape(mp, layers, ffq).astype(F32)
    rel_bqv = rel_small[:, n_up:].reshape(mp, layers, 2, heads_w).astype(F32)
    mine = 2 * plan.c + plan.zl
    my_bqv = pick(rel_bqv, (plan.z - mine) % mp, 0)
    zero_bq = pick(rel_bqv, plan.z % mp, 0)[:, 0, :HD]

    exts = []
    for l in range(layers):
        quarter = plan.relabel(w_qkv[l].reshape(d_model, 3 * heads_w))
        head0 = w_qkv[l][:, :2, :HD].reshape(d_model, 2 * HD)
        got = lax.ppermute(head0, "zl", [(0, 1)])
        head0 = jnp.where(plan.zl == 0, head0, got)
        got = lax.ppermute(head0, "zh", [(0, 1)])
        head0 = jnp.where(plan.zh == 0, head0, got)
        exts.append(jnp.concatenate([quarter, head0], axis=1))

    ups, downs, outs = [], [], []
    for l in range(layers):
        po = plan.piece(w_out[l])
        pu = jnp.concatenate([plan.piece(w_up[l]), po], axis=0)
        pd = plan.piece(w_down[l])
        n_out, n_d = po.shape[0], pd.shape[0]
        both = plan.ring_gather(jnp.concatenate([pu, pd], axis=0))
        stacked = jnp.stack(both)
        n_u = pu.shape[0]
        gu = plan.plane_gather(stacked[:, :n_u], fwd_axes)
        gd = plan.plane_gather(stacked[:, n_u:], alt_axes)
        up = gu[:, :, : n_u - n_out].reshape(mp - 1, d_model, ffq)
        ups.append(jnp.concatenate([w_up[l]] + [up[r] for r in range(mp - 1)], axis=1))
        out = gu[:, :, n_u - n_out :].reshape(mp - 1, heads_w, d_model)
        out = jnp.concatenate([w_out[l][None], out], axis=0)
        outs.append(
            jnp.concatenate([pick(out, (plan.z - q) % mp, 0) for q in range(mp)], axis=0)
        )
        downs.append(
            jnp.concatenate([w_down[l], gd.reshape((mp - 1) * ffq, d_model)], axis=0)
        )

    dy = plan.relabel(jnp.concatenate([dy_long[0], dy_short[0]], axis=0))

    limits = threshold.astype(F32) / 64.0
    resid = x.astype(F32)
    saved = []
    shares = []
    for l in range(layers):
        normed, hat1, inv1 = normalize(resid, gain[l, 0], shift[l, 0])
        normed = normed.astype(BF)
        full = [plan.gather(normed[:rl]), plan.gather(normed[rl:])]
        bias = jnp.concatenate(
            [
                my_bqv[l, 0],
                jnp.zeros((heads_w,), F32),
                my_bqv[l, 1],
                zero_bq[l],
                jnp.zeros((HD,), F32),
            ]
        )
        proj = [(dot(n, exts[l]) + bias).astype(BF) for n in full]
        att = [attend_fwd(p) for p in proj]
        share = jnp.zeros((), F32)
        for p, a in zip(proj, att):
            size = p.shape[0]
            sel = a[2][size // BR]
            left = (size - 1 - lax.broadcasted_iota(jnp.int32, (size,), 0)).astype(F32)
            share = share + jnp.sum(
                jax.nn.sigmoid(4.0 * (sel / jnp.maximum(left, 1.0) - limits[l]))
            )
        shares.append(share)
        attended = jnp.concatenate([plan.to_rows(a[0]) for a in att], axis=0)
        middle = resid + dot(attended, outs[l]) + b_out[l].astype(F32)
        normed2, hat2, inv2 = normalize(middle, gain[l, 1], shift[l, 1])
        normed2 = normed2.astype(BF)
        upper = dot(normed2, ups[l]) + rel_bup[:, l].reshape(-1)
        active = gelu_both(upper)[0].astype(BF)
        saved.append((resid, middle, full, proj, att, attended, normed2, upper, active))
        resid = middle + dot(active, downs[l]) + b_down[l].astype(F32)

    y = plan.relabel(resid.astype(BF))

    g = dy.astype(F32)
    vec = {}
    weight_grads = [None] * layers
    for l in reversed(range(layers)):
        resid, middle, full, proj, att, attended, normed2, upper, active = saved[l]
        g_bdown = jnp.sum(g, axis=0)
        gm = g.astype(BF)
        gact = dot(gm, downs[l], 1, 1)
        slope = gelu_both(upper)[1]
        gu = (slope * gact).astype(BF)
        w_down_t = dot(gm, active, 0, 0).astype(BF)
        w_up_g = dot(normed2, gu, 0, 0).astype(BF)
        g_bup = jnp.sum(gu.astype(F32), axis=0)
        gn2 = dot(gu, ups[l], 1, 1)
        _, hat2, inv2 = normalize(middle, gain[l, 1], shift[l, 1])
        back, g_gain2, g_shift2 = normalize_back(gn2, hat2, inv2, gain[l, 1])
        gmid = g + back
        g_bout = jnp.sum(gmid, axis=0)
        ga = gmid.astype(BF)
        go = dot(ga, outs[l], 1, 1).astype(BF)
        w_out_t = dot(ga, attended, 0, 0).astype(BF)
        gh = [plan.to_heads(go[:rl]), plan.to_heads(go[rl:])]
        dext = [attend_bwd(p, h, a[0], a[1], a[2]) for p, h, a in zip(proj, gh, att)]
        gn1 = jnp.concatenate(
            [plan.scatter(dot(e, exts[l], 1, 1).astype(BF)) for e in dext], axis=0
        )
        w_ext_g = sum(dot(n, e, 0, 0) for n, e in zip(full, dext)).astype(BF)
        g_bext = sum(jnp.sum(e.astype(F32), axis=0) for e in dext)
        _, hat1, inv1 = normalize(resid, gain[l, 0], shift[l, 0])
        back, g_gain1, g_shift1 = normalize_back(gn1, hat1, inv1, gain[l, 0])
        g = gmid + back

        w_up_g = plan.plane_scatter(w_up_g, (plan.core,) + core_rest)
        w_up_g = plan.ring_scatter([w_up_g[:, r * ffq : (r + 1) * ffq] for r in range(mp)])
        w_down_t = plan.plane_scatter(w_down_t, (plan.core,) + core_rest[::-1])
        w_down_t = plan.ring_scatter([w_down_t[:, r * ffq : (r + 1) * ffq] for r in range(mp)])
        w_out_t = plan.plane_scatter(w_out_t, (plan.core,) + core_rest)
        w_out_t = w_out_t.reshape(-1, mp, heads_w)
        w_out_t = plan.ring_scatter([pick(w_out_t, (plan.z - r) % mp, 1) for r in range(mp)])
        w_ext_g = plan.plane_scatter(w_ext_g, core_rest[::-1])
        w_ext_g = w_ext_g.reshape(2, -1, w_ext_g.shape[1])
        part, zero = w_ext_g[..., : 3 * heads_w], w_ext_g[..., 3 * heads_w :]
        got = lax.ppermute(part, (plan.core, "zh"), [(1, 0), (2, 3)])
        part = part.astype(F32) + got.astype(F32)
        got = lax.ppermute(
            pick(part, 1 - plan.c, 0).astype(BF), (plan.core, "zh"), [(0, 2), (3, 1)]
        )
        w_qkv_g = jnp.where(plan.c == plan.zh, pick(part, plan.c, 0), got.astype(F32))
        got = swap(pick(zero, 1 - plan.c, 0), plan.core)
        zero = (pick(zero, plan.c, 0).astype(F32) + got.astype(F32)).astype(BF)
        zero = zero.astype(F32) + swap(zero, "zl").astype(F32)
        zero = zero + swap(zero.astype(BF), "zh").astype(F32)
        zero = jnp.where(plan.z == 0, zero, 0.0)
        w_qkv_g = w_qkv_g.reshape(-1, 3, heads_w)
        zero = zero.reshape(-1, 2, HD)
        w_qkv_g = w_qkv_g + jnp.pad(zero, ((0, 0), (0, 1), (0, heads_w - HD)))
        weight_grads[l] = (w_qkv_g, jnp.transpose(w_out_t), w_up_g, jnp.transpose(w_down_t))

        hot = (lax.broadcasted_iota(jnp.int32, (mp, 1), 0) == mine).astype(F32)
        gq = hot * g_bext[None, :heads_w]
        gv = hot * g_bext[None, 2 * heads_w : 3 * heads_w]
        gq = gq.reshape(-1).at[:HD].add(g_bext[3 * heads_w : 3 * heads_w + HD])
        g_bup = g_bup.reshape(mp, ffq)
        g_bup = jnp.stack([pick(g_bup, (plan.z - q) % mp, 0) for q in range(mp)])
        vec[l] = jnp.concatenate(
            [
                g_gain1, g_gain2, g_shift1, g_shift2, g_bout, g_bdown,
                gq, gv.reshape(-1), g_bup.reshape(-1), jnp.full((128,), shares[l] / mp),
            ]
        )

    dx = plan.relabel(g.astype(BF)).astype(F32)
    total = lax.psum(jnp.stack([vec[l] for l in range(layers)]), dims + ("zh", "zl"))
    n = d_model
    g_gain = total[:, : 2 * n].reshape(layers, 2, n)
    g_bias = total[:, 2 * n : 4 * n].reshape(layers, 2, n)
    g_bout = total[:, 4 * n : 5 * n]
    g_bdown = total[:, 5 * n : 6 * n]
    at = 6 * n
    g_bqv = total[:, at : at + 2 * mp * heads_w].reshape(layers, 2, mp, heads_w)
    at += 2 * mp * heads_w
    g_bup = total[:, at : at + mp * ffq].reshape(layers, mp, ffq)
    at += mp * ffq
    key_share = total[:, at] / (dp * (rows * mp))
    return (
        y[None, :rl],
        y[None, rl:],
        dx[None, :rl],
        dx[None, rl:],
        g_gain,
        g_bias,
        jnp.stack([weight_grads[l][0] for l in range(layers)]),
        pick(g_bqv, plan.z, 2),
        jnp.stack([weight_grads[l][1] for l in range(layers)]),
        g_bout,
        jnp.stack([weight_grads[l][2] for l in range(layers)]),
        pick(g_bup, plan.z, 1),
        jnp.stack([weight_grads[l][3] for l in range(layers)]),
        g_bdown,
        key_share,
    )


MESH = pl.DeviceIdType.MESH
ANY = pl.BlockSpec(memory_space=pl.ANY)


class Net:
    def __init__(self, dims):
        self.dims = dims
        self.y, self.x, self.c = (lax.axis_index(ax) for ax in dims)
        self.zh, self.zl = lax.axis_index("zh"), lax.axis_index("zl")
        self.z = 2 * self.zh + self.zl
        self.yx = 2 * self.y + self.x
        self.me = 2 * self.c + self.zl
        self.moves = self.c != self.zh

    def group(self, delta):
        return {self.dims[2]: self.c ^ (delta >> 1), "zl": self.zl ^ (delta & 1)}

    def member(self, m):
        return {self.dims[2]: m >> 1, "zl": m & 1}

    def plane(self, e):
        return {self.dims[0]: self.y ^ (e >> 1), self.dims[1]: self.x ^ (e & 1)}

    def line(self, r):
        to = (self.z + r) % 4
        return {"zh": to // 2, "zl": to % 2}

    def partner(self):
        return {self.dims[2]: 1 - self.c, "zh": 1 - self.zh}

    def greet(self, peers):
        barrier = pltpu.get_barrier_semaphore()
        for peer in peers:
            pl.semaphore_signal(barrier, inc=1, device_id=peer, device_id_type=MESH)
        pl.semaphore_wait(barrier, len(peers))


class Sems:
    def __init__(self, ssem, rsem):
        self.ssem, self.rsem, self.used = ssem, rsem, 0

    def copy(self, src, dst, device):
        i = self.used
        self.used += 1
        assert i < self.ssem.shape[0]
        return send(src, dst, self.ssem.at[i], self.rsem.at[i], device)


class Batch:
    def __init__(self, copies, when=None):
        self.copies, self.when = copies, when

    def _do(self, f):
        if self.when is None:
            f()
        else:
            pl.when(self.when)(f)

    def start(self):
        self._do(lambda: [c.start() for c in self.copies] and None)

    def recv(self):
        self._do(lambda: [c.wait_recv() for c in self.copies] and None)

    def sent(self):
        self._do(lambda: [c.wait_send() for c in self.copies] and None)

    def end(self):
        self.recv()
        self.sent()


def aligned(v, n=16):
    return pl.multiple_of(v, n)


class Projections:
    def __init__(self, net, sems, wq, w0, qland, zland, ext):
        self.net, self.wq, self.w0, self.qland, self.zland, self.ext = net, wq, w0, qland, zland, ext
        rows = qland.shape[1]
        here = pl.ds(aligned(net.yx * rows), rows)
        at = net.yx
        self.q1 = Batch([sems.copy(wq.at[here], qland.at[at], net.partner())], net.moves)
        self.q2 = Batch([sems.copy(qland.at[at], qland.at[at], net.plane(e)) for e in (1, 2, 3)], net.moves)
        self.h1 = []
        for r in (1, 2, 3):
            copy = sems.copy(w0.at[here], zland.at[at], net.line(r))
            self.h1.append(copy)
        self.h2 = Batch([sems.copy(zland.at[at], zland.at[at], net.plane(e)) for e in (1, 2, 3)], net.z != 0)

    def start(self):
        self.q1.start()

        @pl.when(self.net.z == 0)
        def _():
            for copy in self.h1:
                copy.start()

    def forward(self):
        self.q1.recv()
        self.q2.start()
        for r in (1, 2, 3):
            pl.when(self.net.z == r)(lambda: self.h1[r - 1].wait_recv())
        self.h2.start()

    def finish(self):
        rows, n = self.qland.shape[1:]
        self.q2.recv()
        self.h2.recv()

        @pl.when(self.net.moves)
        def _():
            for k in range(4):
                self.ext[k * rows : (k + 1) * rows, :n] = self.qland[k]

        @pl.when(jnp.logical_not(self.net.moves))
        def _():
            self.ext[:, :n] = self.wq[...]

        @pl.when(self.net.z != 0)
        def _():
            for k in range(4):
                self.ext[k * rows : (k + 1) * rows, n:] = self.zland[k]

        @pl.when(self.net.z == 0)
        def _():
            self.ext[:, n:] = self.w0[...]

        self.q1.sent()
        self.q2.sent()
        self.h2.sent()

        @pl.when(self.net.z == 0)
        def _():
            for copy in self.h1:
                copy.wait_send()


def project_part(net, sems, resid, gain, shift, w, bias, fl, fs, pj_l, pj_s, after_chip):
    nl, ns = fl.shape[0] // 4, fs.shape[0] // 4
    half = nl // 2
    parts = ((fs, pj_s, ns, 0, ns, nl), (fl, pj_l, nl, 0, half, 0), (fl, pj_l, nl, half, half, half))
    me = net.me

    def rows(k, m):
        ref, _, n, at, size, _ = parts[k]
        return ref.at[pl.ds(aligned(m * n + at), size)]

    def compute(k, m):
        ref, out, n, at, size, _ = parts[k]
        here = pl.ds(aligned(m * n + at), size)
        out[here] = (mm(ref[here], w[...]) + bias[...]).astype(jnp.bfloat16)

    chip = [sems.copy(rows(k, me), rows(k, me), net.group(1)) for k in range(3)]
    core = [sems.copy(rows(k, me), rows(k, me), net.group(2)) for k in range(3)]
    over = [sems.copy(rows(k, me ^ 1), rows(k, me ^ 1), net.group(2)) for k in range(3)]
    for k in range(3):
        ref, _, n, at, size, src = parts[k]
        hat, _ = norm_rows(resid[src : src + size].astype(jnp.float32))
        ref[pl.ds(aligned(me * n + at), size)] = (hat * gain[...] + shift[...]).astype(jnp.bfloat16)
        chip[k].start()
        core[k].start()
    for k in range(3):
        compute(k, me)
    for k in range(3):
        core[k].wait_recv()
        compute(k, me ^ 2)
    for k in range(3):
        chip[k].wait_recv()
        over[k].start()
        if k == 2:
            after_chip()
        compute(k, me ^ 1)
    for k in range(3):
        over[k].wait_recv()
        compute(k, me ^ 3)
    return chip + core + over


def attend_part(net, sems, xl, xs, att, ol, os, lsel, lses, cl, cs, land, hooks):
    nl, ns = xl.shape[0] // 4, xs.shape[0] // 4
    w = ol.shape[1]
    base = sems.used
    sems.used += 8

    def part(k):
        return ((ol, nl, 0), (os, ns, nl))[k]

    def copy(k, m):
        src, n, at = part(k)
        return send(
            src.at[pl.ds(m * n, n)],
            land.at[net.me, pl.ds(at, n)],
            sems.ssem.at[base + 4 * k + m],
            sems.rsem.at[base + 4 * k + net.me],
            net.member(m),
        )

    def arrived(k, m):
        src, n, at = part(k)
        i = base + 4 * k + m
        return send(src.at[pl.ds(0, n)], land.at[m, pl.ds(at, n)], sems.ssem.at[i], sems.rsem.at[i], net.member(m))

    def start(k, m):
        src, n, at = part(k)

        @pl.when(net.me != m)
        def _():
            copy(k, m).start()

        @pl.when(net.me == m)
        def _():
            land[m, at : at + n] = src[m * n : (m + 1) * n]

    def started(k, n):
        def done(b):
            for m in range(b * BR // n, (b + 1) * BR // n):
                start(k, m)
            if k == 0 and b in hooks:
                hooks[b]()

        return done

    fwd_one(xs, os, lses, cs, started(1, ns))
    fwd_one(xl, ol, lsel, cl, started(0, nl))
    for m in range(4):

        @pl.when(net.me != m)
        def _():
            for k in range(2):
                copy(k, m).wait_send()
                arrived(k, m).wait_recv()

    for m in range(4):
        att[:, m * w : (m + 1) * w] = land[m]


def gelu_pair(u):
    k = 0.7978845608028654
    sq = u * u
    t = jnp.tanh(u * (k + k * 0.044715 * sq))
    h = 0.5 * (1.0 + t)
    act = u * h
    slope = h + act * (1.0 - t) * (k + 3 * k * 0.044715 * sq)
    return act, slope


TN = (((0,), (0,)), ((), ()))


def ext_scatter(net, sems, dw, land):
    return [sems.copy(dw.at[net.yx ^ e], land.at[e - 1], net.plane(e)) for e in (1, 2, 3)]


class FinishLine:
    def __init__(self, net, sems, s, so, land, oland, own=None):
        self.own = s.at[0] if own is None else own
        self.net, self.s, self.so, self.land, self.oland = net, s, so, land, oland
        self.main = [
            Batch([sems.copy(s.at[r, i], land.at[3 - r, i], net.line(r)) for r in (1, 2, 3)])
            for i in range(land.shape[1])
        ]
        self.out = []
        for r in (1, 2, 3):
            to = (net.z + r) % 4
            copy = sems.copy(so.at[to % 2], oland.at[3 - r], net.line(r))
            self.out.append((copy, to // 2 == net.c))
        self.owner = net.zh == net.c

    def start(self):
        for part in self.main:
            part.start()
        self.start_rest()

    def start_rest(self):
        for copy, use in self.out:
            pl.when(use)(copy.start)

    def finish(self, f_out, fo_out):
        for part in self.main:
            part.recv()
        f_out[...] = (
            self.own[...].astype(jnp.float32)
            + self.land[0].astype(jnp.float32)
            + self.land[1].astype(jnp.float32)
            + self.land[2].astype(jnp.float32)
        ).astype(f_out.dtype)

        @pl.when(self.owner)
        def _():
            for copy, _ in self.out:
                copy.wait_recv()
            fo_out[...] = (
                self.so[self.net.zl].astype(jnp.float32)
                + self.oland[0].astype(jnp.float32)
                + self.oland[1].astype(jnp.float32)
                + self.oland[2].astype(jnp.float32)
            ).astype(fo_out.dtype)

        @pl.when(jnp.logical_not(self.owner))
        def _():
            fo_out[...] = jnp.zeros_like(fo_out)

        for part in self.main:
            part.sent()
        for copy, use in self.out:
            pl.when(use)(copy.wait_send)


class Local:
    def __init__(self, sem):
        self.sem, self.copies = sem, []

    def start(self, src, dst):
        assert len(self.copies) < self.sem.shape[0]
        copy = pltpu.make_async_copy(src, dst, self.sem.at[len(self.copies)])
        self.copies.append(copy)
        copy.start()
        return copy


class LineWeights:
    def __init__(self, net, sems, layer, w_up, w_down, zup, zdn):
        rows, n = zup.shape[0], zup.shape[1] // 3
        part = zdn.shape[1]
        own = (
            w_up.at[layer, pl.ds(aligned(net.yx * rows), rows), pl.ds(aligned(net.c * n, 128), n)],
            w_down.at[layer, pl.ds(aligned(net.c * n + net.yx * part), part)],
        )

        def slot(k):
            return (zup.at[:, pl.ds(k * n, n)], zdn.at[k])

        self.steps = []
        for s in (1, 2, 3):
            up_src = own if s == 1 else slot(4 - s)
            dn_src = own if s == 1 else slot(s - 2)
            up = [sems.copy(up_src[i], slot(3 - s)[i], net.line(1)) for i in range(2)]
            dn = [sems.copy(dn_src[i], slot(s - 1)[i], net.line(3)) for i in range(2)]
            sends_up = jnp.logical_and(net.z >= s - 1, net.z <= 2)
            sends_dn = jnp.logical_and(net.z <= 4 - s, net.z >= 1)
            self.steps.append(((up, sends_up, net.z >= s), (dn, sends_dn, net.z + s <= 3)))

    def start(self, s):
        for copies, sends, _ in self.steps[s]:
            Batch(copies, sends).start()

    def recv(self, s):
        for copies, _, gets in self.steps[s]:
            Batch(copies, gets).recv()

    def sent(self):
        for step in self.steps:
            for copies, sends, _ in step:
                Batch(copies, sends).sent()


def plane_weights(net, sems, zup, zdn, wup, wdn):
    rows, n = zup.shape[0], zup.shape[1] // 3
    part = zdn.shape[1]
    at_up = pl.ds(aligned(net.yx * rows), rows)
    at_dn = pl.ds(aligned(net.yx * part), part)
    out = []
    for e in (1, 2, 3):
        out.append(sems.copy(zup, wup.at[at_up, pl.ds(n, 3 * n)], net.plane(e)))
        out.append(sems.copy(zdn, wdn.at[pl.ds(1, 3), at_dn], net.plane(e)))
    return Batch(out)


def first_x(dims, R):
    net, sems = Net(dims), Sems(R.ssem, R.rsem)
    nl = R.xl.shape[0]
    moved = Batch(
        [
            sems.copy(R.xl, R.xr.at[pl.ds(0, nl)], net.partner()),
            sems.copy(R.xs, R.xr.at[pl.ds(nl, R.xs.shape[0])], net.partner()),
        ],
        net.moves,
    )
    proj = Projections(net, sems, R.wq, R.w0, R.qland, R.zland, R.ext)
    tiny = Batch([sems.copy(R.small, R.smalls.at[4 - r], net.line(r)) for r in (1, 2, 3)])
    weights = LineWeights(net, sems, 0, R.w_up, R.w_down, R.zup, R.zdn)
    net.greet([net.partner()] + [net.line(r) for r in (1, 2, 3)] + [net.plane(e) for e in (1, 2, 3)])
    proj.start()
    moved.start()
    tiny.start()
    weights.start(0)
    R.smalls[0] = R.small[...]

    @pl.when(jnp.logical_not(net.moves))
    def _():
        R.xr[:nl] = R.xl[...]
        R.xr[nl:] = R.xs[...]

    proj.forward()
    weights.recv(0)
    weights.start(1)
    proj.finish()
    weights.recv(1)
    weights.start(2)
    moved.end()
    tiny.end()
    weights.recv(2)
    weights.sent()


def forward_x(dims, first, last, R):
    net, sems, loc = Net(dims), Sems(R.ssem, R.rsem), Local(R.lsem)
    n, d = R.resid.shape
    f = R.wup.shape[1] // 4
    layer = 0 if first else 1
    weights = plane_weights(net, sems, R.zup, R.zdn, R.wup, R.wdn)
    peers = [net.group(2), net.group(3), net.partner()]
    peers += [net.plane(e) for e in (1, 2, 3)] + [net.line(r) for r in (1, 2, 3)]
    if first:
        proj = Projections(net, sems, R.wq, R.w0, R.qland, R.zland, R.ext_next)
        later = LineWeights(net, sems, 1, R.w_up, R.w_down, R.zup_next, R.zdn_next)
    else:
        nl = R.dl.shape[0]
        moved = Batch(
            [
                sems.copy(R.dl, R.dyr.at[pl.ds(0, nl)], net.partner()),
                sems.copy(R.ds, R.dyr.at[pl.ds(nl, R.ds.shape[0])], net.partner()),
            ],
            net.moves,
        )
    there = sems.copy(R.n2.at[pl.ds(0, n)], R.n2.at[pl.ds(n, n)], net.group(2))
    back = sems.copy(R.out, R.got, net.group(2))
    net.greet(peers)
    weights.start()
    own = [
        loc.start(R.w_up.at[layer, :, pl.ds(aligned(net.c * f, 128), f)], R.wup.at[:, pl.ds(0, f)]),
        loc.start(R.w_down.at[layer, pl.ds(aligned(net.c * f), f)], R.wdn.at[0]),
    ]
    hooks = {}
    if first:

        def after_chip():
            proj.start()
            later.start(0)

        def second():
            later.recv(0)
            later.start(1)

        hooks = {1: second}
    else:
        after_chip = moved.start
    pending = project_part(
        net, sems, R.resid, R.gain1, R.shift1, R.ext, R.bias, R.fl, R.fs, R.pj_l, R.pj_s, after_chip
    )
    if not first:

        @pl.when(jnp.logical_not(net.moves))
        def _():
            R.dyr[:nl] = R.dl[...]
            R.dyr[nl:] = R.ds[...]

    for src, dst in ((R.fl, R.fl_o), (R.fs, R.fs_o), (R.pj_l, R.pjl_o), (R.pj_s, R.pjs_o)):
        loc.start(src, dst)
    rows, part = R.zup.shape[0], R.zdn.shape[1]
    R.wup[pl.ds(aligned(net.yx * rows), rows), f:] = R.zup[...]
    for k in range(3):
        R.wdn[k + 1, pl.ds(aligned(net.yx * part), part)] = R.zdn[k]
    attend_part(
        net, sems, R.pj_l, R.pj_s, R.att, R.ol, R.os, R.lsel, R.lses, R.cl, R.cs, R.land, hooks
    )
    if first:
        later.recv(1)
        later.start(2)
        proj.forward()
    share = jnp.zeros((1, 1), jnp.float32)
    for carry in (R.cl, R.cs):
        size = carry.shape[1]
        left = (size - 1 - lax.broadcasted_iota(jnp.int32, (1, size), 1)).astype(jnp.float32)
        ratio = carry[size // BR : size // BR + 1] / jnp.maximum(left, 1.0)
        t = 4.0 * (ratio - R.limit[...])
        share = share + jnp.sum(1.0 / (1.0 + jnp.exp(-t)), axis=1, keepdims=True)
    R.share[...] = jnp.broadcast_to(share * 0.25, R.share.shape)
    half = n // 2
    for i in range(2):
        at = slice(i * half, (i + 1) * half)
        R.middle[at] = R.resid[at].astype(jnp.float32) + mm(R.att[at], R.wout[...]) + R.bout[...]
        hat, _ = norm_rows(R.middle[at])
        R.n2[at] = (hat * R.gain2[...] + R.shift2[...]).astype(jnp.bfloat16)
    there.start()
    weights.recv()
    for copy in own:
        copy.wait()
    for src, dst in ((R.wup, R.wup_o), (R.wdn, R.wdn_o)):
        loc.start(src, dst)

    def hidden(at):
        u = mm(R.n2[at], R.wup[...]) + R.bup[...]
        a, s = gelu_pair(u)
        low = a.astype(jnp.bfloat16)
        for i in range(2):
            R.act[i, at] = low[:, 2 * i * f : 2 * (i + 1) * f]
            loc.start(R.act.at[i, at], R.act_o.at[i, at])
        R.slope[at] = s.astype(jnp.bfloat16)
        loc.start(R.slope.at[at], R.slope_o.at[at])

    def down(at):
        return mm(R.act[0, at], R.wdn[0:2].reshape(2 * f, d)) + mm(
            R.act[1, at], R.wdn[2:4].reshape(2 * f, d)
        )

    quarter = n // 2
    for i in range(2):
        hidden(slice(i * quarter, (i + 1) * quarter))
    there.wait_recv()
    for i in range(2):
        hidden(slice(n + i * quarter, n + (i + 1) * quarter))
    for i in range(2):
        R.out[i * half : (i + 1) * half] = down(slice(n + i * half, n + (i + 1) * half)).astype(
            jnp.bfloat16
        )
    back.start()
    for i in range(2):
        at = slice(i * half, (i + 1) * half)
        R.new[at] = R.middle[at] + down(at) + R.bdown[...]
    back.wait_recv()
    R.new[...] += R.got[...].astype(jnp.float32)
    if last:
        R.y[...] = R.new[...].astype(jnp.bfloat16)
    there.wait_send()
    back.wait_send()
    for copy in pending:
        copy.wait_send()
    weights.sent()
    if first:
        proj.finish()
        later.recv(2)
        later.sent()
    else:
        moved.end()
    for copy in loc.copies[2:]:
        copy.wait()


def backward_x(dims, last, R):
    net, sems, loc = Net(dims), Sems(R.ssem, R.rsem), Local(R.lsem)
    f32, bf = jnp.float32, jnp.bfloat16
    n, d = R.g.shape
    f = R.wup.shape[1] // 4
    nl, ns = R.pj_l.shape[0] // 4, R.pj_s.shape[0] // 4
    wid = R.ol.shape[1]
    me, yx = net.me, net.yx
    chunk = d // 4
    there = sems.copy(R.gm.at[pl.ds(0, n)], R.gm.at[pl.ds(n, n)], net.group(2))
    back = sems.copy(R.out.at[0], R.got.at[0], net.group(2))
    cross = sems.copy(R.oself, R.olands, net.group(2))
    big_dn = Batch([sems.copy(R.ddn.at[yx ^ e], R.rdn.at[e - 1], net.plane(e)) for e in (1, 2, 3)])
    big_up = Batch([sems.copy(R.dup.at[yx ^ e], R.rup.at[e - 1], net.plane(e)) for e in (1, 2, 3)])
    big_out = Batch([sems.copy(R.dout.at[yx ^ e], R.rout.at[e - 1], net.plane(e)) for e in (1, 2, 3)])
    base = sems.used
    sems.used += 8
    peers = [net.group(d_) for d_ in (1, 2, 3)] + [net.plane(e) for e in (1, 2, 3)]
    if last:
        moved = Batch(
            [
                sems.copy(R.y.at[pl.ds(0, nl)], R.yr_l, net.partner()),
                sems.copy(R.y.at[pl.ds(nl, ns)], R.yr_s, net.partner()),
            ],
            net.moves,
        )
        peers += [net.partner()]
    else:
        carry = FinishLine(net, sems, R.s_in, R.so_in, R.fland, R.foland, R.s_own)
        ext = Batch(ext_scatter(net, sems, R.dq_in, R.qland) + ext_scatter(net, sems, R.d0_in, R.zland))
        ext_line = ExtLine(net, sems, R.q_sum, R.z_sum, R.qline, R.zline)
        low = Batch([sems.copy(R.s.at[r, 1], R.dnland.at[3 - r], net.line(r)) for r in (1, 2, 3)])
        peers += [net.line(2), net.line(4 - net.zl * 2 - 1)]
    R.gm[:n] = R.g[...].astype(bf)
    net.greet(peers)
    there.start()
    fetched = [loc.start(R.act.at[i], R.buf.at[pl.ds(i * 2 * n, 2 * n)]) for i in range(2)]
    for src, dst in ((R.pjl_i, R.pj_l), (R.pjs_i, R.pj_s), (R.ext_i, R.ext)):
        loc.start(src, dst)
    if last:
        moved.start()

        @pl.when(jnp.logical_not(net.moves))
        def _():
            R.yr_l[...] = R.y[:nl]
            R.yr_s[...] = R.y[nl:]

    else:
        carry.main[0].start()
        for src, dst in ((R.s_in.at[0], R.s_own), (R.dq_in.at[yx], R.dq_own), (R.d0_in.at[yx], R.d0_own)):
            loc.start(src, dst)
    R.rows[...] = jnp.zeros_like(R.rows)
    R.rows[5:6] = jnp.sum(R.g[...].astype(f32), axis=0, keepdims=True)
    half = n // 2
    wdn2 = lambda: R.wdn[...].reshape(4 * f, d)

    def hidden(at):
        u = mm(R.gm[at], wdn2(), NT)
        R.gu[at] = (u * R.slope[at].astype(f32)).astype(bf)

    hidden(slice(0, half))
    there.wait_recv()
    for c in fetched:
        c.wait()
    for k in range(4):
        for i in range(2):
            t = mm(R.gm[:, k * chunk : (k + 1) * chunk], R.buf[i * 2 * n : (i + 1) * 2 * n], TN)
            t = t.astype(bf)
            R.ddn[k, 2 * i] = t[:, :f]
            R.ddn[k, 2 * i + 1] = t[:, f:]
    big_dn.start()
    if not last:
        ext.start()
    fl, fs = R.buf.at[pl.ds(0, 4 * nl)], R.buf.at[pl.ds(4 * nl, 4 * ns)]
    late = [loc.start(R.fl_i, fl), loc.start(R.fs_i, fs)]
    hidden(slice(half, n))
    for i in range(2):
        hidden(slice(n + i * half, n + (i + 1) * half))
    for i in range(2):
        R.out[0, i * half : (i + 1) * half] = mm(
            R.gu[n + i * half : n + (i + 1) * half], R.wup[...], NT
        ).astype(bf)
    back.start()
    for i in range(2):
        R.mine[i * half : (i + 1) * half] = mm(R.gu[i * half : (i + 1) * half], R.wup[...], NT)

    back.wait_recv()
    gn = R.mine[...] + R.got[0].astype(f32)
    hat, inv = norm_rows(R.middle[...])
    gh = gn * R.gain2[...]
    a = jnp.mean(gh, axis=-1, keepdims=True)
    b = jnp.mean(gh * hat, axis=-1, keepdims=True)
    R.gmid[...] = R.g[...].astype(f32) + inv * (gh - a - hat * b)
    R.rows[1:2] = jnp.sum(gn * hat, axis=0, keepdims=True)
    R.rows[3:4] = jnp.sum(gn, axis=0, keepdims=True)
    R.rows[4:5] = jnp.sum(R.gmid[...], axis=0, keepdims=True)
    R.ga[...] = R.gmid[...].astype(bf)
    go = mm(R.ga[...], R.wout[...], NT).astype(bf)
    for m in range(4):
        R.outg[m] = go[:, m * wid : (m + 1) * wid]

    def part(k):
        return ((R.gl, nl, 0), (R.gs, ns, nl))[k]

    def copy(k, m):
        dst, size, at = part(k)
        return send(
            R.outg.at[m, pl.ds(at, size)],
            dst.at[pl.ds(aligned(me * size), size)],
            sems.ssem.at[base + 4 * k + m],
            sems.rsem.at[base + 4 * k + me],
            net.member(m),
        )

    def arrived(k, m):
        dst, size, at = part(k)
        i = base + 4 * k + m
        return send(
            R.outg.at[m, pl.ds(at, size)], dst.at[pl.ds(m * size, size)], sems.ssem.at[i], sems.rsem.at[i], net.member(m)
        )

    for k in (1, 0):
        for m in range(4):
            dst, size, at = part(k)

            @pl.when(me != m)
            def _():
                copy(k, m).start()

            @pl.when(me == m)
            def _():
                dst[m * size : (m + 1) * size] = R.outg[m, at : at + size]

    e = R.att.shape[1] // 2
    other = R.att[:, pl.ds(aligned((1 - net.c) * e, 128), e)]
    R.oself[...] = mm(R.ga[...], other, TN).astype(bf)
    cross.start()
    for k in range(4):
        t = mm(R.n2[:, k * chunk : (k + 1) * chunk], R.gu[...], TN).astype(bf)
        for r in range(4):
            R.dup[k, r] = t[:, r * f : (r + 1) * f]
    big_up.start()
    bup = jnp.sum(R.gu[...].astype(f32), axis=0, keepdims=True)
    for c in range(2):

        @pl.when(net.c == c)
        def _():
            for r in range(4):
                R.rows[pl.ds(16 + (net.z + r) % 4, 1), c * f : (c + 1) * f] = bup[:, r * f : (r + 1) * f]

    own = mm(R.ga[...], R.att[:, pl.ds(aligned(net.c * e, 128), e)], TN)
    cross.wait_recv()
    own = (own + R.olands[...].astype(f32)).astype(bf)
    for k in range(4):
        R.dout[k] = own[k * chunk : (k + 1) * chunk]
    big_out.start()
    if not last:
        late.append(loc.start(R.resid, R.ga))
    done = [id(c) for c in fetched + late]
    for c in loc.copies:
        if id(c) not in done:
            c.wait()
    def add_up(own, land, i):
        for r in range(4):
            t = own[yx, r].astype(f32)
            for k in range(3):
                t = t + land[k, r].astype(f32)
            R.s[r, i] = t.astype(bf)

    def midway(b):
        if b == 2 and not last:
            big_dn.recv()
            add_up(R.ddn, R.rdn, 1)
            low.start()

    for k in (1, 0):
        for m in range(4):

            @pl.when(me != m)
            def _():
                arrived(k, m).wait_recv()

        if k:
            if not last:
                carry.main[1].start()
                carry.start_rest()
            bwd_one(R.pj_s, R.gs, R.os, R.lses, R.cs, R.ds, R.acc, R.kt)
            if not last:
                ext.recv()
                for own_, lands, dst in ((R.dq_own, R.qland, R.q_sum), (R.d0_own, R.zland, R.z_sum)):
                    t = own_[...].astype(f32)
                    for i in range(3):
                        t = t + lands[i].astype(f32)
                    dst[...] = t.astype(bf)
                ext_line.start()
        else:
            bwd_one(R.pj_l, R.gl, R.ol, R.lsel, R.cl, R.dl, R.acc, R.kt, midway)


    def partial(m):
        a = mm(R.dl[pl.ds(aligned(m * nl), nl)], R.ext[...], NT)
        b = mm(R.ds[pl.ds(aligned(m * ns), ns)], R.ext[...], NT)
        return jnp.concatenate([a, b], axis=0)

    back.wait_send()
    to_core = [sems.copy(R.out.at[k], R.got.at[k + 1], net.group(2)) for k in (0, 1)]
    to_chip = sems.copy(R.out.at[2], R.got.at[3], net.group(1))
    R.out[0] = partial(me ^ 3).astype(bf)
    to_core[0].start()
    R.mine[...] = partial(me ^ 1)
    to_core[0].wait_recv()
    R.out[2] = (R.mine[...] + R.got[1].astype(f32)).astype(bf)
    to_chip.start()
    R.out[1] = partial(me ^ 2).astype(bf)
    to_core[1].start()
    R.mine[...] = partial(me)
    nq = R.dq.shape[2]
    for c in late:
        c.wait()
    for k in range(4):
        at = slice(k * chunk, (k + 1) * chunk)
        both = mm(fl[:, at], R.dl[...], TN) + mm(fs[:, at], R.ds[...], TN)
        R.dq[k] = both[:, :nq].astype(bf)
        R.d0[k] = both[:, nq:].astype(bf)
    bsum = jnp.sum(R.dl[...].astype(f32), axis=0, keepdims=True) + jnp.sum(
        R.ds[...].astype(f32), axis=0, keepdims=True
    )
    R.rows[pl.ds(8 + me, 1), :wid] = bsum[:, :wid]
    R.rows[pl.ds(12 + me, 1), :wid] = bsum[:, 2 * wid : 3 * wid]
    R.rows[8:9, :HD] += bsum[:, nq : nq + HD]
    hat, inv = norm_rows(R.resid[...] if last else R.ga[...].astype(f32))
    to_core[1].wait_recv()
    to_chip.wait_recv()
    grad = R.mine[...] + R.got[2].astype(f32) + R.got[3].astype(f32)
    gh = grad * R.gain1[...]
    a = jnp.mean(gh, axis=-1, keepdims=True)
    b = jnp.mean(gh * hat, axis=-1, keepdims=True)
    R.g_new[...] = (R.gmid[...] + inv * (gh - a - hat * b)).astype(R.g_new.dtype)
    R.rows[0:1] = jnp.sum(grad * hat, axis=0, keepdims=True)
    R.rows[2:3] = jnp.sum(grad, axis=0, keepdims=True)
    for c in to_core + [to_chip, there, cross]:
        c.wait_send()
    for m in range(4):

        @pl.when(me != m)
        def _():
            for k in range(2):
                copy(k, m).wait_send()

    if last:
        moved.end()
    else:
        carry.finish(R.f_out, R.fo_out)
        ext.sent()
        ext_line.finish(R.q_out, R.z_out)
        low.recv()
        t = R.s[0, 1].astype(f32)
        for k in range(3):
            t = t + R.dnland[k].astype(f32)
        R.dn_out[...] = t.astype(bf)
        low.sent()

    if last:
        big_dn.recv()
        add_up(R.ddn, R.rdn, 1)
    big_up.recv()
    add_up(R.dup, R.rup, 0)
    big_out.recv()
    t = R.dout[yx].astype(f32)
    for k in range(3):
        t = t + R.rout[k].astype(f32)
    for i in range(2):
        R.so[i] = t[:, i * wid : (i + 1) * wid].astype(bf)
    big_dn.sent()
    big_up.sent()
    big_out.sent()


class ExtLine:
    def __init__(self, net, sems, q, z, qline, zline):
        self.net, self.q, self.z, self.qline, self.zline = net, q, z, qline, zline
        self.qsend = Batch([sems.copy(q, qline, net.line(2))], net.moves)
        self.stays = jnp.logical_not(net.moves)
        self.zsend = [sems.copy(z, zline.at[r - 1], net.line(r)) for r in (1, 2, 3)]

    def start(self):
        self.qsend.start()
        for r in (1, 2, 3):
            pl.when(self.net.z == 4 - r)(self.zsend[r - 1].start)

    def finish(self, q_out, z_out):
        f32 = jnp.float32
        q_out[...] = self.q[...].astype(q_out.dtype)
        z_out[...] = self.z[...].astype(z_out.dtype)

        @pl.when(self.stays)
        def _():
            self.qsend.copies[0].wait_recv()
            q_out[...] = (self.q[...].astype(f32) + self.qline[...].astype(f32)).astype(q_out.dtype)

        @pl.when(self.net.z == 0)
        def _():
            t = self.z[...].astype(f32)
            for r in (1, 2, 3):
                self.zsend[r - 1].wait_recv()
                t = t + self.zline[r - 1].astype(f32)
            z_out[...] = t.astype(z_out.dtype)

        self.qsend.sent()
        for r in (1, 2, 3):
            pl.when(self.net.z == 4 - r)(self.zsend[r - 1].wait_send)


def tail_x(axes, R):
    dims = axes[:-2]
    net, sems = Net(dims), Sems(R.ssem, R.rsem)
    f32, bf = jnp.float32, jnp.bfloat16
    moved = Batch([sems.copy(R.dx, R.dxr, net.partner())], net.moves)
    line = FinishLine(net, sems, R.s.at[:, pl.ds(0, 1)], R.so, R.land, R.oland)
    ext = Batch(ext_scatter(net, sems, R.dq, R.qland) + ext_scatter(net, sems, R.d0, R.zland))
    nv = len(axes)
    rounds = [{ax: 1 - lax.axis_index(ax)} for ax in axes[::-1]]
    steps = [sems.copy(R.vland.at[i], R.vland.at[nv + 1 + i], peer) for i, peer in enumerate(rounds)]
    ext_line = ExtLine(net, sems, R.q_sum, R.z_sum, R.qline, R.zline)
    qrecv = jnp.logical_not(net.moves)
    cross = Batch(
        [sems.copy(R.fself, R.fland, net.group(2)), sems.copy(R.zself, R.zlands, net.group(2))]
    )
    owned = Batch(
        [sems.copy(R.oself, R.olands, net.group(2)), sems.copy(R.qself, R.qlands, net.group(2))],
        None,
    )
    net.greet(
        [net.partner(), net.group(2)]
        + [net.line(r) for r in (1, 2, 3)]
        + [net.plane(e) for e in (1, 2, 3)]
    )
    ext.start()
    line.start()
    nr = R.rows0.shape[0]
    R.vland[0, :nr] = R.rows0[...]
    R.vland[0, nr:] = R.rows1[...]
    R.vland[0, 6:7] = jnp.broadcast_to(R.share0[:1, :1], (1, R.rows0.shape[1]))
    R.vland[0, nr + 6 : nr + 7] = jnp.broadcast_to(R.share1[:1, :1], (1, R.rows0.shape[1]))

    def step(i):
        steps[i].wait()
        R.vland[i + 1] = R.vland[i] + R.vland[nv + 1 + i]
        if i + 1 < nv:
            steps[i + 1].start()

    steps[0].start()
    step(0)
    step(1)
    ext.recv()
    yx = net.yx
    for own, lands, dst in ((R.dq, R.qland, R.q_sum), (R.d0, R.zland, R.z_sum)):
        t = own[yx].astype(f32)
        for e in range(3):
            t = t + lands[e].astype(f32)
        dst[...] = t.astype(bf)
    ext_line.start()
    moved.start()
    step(2)
    step(3)
    step(4)
    nl = R.dx_l.shape[0]
    half = R.f0.shape[1] // 2
    theirs = pl.ds(aligned((1 - net.c) * half), half)
    ours = pl.ds(aligned(net.c * half), half)

    @pl.when(qrecv)
    def _():
        R.dx_l[...] = R.dx[:nl].astype(f32)
        R.dx_s[...] = R.dx[nl:].astype(f32)

    wq = R.gqkv.shape[3]

    def put(l, v):
        for i in range(3):
            R.gqkv[l, i] = v[:, i * wq : (i + 1) * wq]

    ext_line.finish(R.q0, R.z0)

    @pl.when(qrecv)
    def _():
        for l, q in ((0, R.q0), (1, R.q1)):
            R.qself[l] = q[theirs].astype(bf)
            put(l, q[ours].astype(f32))

    tot = R.vland.at[nv]
    for l in range(2):
        at = l * nr
        for i in range(2):
            R.g_gain[l, i : i + 1] = tot[at + i : at + i + 1]
            R.g_bias[l, i : i + 1] = tot[at + 2 + i : at + 3 + i]
            R.g_bqv[l, i : i + 1] = tot[pl.ds(at + 8 + 4 * i + net.z, 1), : R.g_bqv.shape[2]]
        R.g_bout[l : l + 1] = tot[at + 4 : at + 5]
        R.g_bdown[l : l + 1] = tot[at + 5 : at + 6]
        R.g_bup[l : l + 1] = tot[pl.ds(at + 16 + net.z, 1)]
        R.shares[l : l + 1] = tot[at + 6 : at + 7, :128] / (32 * R.dx.shape[0])
    line.finish(R.f0, R.fo0)

    @pl.when(qrecv)
    def _():
        for l, fo in ((0, R.fo0), (1, R.fo1)):
            R.oself[l] = fo[theirs].astype(bf)
            R.gout[l] = jnp.transpose(fo[ours].astype(f32))
        for c in owned.copies:
            c.start()

    for l, fs in ((0, (R.f0.at[0], R.dn0)), (1, (R.f1.at[0], R.f1.at[1]))):
        for i in range(2):
            R.fself[l, i] = fs[i][theirs].astype(bf)
    for l, z in ((0, R.z0), (1, R.z1)):
        R.zself[l] = z[theirs].astype(bf)
    cross.start()
    n = R.f0.shape[2]
    for c in range(2):

        @pl.when(net.c == c)
        def _():
            for l, fs in ((0, (R.f0.at[0], R.dn0)), (1, (R.f1.at[0], R.f1.at[1]))):
                R.gup[l, :, c * n : (c + 1) * n] = fs[0][ours].astype(f32)
                R.gdn[l, :, c * n : (c + 1) * n] = fs[1][ours].astype(f32)

    cross.recv()
    for c in range(2):

        @pl.when(net.c != c)
        def _():
            for l in range(2):
                R.gup[l, :, c * n : (c + 1) * n] = R.fland[l, 0].astype(f32)
                R.gdn[l, :, c * n : (c + 1) * n] = R.fland[l, 1].astype(f32)

    @pl.when(net.moves)
    def _():
        for c in owned.copies:
            c.wait_recv()
        for l in range(2):
            put(l, R.qlands[l].astype(f32))
            R.gout[l] = jnp.transpose(R.olands[l].astype(f32))

    @pl.when(net.z == 0)
    def _():
        wid = R.gout.shape[1]
        for l, z in ((0, R.z0), (1, R.z1)):
            t = z[ours].astype(f32) + R.zlands[l].astype(f32)
            R.gqkv[l, 0, :, :HD] += t[:, :HD]
            R.gqkv[l, 1, :, :HD] += t[:, HD:]

    moved.recv()

    @pl.when(net.moves)
    def _():
        R.dx_l[...] = R.dxr[:nl].astype(f32)
        R.dx_s[...] = R.dxr[nl:].astype(f32)

    pl.when(qrecv)(lambda: [c.wait_send() for c in owned.copies] and None)
    cross.sent()
    ext.sent()
    moved.sent()


def results_k(*refs):
    k = len(refs) // 2
    sem = refs[-1]
    copies = [pltpu.make_async_copy(refs[i], refs[k + i], sem.at[i]) for i in range(k)]
    for copy in copies:
        copy.start()
    for copy in copies:
        copy.wait()


def results(arrays):
    return pl.pallas_call(
        results_k,
        out_shape=tuple(jax.ShapeDtypeStruct(a.shape, a.dtype) for a in arrays),
        in_specs=[ANY] * len(arrays),
        out_specs=(VMEM,) * len(arrays),
        scratch_shapes=[DMA((len(arrays),))],
        compiler_params=pltpu.CompilerParams(vmem_limit_bytes=60 * 1024 * 1024),
        name="results_k",
    )(*arrays)


def run(kernel, static, ins, outs, scratch, ident, name, flops):
    names = list(ins) + list(outs) + list(scratch)

    def body_of(*refs):
        kernel(*static, types.SimpleNamespace(**dict(zip(names, refs))))

    res = pl.pallas_call(
        body_of,
        out_shape=tuple(jax.ShapeDtypeStruct(tuple(s), t) for s, t, _ in outs.values()),
        in_specs=[VMEM if v else ANY for _, v in ins.values()],
        out_specs=tuple(VMEM if v else ANY for _, _, v in outs.values()),
        scratch_shapes=list(scratch.values()),
        compiler_params=pltpu.CompilerParams(
            vmem_limit_bytes=60 * 1024 * 1024, collective_id=ident, has_side_effects=True
        ),
        cost_estimate=pl.CostEstimate(flops=flops, bytes_accessed=10**7, transcendentals=10**6),
        name=name,
    )(*[a for a, _ in ins.values()])
    return types.SimpleNamespace(**dict(zip(outs, res)))


def fast_body(
    dims, x_long, x_short, dy_long, dy_short, ln_gain, ln_bias, w_qkv, b_qv, w_out, b_out, w_up, b_up, w_down, b_down, threshold
):
    bf, f32 = jnp.bfloat16, jnp.float32
    layers, d = w_qkv.shape[0], w_qkv.shape[1]
    wid, ffq = w_qkv.shape[3], w_up.shape[2]
    rl, rs = x_long.shape[1], x_short.shape[1]
    n = rl + rs
    sl, ss = 4 * rl, 4 * rs
    nq, nx, n0 = 3 * wid, 3 * wid + 2 * HD, 2 * HD
    nh = wid // HD
    f = ffq // 2
    ff = 4 * f
    chunk, part = d // 4, f // 4
    half = chunk // 2
    net = Net(dims)
    axes = dims + ("zh", "zl")
    vm = lambda *s: pltpu.VMEM(tuple(s), bf)
    vf = lambda *s: pltpu.VMEM(tuple(s), f32)
    sem2 = lambda k: dict(ssem=DMA((k,)), rsem=DMA((k,)))

    wqs = [w_qkv[l].reshape(d, nq) for l in range(layers)]
    w0s = [w_qkv[l][:, :2, :HD].reshape(d, n0) for l in range(layers)]
    flat = jnp.concatenate([b_up.reshape(-1), b_qv.reshape(-1)])
    flat = jnp.pad(flat, (0, -flat.shape[0] % 4096)).reshape(16, -1)
    share_rows = wid // 8
    wo = lax.dynamic_slice_in_dim(w_out, (4 * net.y + 2 * net.x + net.c) * share_rows, share_rows, 1)
    wo = [lax.all_gather(wo[l], ("zh", "zl") + dims, axis=0, tiled=True) for l in range(layers)]

    lands = dict(qland=vm(4, chunk, nq), zland=vm(4, chunk, n0))
    P0 = run(
        first_x,
        (dims,),
        dict(xl=(x_long[0], 1), xs=(x_short[0], 1), wq=(wqs[0], 1), w0=(w0s[0], 1), small=(flat, 1), w_up=(w_up, 0), w_down=(w_down, 0)),
        dict(
            xr=((n, d), bf, 1), ext=((d, nx), bf, 1), smalls=((4,) + flat.shape, bf, 1),
            zup=((chunk, 3 * f), bf, 0), zdn=((3, part, d), bf, 0),
        ),
        dict(**lands, **sem2(32)),
        1,
        "first_x",
        10**9,
    )
    n_up = layers * ffq
    smalls = P0.smalls.reshape(4, -1)
    rel_bup = smalls[:, :n_up].reshape(4, layers, 2, f).astype(f32)
    rel_bup = lax.dynamic_index_in_dim(rel_bup, net.c, 2, keepdims=False)
    rel_bup = jnp.swapaxes(rel_bup, 0, 1).reshape(layers, ff)
    rel_bqv = smalls[:, n_up : n_up + layers * 2 * wid].reshape(4, layers, 2, wid).astype(f32)
    my_bqv = lax.dynamic_index_in_dim(rel_bqv, (net.me - net.z) % 4, 0, keepdims=False)
    zero_bq = lax.dynamic_index_in_dim(rel_bqv, (0 - net.z) % 4, 0, keepdims=False)[:, 0, :HD]
    none = jnp.zeros((layers, wid), f32)
    bias = jnp.concatenate([my_bqv[:, 0], none, my_bqv[:, 1], zero_bq, none[:, :HD]], axis=1)
    gain, shift = ln_gain.astype(f32), ln_bias.astype(f32)
    bo, bd = b_out.astype(f32), b_down.astype(f32)
    limits = (threshold.astype(f32) / 64.0)[:, None]

    resid, zup, zdn = P0.xr, P0.zup, P0.zdn
    exts = [P0.ext]
    saved = []
    for l in range(layers):
        first, last = l == 0, l == layers - 1
        ins = dict(
            resid=(resid, 1), gain1=(gain[l, :1], 1), shift1=(shift[l, :1], 1), gain2=(gain[l, 1:], 1), shift2=(shift[l, 1:], 1),
            ext=(exts[l], 1), bias=(bias[l : l + 1], 1), w_up=(w_up, 0), w_down=(w_down, 0), zup=(zup, 1), zdn=(zdn, 1),
            wout=(wo[l], 1), bout=(bo[l : l + 1], 1), bup=(rel_bup[l : l + 1], 1), bdown=(bd[l : l + 1], 1), limit=(limits[l : l + 1], 1),
        )
        outs = dict(
            fl_o=((sl, d), bf, 0), fs_o=((ss, d), bf, 0), pjl_o=((sl, nx), bf, 0), pjs_o=((ss, nx), bf, 0),
            att=((n, 4 * wid), bf, 1), ol=((sl, wid), bf, 1), os=((ss, wid), bf, 1),
            lsel=((8, sl), f32, 1), lses=((8, ss), f32, 1), cl=((8, sl), f32, 1), cs=((8, ss), f32, 1),
            wup_o=((d, ff), bf, 0), wdn_o=((4, f, d), bf, 0), middle=((n, d), f32, 1), n2=((2 * n, d), bf, 1),
            act_o=((2, 2 * n, 2 * f), bf, 0), slope_o=((2 * n, ff), bf, 0), new=((n, d), f32, 1), share=((8, 128), f32, 1),
        )
        scratch = dict(
            fl=vm(sl, d), fs=vm(ss, d), pj_l=vm(sl, nx), pj_s=vm(ss, nx), wup=vm(d, ff), wdn=vm(4, f, d),
            act=vm(2, 2 * n, 2 * f), slope=vm(2 * n, ff), land=vm(4, n, wid), out=vm(n, d), got=vm(n, d), lsem=DMA((24,)),
            **sem2(48),
        )
        if first:
            ins.update(wq=(wqs[1], 1), w0=(w0s[1], 1))
            outs.update(ext_next=((d, nx), bf, 1), zup_next=((chunk, 3 * f), bf, 0), zdn_next=((3, part, d), bf, 0))
            scratch.update(lands)
        else:
            ins.update(dl=(dy_long[0], 1), ds=(dy_short[0], 1))
            outs.update(dyr=((n, d), bf, 1))
        if last:
            outs.update(y=((n, d), bf, 1))
        A = run(forward_x, (dims, first, last), ins, outs, scratch, 2 + l, "forward_x", 10**10)
        A.resid = resid
        saved.append(A)
        resid = A.new
        if first:
            exts.append(A.ext_next)
            zup, zdn = A.zup_next, A.zdn_next

    g = saved[-1].dyr
    back = [None] * layers
    B = None
    for l in reversed(range(layers)):
        A = saved[l]
        last = l == layers - 1
        ins = dict(
            g=(g, 1), att=(A.att, 1), wout=(wo[l], 1), gain1=(gain[l, :1], 1), gain2=(gain[l, 1:], 1), wup=(A.wup_o, 1), wdn=(A.wdn_o, 1),
            middle=(A.middle, 1), n2=(A.n2, 1), act=(A.act_o, 0), slope=(A.slope_o, 1), resid=(A.resid, int(last)),
            pjl_i=(A.pjl_o, 0), pjs_i=(A.pjs_o, 0), ext_i=(exts[l], 0), fl_i=(A.fl_o, 0), fs_i=(A.fs_o, 0),
            ol=(A.ol, 1), os=(A.os, 1), lsel=(A.lsel, 1), lses=(A.lses, 1), cl=(A.cl, 1), cs=(A.cs, 1),
        )
        outs = dict(
            g_new=((n, d), f32 if l else bf, 1), rows=((24, d), f32, 1), dq=((4, chunk, nq), bf, 1), d0=((4, chunk, n0), bf, 1),
            s=((4, 2, chunk, f), bf, 1), so=((2, chunk, wid), bf, 1),
        )
        scratch = dict(
            gm=vm(2 * n, d), gu=vm(2 * n, ff), mine=vf(n, d), out=vm(3, n, d), got=vm(4, n, d), gmid=vf(n, d), ga=vm(n, d),
            oself=vm(d, 2 * wid), olands=vm(d, 2 * wid), dup=vm(4, 4, chunk, f), ddn=vm(4, 4, chunk, f), dout=vm(4, chunk, 2 * wid),
            rup=vm(3, 4, chunk, f), rdn=vm(3, 4, chunk, f), rout=vm(3, chunk, 2 * wid),
            outg=vm(4, n, wid), gl=vm(sl, wid), gs=vm(ss, wid), pj_l=vm(sl, nx), pj_s=vm(ss, nx), ext=vm(d, nx),
            buf=vm(sl + ss, d), dl=vm(sl, nx), ds=vm(ss, nx), acc=vf(2 * nh + 1, sl, HD), kt=vm(nh + 1, HD, sl),
            lsem=DMA((12,)), **sem2(48),
        )
        if last:
            ins.update(y=(A.y, 1))
            outs.update(yr_l=((rl, d), bf, 1), yr_s=((rs, d), bf, 1))
        else:
            ins.update(s_in=(B.s, 0), so_in=(B.so, 1), dq_in=(B.dq, 0), d0_in=(B.d0, 0))
            outs.update(
                dn_out=((chunk, f), bf, 1), f_out=((2, chunk, f), bf, 1), fo_out=((chunk, wid), bf, 1), q_out=((chunk, nq), bf, 1), z_out=((chunk, n0), bf, 1)
            )
            scratch.update(
                q_sum=vm(chunk, nq), z_sum=vm(chunk, n0), qline=vm(chunk, nq), zline=vm(3, chunk, n0), dnland=vm(3, chunk, f),
                s_own=vm(2, chunk, f), dq_own=vm(chunk, nq), d0_own=vm(chunk, n0), fland=vm(3, 2, chunk, f), foland=vm(3, chunk, wid), qland=vm(3, chunk, nq), zland=vm(3, chunk, n0))
        B = run(backward_x, (dims, last), ins, outs, scratch, 6 + l, "backward_x", 2 * 10**10)
        back[l] = B
        g = B.g_new
        if last:
            y_l, y_s = B.yr_l, B.yr_s

    nv = len(axes)
    T = run(
        tail_x,
        (axes,),
        dict(
            s=(B.s, 1), so=(B.so, 1), dq=(B.dq, 1), d0=(B.d0, 1), f1=(B.f_out, 1), fo1=(B.fo_out, 1), q1=(B.q_out, 1), z1=(B.z_out, 1),
            rows0=(back[0].rows, 1), dn0=(B.dn_out, 1), rows1=(back[1].rows, 1), share0=(saved[0].share, 1), share1=(saved[1].share, 1), dx=(g, 1),
        ),
        dict(
            gup=((2, half, ffq), f32, 1), gdn=((2, half, ffq), f32, 1), gout=((2, wid, half), f32, 1), gqkv=((2, 3, half, wid), f32, 1),
            dx_l=((rl, d), f32, 1), dx_s=((rs, d), f32, 1), g_gain=((2, 2, d), f32, 1), g_bias=((2, 2, d), f32, 1),
            g_bqv=((2, 2, wid), f32, 1), g_bout=((2, d), f32, 1), g_bdown=((2, d), f32, 1), g_bup=((2, ffq), f32, 1),
            shares=((2, 128), f32, 1),
        ),
        dict(
            land=vm(3, 1, chunk, f), oland=vm(3, chunk, wid), f0=vf(1, chunk, f), fo0=vf(chunk, wid), q0=vf(chunk, nq), z0=vf(chunk, n0),
            qland=vm(3, chunk, nq), zland=vm(3, chunk, n0), q_sum=vm(chunk, nq), z_sum=vm(chunk, n0), qline=vm(chunk, nq),
            zline=vm(3, chunk, n0), fself=vm(2, 2, half, f), fland=vm(2, 2, half, f), oself=vm(2, half, wid),
            olands=vm(2, half, wid), qself=vm(2, half, nq), qlands=vm(2, half, nq), zself=vm(2, half, n0), zlands=vm(2, half, n0),
            vland=vf(2 * nv + 1, 48, d), dxr=vm(n, d), **sem2(32),
        ),
        10,
        "tail_x",
        10**9,
    )
    done = results(
        (
            y_l, y_s, T.dx_l, T.dx_s, T.g_gain, T.g_bias, T.gqkv, T.g_bqv, T.gout, T.g_bout, T.gup, T.g_bup, T.gdn, T.g_bdown
        )
    )
    y_l, y_s, dx_l, dx_s, g_gain, g_bias, gqkv, g_bqv, gout, g_bout, gup, g_bup, gdn, g_bdown = done
    return (
        y_l[None], y_s[None], dx_l[None], dx_s[None], g_gain, g_bias, jnp.swapaxes(gqkv, 1, 2), g_bqv, gout, g_bout, gup, g_bup,
        jnp.swapaxes(gdn, 1, 2), g_bdown, T.shares[:, 0],
    )


def solution(mesh):
    dp, mp = mesh.shape["dp"], mesh.shape["mp"]
    bits = dp.bit_length() - 1
    dims = tuple(f"d{i}" for i in range(bits))
    fine = Mesh(mesh.devices.reshape((2,) * bits + (2, mp // 2)), dims + ("zh", "zl"))
    z = ("zh", "zl")
    in_specs = (
        P(dims, z, None), P(dims, z, None), P(dims, z, None), P(dims, z, None),
        P(), P(), P(None, None, None, z), P(None, None, z), P(None, z, None), P(),
        P(None, None, z), P(None, z), P(None, z, None), P(), P(),
    )
    out_specs = (
        P(dims, z, None), P(dims, z, None), P(dims, z, None), P(dims, z, None),
        P(), P(), P(None, dims, None, z), P(None, None, z), P(None, z, dims), P(),
        P(None, dims, z), P(None, z), P(None, z, dims), P(), P(),
    )
    run = functools.partial(fast_body, dims) if dp == 8 else functools.partial(body, dims, dp, mp)
    return jax.shard_map(
        run, mesh=fine, in_specs=in_specs, out_specs=out_specs, check_vma=False
    )
```

```python
import functools
import types

import jax, jax.numpy as jnp
from jax import lax
from jax.experimental import pallas as pl
from jax.experimental.pallas import tpu as pltpu
from jax.sharding import Mesh
from jax.sharding import PartitionSpec as P

HD = 64
BR = 256
BIG = 1e30
NT = (((1,), (1,)), ((), ()))
NN = (((1,), (0,)), ((), ()))


def mm(a, b, dims=NN):
    return lax.dot_general(a, b, dims, preferred_element_type=jnp.float32)


def halves(v):
    hi = v.astype(jnp.bfloat16)
    lo = (v - hi.astype(jnp.float32)).astype(jnp.bfloat16)
    return hi, lo


def softplus(v):
    return jnp.maximum(v, 0.0) + jnp.log(1.0 + jnp.exp(-jnp.abs(v)))


def fwd_one(x_ref, o_ref, lse_ref, carry_ref, done=None):
    size = x_ref.shape[0]
    nh = (x_ref.shape[1] - 2 * HD) // (3 * HD)
    w = nh * HD
    nb = size // BR
    first = lax.broadcasted_iota(jnp.int32, (BR, BR), 0)
    second = lax.broadcasted_iota(jnp.int32, (BR, BR), 1)
    tri = (first > second).astype(jnp.bfloat16)
    lanes = lax.broadcasted_iota(jnp.int32, (BR, 128), 1)
    lse_ref[...] = jnp.zeros_like(lse_ref)
    carry_ref[...] = jnp.zeros_like(carry_ref)
    for b in range(nb):
        rows = pl.ds(b * BR, BR)
        q0 = x_ref[rows, 3 * w : 3 * w + HD] * 0.125
        pens = []
        for c in range(b + 1):
            cols = pl.ds(c * BR, BR)
            sp = softplus(mm(q0, x_ref[cols, 3 * w + HD : 3 * w + 2 * HD], NT))
            if c == b:
                keep = first > second
                if c == 0:
                    keep = jnp.logical_and(keep, second >= 1)
                sp = jnp.where(keep, sp, 0.0)
            elif c == 0:
                sp = jnp.where(second >= 1, sp, 0.0)
            hi, lo = halves(sp)
            pen = mm(tri, hi) + mm(tri, lo) + carry_ref[b : b + 1, cols]
            carry_ref[b + 1 : b + 2, cols] = pen[BR - 1 :] + sp[BR - 1 :]
            if c == b:
                pen = jnp.where(first >= second, pen, BIG)
            pens.append(pen)
        stats = jnp.zeros((BR, 128), jnp.float32)
        for h in range(nh):
            qh = x_ref[rows, h * HD : (h + 1) * HD] * 0.125
            scores = [
                mm(qh, x_ref[c * BR : (c + 1) * BR, w + h * HD : w + (h + 1) * HD], NT) - pens[c]
                for c in range(b + 1)
            ]
            top = scores[0]
            for s in scores[1:]:
                top = jnp.maximum(top, s)
            top = jnp.max(top, axis=1, keepdims=True)
            total = None
            acc = None
            for c in range(b + 1):
                e = jnp.exp(scores[c] - top)
                total = e if total is None else total + e
                part = mm(
                    e.astype(jnp.bfloat16),
                    x_ref[c * BR : (c + 1) * BR, 2 * w + h * HD : 2 * w + (h + 1) * HD],
                )
                acc = part if acc is None else acc + part
            total = jnp.sum(total, axis=1, keepdims=True)
            o_ref[rows, h * HD : (h + 1) * HD] = (acc / total).astype(jnp.bfloat16)
            stats = jnp.where(lanes == h, top + jnp.log(total), stats)
        lse_ref[:, rows] = jnp.transpose(stats)[:8]
        if done is not None:
            done(b)


def bwd_one(x_ref, g_ref, o_ref, lse_ref, carry_ref, d_ref, acc, kt, midway=None):
    size = x_ref.shape[0]
    nh = (x_ref.shape[1] - 2 * HD) // (3 * HD)
    w = nh * HD
    nb = size // BR
    jj = lax.broadcasted_iota(jnp.int32, (BR, BR), 0)
    ii = lax.broadcasted_iota(jnp.int32, (BR, BR), 1)
    below = (jj < ii).astype(jnp.bfloat16)
    above = (jj > ii).astype(jnp.bfloat16)
    ones = jnp.ones((8, HD), jnp.bfloat16)
    for h in range(nh + 1):
        lo = 3 * w + HD if h == nh else w + h * HD
        kt[h, :, :size] = jnp.transpose(x_ref[:, lo : lo + HD].astype(jnp.float32)).astype(
            jnp.bfloat16
        )
    later = [None] * nb
    for b in reversed(range(nb)):
        rows = pl.ds(b * BR, BR)
        q0 = x_ref[rows, 3 * w : 3 * w + HD] * 0.125
        pens, sigs, sums = [], [], [None] * (b + 1)
        for c in range(b + 1):
            sel = mm(x_ref[c * BR : (c + 1) * BR, 3 * w + HD : 3 * w + 2 * HD], q0, NT)
            small = jnp.exp(-jnp.abs(sel))
            sp = jnp.maximum(sel, 0.0) + jnp.log(1.0 + small)
            sig = jnp.where(sel >= 0, 1.0, small) / (1.0 + small)
            if c == b or c == 0:
                keep = None
                if c == b:
                    keep = ii > jj
                if c == 0:
                    keep = jj >= 1 if keep is None else jnp.logical_and(keep, jj >= 1)
                sp = jnp.where(keep, sp, 0.0)
                sig = jnp.where(keep, sig, 0.0)
            hi, lo = halves(sp)
            start = jnp.transpose(
                jnp.broadcast_to(carry_ref[b : b + 1, c * BR : (c + 1) * BR], (128, BR))
            )
            pen = mm(hi, below) + mm(lo, below) + start[:, :1]
            if c == b:
                pen = jnp.where(ii >= jj, pen, BIG)
            pens.append(pen)
            sigs.append(sig)
        for h in range(nh):
            qh = x_ref[rows, h * HD : (h + 1) * HD] * 0.125
            gh = g_ref[rows, h * HD : (h + 1) * HD]
            prod = gh.astype(jnp.float32) * o_ref[rows, h * HD : (h + 1) * HD].astype(jnp.float32)
            phi, plo = halves(prod)
            delta = (mm(ones, phi, NT) + mm(ones, plo, NT))[:1]
            lse = lse_ref[h : h + 1, rows]
            dqt = None
            for c in range(b + 1):
                cols = pl.ds(c * BR, BR)
                s = mm(x_ref[cols, w + h * HD : w + (h + 1) * HD], qh, NT)
                p = jnp.exp((s - pens[c]) - lse)
                dp = mm(x_ref[cols, 2 * w + h * HD : 2 * w + (h + 1) * HD], gh, NT)
                ds = p * (dp - delta)
                low = ds.astype(jnp.bfloat16)
                dk = mm(low, qh)
                dv = mm(p.astype(jnp.bfloat16), gh)
                part = mm(kt[h, :, c * BR : (c + 1) * BR], low)
                dqt = part if dqt is None else dqt + part
                if b == nb - 1:
                    acc[h, cols] = dk
                    acc[nh + h, cols] = dv
                else:
                    acc[h, cols] += dk
                    acc[nh + h, cols] += dv
                sums[c] = ds if sums[c] is None else sums[c] + ds
            d_ref[rows, h * HD : (h + 1) * HD] = jnp.transpose(dqt * 0.125).astype(jnp.bfloat16)
        dqt = None
        for c in range(b + 1):
            cols = pl.ds(c * BR, BR)
            hi, lo = halves(sums[c])
            grad = mm(hi, above) + mm(lo, above)
            full = grad[:, :1] + sums[c][:, :1]
            if later[c] is not None:
                grad = grad + later[c]
                full = full + later[c]
            later[c] = full
            low = (-(grad * sigs[c])).astype(jnp.bfloat16)
            dk = mm(low, q0)
            part = mm(kt[nh, :, c * BR : (c + 1) * BR], low)
            dqt = part if dqt is None else dqt + part
            if b == nb - 1:
                acc[2 * nh, cols] = dk
            else:
                acc[2 * nh, cols] += dk
        d_ref[rows, 3 * w : 3 * w + HD] = jnp.transpose(dqt * 0.125).astype(jnp.bfloat16)
        if midway is not None:
            midway(b)
    for h in range(nh):
        d_ref[:, w + h * HD : w + (h + 1) * HD] = acc[h, :size].astype(jnp.bfloat16)
        d_ref[:, 2 * w + h * HD : 2 * w + (h + 1) * HD] = acc[nh + h, :size].astype(jnp.bfloat16)
    d_ref[:, 3 * w + HD : 3 * w + 2 * HD] = acc[2 * nh, :size].astype(jnp.bfloat16)


VMEM = pl.BlockSpec(memory_space=pltpu.VMEM)
LIMIT = 48 * 1024 * 1024


def attend_fwd(x):
    size, w = x.shape[0], (x.shape[1] - 2 * HD) // 3
    return pl.pallas_call(
        fwd_one,
        out_shape=(
            jax.ShapeDtypeStruct((size, w), jnp.bfloat16),
            jax.ShapeDtypeStruct((8, size), jnp.float32),
            jax.ShapeDtypeStruct((8, size), jnp.float32),
        ),
        in_specs=[VMEM],
        out_specs=(VMEM,) * 3,
        compiler_params=pltpu.CompilerParams(vmem_limit_bytes=LIMIT),
        cost_estimate=pl.CostEstimate(
            flops=size * size * 64 * 40, bytes_accessed=size * 2000, transcendentals=size * size * 3
        ),
        name="attend_fwd",
    )(x)


def attend_bwd(x, g, o, lse, carry):
    size, w = x.shape[0], (x.shape[1] - 2 * HD) // 3
    nh = w // HD
    return pl.pallas_call(
        bwd_one,
        out_shape=jax.ShapeDtypeStruct(x.shape, jnp.bfloat16),
        in_specs=[VMEM] * 5,
        out_specs=VMEM,
        scratch_shapes=[
            pltpu.VMEM((2 * nh + 1, size, HD), jnp.float32),
            pltpu.VMEM((nh + 1, HD, size), jnp.bfloat16),
        ],
        compiler_params=pltpu.CompilerParams(vmem_limit_bytes=LIMIT),
        cost_estimate=pl.CostEstimate(
            flops=size * size * 64 * 80, bytes_accessed=size * 4000, transcendentals=size * size * 3
        ),
        name="attend_bwd",
    )(x, g, o, lse, carry)


class Group:
    def __init__(self, core):
        self.core = core
        self.c = lax.axis_index(core)
        self.zl = lax.axis_index("zl")
        self.me = 2 * self.c + self.zl

    def peer(self, delta):
        return {self.core: self.c ^ (delta >> 1), "zl": self.zl ^ (delta & 1)}

    def member(self, m):
        return {self.core: m >> 1, "zl": m & 1}

    def greet(self, deltas):
        barrier = pltpu.get_barrier_semaphore()
        for delta in deltas:
            pl.semaphore_signal(
                barrier, inc=1, device_id=self.peer(delta), device_id_type=pl.DeviceIdType.MESH
            )
        pl.semaphore_wait(barrier, len(deltas))


def send(src, dst, ssem, rsem, device):
    return pltpu.make_async_remote_copy(
        src_ref=src,
        dst_ref=dst,
        send_sem=ssem,
        recv_sem=rsem,
        device_id=device,
        device_id_type=pl.DeviceIdType.MESH,
    )


def fwd_x(core, xl, xs, att, ol, os, lsel, lses, cl, cs, land, ssem, rsem):
    group = Group(core)
    nl, ns = xl.shape[0] // 4, xs.shape[0] // 4
    group.greet((1, 2, 3))

    def copy(k, m):
        src, n, at = ((ol, nl, 0), (os, ns, nl))[k]
        return send(
            src.at[pl.ds(m * n, n)],
            land.at[group.me, pl.ds(at, n)],
            ssem.at[k, m],
            rsem.at[k, group.me],
            group.member(m),
        )

    def arrived(k, m):
        src, n, at = ((ol, nl, 0), (os, ns, nl))[k]
        return send(
            src.at[pl.ds(0, n)], land.at[m, pl.ds(at, n)], ssem.at[k, m], rsem.at[k, m], group.member(m)
        )

    def start(k, m):
        src, n, at = ((ol, nl, 0), (os, ns, nl))[k]

        @pl.when(group.me != m)
        def _():
            copy(k, m).start()

        @pl.when(group.me == m)
        def _():
            land[m, at : at + n] = src[m * n : (m + 1) * n]

    def started(k, n):
        def done(b):
            for m in range(b * BR // n, (b + 1) * BR // n):
                start(k, m)

        return done

    fwd_one(xs, os, lses, cs, started(1, ns))
    fwd_one(xl, ol, lsel, cl, started(0, nl))
    w = ol.shape[1]
    for m in range(4):

        @pl.when(group.me != m)
        def _():
            for k in range(2):
                copy(k, m).wait_send()
                arrived(k, m).wait_recv()

    for m in range(4):
        att[:, m * w : (m + 1) * w] = land[m]


def bwd_x(core, xl, xs, go, ol, os, lsel, lses, cl, cs, dl, ds, acc, kt, out, gl, gs, ssem, rsem):
    group = Group(core)
    nl, ns = xl.shape[0] // 4, xs.shape[0] // 4
    w = ol.shape[1]
    for m in range(4):
        out[m] = go[:, m * w : (m + 1) * w]
    group.greet((1, 2, 3))

    def part(k):
        return ((gl, nl, 0), (gs, ns, nl))[k]

    def copy(k, m):
        dst, n, at = part(k)
        return send(
            out.at[m, pl.ds(at, n)],
            dst.at[pl.ds(pl.multiple_of(group.me * n, 16), n)],
            ssem.at[k, m],
            rsem.at[k, group.me],
            group.member(m),
        )

    def arrived(k, m):
        dst, n, at = part(k)
        return send(
            out.at[m, pl.ds(at, n)], dst.at[pl.ds(m * n, n)], ssem.at[k, m], rsem.at[k, m], group.member(m)
        )

    for k in (1, 0):
        for m in range(4):
            dst, n, at = part(k)

            @pl.when(group.me != m)
            def _():
                copy(k, m).start()

            @pl.when(group.me == m)
            def _():
                dst[m * n : (m + 1) * n] = out[m, at : at + n]

    for k in (1, 0):
        for m in range(4):

            @pl.when(group.me != m)
            def _():
                arrived(k, m).wait_recv()

        if k:
            bwd_one(xs, gs, os, lses, cs, ds, acc, kt)
        else:
            bwd_one(xl, gl, ol, lsel, cl, dl, acc, kt)
    for m in range(4):

        @pl.when(group.me != m)
        def _():
            for k in range(2):
                copy(k, m).wait_send()


def norm_rows(v):
    mean = jnp.mean(v, axis=-1, keepdims=True)
    cen = v - mean
    inv = lax.rsqrt(jnp.mean(cen * cen, axis=-1, keepdims=True) + 1e-05)
    return cen * inv, inv


def project_x(core, resid, gain, shift, w, bias, nl_ref, ns_ref, pl_ref, ps_ref, ssem, rsem):
    group = Group(core)
    nl, ns = nl_ref.shape[0] // 4, ns_ref.shape[0] // 4
    half = nl // 2
    parts = ((ns_ref, ps_ref, ns, 0, ns, nl), (nl_ref, pl_ref, nl, 0, half, 0), (nl_ref, pl_ref, nl, half, half, half))

    def rows(k, m):
        ref, _, n, at, size, _ = parts[k]
        return ref.at[pl.ds(pl.multiple_of(m * n + at, 16), size)]

    def copy(k, j, m, delta):
        return send(rows(k, m), rows(k, m), ssem.at[k, j], rsem.at[k, j], group.peer(delta))

    def compute(k, m):
        ref, out, n, at, size, _ = parts[k]
        here = pl.ds(pl.multiple_of(m * n + at, 16), size)
        out[here] = (mm(ref[here], w[...]) + bias[...]).astype(jnp.bfloat16)

    me = group.me
    for k in range(3):
        ref, _, n, at, size, src = parts[k]
        hat, _ = norm_rows(resid[src : src + size])
        ref[pl.ds(pl.multiple_of(me * n + at, 16), size)] = (hat * gain[...] + shift[...]).astype(
            jnp.bfloat16
        )
        if k == 0:
            group.greet((1, 2))
        copy(k, 0, me, 1).start()
        copy(k, 1, me, 2).start()
    for k in range(3):
        compute(k, me)
    for k in range(3):
        copy(k, 1, me ^ 2, 2).wait_recv()
        compute(k, me ^ 2)
    for k in range(3):
        copy(k, 0, me ^ 1, 1).wait_recv()
        copy(k, 2, me ^ 1, 2).start()
        compute(k, me ^ 1)
    for k in range(3):
        copy(k, 2, me ^ 3, 2).wait_recv()
        compute(k, me ^ 3)
    for k in range(3):
        copy(k, 0, me, 1).wait_send()
        copy(k, 1, me, 2).wait_send()
        copy(k, 2, me ^ 1, 2).wait_send()


def collect_x(core, dl, ds, w, resid, gain, gmid, g_ref, sums, mine, out, got, ssem, rsem):
    group = Group(core)
    nl, ns = dl.shape[0] // 4, ds.shape[0] // 4
    me = group.me

    def partial(m):
        a = mm(dl[pl.ds(pl.multiple_of(m * nl, 16), nl)], w[...], NT)
        b = mm(ds[pl.ds(pl.multiple_of(m * ns, 16), ns)], w[...], NT)
        return jnp.concatenate([a, b], axis=0)

    def copy(k, delta):
        return send(out.at[k], got.at[k], ssem.at[k], rsem.at[k], group.peer(delta))

    out[0] = partial(me ^ 3).astype(jnp.bfloat16)
    group.greet((1, 2))
    copy(0, 2).start()
    mine[...] = partial(me ^ 1)
    copy(0, 2).wait_recv()
    out[1] = (mine[...] + got[0].astype(jnp.float32)).astype(jnp.bfloat16)
    copy(1, 1).start()
    out[2] = partial(me ^ 2).astype(jnp.bfloat16)
    copy(2, 2).start()
    mine[...] = partial(me)
    hat, inv = norm_rows(resid[...])
    copy(2, 2).wait_recv()
    copy(1, 1).wait_recv()
    grad = mine[...] + got[2].astype(jnp.float32) + got[1].astype(jnp.float32)
    gh = grad * gain[...]
    a = jnp.mean(gh, axis=-1, keepdims=True)
    b = jnp.mean(gh * hat, axis=-1, keepdims=True)
    g_ref[...] = gmid[...] + inv * (gh - a - hat * b)
    sums[0:1] = jnp.sum(grad * hat, axis=0, keepdims=True)
    sums[1:2] = jnp.sum(grad, axis=0, keepdims=True)
    copy(0, 2).wait_send()
    copy(1, 1).wait_send()
    copy(2, 2).wait_send()


def shape(dims, dtype):
    return jax.ShapeDtypeStruct(tuple(dims), dtype)


def remote(kernel, core, outs, scratch, ident, name, args, flops=10**9):
    return pl.pallas_call(
        functools.partial(kernel, core),
        out_shape=tuple(outs),
        in_specs=[VMEM] * len(args),
        out_specs=(VMEM,) * len(outs),
        scratch_shapes=scratch,
        compiler_params=pltpu.CompilerParams(
            vmem_limit_bytes=LIMIT, collective_id=ident, has_side_effects=True
        ),
        cost_estimate=pl.CostEstimate(flops=flops, bytes_accessed=10**7, transcendentals=10**6),
        name=name,
    )(*args)


DMA = pltpu.SemaphoreType.DMA


def attend_fwd_x(core, xl, xs):
    w = (xl.shape[1] - 2 * HD) // 3
    rows = (xl.shape[0] + xs.shape[0]) // 4
    outs = [shape((rows, 4 * w), jnp.bfloat16)]
    outs += [shape((x.shape[0], w), jnp.bfloat16) for x in (xl, xs)]
    outs += [shape((8, x.shape[0]), jnp.float32) for x in (xl, xs)] * 2
    scratch = [pltpu.VMEM((4, rows, w), jnp.bfloat16), DMA((2, 4)), DMA((2, 4))]
    return remote(fwd_x, core, outs, scratch, 1, "attend_fwd_x", (xl, xs), 10**10)


def attend_bwd_x(core, xl, xs, go, ol, os, lsel, lses, cl, cs):
    w = ol.shape[1]
    nh = w // HD
    size = xl.shape[0]
    outs = [shape(x.shape, jnp.bfloat16) for x in (xl, xs)]
    scratch = [
        pltpu.VMEM((2 * nh + 1, size, HD), jnp.float32),
        pltpu.VMEM((nh + 1, HD, size), jnp.bfloat16),
        pltpu.VMEM((4, go.shape[0], w), jnp.bfloat16),
        pltpu.VMEM(ol.shape, jnp.bfloat16),
        pltpu.VMEM(os.shape, jnp.bfloat16),
        DMA((2, 4)),
        DMA((2, 4)),
    ]
    args = (xl, xs, go, ol, os, lsel, lses, cl, cs)
    return remote(bwd_x, core, outs, scratch, 2, "attend_bwd_x", args, 2 * 10**10)


def project(core, resid, gain, shift, w, bias, nl, ns):
    d, n = w.shape
    outs = [shape((4 * nl, d), jnp.bfloat16), shape((4 * ns, d), jnp.bfloat16)]
    outs += [shape((4 * nl, n), jnp.bfloat16), shape((4 * ns, n), jnp.bfloat16)]
    args = (resid, gain[None], shift[None], w, bias[None])
    return remote(project_x, core, outs, [DMA((3, 3)), DMA((3, 3))], 3, "project_x", args)


def collect(core, dl, ds, w, resid, gain, gmid):
    outs = [shape(resid.shape, jnp.float32), shape((8, w.shape[0]), jnp.float32)]
    scratch = [
        pltpu.VMEM(resid.shape, jnp.float32),
        pltpu.VMEM((3,) + resid.shape, jnp.bfloat16),
        pltpu.VMEM((3,) + resid.shape, jnp.bfloat16),
        DMA((3,)),
        DMA((3,)),
    ]
    return remote(collect_x, core, outs, scratch, 4, "collect_x", (dl, ds, w, resid, gain[None], gmid))


def total_x(axes, v, out, land, ssem, rsem):
    barrier = pltpu.get_barrier_semaphore()
    peers = [{ax: 1 - lax.axis_index(ax)} for ax in axes]
    for peer in peers:
        pl.semaphore_signal(barrier, inc=1, device_id=peer, device_id_type=pl.DeviceIdType.MESH)
    pl.semaphore_wait(barrier, len(peers))
    land[0] = v[...]
    n = len(axes)
    for i, peer in enumerate(peers):
        copy = send(land.at[i], land.at[n + 1 + i], ssem.at[i], rsem.at[i], peer)
        copy.start()
        copy.wait()
        land[i + 1] = land[i] + land[n + 1 + i]
    out[...] = land[n]


def total(axes, v):
    n = len(axes)
    scratch = [pltpu.VMEM((2 * n + 1,) + v.shape, jnp.float32), DMA((n,)), DMA((n,))]
    return remote(total_x, axes, [shape(v.shape, jnp.float32)], scratch, 5, "total_x", (v,))[0]


EPS = 1e-05
F32 = jnp.float32
BF = jnp.bfloat16


def swap(v, *axes):
    count = 2 ** len(axes)
    return lax.ppermute(
        v, axes if len(axes) > 1 else axes[0], [(i, count - 1 - i) for i in range(count)]
    )


def ordered(own, other, index, axis):
    return jnp.where(
        index == 0,
        jnp.concatenate([own, other], axis=axis),
        jnp.concatenate([other, own], axis=axis),
    )


def pick(v, index, axis):
    return lax.dynamic_index_in_dim(v, index, axis, keepdims=False)


def normalize(v, gain, shift):
    mean = jnp.mean(v, axis=-1, keepdims=True)
    cen = v - mean
    var = jnp.mean(cen * cen, axis=-1, keepdims=True)
    inv = lax.rsqrt(var + EPS)
    hat = cen * inv
    return hat * gain + shift, hat, inv


def normalize_back(grad, hat, inv, gain):
    gh = grad * gain
    a = jnp.mean(gh, axis=-1, keepdims=True)
    b = jnp.mean(gh * hat, axis=-1, keepdims=True)
    return inv * (gh - a - hat * b), jnp.sum(grad * hat, axis=0), jnp.sum(grad, axis=0)


def gelu_both(u):
    k = 0.7978845608028654
    inner = k * (u + 0.044715 * u * u * u)
    t = jnp.tanh(inner)
    act = 0.5 * u * (1.0 + t)
    slope = 0.5 * (1.0 + t) + 0.5 * u * (1.0 - t * t) * k * (1.0 + 3 * 0.044715 * u * u)
    return act, slope


def dot(a, b, ca=1, cb=0):
    return lax.dot_general(a, b, (((ca,), (cb,)), ((), ())), preferred_element_type=F32)


class Plan:
    def __init__(self, dims, dp, mp):
        self.dims, self.dp, self.mp = dims, dp, mp
        self.core = dims[-1]
        self.plane = dims[:-1]
        self.c = lax.axis_index(self.core)
        self.zh = lax.axis_index("zh")
        self.zl = lax.axis_index("zl")
        self.z = lax.axis_index(("zh", "zl"))
        self.d = lax.axis_index(dims)

    def relabel(self, v):
        got = lax.ppermute(v, (self.core, "zh"), [(1, 2), (2, 1)])
        return jnp.where(self.c == self.zh, v, got)

    def ring(self, v, step):
        n = self.mp
        return lax.ppermute(v, ("zh", "zl"), [(i, (i + step) % n) for i in range(n)])

    def gather(self, v):
        v = ordered(v, swap(v, "zl"), self.zl, 0)
        return ordered(v, swap(v, self.core), self.c, 0)

    def scatter(self, v):
        rows = v.shape[0] // 4
        v = v.reshape(2, 2, rows, v.shape[1])
        got = swap(pick(v, 1 - self.c, 0), self.core)
        mine = pick(v, self.c, 0).astype(F32) + got.astype(F32)
        got = swap(pick(mine, 1 - self.zl, 0).astype(BF), "zl")
        return pick(mine, self.zl, 0) + got.astype(F32)

    def to_rows(self, o):
        rows = o.shape[0] // 4
        o = o.reshape(2, 2, rows, o.shape[1])
        got = []
        for dc in range(2):
            line = []
            for dz in range(2):
                part = pick(pick(o, self.c ^ dc, 0), self.zl ^ dz, 0)
                axes = ((self.core,) if dc else ()) + (("zl",) if dz else ())
                line.append(swap(part, *axes) if axes else part)
            got.append(ordered(line[0], line[1], self.zl, 1))
        return ordered(got[0], got[1], self.c, 1)

    def to_heads(self, g):
        rows, w = g.shape[0], g.shape[1] // 4
        g = g.reshape(rows, 2, 2, w)
        got = []
        for dc in range(2):
            line = []
            for dz in range(2):
                part = pick(pick(g, self.c ^ dc, 1), self.zl ^ dz, 1)
                axes = ((self.core,) if dc else ()) + (("zl",) if dz else ())
                line.append(swap(part, *axes) if axes else part)
            got.append(ordered(line[0], line[1], self.zl, 0))
        return ordered(got[0], got[1], self.c, 0)

    def piece(self, w):
        rows = w.shape[0] // self.dp
        return lax.dynamic_slice_in_dim(w, self.d * rows, rows, 0)

    def ring_gather(self, v):
        parts = []
        for _ in range(self.mp - 1):
            v = self.ring(v, 1)
            parts.append(v)
        return parts

    def plane_gather(self, v, axes):
        k, rows, n = v.shape
        have = []
        shape = [k]
        for ax in axes:
            pos = sum(self.dims.index(h) < self.dims.index(ax) for h in have)
            got = swap(v, ax)
            cur = v.reshape(k, *([2] * len(have)), rows, n)
            oth = got.reshape(cur.shape)
            a = jnp.stack([cur, oth], axis=1 + pos)
            b = jnp.stack([oth, cur], axis=1 + pos)
            v = jnp.where(lax.axis_index(ax) == 0, a, b)
            have.append(ax)
            v = v.reshape(k, -1, rows, n).reshape(k, -1, n)
            rows_all = v.shape[1]
            v = v.reshape(k, rows_all, n)
        return v.reshape(k, self.dp, rows, n)

    def plane_scatter(self, g, axes):
        n = g.shape[1]
        left = [ax for ax in self.dims]
        rows = g.shape[0] // self.dp
        v = g.reshape(*([2] * len(left)), rows, n)
        for ax in axes:
            pos = left.index(ax)
            i = lax.axis_index(ax)
            got = swap(pick(v, 1 - i, pos), ax)
            v = (pick(v, i, pos).astype(F32) + got.astype(F32)).astype(BF)
            left.remove(ax)
        return v.reshape(-1, n)

    def ring_scatter(self, chunks):
        t = chunks[-1]
        for r in range(self.mp - 2, -1, -1):
            got = self.ring(t, -1)
            t = chunks[r].astype(F32) + got.astype(F32)
            if r:
                t = t.astype(BF)
        return t


def body(
    dims, dp, mp,
    x_long, x_short, dy_long, dy_short, ln_gain, ln_bias, w_qkv, b_qv, w_out, b_out, w_up, b_up, w_down, b_down, threshold,
):
    plan = Plan(dims, dp, mp)
    layers = w_qkv.shape[0]
    d_model = x_long.shape[-1]
    heads_w = w_qkv.shape[-1]
    ffq = w_up.shape[-1]
    rl, rs = x_long.shape[1], x_short.shape[1]
    rows = rl + rs
    core_rest = tuple(plan.plane)
    fwd_axes = core_rest + (plan.core,)
    alt_axes = core_rest[::-1] + (plan.core,)
    gain = ln_gain.astype(F32)
    shift = ln_bias.astype(F32)

    x = jnp.concatenate([x_long[0], x_short[0]], axis=0)
    x = plan.relabel(x)

    small = jnp.concatenate([b_up.reshape(-1), b_qv.reshape(-1)])
    rel_small = jnp.stack([small] + plan.ring_gather(small))
    n_up = layers * ffq
    rel_bup = rel_small[:, :n_up].reshape(mp, layers, ffq).astype(F32)
    rel_bqv = rel_small[:, n_up:].reshape(mp, layers, 2, heads_w).astype(F32)
    mine = 2 * plan.c + plan.zl
    my_bqv = pick(rel_bqv, (plan.z - mine) % mp, 0)
    zero_bq = pick(rel_bqv, plan.z % mp, 0)[:, 0, :HD]

    exts = []
    for l in range(layers):
        quarter = plan.relabel(w_qkv[l].reshape(d_model, 3 * heads_w))
        head0 = w_qkv[l][:, :2, :HD].reshape(d_model, 2 * HD)
        got = lax.ppermute(head0, "zl", [(0, 1)])
        head0 = jnp.where(plan.zl == 0, head0, got)
        got = lax.ppermute(head0, "zh", [(0, 1)])
        head0 = jnp.where(plan.zh == 0, head0, got)
        exts.append(jnp.concatenate([quarter, head0], axis=1))

    ups, downs, outs = [], [], []
    for l in range(layers):
        po = plan.piece(w_out[l])
        pu = jnp.concatenate([plan.piece(w_up[l]), po], axis=0)
        pd = plan.piece(w_down[l])
        n_out, n_d = po.shape[0], pd.shape[0]
        both = plan.ring_gather(jnp.concatenate([pu, pd], axis=0))
        stacked = jnp.stack(both)
        n_u = pu.shape[0]
        gu = plan.plane_gather(stacked[:, :n_u], fwd_axes)
        gd = plan.plane_gather(stacked[:, n_u:], alt_axes)
        up = gu[:, :, : n_u - n_out].reshape(mp - 1, d_model, ffq)
        ups.append(jnp.concatenate([w_up[l]] + [up[r] for r in range(mp - 1)], axis=1))
        out = gu[:, :, n_u - n_out :].reshape(mp - 1, heads_w, d_model)
        out = jnp.concatenate([w_out[l][None], out], axis=0)
        outs.append(
            jnp.concatenate([pick(out, (plan.z - q) % mp, 0) for q in range(mp)], axis=0)
        )
        downs.append(
            jnp.concatenate([w_down[l], gd.reshape((mp - 1) * ffq, d_model)], axis=0)
        )

    dy = plan.relabel(jnp.concatenate([dy_long[0], dy_short[0]], axis=0))

    limits = threshold.astype(F32) / 64.0
    resid = x.astype(F32)
    saved = []
    shares = []
    for l in range(layers):
        normed, hat1, inv1 = normalize(resid, gain[l, 0], shift[l, 0])
        normed = normed.astype(BF)
        full = [plan.gather(normed[:rl]), plan.gather(normed[rl:])]
        bias = jnp.concatenate(
            [
                my_bqv[l, 0],
                jnp.zeros((heads_w,), F32),
                my_bqv[l, 1],
                zero_bq[l],
                jnp.zeros((HD,), F32),
            ]
        )
        proj = [(dot(n, exts[l]) + bias).astype(BF) for n in full]
        att = [attend_fwd(p) for p in proj]
        share = jnp.zeros((), F32)
        for p, a in zip(proj, att):
            size = p.shape[0]
            sel = a[2][size // BR]
            left = (size - 1 - lax.broadcasted_iota(jnp.int32, (size,), 0)).astype(F32)
            share = share + jnp.sum(
                jax.nn.sigmoid(4.0 * (sel / jnp.maximum(left, 1.0) - limits[l]))
            )
        shares.append(share)
        attended = jnp.concatenate([plan.to_rows(a[0]) for a in att], axis=0)
        middle = resid + dot(attended, outs[l]) + b_out[l].astype(F32)
        normed2, hat2, inv2 = normalize(middle, gain[l, 1], shift[l, 1])
        normed2 = normed2.astype(BF)
        upper = dot(normed2, ups[l]) + rel_bup[:, l].reshape(-1)
        active = gelu_both(upper)[0].astype(BF)
        saved.append((resid, middle, full, proj, att, attended, normed2, upper, active))
        resid = middle + dot(active, downs[l]) + b_down[l].astype(F32)

    y = plan.relabel(resid.astype(BF))

    g = dy.astype(F32)
    vec = {}
    weight_grads = [None] * layers
    for l in reversed(range(layers)):
        resid, middle, full, proj, att, attended, normed2, upper, active = saved[l]
        g_bdown = jnp.sum(g, axis=0)
        gm = g.astype(BF)
        gact = dot(gm, downs[l], 1, 1)
        slope = gelu_both(upper)[1]
        gu = (slope * gact).astype(BF)
        w_down_t = dot(gm, active, 0, 0).astype(BF)
        w_up_g = dot(normed2, gu, 0, 0).astype(BF)
        g_bup = jnp.sum(gu.astype(F32), axis=0)
        gn2 = dot(gu, ups[l], 1, 1)
        _, hat2, inv2 = normalize(middle, gain[l, 1], shift[l, 1])
        back, g_gain2, g_shift2 = normalize_back(gn2, hat2, inv2, gain[l, 1])
        gmid = g + back
        g_bout = jnp.sum(gmid, axis=0)
        ga = gmid.astype(BF)
        go = dot(ga, outs[l], 1, 1).astype(BF)
        w_out_t = dot(ga, attended, 0, 0).astype(BF)
        gh = [plan.to_heads(go[:rl]), plan.to_heads(go[rl:])]
        dext = [attend_bwd(p, h, a[0], a[1], a[2]) for p, h, a in zip(proj, gh, att)]
        gn1 = jnp.concatenate(
            [plan.scatter(dot(e, exts[l], 1, 1).astype(BF)) for e in dext], axis=0
        )
        w_ext_g = sum(dot(n, e, 0, 0) for n, e in zip(full, dext)).astype(BF)
        g_bext = sum(jnp.sum(e.astype(F32), axis=0) for e in dext)
        _, hat1, inv1 = normalize(resid, gain[l, 0], shift[l, 0])
        back, g_gain1, g_shift1 = normalize_back(gn1, hat1, inv1, gain[l, 0])
        g = gmid + back

        w_up_g = plan.plane_scatter(w_up_g, (plan.core,) + core_rest)
        w_up_g = plan.ring_scatter([w_up_g[:, r * ffq : (r + 1) * ffq] for r in range(mp)])
        w_down_t = plan.plane_scatter(w_down_t, (plan.core,) + core_rest[::-1])
        w_down_t = plan.ring_scatter([w_down_t[:, r * ffq : (r + 1) * ffq] for r in range(mp)])
        w_out_t = plan.plane_scatter(w_out_t, (plan.core,) + core_rest)
        w_out_t = w_out_t.reshape(-1, mp, heads_w)
        w_out_t = plan.ring_scatter([pick(w_out_t, (plan.z - r) % mp, 1) for r in range(mp)])
        w_ext_g = plan.plane_scatter(w_ext_g, core_rest[::-1])
        w_ext_g = w_ext_g.reshape(2, -1, w_ext_g.shape[1])
        part, zero = w_ext_g[..., : 3 * heads_w], w_ext_g[..., 3 * heads_w :]
        got = lax.ppermute(part, (plan.core, "zh"), [(1, 0), (2, 3)])
        part = part.astype(F32) + got.astype(F32)
        got = lax.ppermute(
            pick(part, 1 - plan.c, 0).astype(BF), (plan.core, "zh"), [(0, 2), (3, 1)]
        )
        w_qkv_g = jnp.where(plan.c == plan.zh, pick(part, plan.c, 0), got.astype(F32))
        got = swap(pick(zero, 1 - plan.c, 0), plan.core)
        zero = (pick(zero, plan.c, 0).astype(F32) + got.astype(F32)).astype(BF)
        zero = zero.astype(F32) + swap(zero, "zl").astype(F32)
        zero = zero + swap(zero.astype(BF), "zh").astype(F32)
        zero = jnp.where(plan.z == 0, zero, 0.0)
        w_qkv_g = w_qkv_g.reshape(-1, 3, heads_w)
        zero = zero.reshape(-1, 2, HD)
        w_qkv_g = w_qkv_g + jnp.pad(zero, ((0, 0), (0, 1), (0, heads_w - HD)))
        weight_grads[l] = (w_qkv_g, jnp.transpose(w_out_t), w_up_g, jnp.transpose(w_down_t))

        hot = (lax.broadcasted_iota(jnp.int32, (mp, 1), 0) == mine).astype(F32)
        gq = hot * g_bext[None, :heads_w]
        gv = hot * g_bext[None, 2 * heads_w : 3 * heads_w]
        gq = gq.reshape(-1).at[:HD].add(g_bext[3 * heads_w : 3 * heads_w + HD])
        g_bup = g_bup.reshape(mp, ffq)
        g_bup = jnp.stack([pick(g_bup, (plan.z - q) % mp, 0) for q in range(mp)])
        vec[l] = jnp.concatenate(
            [
                g_gain1, g_gain2, g_shift1, g_shift2, g_bout, g_bdown,
                gq, gv.reshape(-1), g_bup.reshape(-1), jnp.full((128,), shares[l] / mp),
            ]
        )

    dx = plan.relabel(g.astype(BF)).astype(F32)
    total = lax.psum(jnp.stack([vec[l] for l in range(layers)]), dims + ("zh", "zl"))
    n = d_model
    g_gain = total[:, : 2 * n].reshape(layers, 2, n)
    g_bias = total[:, 2 * n : 4 * n].reshape(layers, 2, n)
    g_bout = total[:, 4 * n : 5 * n]
    g_bdown = total[:, 5 * n : 6 * n]
    at = 6 * n
    g_bqv = total[:, at : at + 2 * mp * heads_w].reshape(layers, 2, mp, heads_w)
    at += 2 * mp * heads_w
    g_bup = total[:, at : at + mp * ffq].reshape(layers, mp, ffq)
    at += mp * ffq
    key_share = total[:, at] / (dp * (rows * mp))
    return (
        y[None, :rl],
        y[None, rl:],
        dx[None, :rl],
        dx[None, rl:],
        g_gain,
        g_bias,
        jnp.stack([weight_grads[l][0] for l in range(layers)]),
        pick(g_bqv, plan.z, 2),
        jnp.stack([weight_grads[l][1] for l in range(layers)]),
        g_bout,
        jnp.stack([weight_grads[l][2] for l in range(layers)]),
        pick(g_bup, plan.z, 1),
        jnp.stack([weight_grads[l][3] for l in range(layers)]),
        g_bdown,
        key_share,
    )


MESH = pl.DeviceIdType.MESH
ANY = pl.BlockSpec(memory_space=pl.ANY)


class Net:
    def __init__(self, dims):
        self.dims = dims
        self.y, self.x, self.c = (lax.axis_index(ax) for ax in dims)
        self.zh, self.zl = lax.axis_index("zh"), lax.axis_index("zl")
        self.z = 2 * self.zh + self.zl
        self.yx = 2 * self.y + self.x
        self.me = 2 * self.c + self.zl
        self.moves = self.c != self.zh

    def group(self, delta):
        return {self.dims[2]: self.c ^ (delta >> 1), "zl": self.zl ^ (delta & 1)}

    def member(self, m):
        return {self.dims[2]: m >> 1, "zl": m & 1}

    def plane(self, e):
        return {self.dims[0]: self.y ^ (e >> 1), self.dims[1]: self.x ^ (e & 1)}

    def line(self, r):
        to = (self.z + r) % 4
        return {"zh": to // 2, "zl": to % 2}

    def partner(self):
        return {self.dims[2]: 1 - self.c, "zh": 1 - self.zh}

    def greet(self, peers):
        barrier = pltpu.get_barrier_semaphore()
        for peer in peers:
            pl.semaphore_signal(barrier, inc=1, device_id=peer, device_id_type=MESH)
        pl.semaphore_wait(barrier, len(peers))


class Sems:
    def __init__(self, ssem, rsem):
        self.ssem, self.rsem, self.used = ssem, rsem, 0

    def copy(self, src, dst, device):
        i = self.used
        self.used += 1
        assert i < self.ssem.shape[0]
        return send(src, dst, self.ssem.at[i], self.rsem.at[i], device)


class Batch:
    def __init__(self, copies, when=None):
        self.copies, self.when = copies, when

    def _do(self, f):
        if self.when is None:
            f()
        else:
            pl.when(self.when)(f)

    def start(self):
        self._do(lambda: [c.start() for c in self.copies] and None)

    def recv(self):
        self._do(lambda: [c.wait_recv() for c in self.copies] and None)

    def sent(self):
        self._do(lambda: [c.wait_send() for c in self.copies] and None)

    def end(self):
        self.recv()
        self.sent()


def aligned(v, n=16):
    return pl.multiple_of(v, n)


class Projections:
    def __init__(self, net, sems, wq, w0, qland, zland, ext):
        self.net, self.wq, self.w0, self.qland, self.zland, self.ext = net, wq, w0, qland, zland, ext
        rows = qland.shape[1]
        here = pl.ds(aligned(net.yx * rows), rows)
        at = net.yx
        self.q1 = Batch([sems.copy(wq.at[here], qland.at[at], net.partner())], net.moves)
        self.q2 = Batch([sems.copy(qland.at[at], qland.at[at], net.plane(e)) for e in (1, 2, 3)], net.moves)
        self.h1 = []
        for r in (1, 2, 3):
            copy = sems.copy(w0.at[here], zland.at[at], net.line(r))
            self.h1.append(copy)
        self.h2 = Batch([sems.copy(zland.at[at], zland.at[at], net.plane(e)) for e in (1, 2, 3)], net.z != 0)

    def start(self):
        self.q1.start()

        @pl.when(self.net.z == 0)
        def _():
            for copy in self.h1:
                copy.start()

    def forward(self):
        self.q1.recv()
        self.q2.start()
        for r in (1, 2, 3):
            pl.when(self.net.z == r)(lambda: self.h1[r - 1].wait_recv())
        self.h2.start()

    def finish(self):
        rows, n = self.qland.shape[1:]
        self.q2.recv()
        self.h2.recv()

        @pl.when(self.net.moves)
        def _():
            for k in range(4):
                self.ext[k * rows : (k + 1) * rows, :n] = self.qland[k]

        @pl.when(jnp.logical_not(self.net.moves))
        def _():
            self.ext[:, :n] = self.wq[...]

        @pl.when(self.net.z != 0)
        def _():
            for k in range(4):
                self.ext[k * rows : (k + 1) * rows, n:] = self.zland[k]

        @pl.when(self.net.z == 0)
        def _():
            self.ext[:, n:] = self.w0[...]

        self.q1.sent()
        self.q2.sent()
        self.h2.sent()

        @pl.when(self.net.z == 0)
        def _():
            for copy in self.h1:
                copy.wait_send()


def project_part(net, sems, resid, gain, shift, w, bias, fl, fs, pj_l, pj_s, after_chip):
    nl, ns = fl.shape[0] // 4, fs.shape[0] // 4
    half = nl // 2
    parts = ((fs, pj_s, ns, 0, ns, nl), (fl, pj_l, nl, 0, half, 0), (fl, pj_l, nl, half, half, half))
    me = net.me

    def rows(k, m):
        ref, _, n, at, size, _ = parts[k]
        return ref.at[pl.ds(aligned(m * n + at), size)]

    def compute(k, m):
        ref, out, n, at, size, _ = parts[k]
        here = pl.ds(aligned(m * n + at), size)
        out[here] = (mm(ref[here], w[...]) + bias[...]).astype(jnp.bfloat16)

    chip = [sems.copy(rows(k, me), rows(k, me), net.group(1)) for k in range(3)]
    core = [sems.copy(rows(k, me), rows(k, me), net.group(2)) for k in range(3)]
    over = [sems.copy(rows(k, me ^ 1), rows(k, me ^ 1), net.group(2)) for k in range(3)]
    for k in range(3):
        ref, _, n, at, size, src = parts[k]
        hat, _ = norm_rows(resid[src : src + size].astype(jnp.float32))
        ref[pl.ds(aligned(me * n + at), size)] = (hat * gain[...] + shift[...]).astype(jnp.bfloat16)
        chip[k].start()
        core[k].start()
    for k in range(3):
        compute(k, me)
    for k in range(3):
        core[k].wait_recv()
        compute(k, me ^ 2)
    for k in range(3):
        chip[k].wait_recv()
        over[k].start()
        if k == 2:
            after_chip()
        compute(k, me ^ 1)
    for k in range(3):
        over[k].wait_recv()
        compute(k, me ^ 3)
    return chip + core + over


def attend_part(net, sems, xl, xs, att, ol, os, lsel, lses, cl, cs, land, hooks):
    nl, ns = xl.shape[0] // 4, xs.shape[0] // 4
    w = ol.shape[1]
    base = sems.used
    sems.used += 8

    def part(k):
        return ((ol, nl, 0), (os, ns, nl))[k]

    def copy(k, m):
        src, n, at = part(k)
        return send(
            src.at[pl.ds(m * n, n)],
            land.at[net.me, pl.ds(at, n)],
            sems.ssem.at[base + 4 * k + m],
            sems.rsem.at[base + 4 * k + net.me],
            net.member(m),
        )

    def arrived(k, m):
        src, n, at = part(k)
        i = base + 4 * k + m
        return send(src.at[pl.ds(0, n)], land.at[m, pl.ds(at, n)], sems.ssem.at[i], sems.rsem.at[i], net.member(m))

    def start(k, m):
        src, n, at = part(k)

        @pl.when(net.me != m)
        def _():
            copy(k, m).start()

        @pl.when(net.me == m)
        def _():
            land[m, at : at + n] = src[m * n : (m + 1) * n]

    def started(k, n):
        def done(b):
            for m in range(b * BR // n, (b + 1) * BR // n):
                start(k, m)
            if k == 0 and b in hooks:
                hooks[b]()

        return done

    fwd_one(xs, os, lses, cs, started(1, ns))
    fwd_one(xl, ol, lsel, cl, started(0, nl))
    for m in range(4):

        @pl.when(net.me != m)
        def _():
            for k in range(2):
                copy(k, m).wait_send()
                arrived(k, m).wait_recv()

    for m in range(4):
        att[:, m * w : (m + 1) * w] = land[m]


def gelu_pair(u):
    k = 0.7978845608028654
    sq = u * u
    t = jnp.tanh(u * (k + k * 0.044715 * sq))
    h = 0.5 * (1.0 + t)
    act = u * h
    slope = h + act * (1.0 - t) * (k + 3 * k * 0.044715 * sq)
    return act, slope


TN = (((0,), (0,)), ((), ()))


def ext_scatter(net, sems, dw, land):
    return [sems.copy(dw.at[net.yx ^ e], land.at[e - 1], net.plane(e)) for e in (1, 2, 3)]


class FinishLine:
    def __init__(self, net, sems, s, so, land, oland, own=None):
        self.own = s.at[0] if own is None else own
        self.net, self.s, self.so, self.land, self.oland = net, s, so, land, oland
        self.main = [
            Batch([sems.copy(s.at[r, i], land.at[3 - r, i], net.line(r)) for r in (1, 2, 3)])
            for i in range(land.shape[1])
        ]
        self.out = []
        for r in (1, 2, 3):
            to = (net.z + r) % 4
            copy = sems.copy(so.at[to % 2], oland.at[3 - r], net.line(r))
            self.out.append((copy, to // 2 == net.c))
        self.owner = net.zh == net.c

    def start(self):
        for part in self.main:
            part.start()
        self.start_rest()

    def start_rest(self):
        for copy, use in self.out:
            pl.when(use)(copy.start)

    def finish(self, f_out, fo_out):
        for part in self.main:
            part.recv()
        f_out[...] = (
            self.own[...].astype(jnp.float32)
            + self.land[0].astype(jnp.float32)
            + self.land[1].astype(jnp.float32)
            + self.land[2].astype(jnp.float32)
        ).astype(f_out.dtype)

        @pl.when(self.owner)
        def _():
            for copy, _ in self.out:
                copy.wait_recv()
            fo_out[...] = (
                self.so[self.net.zl].astype(jnp.float32)
                + self.oland[0].astype(jnp.float32)
                + self.oland[1].astype(jnp.float32)
                + self.oland[2].astype(jnp.float32)
            ).astype(fo_out.dtype)

        @pl.when(jnp.logical_not(self.owner))
        def _():
            fo_out[...] = jnp.zeros_like(fo_out)

        for part in self.main:
            part.sent()
        for copy, use in self.out:
            pl.when(use)(copy.wait_send)


class Local:
    def __init__(self, sem):
        self.sem, self.copies = sem, []

    def start(self, src, dst):
        assert len(self.copies) < self.sem.shape[0]
        copy = pltpu.make_async_copy(src, dst, self.sem.at[len(self.copies)])
        self.copies.append(copy)
        copy.start()
        return copy


class LineWeights:
    def __init__(self, net, sems, layer, w_up, w_down, zup, zdn):
        rows, n = zup.shape[0], zup.shape[1] // 3
        part = zdn.shape[1]
        own = (
            w_up.at[layer, pl.ds(aligned(net.yx * rows), rows), pl.ds(aligned(net.c * n, 128), n)],
            w_down.at[layer, pl.ds(aligned(net.c * n + net.yx * part), part)],
        )

        def slot(k):
            return (zup.at[:, pl.ds(k * n, n)], zdn.at[k])

        self.steps = []
        for s in (1, 2, 3):
            up_src = own if s == 1 else slot(4 - s)
            dn_src = own if s == 1 else slot(s - 2)
            up = [sems.copy(up_src[i], slot(3 - s)[i], net.line(1)) for i in range(2)]
            dn = [sems.copy(dn_src[i], slot(s - 1)[i], net.line(3)) for i in range(2)]
            sends_up = jnp.logical_and(net.z >= s - 1, net.z <= 2)
            sends_dn = jnp.logical_and(net.z <= 4 - s, net.z >= 1)
            self.steps.append(((up, sends_up, net.z >= s), (dn, sends_dn, net.z + s <= 3)))

    def start(self, s):
        for copies, sends, _ in self.steps[s]:
            Batch(copies, sends).start()

    def recv(self, s):
        for copies, _, gets in self.steps[s]:
            Batch(copies, gets).recv()

    def sent(self):
        for step in self.steps:
            for copies, sends, _ in step:
                Batch(copies, sends).sent()


def plane_weights(net, sems, zup, zdn, wup, wdn):
    rows, n = zup.shape[0], zup.shape[1] // 3
    part = zdn.shape[1]
    at_up = pl.ds(aligned(net.yx * rows), rows)
    at_dn = pl.ds(aligned(net.yx * part), part)
    out = []
    for e in (1, 2, 3):
        out.append(sems.copy(zup, wup.at[at_up, pl.ds(n, 3 * n)], net.plane(e)))
        out.append(sems.copy(zdn, wdn.at[pl.ds(1, 3), at_dn], net.plane(e)))
    return Batch(out)


def first_x(dims, R):
    net, sems = Net(dims), Sems(R.ssem, R.rsem)
    nl = R.xl.shape[0]
    moved = Batch(
        [
            sems.copy(R.xl, R.xr.at[pl.ds(0, nl)], net.partner()),
            sems.copy(R.xs, R.xr.at[pl.ds(nl, R.xs.shape[0])], net.partner()),
        ],
        net.moves,
    )
    proj = Projections(net, sems, R.wq, R.w0, R.qland, R.zland, R.ext)
    tiny = Batch([sems.copy(R.small, R.smalls.at[4 - r], net.line(r)) for r in (1, 2, 3)])
    weights = LineWeights(net, sems, 0, R.w_up, R.w_down, R.zup, R.zdn)
    net.greet([net.partner()] + [net.line(r) for r in (1, 2, 3)] + [net.plane(e) for e in (1, 2, 3)])
    proj.start()
    moved.start()
    tiny.start()
    weights.start(0)
    R.smalls[0] = R.small[...]

    @pl.when(jnp.logical_not(net.moves))
    def _():
        R.xr[:nl] = R.xl[...]
        R.xr[nl:] = R.xs[...]

    proj.forward()
    weights.recv(0)
    weights.start(1)
    proj.finish()
    weights.recv(1)
    weights.start(2)
    moved.end()
    tiny.end()
    weights.recv(2)
    weights.sent()


def forward_x(dims, first, last, R):
    net, sems, loc = Net(dims), Sems(R.ssem, R.rsem), Local(R.lsem)
    n, d = R.resid.shape
    f = R.wup.shape[1] // 4
    layer = 0 if first else 1
    weights = plane_weights(net, sems, R.zup, R.zdn, R.wup, R.wdn)
    peers = [net.group(2), net.group(3), net.partner()]
    peers += [net.plane(e) for e in (1, 2, 3)] + [net.line(r) for r in (1, 2, 3)]
    if first:
        proj = Projections(net, sems, R.wq, R.w0, R.qland, R.zland, R.ext_next)
        later = LineWeights(net, sems, 1, R.w_up, R.w_down, R.zup_next, R.zdn_next)
    else:
        nl = R.dl.shape[0]
        moved = Batch(
            [
                sems.copy(R.dl, R.dyr.at[pl.ds(0, nl)], net.partner()),
                sems.copy(R.ds, R.dyr.at[pl.ds(nl, R.ds.shape[0])], net.partner()),
            ],
            net.moves,
        )
    there = sems.copy(R.n2.at[pl.ds(0, n)], R.n2.at[pl.ds(n, n)], net.group(2))
    back = sems.copy(R.out, R.got, net.group(2))
    net.greet(peers)
    weights.start()
    own = [
        loc.start(R.w_up.at[layer, :, pl.ds(aligned(net.c * f, 128), f)], R.wup.at[:, pl.ds(0, f)]),
        loc.start(R.w_down.at[layer, pl.ds(aligned(net.c * f), f)], R.wdn.at[0]),
    ]
    hooks = {}
    if first:

        def after_chip():
            proj.start()
            later.start(0)

        def second():
            later.recv(0)
            later.start(1)

        hooks = {1: second}
    else:
        after_chip = moved.start
    pending = project_part(
        net, sems, R.resid, R.gain1, R.shift1, R.ext, R.bias, R.fl, R.fs, R.pj_l, R.pj_s, after_chip
    )
    if not first:

        @pl.when(jnp.logical_not(net.moves))
        def _():
            R.dyr[:nl] = R.dl[...]
            R.dyr[nl:] = R.ds[...]

    for src, dst in ((R.fl, R.fl_o), (R.fs, R.fs_o), (R.pj_l, R.pjl_o), (R.pj_s, R.pjs_o)):
        loc.start(src, dst)
    rows, part = R.zup.shape[0], R.zdn.shape[1]
    R.wup[pl.ds(aligned(net.yx * rows), rows), f:] = R.zup[...]
    for k in range(3):
        R.wdn[k + 1, pl.ds(aligned(net.yx * part), part)] = R.zdn[k]
    attend_part(
        net, sems, R.pj_l, R.pj_s, R.att, R.ol, R.os, R.lsel, R.lses, R.cl, R.cs, R.land, hooks
    )
    if first:
        later.recv(1)
        later.start(2)
        proj.forward()
    share = jnp.zeros((1, 1), jnp.float32)
    for carry in (R.cl, R.cs):
        size = carry.shape[1]
        left = (size - 1 - lax.broadcasted_iota(jnp.int32, (1, size), 1)).astype(jnp.float32)
        ratio = carry[size // BR : size // BR + 1] / jnp.maximum(left, 1.0)
        t = 4.0 * (ratio - R.limit[...])
        share = share + jnp.sum(1.0 / (1.0 + jnp.exp(-t)), axis=1, keepdims=True)
    R.share[...] = jnp.broadcast_to(share * 0.25, R.share.shape)
    half = n // 2
    for i in range(2):
        at = slice(i * half, (i + 1) * half)
        R.middle[at] = R.resid[at].astype(jnp.float32) + mm(R.att[at], R.wout[...]) + R.bout[...]
        hat, _ = norm_rows(R.middle[at])
        R.n2[at] = (hat * R.gain2[...] + R.shift2[...]).astype(jnp.bfloat16)
    there.start()
    weights.recv()
    for copy in own:
        copy.wait()
    for src, dst in ((R.wup, R.wup_o), (R.wdn, R.wdn_o)):
        loc.start(src, dst)

    def hidden(at):
        u = mm(R.n2[at], R.wup[...]) + R.bup[...]
        a, s = gelu_pair(u)
        low = a.astype(jnp.bfloat16)
        for i in range(2):
            R.act[i, at] = low[:, 2 * i * f : 2 * (i + 1) * f]
            loc.start(R.act.at[i, at], R.act_o.at[i, at])
        R.slope[at] = s.astype(jnp.bfloat16)
        loc.start(R.slope.at[at], R.slope_o.at[at])

    def down(at):
        return mm(R.act[0, at], R.wdn[0:2].reshape(2 * f, d)) + mm(
            R.act[1, at], R.wdn[2:4].reshape(2 * f, d)
        )

    quarter = n // 2
    for i in range(2):
        hidden(slice(i * quarter, (i + 1) * quarter))
    there.wait_recv()
    for i in range(2):
        hidden(slice(n + i * quarter, n + (i + 1) * quarter))
    for i in range(2):
        R.out[i * half : (i + 1) * half] = down(slice(n + i * half, n + (i + 1) * half)).astype(
            jnp.bfloat16
        )
    back.start()
    for i in range(2):
        at = slice(i * half, (i + 1) * half)
        R.new[at] = R.middle[at] + down(at) + R.bdown[...]
    back.wait_recv()
    R.new[...] += R.got[...].astype(jnp.float32)
    if last:
        R.y[...] = R.new[...].astype(jnp.bfloat16)
    there.wait_send()
    back.wait_send()
    for copy in pending:
        copy.wait_send()
    weights.sent()
    if first:
        proj.finish()
        later.recv(2)
        later.sent()
    else:
        moved.end()
    for copy in loc.copies[2:]:
        copy.wait()


def backward_x(dims, last, R):
    net, sems, loc = Net(dims), Sems(R.ssem, R.rsem), Local(R.lsem)
    f32, bf = jnp.float32, jnp.bfloat16
    n, d = R.g.shape
    f = R.wup.shape[1] // 4
    nl, ns = R.pj_l.shape[0] // 4, R.pj_s.shape[0] // 4
    wid = R.ol.shape[1]
    me, yx = net.me, net.yx
    chunk = d // 4
    there = sems.copy(R.gm.at[pl.ds(0, n)], R.gm.at[pl.ds(n, n)], net.group(2))
    back = sems.copy(R.out.at[0], R.got.at[0], net.group(2))
    cross = sems.copy(R.oself, R.olands, net.group(2))
    big_dn = Batch([sems.copy(R.ddn.at[yx ^ e], R.rdn.at[e - 1], net.plane(e)) for e in (1, 2, 3)])
    big_up = Batch([sems.copy(R.dup.at[yx ^ e], R.rup.at[e - 1], net.plane(e)) for e in (1, 2, 3)])
    big_out = Batch([sems.copy(R.dout.at[yx ^ e], R.rout.at[e - 1], net.plane(e)) for e in (1, 2, 3)])
    base = sems.used
    sems.used += 8
    peers = [net.group(d_) for d_ in (1, 2, 3)] + [net.plane(e) for e in (1, 2, 3)]
    if last:
        moved = Batch(
            [
                sems.copy(R.y.at[pl.ds(0, nl)], R.yr_l, net.partner()),
                sems.copy(R.y.at[pl.ds(nl, ns)], R.yr_s, net.partner()),
            ],
            net.moves,
        )
        peers += [net.partner()]
    else:
        carry = FinishLine(net, sems, R.s_in, R.so_in, R.fland, R.foland, R.s_own)
        ext = Batch(ext_scatter(net, sems, R.dq_in, R.qland) + ext_scatter(net, sems, R.d0_in, R.zland))
        ext_line = ExtLine(net, sems, R.q_sum, R.z_sum, R.qline, R.zline)
        low = Batch([sems.copy(R.s.at[r, 1], R.dnland.at[3 - r], net.line(r)) for r in (1, 2, 3)])
        peers += [net.line(2), net.line(4 - net.zl * 2 - 1)]
    R.gm[:n] = R.g[...].astype(bf)
    net.greet(peers)
    there.start()
    fetched = [loc.start(R.act.at[i], R.buf.at[pl.ds(i * 2 * n, 2 * n)]) for i in range(2)]
    for src, dst in ((R.pjl_i, R.pj_l), (R.pjs_i, R.pj_s), (R.ext_i, R.ext)):
        loc.start(src, dst)
    if last:
        moved.start()

        @pl.when(jnp.logical_not(net.moves))
        def _():
            R.yr_l[...] = R.y[:nl]
            R.yr_s[...] = R.y[nl:]

    else:
        ext.start()
        carry.start()
        for src, dst in ((R.s_in.at[0], R.s_own), (R.dq_in.at[yx], R.dq_own), (R.d0_in.at[yx], R.d0_own)):
            loc.start(src, dst)
    R.rows[...] = jnp.zeros_like(R.rows)
    R.rows[5:6] = jnp.sum(R.g[...].astype(f32), axis=0, keepdims=True)
    half = n // 2
    wdn2 = lambda: R.wdn[...].reshape(4 * f, d)

    def hidden(at):
        u = mm(R.gm[at], wdn2(), NT)
        R.gu[at] = (u * R.slope[at].astype(f32)).astype(bf)

    hidden(slice(0, half))
    there.wait_recv()
    for c in fetched:
        c.wait()
    for k in range(4):
        for i in range(2):
            t = mm(R.gm[:, k * chunk : (k + 1) * chunk], R.buf[i * 2 * n : (i + 1) * 2 * n], TN)
            t = t.astype(bf)
            R.ddn[k, 2 * i] = t[:, :f]
            R.ddn[k, 2 * i + 1] = t[:, f:]
    big_dn.start()
    fl, fs = R.buf.at[pl.ds(0, 4 * nl)], R.buf.at[pl.ds(4 * nl, 4 * ns)]
    late = [loc.start(R.fl_i, fl), loc.start(R.fs_i, fs)]
    hidden(slice(half, n))
    for i in range(2):
        hidden(slice(n + i * half, n + (i + 1) * half))
    for i in range(2):
        R.out[0, i * half : (i + 1) * half] = mm(
            R.gu[n + i * half : n + (i + 1) * half], R.wup[...], NT
        ).astype(bf)
    back.start()
    for i in range(2):
        R.mine[i * half : (i + 1) * half] = mm(R.gu[i * half : (i + 1) * half], R.wup[...], NT)

    back.wait_recv()
    gn = R.mine[...] + R.got[0].astype(f32)
    hat, inv = norm_rows(R.middle[...])
    gh = gn * R.gain2[...]
    a = jnp.mean(gh, axis=-1, keepdims=True)
    b = jnp.mean(gh * hat, axis=-1, keepdims=True)
    R.gmid[...] = R.g[...].astype(f32) + inv * (gh - a - hat * b)
    R.rows[1:2] = jnp.sum(gn * hat, axis=0, keepdims=True)
    R.rows[3:4] = jnp.sum(gn, axis=0, keepdims=True)
    R.rows[4:5] = jnp.sum(R.gmid[...], axis=0, keepdims=True)
    R.ga[...] = R.gmid[...].astype(bf)
    go = mm(R.ga[...], R.wout[...], NT).astype(bf)
    for m in range(4):
        R.outg[m] = go[:, m * wid : (m + 1) * wid]

    def part(k):
        return ((R.gl, nl, 0), (R.gs, ns, nl))[k]

    def copy(k, m):
        dst, size, at = part(k)
        return send(
            R.outg.at[m, pl.ds(at, size)],
            dst.at[pl.ds(aligned(me * size), size)],
            sems.ssem.at[base + 4 * k + m],
            sems.rsem.at[base + 4 * k + me],
            net.member(m),
        )

    def arrived(k, m):
        dst, size, at = part(k)
        i = base + 4 * k + m
        return send(
            R.outg.at[m, pl.ds(at, size)], dst.at[pl.ds(m * size, size)], sems.ssem.at[i], sems.rsem.at[i], net.member(m)
        )

    for k in (1, 0):
        for m in range(4):
            dst, size, at = part(k)

            @pl.when(me != m)
            def _():
                copy(k, m).start()

            @pl.when(me == m)
            def _():
                dst[m * size : (m + 1) * size] = R.outg[m, at : at + size]

    e = R.att.shape[1] // 2
    other = R.att[:, pl.ds(aligned((1 - net.c) * e, 128), e)]
    R.oself[...] = mm(R.ga[...], other, TN).astype(bf)
    cross.start()
    for k in range(4):
        t = mm(R.n2[:, k * chunk : (k + 1) * chunk], R.gu[...], TN).astype(bf)
        for r in range(4):
            R.dup[k, r] = t[:, r * f : (r + 1) * f]
    big_up.start()
    bup = jnp.sum(R.gu[...].astype(f32), axis=0, keepdims=True)
    for c in range(2):

        @pl.when(net.c == c)
        def _():
            for r in range(4):
                R.rows[pl.ds(16 + (net.z + r) % 4, 1), c * f : (c + 1) * f] = bup[:, r * f : (r + 1) * f]

    own = mm(R.ga[...], R.att[:, pl.ds(aligned(net.c * e, 128), e)], TN)
    cross.wait_recv()
    own = (own + R.olands[...].astype(f32)).astype(bf)
    for k in range(4):
        R.dout[k] = own[k * chunk : (k + 1) * chunk]
    big_out.start()
    if not last:
        late.append(loc.start(R.resid, R.ga))
    done = [id(c) for c in fetched + late]
    for c in loc.copies:
        if id(c) not in done:
            c.wait()
    def add_up(own, land, i):
        for r in range(4):
            t = own[yx, r].astype(f32)
            for k in range(3):
                t = t + land[k, r].astype(f32)
            R.s[r, i] = t.astype(bf)

    def midway(b):
        if b == 2 and not last:
            big_dn.recv()
            add_up(R.ddn, R.rdn, 1)
            low.start()

    for k in (1, 0):
        for m in range(4):

            @pl.when(me != m)
            def _():
                arrived(k, m).wait_recv()

        if k:
            bwd_one(R.pj_s, R.gs, R.os, R.lses, R.cs, R.ds, R.acc, R.kt)
            if not last:
                ext.recv()
                for own_, lands, dst in ((R.dq_own, R.qland, R.q_sum), (R.d0_own, R.zland, R.z_sum)):
                    t = own_[...].astype(f32)
                    for i in range(3):
                        t = t + lands[i].astype(f32)
                    dst[...] = t.astype(bf)
                ext_line.start()
        else:
            bwd_one(R.pj_l, R.gl, R.ol, R.lsel, R.cl, R.dl, R.acc, R.kt, midway)


    def partial(m):
        a = mm(R.dl[pl.ds(aligned(m * nl), nl)], R.ext[...], NT)
        b = mm(R.ds[pl.ds(aligned(m * ns), ns)], R.ext[...], NT)
        return jnp.concatenate([a, b], axis=0)

    back.wait_send()
    to_core = [sems.copy(R.out.at[k], R.got.at[k + 1], net.group(2)) for k in (0, 1)]
    to_chip = sems.copy(R.out.at[2], R.got.at[3], net.group(1))
    R.out[0] = partial(me ^ 3).astype(bf)
    to_core[0].start()
    R.mine[...] = partial(me ^ 1)
    to_core[0].wait_recv()
    R.out[2] = (R.mine[...] + R.got[1].astype(f32)).astype(bf)
    to_chip.start()
    R.out[1] = partial(me ^ 2).astype(bf)
    to_core[1].start()
    R.mine[...] = partial(me)
    nq = R.dq.shape[2]
    for c in late:
        c.wait()
    for k in range(4):
        at = slice(k * chunk, (k + 1) * chunk)
        both = mm(fl[:, at], R.dl[...], TN) + mm(fs[:, at], R.ds[...], TN)
        R.dq[k] = both[:, :nq].astype(bf)
        R.d0[k] = both[:, nq:].astype(bf)
    bsum = jnp.sum(R.dl[...].astype(f32), axis=0, keepdims=True) + jnp.sum(
        R.ds[...].astype(f32), axis=0, keepdims=True
    )
    R.rows[pl.ds(8 + me, 1), :wid] = bsum[:, :wid]
    R.rows[pl.ds(12 + me, 1), :wid] = bsum[:, 2 * wid : 3 * wid]
    R.rows[8:9, :HD] += bsum[:, nq : nq + HD]
    hat, inv = norm_rows(R.resid[...] if last else R.ga[...].astype(f32))
    to_core[1].wait_recv()
    to_chip.wait_recv()
    grad = R.mine[...] + R.got[2].astype(f32) + R.got[3].astype(f32)
    gh = grad * R.gain1[...]
    a = jnp.mean(gh, axis=-1, keepdims=True)
    b = jnp.mean(gh * hat, axis=-1, keepdims=True)
    R.g_new[...] = (R.gmid[...] + inv * (gh - a - hat * b)).astype(R.g_new.dtype)
    R.rows[0:1] = jnp.sum(grad * hat, axis=0, keepdims=True)
    R.rows[2:3] = jnp.sum(grad, axis=0, keepdims=True)
    for c in to_core + [to_chip, there, cross]:
        c.wait_send()
    for m in range(4):

        @pl.when(me != m)
        def _():
            for k in range(2):
                copy(k, m).wait_send()

    if last:
        moved.end()
    else:
        carry.finish(R.f_out, R.fo_out)
        ext.sent()
        ext_line.finish(R.q_out, R.z_out)
        low.recv()
        t = R.s[0, 1].astype(f32)
        for k in range(3):
            t = t + R.dnland[k].astype(f32)
        R.dn_out[...] = t.astype(bf)
        low.sent()

    if last:
        big_dn.recv()
        add_up(R.ddn, R.rdn, 1)
    big_up.recv()
    add_up(R.dup, R.rup, 0)
    big_out.recv()
    t = R.dout[yx].astype(f32)
    for k in range(3):
        t = t + R.rout[k].astype(f32)
    for i in range(2):
        R.so[i] = t[:, i * wid : (i + 1) * wid].astype(bf)
    big_dn.sent()
    big_up.sent()
    big_out.sent()


class ExtLine:
    def __init__(self, net, sems, q, z, qline, zline):
        self.net, self.q, self.z, self.qline, self.zline = net, q, z, qline, zline
        self.qsend = Batch([sems.copy(q, qline, net.line(2))], net.moves)
        self.stays = jnp.logical_not(net.moves)
        self.zsend = [sems.copy(z, zline.at[r - 1], net.line(r)) for r in (1, 2, 3)]

    def start(self):
        self.qsend.start()
        for r in (1, 2, 3):
            pl.when(self.net.z == 4 - r)(self.zsend[r - 1].start)

    def finish(self, q_out, z_out):
        f32 = jnp.float32
        q_out[...] = self.q[...].astype(q_out.dtype)
        z_out[...] = self.z[...].astype(z_out.dtype)

        @pl.when(self.stays)
        def _():
            self.qsend.copies[0].wait_recv()
            q_out[...] = (self.q[...].astype(f32) + self.qline[...].astype(f32)).astype(q_out.dtype)

        @pl.when(self.net.z == 0)
        def _():
            t = self.z[...].astype(f32)
            for r in (1, 2, 3):
                self.zsend[r - 1].wait_recv()
                t = t + self.zline[r - 1].astype(f32)
            z_out[...] = t.astype(z_out.dtype)

        self.qsend.sent()
        for r in (1, 2, 3):
            pl.when(self.net.z == 4 - r)(self.zsend[r - 1].wait_send)


def tail_x(axes, R):
    dims = axes[:-2]
    net, sems = Net(dims), Sems(R.ssem, R.rsem)
    f32, bf = jnp.float32, jnp.bfloat16
    moved = Batch([sems.copy(R.dx, R.dxr, net.partner())], net.moves)
    line = FinishLine(net, sems, R.s.at[:, pl.ds(0, 1)], R.so, R.land, R.oland)
    ext = Batch(ext_scatter(net, sems, R.dq, R.qland) + ext_scatter(net, sems, R.d0, R.zland))
    nv = len(axes)
    rounds = [{ax: 1 - lax.axis_index(ax)} for ax in axes[::-1]]
    steps = [sems.copy(R.vland.at[i], R.vland.at[nv + 1 + i], peer) for i, peer in enumerate(rounds)]
    ext_line = ExtLine(net, sems, R.q_sum, R.z_sum, R.qline, R.zline)
    qrecv = jnp.logical_not(net.moves)
    cross = Batch(
        [sems.copy(R.fself, R.fland, net.group(2)), sems.copy(R.zself, R.zlands, net.group(2))]
    )
    owned = Batch(
        [sems.copy(R.oself, R.olands, net.group(2)), sems.copy(R.qself, R.qlands, net.group(2))],
        None,
    )
    net.greet(
        [net.partner(), net.group(2)]
        + [net.line(r) for r in (1, 2, 3)]
        + [net.plane(e) for e in (1, 2, 3)]
    )
    ext.start()
    line.start()
    nr = R.rows0.shape[0]
    R.vland[0, :nr] = R.rows0[...]
    R.vland[0, nr:] = R.rows1[...]
    R.vland[0, 6:7] = jnp.broadcast_to(R.share0[:1, :1], (1, R.rows0.shape[1]))
    R.vland[0, nr + 6 : nr + 7] = jnp.broadcast_to(R.share1[:1, :1], (1, R.rows0.shape[1]))

    def step(i):
        steps[i].wait()
        R.vland[i + 1] = R.vland[i] + R.vland[nv + 1 + i]
        if i + 1 < nv:
            steps[i + 1].start()

    steps[0].start()
    step(0)
    step(1)
    ext.recv()
    yx = net.yx
    for own, lands, dst in ((R.dq, R.qland, R.q_sum), (R.d0, R.zland, R.z_sum)):
        t = own[yx].astype(f32)
        for e in range(3):
            t = t + lands[e].astype(f32)
        dst[...] = t.astype(bf)
    ext_line.start()
    moved.start()
    step(2)
    step(3)
    step(4)
    nl = R.dx_l.shape[0]
    half = R.f0.shape[1] // 2
    theirs = pl.ds(aligned((1 - net.c) * half), half)
    ours = pl.ds(aligned(net.c * half), half)

    @pl.when(qrecv)
    def _():
        R.dx_l[...] = R.dx[:nl].astype(f32)
        R.dx_s[...] = R.dx[nl:].astype(f32)

    wq = R.gqkv.shape[3]

    def put(l, v):
        for i in range(3):
            R.gqkv[l, i] = v[:, i * wq : (i + 1) * wq]

    ext_line.finish(R.q0, R.z0)

    @pl.when(qrecv)
    def _():
        for l, q in ((0, R.q0), (1, R.q1)):
            R.qself[l] = q[theirs].astype(bf)
            put(l, q[ours].astype(f32))

    tot = R.vland.at[nv]
    for l in range(2):
        at = l * nr
        for i in range(2):
            R.g_gain[l, i : i + 1] = tot[at + i : at + i + 1]
            R.g_bias[l, i : i + 1] = tot[at + 2 + i : at + 3 + i]
            R.g_bqv[l, i : i + 1] = tot[pl.ds(at + 8 + 4 * i + net.z, 1), : R.g_bqv.shape[2]]
        R.g_bout[l : l + 1] = tot[at + 4 : at + 5]
        R.g_bdown[l : l + 1] = tot[at + 5 : at + 6]
        R.g_bup[l : l + 1] = tot[pl.ds(at + 16 + net.z, 1)]
        R.shares[l : l + 1] = tot[at + 6 : at + 7, :128] / (32 * R.dx.shape[0])
    line.finish(R.f0, R.fo0)

    @pl.when(qrecv)
    def _():
        for l, fo in ((0, R.fo0), (1, R.fo1)):
            R.oself[l] = fo[theirs].astype(bf)
            R.gout[l] = jnp.transpose(fo[ours].astype(f32))
        for c in owned.copies:
            c.start()

    for l, fs in ((0, (R.f0.at[0], R.dn0)), (1, (R.f1.at[0], R.f1.at[1]))):
        for i in range(2):
            R.fself[l, i] = fs[i][theirs].astype(bf)
    for l, z in ((0, R.z0), (1, R.z1)):
        R.zself[l] = z[theirs].astype(bf)
    cross.start()
    n = R.f0.shape[2]
    for c in range(2):

        @pl.when(net.c == c)
        def _():
            for l, fs in ((0, (R.f0.at[0], R.dn0)), (1, (R.f1.at[0], R.f1.at[1]))):
                R.gup[l, :, c * n : (c + 1) * n] = fs[0][ours].astype(f32)
                R.gdn[l, :, c * n : (c + 1) * n] = fs[1][ours].astype(f32)

    cross.recv()
    for c in range(2):

        @pl.when(net.c != c)
        def _():
            for l in range(2):
                R.gup[l, :, c * n : (c + 1) * n] = R.fland[l, 0].astype(f32)
                R.gdn[l, :, c * n : (c + 1) * n] = R.fland[l, 1].astype(f32)

    @pl.when(net.moves)
    def _():
        for c in owned.copies:
            c.wait_recv()
        for l in range(2):
            put(l, R.qlands[l].astype(f32))
            R.gout[l] = jnp.transpose(R.olands[l].astype(f32))

    @pl.when(net.z == 0)
    def _():
        wid = R.gout.shape[1]
        for l, z in ((0, R.z0), (1, R.z1)):
            t = z[ours].astype(f32) + R.zlands[l].astype(f32)
            R.gqkv[l, 0, :, :HD] += t[:, :HD]
            R.gqkv[l, 1, :, :HD] += t[:, HD:]

    moved.recv()

    @pl.when(net.moves)
    def _():
        R.dx_l[...] = R.dxr[:nl].astype(f32)
        R.dx_s[...] = R.dxr[nl:].astype(f32)

    pl.when(qrecv)(lambda: [c.wait_send() for c in owned.copies] and None)
    cross.sent()
    ext.sent()
    moved.sent()


def results_k(*refs):
    k = len(refs) // 2
    sem = refs[-1]
    copies = [pltpu.make_async_copy(refs[i], refs[k + i], sem.at[i]) for i in range(k)]
    for copy in copies:
        copy.start()
    for copy in copies:
        copy.wait()


def results(arrays):
    return pl.pallas_call(
        results_k,
        out_shape=tuple(jax.ShapeDtypeStruct(a.shape, a.dtype) for a in arrays),
        in_specs=[ANY] * len(arrays),
        out_specs=(VMEM,) * len(arrays),
        scratch_shapes=[DMA((len(arrays),))],
        compiler_params=pltpu.CompilerParams(vmem_limit_bytes=60 * 1024 * 1024),
        name="results_k",
    )(*arrays)


def run(kernel, static, ins, outs, scratch, ident, name, flops):
    names = list(ins) + list(outs) + list(scratch)

    def body_of(*refs):
        kernel(*static, types.SimpleNamespace(**dict(zip(names, refs))))

    res = pl.pallas_call(
        body_of,
        out_shape=tuple(jax.ShapeDtypeStruct(tuple(s), t) for s, t, _ in outs.values()),
        in_specs=[VMEM if v else ANY for _, v in ins.values()],
        out_specs=tuple(VMEM if v else ANY for _, _, v in outs.values()),
        scratch_shapes=list(scratch.values()),
        compiler_params=pltpu.CompilerParams(
            vmem_limit_bytes=60 * 1024 * 1024, collective_id=ident, has_side_effects=True
        ),
        cost_estimate=pl.CostEstimate(flops=flops, bytes_accessed=10**7, transcendentals=10**6),
        name=name,
    )(*[a for a, _ in ins.values()])
    return types.SimpleNamespace(**dict(zip(outs, res)))


def fast_body(
    dims, x_long, x_short, dy_long, dy_short, ln_gain, ln_bias, w_qkv, b_qv, w_out, b_out, w_up, b_up, w_down, b_down, threshold
):
    bf, f32 = jnp.bfloat16, jnp.float32
    layers, d = w_qkv.shape[0], w_qkv.shape[1]
    wid, ffq = w_qkv.shape[3], w_up.shape[2]
    rl, rs = x_long.shape[1], x_short.shape[1]
    n = rl + rs
    sl, ss = 4 * rl, 4 * rs
    nq, nx, n0 = 3 * wid, 3 * wid + 2 * HD, 2 * HD
    nh = wid // HD
    f = ffq // 2
    ff = 4 * f
    chunk, part = d // 4, f // 4
    half = chunk // 2
    net = Net(dims)
    axes = dims + ("zh", "zl")
    vm = lambda *s: pltpu.VMEM(tuple(s), bf)
    vf = lambda *s: pltpu.VMEM(tuple(s), f32)
    sem2 = lambda k: dict(ssem=DMA((k,)), rsem=DMA((k,)))

    wqs = [w_qkv[l].reshape(d, nq) for l in range(layers)]
    w0s = [w_qkv[l][:, :2, :HD].reshape(d, n0) for l in range(layers)]
    flat = jnp.concatenate([b_up.reshape(-1), b_qv.reshape(-1)])
    flat = jnp.pad(flat, (0, -flat.shape[0] % 4096)).reshape(16, -1)
    share_rows = wid // 8
    wo = lax.dynamic_slice_in_dim(w_out, (4 * net.y + 2 * net.x + net.c) * share_rows, share_rows, 1)
    wo = [lax.all_gather(wo[l], ("zh", "zl") + dims, axis=0, tiled=True) for l in range(layers)]

    lands = dict(qland=vm(4, chunk, nq), zland=vm(4, chunk, n0))
    P0 = run(
        first_x,
        (dims,),
        dict(xl=(x_long[0], 1), xs=(x_short[0], 1), wq=(wqs[0], 1), w0=(w0s[0], 1), small=(flat, 1), w_up=(w_up, 0), w_down=(w_down, 0)),
        dict(
            xr=((n, d), bf, 1), ext=((d, nx), bf, 1), smalls=((4,) + flat.shape, bf, 1),
            zup=((chunk, 3 * f), bf, 0), zdn=((3, part, d), bf, 0),
        ),
        dict(**lands, **sem2(32)),
        1,
        "first_x",
        10**9,
    )
    n_up = layers * ffq
    smalls = P0.smalls.reshape(4, -1)
    rel_bup = smalls[:, :n_up].reshape(4, layers, 2, f).astype(f32)
    rel_bup = lax.dynamic_index_in_dim(rel_bup, net.c, 2, keepdims=False)
    rel_bup = jnp.swapaxes(rel_bup, 0, 1).reshape(layers, ff)
    rel_bqv = smalls[:, n_up : n_up + layers * 2 * wid].reshape(4, layers, 2, wid).astype(f32)
    my_bqv = lax.dynamic_index_in_dim(rel_bqv, (net.me - net.z) % 4, 0, keepdims=False)
    zero_bq = lax.dynamic_index_in_dim(rel_bqv, (0 - net.z) % 4, 0, keepdims=False)[:, 0, :HD]
    none = jnp.zeros((layers, wid), f32)
    bias = jnp.concatenate([my_bqv[:, 0], none, my_bqv[:, 1], zero_bq, none[:, :HD]], axis=1)
    gain, shift = ln_gain.astype(f32), ln_bias.astype(f32)
    bo, bd = b_out.astype(f32), b_down.astype(f32)
    limits = (threshold.astype(f32) / 64.0)[:, None]

    resid, zup, zdn = P0.xr, P0.zup, P0.zdn
    exts = [P0.ext]
    saved = []
    for l in range(layers):
        first, last = l == 0, l == layers - 1
        ins = dict(
            resid=(resid, 1), gain1=(gain[l, :1], 1), shift1=(shift[l, :1], 1), gain2=(gain[l, 1:], 1), shift2=(shift[l, 1:], 1),
            ext=(exts[l], 1), bias=(bias[l : l + 1], 1), w_up=(w_up, 0), w_down=(w_down, 0), zup=(zup, 1), zdn=(zdn, 1),
            wout=(wo[l], 1), bout=(bo[l : l + 1], 1), bup=(rel_bup[l : l + 1], 1), bdown=(bd[l : l + 1], 1), limit=(limits[l : l + 1], 1),
        )
        outs = dict(
            fl_o=((sl, d), bf, 0), fs_o=((ss, d), bf, 0), pjl_o=((sl, nx), bf, 0), pjs_o=((ss, nx), bf, 0),
            att=((n, 4 * wid), bf, 1), ol=((sl, wid), bf, 1), os=((ss, wid), bf, 1),
            lsel=((8, sl), f32, 1), lses=((8, ss), f32, 1), cl=((8, sl), f32, 1), cs=((8, ss), f32, 1),
            wup_o=((d, ff), bf, 0), wdn_o=((4, f, d), bf, 0), middle=((n, d), f32, 1), n2=((2 * n, d), bf, 1),
            act_o=((2, 2 * n, 2 * f), bf, 0), slope_o=((2 * n, ff), bf, 0), new=((n, d), f32, 1), share=((8, 128), f32, 1),
        )
        scratch = dict(
            fl=vm(sl, d), fs=vm(ss, d), pj_l=vm(sl, nx), pj_s=vm(ss, nx), wup=vm(d, ff), wdn=vm(4, f, d),
            act=vm(2, 2 * n, 2 * f), slope=vm(2 * n, ff), land=vm(4, n, wid), out=vm(n, d), got=vm(n, d), lsem=DMA((24,)),
            **sem2(48),
        )
        if first:
            ins.update(wq=(wqs[1], 1), w0=(w0s[1], 1))
            outs.update(ext_next=((d, nx), bf, 1), zup_next=((chunk, 3 * f), bf, 0), zdn_next=((3, part, d), bf, 0))
            scratch.update(lands)
        else:
            ins.update(dl=(dy_long[0], 1), ds=(dy_short[0], 1))
            outs.update(dyr=((n, d), bf, 1))
        if last:
            outs.update(y=((n, d), bf, 1))
        A = run(forward_x, (dims, first, last), ins, outs, scratch, 2 + l, "forward_x", 10**10)
        A.resid = resid
        saved.append(A)
        resid = A.new
        if first:
            exts.append(A.ext_next)
            zup, zdn = A.zup_next, A.zdn_next

    g = saved[-1].dyr
    back = [None] * layers
    B = None
    for l in reversed(range(layers)):
        A = saved[l]
        last = l == layers - 1
        ins = dict(
            g=(g, 1), att=(A.att, 1), wout=(wo[l], 1), gain1=(gain[l, :1], 1), gain2=(gain[l, 1:], 1), wup=(A.wup_o, 1), wdn=(A.wdn_o, 1),
            middle=(A.middle, 1), n2=(A.n2, 1), act=(A.act_o, 0), slope=(A.slope_o, 1), resid=(A.resid, int(last)),
            pjl_i=(A.pjl_o, 0), pjs_i=(A.pjs_o, 0), ext_i=(exts[l], 0), fl_i=(A.fl_o, 0), fs_i=(A.fs_o, 0),
            ol=(A.ol, 1), os=(A.os, 1), lsel=(A.lsel, 1), lses=(A.lses, 1), cl=(A.cl, 1), cs=(A.cs, 1),
        )
        outs = dict(
            g_new=((n, d), f32 if l else bf, 1), rows=((24, d), f32, 1), dq=((4, chunk, nq), bf, 1), d0=((4, chunk, n0), bf, 1),
            s=((4, 2, chunk, f), bf, 1), so=((2, chunk, wid), bf, 1),
        )
        scratch = dict(
            gm=vm(2 * n, d), gu=vm(2 * n, ff), mine=vf(n, d), out=vm(3, n, d), got=vm(4, n, d), gmid=vf(n, d), ga=vm(n, d),
            oself=vm(d, 2 * wid), olands=vm(d, 2 * wid), dup=vm(4, 4, chunk, f), ddn=vm(4, 4, chunk, f), dout=vm(4, chunk, 2 * wid),
            rup=vm(3, 4, chunk, f), rdn=vm(3, 4, chunk, f), rout=vm(3, chunk, 2 * wid),
            outg=vm(4, n, wid), gl=vm(sl, wid), gs=vm(ss, wid), pj_l=vm(sl, nx), pj_s=vm(ss, nx), ext=vm(d, nx),
            buf=vm(sl + ss, d), dl=vm(sl, nx), ds=vm(ss, nx), acc=vf(2 * nh + 1, sl, HD), kt=vm(nh + 1, HD, sl),
            lsem=DMA((12,)), **sem2(48),
        )
        if last:
            ins.update(y=(A.y, 1))
            outs.update(yr_l=((rl, d), bf, 1), yr_s=((rs, d), bf, 1))
        else:
            ins.update(s_in=(B.s, 0), so_in=(B.so, 1), dq_in=(B.dq, 0), d0_in=(B.d0, 0))
            outs.update(
                dn_out=((chunk, f), bf, 1), f_out=((2, chunk, f), bf, 1), fo_out=((chunk, wid), bf, 1), q_out=((chunk, nq), bf, 1), z_out=((chunk, n0), bf, 1)
            )
            scratch.update(
                q_sum=vm(chunk, nq), z_sum=vm(chunk, n0), qline=vm(chunk, nq), zline=vm(3, chunk, n0), dnland=vm(3, chunk, f),
                s_own=vm(2, chunk, f), dq_own=vm(chunk, nq), d0_own=vm(chunk, n0), fland=vm(3, 2, chunk, f), foland=vm(3, chunk, wid), qland=vm(3, chunk, nq), zland=vm(3, chunk, n0))
        B = run(backward_x, (dims, last), ins, outs, scratch, 6 + l, "backward_x", 2 * 10**10)
        back[l] = B
        g = B.g_new
        if last:
            y_l, y_s = B.yr_l, B.yr_s

    nv = len(axes)
    T = run(
        tail_x,
        (axes,),
        dict(
            s=(B.s, 1), so=(B.so, 1), dq=(B.dq, 1), d0=(B.d0, 1), f1=(B.f_out, 1), fo1=(B.fo_out, 1), q1=(B.q_out, 1), z1=(B.z_out, 1),
            rows0=(back[0].rows, 1), dn0=(B.dn_out, 1), rows1=(back[1].rows, 1), share0=(saved[0].share, 1), share1=(saved[1].share, 1), dx=(g, 1),
        ),
        dict(
            gup=((2, half, ffq), f32, 1), gdn=((2, half, ffq), f32, 1), gout=((2, wid, half), f32, 1), gqkv=((2, 3, half, wid), f32, 1),
            dx_l=((rl, d), f32, 1), dx_s=((rs, d), f32, 1), g_gain=((2, 2, d), f32, 1), g_bias=((2, 2, d), f32, 1),
            g_bqv=((2, 2, wid), f32, 1), g_bout=((2, d), f32, 1), g_bdown=((2, d), f32, 1), g_bup=((2, ffq), f32, 1),
            shares=((2, 128), f32, 1),
        ),
        dict(
            land=vm(3, 1, chunk, f), oland=vm(3, chunk, wid), f0=vf(1, chunk, f), fo0=vf(chunk, wid), q0=vf(chunk, nq), z0=vf(chunk, n0),
            qland=vm(3, chunk, nq), zland=vm(3, chunk, n0), q_sum=vm(chunk, nq), z_sum=vm(chunk, n0), qline=vm(chunk, nq),
            zline=vm(3, chunk, n0), fself=vm(2, 2, half, f), fland=vm(2, 2, half, f), oself=vm(2, half, wid),
            olands=vm(2, half, wid), qself=vm(2, half, nq), qlands=vm(2, half, nq), zself=vm(2, half, n0), zlands=vm(2, half, n0),
            vland=vf(2 * nv + 1, 48, d), dxr=vm(n, d), **sem2(32),
        ),
        10,
        "tail_x",
        10**9,
    )
    done = results(
        (
            y_l, y_s, T.dx_l, T.dx_s, T.g_gain, T.g_bias, T.gqkv, T.g_bqv, T.gout, T.g_bout, T.gup, T.g_bup, T.gdn, T.g_bdown
        )
    )
    y_l, y_s, dx_l, dx_s, g_gain, g_bias, gqkv, g_bqv, gout, g_bout, gup, g_bup, gdn, g_bdown = done
    return (
        y_l[None], y_s[None], dx_l[None], dx_s[None], g_gain, g_bias, jnp.swapaxes(gqkv, 1, 2), g_bqv, gout, g_bout, gup, g_bup,
        jnp.swapaxes(gdn, 1, 2), g_bdown, T.shares[:, 0],
    )


def solution(mesh):
    dp, mp = mesh.shape["dp"], mesh.shape["mp"]
    bits = dp.bit_length() - 1
    dims = tuple(f"d{i}" for i in range(bits))
    fine = Mesh(mesh.devices.reshape((2,) * bits + (2, mp // 2)), dims + ("zh", "zl"))
    z = ("zh", "zl")
    in_specs = (
        P(dims, z, None), P(dims, z, None), P(dims, z, None), P(dims, z, None),
        P(), P(), P(None, None, None, z), P(None, None, z), P(None, z, None), P(),
        P(None, None, z), P(None, z), P(None, z, None), P(), P(),
    )
    out_specs = (
        P(dims, z, None), P(dims, z, None), P(dims, z, None), P(dims, z, None),
        P(), P(), P(None, dims, None, z), P(None, None, z), P(None, z, dims), P(),
        P(None, dims, z), P(None, z), P(None, z, dims), P(), P(),
    )
    run = functools.partial(fast_body, dims) if dp == 8 else functools.partial(body, dims, dp, mp)
    return jax.shard_map(
        run, mesh=fine, in_specs=in_specs, out_specs=out_specs, check_vma=False
    )
```
